32 devices in a mesh: dp: 8 (over y, x, core), tensor: 4 (over z).
Axes of the slice: x: 2, y: 2, z: 4, core: 2. Of those that a mesh axis runs over, the one named last changes fastest.
Arguments:
- block_input: float32 [8192, 2048], P(('dp', 'tensor')), may hold values from -6 to 6
- out_grad: float32 [8192, 2048], P(('dp', 'tensor')), may hold values from -6 to 6
- seq_lengths: int32 [8, 4], P('dp'), may hold values from 0 to 1024, as said below
- in_weight: float32 [2048, 7, 2048], P('dp', None, 'tensor'), may hold values from -0.125 to 0.125
- down_weight: float32 [5, 2048, 2048], P(None, 'tensor', 'dp'), may hold values from -0.35355339 to 0.35355339
- column_bias: float32 [7, 2048], P(None, ('tensor', 'dp')), may hold values from -1.75 to 1.75
- vector_params: float32 [3, 2048], P(None, 'dp'), may hold values from -1.2 to 1.4
- in_first: float32 [2048, 7, 2048], P('dp', None, 'tensor'), may hold values from -40 to 40
- in_second: float32 [2048, 7, 2048], P('dp', None, 'tensor'), may hold values from 106.496 to 1720.32
- down_first: float32 [5, 2048, 2048], P(None, 'tensor', 'dp'), may hold values from -24 to 24
- down_second: float32 [5, 2048, 2048], P(None, 'tensor', 'dp'), may hold values from 34.4064 to 548.864
- bias_first: float32 [7, 2048], P(None, ('tensor', 'dp')), may hold values from -40 to 40
- bias_second: float32 [7, 2048], P(None, ('tensor', 'dp')), may hold values from 106.496 to 1720.32
- vector_first: float32 [3, 2048], P(None, 'dp'), may hold values from -96 to 96
- vector_second: float32 [3, 2048], P(None, 'dp'), may hold values from 483.328 to 7782.4
Outputs:
- block_out: float32 [8192, 2048], P(('dp', 'tensor'))
- input_grad: float32 [8192, 2048], P(('dp', 'tensor'))
- in_weight_new: float32 [2048, 7, 2048], P('dp', None, 'tensor')
- in_first_new: float32 [2048, 7, 2048], P('dp', None, 'tensor')
- in_second_new: float32 [2048, 7, 2048], P('dp', None, 'tensor')
- down_weight_new: float32 [5, 2048, 2048], P(None, 'tensor', 'dp')
- down_first_new: float32 [5, 2048, 2048], P(None, 'tensor', 'dp')
- down_second_new: float32 [5, 2048, 2048], P(None, 'tensor', 'dp')
- bias_new: float32 [7, 2048], P(None, ('tensor', 'dp'))
- bias_first_new: float32 [7, 2048], P(None, ('tensor', 'dp'))
- bias_second_new: float32 [7, 2048], P(None, ('tensor', 'dp'))
- vector_new: float32 [3, 2048], P(None, 'dp')
- vector_first_new: float32 [3, 2048], P(None, 'dp')
- vector_second_new: float32 [3, 2048], P(None, 'dp')
The draws below stay inside these ranges and needn't reach their ends.
Inputs may be any that keep to these rules, and one draw needn't show every extreme that they name: `seq_lengths`: row i lists, in order, the lengths of the sequences packed from the first of data shard i's 1024 slots; a zero is an unused entry and follows all used ones; a row holds one to three sequences, each of 256 tokens or more, and sums to 512 or more, the slots after its sum being padding; in every draw some shard holds one sequence of 1024 tokens.
All inputs are finite; a program needn't handle non-finite values.
Results may differ from the reference program's by a relative error of at most 0.0098.
Values may be sent and summed in bfloat16 or wider, within the bound.
A program may use at most 256 MiB of HBM per device.

```python
import math
from functools import partial
import jax
import jax.numpy as jnp
from jax import lax

D = 2048
HEADS = 32
HEAD = 64
ROT = 32
FF = 8192
SEQS = 4
STEP = 8
TOK_GRP = 1024
TOKENS = 8192
N_DP = 8


def draw_seq_lengths(key, part):
    key = jax.random.fold_in(key, 5)
    key_total, key_full, key_count, key_cuts = jax.random.split(key, 4)
    least = TOK_GRP // 4
    totals = jax.random.randint(key_total, (N_DP,), TOK_GRP // 2, TOK_GRP + 1).astype(jnp.int32)
    most_count = jnp.minimum(3, totals // least).astype(jnp.int32)
    counts = (1 + jax.random.randint(key_count, (N_DP,), 0, 1024) % most_count).astype(jnp.int32)
    spare = (totals - counts * least).astype(jnp.int32)
    raw_cuts = jax.random.randint(key_cuts, (N_DP, SEQS - 1), 0, 1 << 20).astype(jnp.int32)
    cut_points = jnp.sort(raw_cuts % (spare[:, None] + 1), axis=1).astype(jnp.int32)
    entry = jnp.arange(SEQS - 1, dtype=jnp.int32)[None, :]
    cut_points = jnp.where(entry < counts[:, None] - 1, cut_points, spare[:, None]).astype(jnp.int32)
    bounds = jnp.concatenate([jnp.zeros((N_DP, 1), jnp.int32), cut_points, spare[:, None]], axis=1)
    pieces = bounds[:, 1:] - bounds[:, :-1]
    used = (jnp.arange(SEQS, dtype=jnp.int32)[None, :] < counts[:, None]).astype(jnp.int32)
    lengths = (pieces + least * used).astype(jnp.int32)
    full_shard = jax.random.randint(key_full, (), 0, N_DP)
    single = jnp.concatenate([jnp.full((1,), TOK_GRP, jnp.int32), jnp.zeros((SEQS - 1,), jnp.int32)])
    chosen = (jnp.arange(N_DP) == full_shard)[:, None]
    return jnp.where(chosen, single[None, :], lengths).astype(jnp.int32)


def draw_down_weight(key, part):
    key = jax.random.fold_in(key, 7)
    array_shape = (1 + FF // D, D, D)
    base_draw = jax.random.truncated_normal(key, -4.0, 4.0, array_shape, jnp.float32)
    factor = jnp.where(jnp.arange(array_shape[0]) == 0, 4.0, 0.7).astype(jnp.float32)[:, None, None]
    return base_draw * factor * D ** (-0.5)


def draw_vector_params(key, part):
    key = jax.random.fold_in(key, 9)
    base_draw = jax.random.truncated_normal(key, -4.0, 4.0, (3, D), jnp.float32)
    gain_row = 1.0 + 0.1 * base_draw[0:1]
    bias_rows = 0.3 * base_draw[1:]
    return jnp.concatenate([gain_row, bias_rows], axis=0)


def block_scale(stream_key, shape, cuts, low, largest):
    gain = 1.0
    for dim, shards_of in cuts:
        draws = jax.random.uniform(jax.random.fold_in(jax.random.fold_in(stream_key, 6), dim), (shards_of,), jnp.float32, low / len(cuts), largest / len(cuts))
        gain = gain * jnp.repeat(jnp.exp(draws), shape[dim] // shards_of).reshape((-1,) + (1,) * (len(shape) - 1 - dim))
    return gain


def scatter_about(rng, shape, deviation, bound, cuts=(), kind=jnp.bfloat16):
    loudness = block_scale(rng, shape, cuts, -0.22, 0.18) if cuts else 1.0
    drawn = jax.random.normal(rng, shape, jnp.float32) * deviation * loudness
    return jnp.minimum(jnp.maximum(drawn, -bound), bound).astype(kind)


def setup_inputs(seed: int = 0) -> dict:
    key_list = jax.random.split(jax.random.key(seed), 16)
    return {
        "block_input": scatter_about(key_list[0], (TOKENS, D), 1.0, 6.0, ((0, 32),), jnp.float32),
        "out_grad": scatter_about(key_list[1], (TOKENS, D), 1.0, 6.0, ((0, 32),), jnp.float32),
        "seq_lengths": draw_seq_lengths(jax.random.fold_in(key_list[15], 71), 0),
        "in_weight": scatter_about(key_list[3], (D, 3 + FF // D, D), D ** -0.5, 0.125, ((0, 8), (2, 4)), jnp.float32),
        "down_weight": draw_down_weight(jax.random.fold_in(key_list[15], 71), 0),
        "column_bias": scatter_about(key_list[5], (3 + FF // D, D), 0.3, 1.75, ((1, 32),), jnp.float32),
        "vector_params": draw_vector_params(jax.random.fold_in(key_list[15], 71), 0),
        "in_first": scatter_about(key_list[7], (D, 3 + FF // D, D), (0.078 * TOKENS ** 0.5), 40.0, ((0, 8), (2, 4)), jnp.float32),
        "in_second": jnp.clip(jnp.exp(math.log(1720.32) - 2.7821581 * jax.random.uniform(key_list[8], (D, 3 + FF // D, D), jnp.float32) ** block_scale(key_list[8], (D, 3 + FF // D, D), ((0, 8), (2, 4)), -0.2, 0.2)), 106.496, 1720.32),
        "down_first": scatter_about(key_list[9], (1 + FF // D, D, D), (0.044 * TOKENS ** 0.5), 24.0, ((1, 4), (2, 8)), jnp.float32),
        "down_second": jnp.clip(jnp.exp(math.log(548.864) - 2.7696082 * jax.random.uniform(key_list[10], (1 + FF // D, D, D), jnp.float32) ** block_scale(key_list[10], (1 + FF // D, D, D), ((1, 4), (2, 8)), -0.2, 0.2)), 34.4064, 548.864),
        "bias_first": scatter_about(key_list[11], (3 + FF // D, D), (0.078 * TOKENS ** 0.5), 40.0, ((1, 32),), jnp.float32),
        "bias_second": jnp.clip(jnp.exp(math.log(1720.32) - 2.7821581 * jax.random.uniform(key_list[12], (3 + FF // D, D), jnp.float32) ** block_scale(key_list[12], (3 + FF // D, D), ((1, 32),), -0.2, 0.2)), 106.496, 1720.32),
        "vector_first": scatter_about(key_list[13], (3, D), (0.167 * TOKENS ** 0.5), 96.0, ((1, 8),), jnp.float32),
        "vector_second": jnp.clip(jnp.exp(math.log(7782.4) - 2.7789245 * jax.random.uniform(key_list[14], (3, D), jnp.float32) ** block_scale(key_list[14], (3, D), ((1, 8),), -0.2, 0.2)), 483.328, 7782.4),
    }


@jax.custom_vjp
def low(v):
    return lax.optimization_barrier(v.astype(jnp.bfloat16)).astype(jnp.float32)

@jax.custom_vjp
def low_back(v):
    return v

def low_keep(v):
    return (low(v), None)

def low_pass(kept, grad):
    return (grad,)

def back_keep(v):
    return (v, None)

def back_low(kept, grad):
    return (low(grad),)
low.defvjp(low_keep, low_pass)
low_back.defvjp(back_keep, back_low)
norm_eps = 1e-05
beta_first = 0.9
beta_second = 0.95
adam_eps = 1e-08
masked_score = -1000000000.0
rate_in = 0.02
rate_down = 0.05
rate_vector = 0.2
weight_decay = 0.1
highest = lax.Precision.HIGHEST

def layout(lengths, group_size):
    seq_ends = jnp.cumsum(lengths).astype(jnp.int32)
    places = jnp.arange(group_size, dtype=jnp.int32)
    segment = lax.optimization_barrier(jnp.sum((places[:, None] >= seq_ends[None, :]).astype(jnp.int32), axis=1)).astype(jnp.int32)
    starts = jnp.concatenate([jnp.zeros((1,), jnp.int32), seq_ends])
    picked = segment[:, None] == jnp.arange(lengths.shape[0] + 1, dtype=jnp.int32)[None, :]
    seq_begin = lax.optimization_barrier(jnp.sum(jnp.where(picked, starts[None, :], 0), axis=1)).astype(jnp.int32)
    position = places - seq_begin
    live_mask = (segment < lengths.shape[0]).astype(jnp.int32)
    return (segment, position, live_mask)

def rotary_tables(position):
    half_rot = ROT // 2
    frequency = 10000.0 ** (-2.0 * jnp.arange(half_rot, dtype=jnp.float32) / ROT)
    angles = position.astype(jnp.float32)[:, None] * frequency[None, :]
    return (jnp.cos(angles)[:, None, :], jnp.sin(angles)[:, None, :])

def rotate(values, cosine, sine_table):
    half_rot = ROT // 2
    first_half = values[..., :half_rot]
    second_half = values[..., half_rot:ROT]
    return jnp.concatenate([first_half * cosine - second_half * sine_table, second_half * cosine + first_half * sine_table, values[..., ROT:]], axis=-1)

def head_attention(allowed, queries, key_rows, values):
    scores = jnp.dot(queries, key_rows.T, precision=highest) * HEAD ** (-0.5)
    scores = low_back(jnp.where(allowed, scores, masked_score))
    row_max = lax.optimization_barrier(jnp.max(scores, axis=-1, keepdims=True))
    exp_scores = jnp.exp(scores - row_max)
    attn_probs = exp_scores / lax.optimization_barrier(jnp.sum(exp_scores, axis=-1, keepdims=True))
    return jnp.dot(low(attn_probs), values, precision=highest)

def group_forward(params, inputs):
    in_matrix, down_matrix, bias_matrix, vector_rows = params
    group_rows, lengths = inputs
    segment, position, live_mask = layout(lengths, TOK_GRP)
    centered = group_rows - lax.optimization_barrier(jnp.mean(group_rows, axis=-1, keepdims=True))
    inv_scale = lax.rsqrt(lax.optimization_barrier(jnp.mean(centered * centered, axis=-1, keepdims=True)) + norm_eps)
    normed = low(centered * inv_scale * vector_rows[0] + vector_rows[1])
    proj_width = in_matrix.shape[1]
    projected = jnp.dot(normed, in_matrix.reshape(D, proj_width * D), precision=highest)
    projected = low_back(projected.reshape(TOK_GRP, proj_width, D) + bias_matrix)
    cosine, sine_table = rotary_tables(position)
    queries = low(rotate(projected[:, 0].reshape(TOK_GRP, HEADS, HEAD), cosine, sine_table))
    key_rows = low(rotate(projected[:, 1].reshape(TOK_GRP, HEADS, HEAD), cosine, sine_table))
    values = low(projected[:, 2].reshape(TOK_GRP, HEADS, HEAD))
    places = jnp.arange(TOK_GRP, dtype=jnp.int32)
    allowed = (segment[:, None] == segment[None, :]) & (places[None, :] <= places[:, None])
    attend = jax.checkpoint(partial(head_attention, allowed))

    def head_step(triple):
        return attend(triple[0], triple[1], triple[2])
    heads_out = lax.map(head_step, (queries.transpose(1, 0, 2), key_rows.transpose(1, 0, 2), values.transpose(1, 0, 2)))
    attended = low(low_back(heads_out.transpose(1, 0, 2).reshape(TOK_GRP, D)))
    hidden = low(jax.nn.gelu(projected[:, 3:], approximate=True))
    joined = jnp.concatenate([attended[:, None, :], hidden], axis=1)
    mixed = jnp.einsum('trc,rcd->td', joined, down_matrix, precision=highest) + vector_rows[2]
    return group_rows + low_back(mixed)

def forward(seq_lengths, block_input, in_weight, down_weight, column_bias, vector_params):
    params = (low(in_weight), low(down_weight), low(column_bias), low(vector_params))
    group_step = jax.checkpoint(partial(group_forward, params))
    grouped = block_input.reshape(N_DP, TOK_GRP, D)
    outputs = lax.map(group_step, (grouped, seq_lengths))
    return outputs.reshape(N_DP * TOK_GRP, D)

def live_of(lengths):
    return layout(lengths, TOK_GRP)[2]

def adam_update(weight, moment_one, moment_two, gradient, step_rate, decay_factor):
    first_new = beta_first * moment_one + (1.0 - beta_first) * gradient
    second_new = beta_second * moment_two + (1.0 - beta_second) * gradient * gradient
    corrected = first_new / (1.0 - beta_first ** STEP)
    spread = jnp.sqrt(second_new / (1.0 - beta_second ** STEP))
    return (weight - step_rate * (corrected / (spread + adam_eps) + decay_factor * weight), first_new, second_new)

def reference(block_input, out_grad, seq_lengths, in_weight, down_weight, column_bias, vector_params, in_first, in_second, down_first, down_second, bias_first, bias_second, vector_first, vector_second):
    live_rows = jax.vmap(live_of)(seq_lengths).reshape(N_DP * TOK_GRP).astype(jnp.float32)
    block_out, pull_back = jax.vjp(partial(forward, seq_lengths), block_input.astype(jnp.float32), in_weight.astype(jnp.float32), down_weight.astype(jnp.float32), column_bias.astype(jnp.float32), vector_params.astype(jnp.float32))
    input_grad, in_grad, down_grad, bias_grad, vector_grad = pull_back(out_grad.astype(jnp.float32) * live_rows[:, None])
    in_new, in_one, in_two = adam_update(in_weight, in_first, in_second, in_grad, rate_in, weight_decay)
    down_new, down_one, down_two = adam_update(down_weight, down_first, down_second, down_grad, rate_down, weight_decay)
    bias_new, bias_one, bias_two = adam_update(column_bias, bias_first, bias_second, bias_grad, rate_vector, 0.0)
    vector_new, vector_one, vector_two = adam_update(vector_params, vector_first, vector_second, vector_grad, rate_vector, 0.0)
    return (block_out, input_grad, in_new, in_one, in_two, down_new, down_one, down_two, bias_new, bias_one, bias_two, vector_new, vector_one, vector_two)
```

```python
from functools import partial

import jax
import jax.numpy as jnp
from jax import lax
from jax.experimental import pallas as pl
from jax.experimental.pallas import tpu as pltpu
from jax.sharding import PartitionSpec as P

HEAD = 64
ROT = 32
STEP = 8
LANES = 128
QUERY_ROWS = 256

norm_eps = 1e-05
beta_first = 0.9
beta_second = 0.95
adam_eps = 1e-08
masked_score = -1000000000.0
rate_in = 0.02
rate_down = 0.05
rate_vector = 0.2
weight_decay = 0.1

bf16 = jnp.bfloat16
f32 = jnp.float32


def layout(lengths, group_size):
    seq_ends = jnp.cumsum(lengths)
    places = jnp.arange(group_size, dtype=jnp.int32)
    segment = jnp.sum((places[:, None] >= seq_ends[None, :]).astype(jnp.int32), axis=1)
    starts = jnp.concatenate([jnp.zeros((1,), jnp.int32), seq_ends])
    picked = segment[:, None] == jnp.arange(lengths.shape[0] + 1, dtype=jnp.int32)[None, :]
    seq_begin = jnp.sum(jnp.where(picked, starts[None, :], 0), axis=1)
    live_mask = (segment < lengths.shape[0]).astype(f32)
    return seq_begin, places - seq_begin, live_mask


def rotary_tables(position):
    half_rot = ROT // 2
    frequency = 10000.0 ** (-2.0 * jnp.arange(half_rot, dtype=f32) / ROT)
    angles = position.astype(f32)[:, None] * frequency[None, :]
    cosine, sine = jnp.cos(angles), jnp.sin(angles)
    rows = position.shape[0]
    none = jnp.zeros((rows, half_rot), f32)
    rest = jnp.zeros((rows, HEAD - ROT), f32)
    own = jnp.concatenate([cosine, cosine, rest + 1.0], axis=1)
    ahead = jnp.concatenate([-sine, none, rest], axis=1)
    behind = jnp.concatenate([none, sine, rest], axis=1)
    return tuple(jnp.concatenate([t] * (LANES // HEAD), axis=1) for t in (own, ahead, behind))


def attend_mask(begin, row_start, rows, stop):
    key_place = lax.broadcasted_iota(jnp.int32, (rows, stop), 1)
    query_place = row_start + lax.broadcasted_iota(jnp.int32, (rows, stop), 0)
    return (key_place <= query_place) & (key_place >= begin)


def head_lanes(rows, head):
    lane = lax.broadcasted_iota(jnp.int32, (rows, LANES), 1)
    return (lane >= head * HEAD) & (lane < (head + 1) * HEAD)


def dot_t(a, b):
    return lax.dot_general(a, b, (((1,), (1,)), ((), ())), preferred_element_type=f32)


def dot_n(a, b):
    return lax.dot_general(a, b, (((1,), (0,)), ((), ())), preferred_element_type=f32)


def dot_s(a, b):
    return lax.dot_general(a, b, (((0,), (0,)), ((), ())), preferred_element_type=f32)


def turn(x, own, ahead, behind, sign):
    half = ROT // 2
    return x * own + sign * (
        pltpu.roll(x, LANES - half, 1) * ahead + pltpu.roll(x, half, 1) * behind
    )


def attend_forward_kernel(q_in, k_in, v_in, own, ahead, behind, begin, out, q_out, k_out, v_out, lse):
    total = q_in.shape[0]
    rows = min(QUERY_ROWS, total)
    q_out[...] = turn(q_in[...], own[...], ahead[...], behind[...], 1.0).astype(bf16)
    k_out[...] = turn(k_in[...], own[...], ahead[...], behind[...], 1.0).astype(bf16)
    v_out[...] = v_in[...].astype(bf16)
    for start in range(0, total, rows):
        stop = start + rows
        place = pl.ds(start, rows)
        allowed = attend_mask(begin[place, :], start, rows, stop)
        query = q_out[place, :]
        results, sums = [], []
        for head in range(LANES // HEAD):
            mine = head_lanes(rows, head)
            chosen = jnp.where(mine, query, jnp.zeros_like(query)) * HEAD ** (-0.5)
            scores = jnp.where(allowed, dot_t(chosen.astype(bf16), k_out[:stop, :]), masked_score)
            top = jnp.max(scores, axis=1, keepdims=True)
            weights = jnp.exp(scores - top)
            total_weight = jnp.sum(weights, axis=1, keepdims=True)
            results.append(dot_n(weights.astype(bf16), v_out[:stop, :]) / total_weight)
            sums.append(top + jnp.log(total_weight))
        first = head_lanes(rows, 0)
        out[place, :] = jnp.where(first, results[0], results[1]).astype(bf16)
        lse[place, :] = jnp.where(first, sums[0], sums[1])


def attend_forward(q, k, v, tables, begin):
    total, width = q.shape
    tile = pl.BlockSpec((total, LANES), lambda p: (0, p))
    fixed = pl.BlockSpec((total, LANES), lambda p: (0, 0))
    return pl.pallas_call(
        attend_forward_kernel,
        grid=(width // LANES,),
        in_specs=[tile] * 3 + [fixed] * 3 + [pl.BlockSpec((total, 1), lambda p: (0, 0))],
        out_specs=[tile] * 5,
        out_shape=[jax.ShapeDtypeStruct((total, width), bf16)] * 4
        + [jax.ShapeDtypeStruct((total, width), f32)],
        compiler_params=pltpu.CompilerParams(vmem_limit_bytes=48 << 20),
        cost_estimate=pl.CostEstimate(
            flops=8 * total * total * width, bytes_accessed=24 * total * width, transcendentals=0
        ),
    )(q, k, v, *tables, begin)


def attend_backward_kernel(q_in, k_in, v_in, grad, lse, own, ahead, behind, begin, dq, dk, dv, k_sum, v_sum):
    total = q_in.shape[0]
    rows = min(QUERY_ROWS, total)
    k_sum[...] = jnp.zeros_like(k_sum)
    v_sum[...] = jnp.zeros_like(v_sum)
    scale = HEAD ** (-0.5)
    for start in range(0, total, rows):
        stop = start + rows
        place = pl.ds(start, rows)
        allowed = attend_mask(begin[place, :], start, rows, stop)
        q_sum = jnp.zeros((rows, LANES), f32)
        for head in range(LANES // HEAD):
            mine = head_lanes(rows, head)
            query = jnp.where(mine, q_in[place, :], jnp.zeros((rows, LANES), bf16)) * scale
            query = query.astype(bf16)
            cot = jnp.where(mine, grad[place, :], jnp.zeros((rows, LANES), bf16))
            scores = dot_t(query, k_in[:stop, :]) - lse[place, head * HEAD : head * HEAD + 1]
            probs = jnp.where(allowed, jnp.exp(scores), 0.0)
            prob_grad = dot_t(cot, v_in[:stop, :])
            mean = jnp.sum(probs * prob_grad, axis=1, keepdims=True)
            score_grad = (probs * (prob_grad - mean)).astype(bf16)
            q_step = dot_n(score_grad, k_in[:stop, :])
            q_sum = jnp.where(mine, q_step * scale, q_sum)
            k_sum[:stop, :] += dot_s(score_grad, query)
            v_sum[:stop, :] += dot_s(probs.astype(bf16), cot)
        dq[place, :] = turn(
            q_sum, own[place, :], ahead[place, :], behind[place, :], -1.0
        ).astype(bf16)
    dk[...] = turn(k_sum[...], own[...], ahead[...], behind[...], -1.0).astype(bf16)
    dv[...] = v_sum[...].astype(bf16)


def attend_backward(q, k, v, grad, lse, tables, begin):
    total, width = q.shape
    tile = pl.BlockSpec((total, LANES), lambda p: (0, p))
    fixed = pl.BlockSpec((total, LANES), lambda p: (0, 0))
    return pl.pallas_call(
        attend_backward_kernel,
        grid=(width // LANES,),
        in_specs=[tile] * 5 + [fixed] * 3 + [pl.BlockSpec((total, 1), lambda p: (0, 0))],
        out_specs=[tile] * 3,
        out_shape=[jax.ShapeDtypeStruct((total, width), bf16)] * 3,
        scratch_shapes=[pltpu.VMEM((total, LANES), f32)] * 2,
        compiler_params=pltpu.CompilerParams(vmem_limit_bytes=48 << 20),
        cost_estimate=pl.CostEstimate(
            flops=20 * total * total * width, bytes_accessed=20 * total * width, transcendentals=0
        ),
    )(q, k, v, grad, lse, *tables, begin)


def after(value, *others):
    return lax.optimization_barrier((value,) + others)[0]


def line_gather(own, axis):
    n = lax.axis_size(axis)
    me = lax.axis_index(axis)
    rows = own.shape[0]
    up, down = [own], [own]
    for step in range(1, n):
        up.append(lax.ppermute(up[-1], axis, [(j, j + 1) for j in range(step - 1, n - 1)]))
        down.append(lax.ppermute(down[-1], axis, [(j, j - 1) for j in range(1, n - step + 1)]))
    full = jnp.zeros((n * rows,) + own.shape[1:], own.dtype)
    for step in range(n):
        part = own if step == 0 else jnp.where(me >= step, up[step], down[n - step])
        full = lax.dynamic_update_slice_in_dim(full, part, lax.rem(me - step + n, n) * rows, 0)
    return full, (up[-1], down[-1])


def line_scatter(partials, axis):
    n = lax.axis_size(axis)
    me = lax.axis_index(axis)
    rows = partials.shape[0] // n

    def part(owner):
        owner = jnp.clip(owner, 0, n - 1)
        return lax.dynamic_slice_in_dim(partials, owner * rows, rows, 0)

    up = down = None
    for step in range(n - 1):
        to_up = part(me + n - 1 - step)
        to_down = part(me - n + 1 + step)
        if step:
            to_up = (to_up.astype(f32) + up.astype(f32)).astype(bf16)
            to_down = (to_down.astype(f32) + down.astype(f32)).astype(bf16)
        up = lax.ppermute(to_up, axis, [(j, j + 1) for j in range(0, min(step, n - 2) + 1)])
        down = lax.ppermute(to_down, axis, [(j, j - 1) for j in range(n - 1 - step, n)])
    return part(me).astype(f32) + up.astype(f32) + down.astype(f32)


def flip(value, axis, bit):
    return lax.ppermute(value, axis, [(j, j ^ bit) for j in range(lax.axis_size(axis))])


def low_bit(mask):
    return mask & -mask


def high_bit(mask):
    return 1 << (mask.bit_length() - 1)


def cube_gather(own, axis):
    n = lax.axis_size(axis)
    half = own.shape[0] // 2
    whole = {0: own}
    parts = {0: (own[:half], own[half:])}
    for mask in sorted(range(2, n, 2), key=lambda m: m.bit_count()):
        if mask.bit_count() == 1:
            whole[mask] = flip(own, axis, mask)
            parts[mask] = (whole[mask][:half], whole[mask][half:])
        else:
            last, other = high_bit(mask), low_bit(mask)
            parts[mask] = (
                flip(parts[mask ^ last][0], axis, last),
                flip(parts[mask ^ other][1], axis, other),
            )
    if n > 1:
        for mask in range(0, n, 2):
            if mask in whole:
                whole[mask | 1] = flip(whole[mask], axis, 1)
            else:
                parts[mask | 1] = tuple(flip(p, axis, 1) for p in parts[mask])
    return whole, parts


def cube_assemble(gathered, axis, dim):
    whole, parts = gathered
    n = lax.axis_size(axis)
    me = lax.axis_index(axis)
    shape = list(whole[0].shape)
    step, half = shape[dim], shape[0] // 2
    shape[dim] *= n
    full = jnp.zeros(shape, whole[0].dtype)
    for mask in range(n):
        owner = jnp.bitwise_xor(me, mask)
        pieces = [(0, whole[mask])] if mask in whole else [(0, parts[mask][0]), (half, parts[mask][1])]
        for row, piece in pieces:
            start = [0] * len(shape)
            start[0] = row
            start[dim] = start[dim] + owner * step
            full = lax.dynamic_update_slice(full, piece, start)
    return full


def cube_scatter(send, keep, axis):
    n = lax.axis_size(axis)
    got = flip(send, axis, 1)
    total = {2 * j: (keep[j].astype(f32) + got[j].astype(f32)).astype(bf16) for j in range(n // 2)}
    half = keep.shape[1] // 2
    bits = [1 << b for b in range(1, n.bit_length() - 1)]
    results = []
    for rows, order in ((slice(0, half), bits), (slice(half, None), bits[::-1])):
        held = {m: t[rows] for m, t in total.items()}
        for bit in order:
            away = [m for m in sorted(held) if m & bit]
            came = flip(jnp.stack([held[m] for m in away]), axis, bit)
            held = {
                m ^ bit: held[m ^ bit].astype(f32) + came[j].astype(f32) for j, m in enumerate(away)
            }
            if bit != order[-1]:
                held = {m: t.astype(bf16) for m, t in held.items()}
        results.append(held[0].astype(f32))
    return jnp.concatenate(results, axis=0)


def adam_update(weight, moment_one, moment_two, gradient, step_rate, decay_factor):
    first_new = beta_first * moment_one + (1.0 - beta_first) * gradient
    second_new = beta_second * moment_two + (1.0 - beta_second) * gradient * gradient
    corrected = first_new / (1.0 - beta_first**STEP)
    spread = jnp.sqrt(second_new / (1.0 - beta_second**STEP))
    return (
        weight - step_rate * (corrected / (spread + adam_eps) + decay_factor * weight),
        first_new,
        second_new,
    )


def mm(a, b):
    return jnp.dot(a, b, preferred_element_type=f32)


def columns_of(full, axis, masks, step):
    me = lax.axis_index(axis)
    return jnp.concatenate(
        [
            lax.dynamic_slice_in_dim(full, jnp.bitwise_xor(me, m) * step, step, 1)
            for m in masks
        ],
        axis=1,
    )


def per_device(
    block_input,
    out_grad,
    seq_lengths,
    in_weight,
    down_weight,
    column_bias,
    vector_params,
    in_first,
    in_second,
    down_first,
    down_second,
    bias_first,
    bias_second,
    vector_first,
    vector_second,
):
    n_dp = lax.axis_size("dp")
    n_tensor = lax.axis_size("tensor")
    own_rows, model = block_input.shape
    group = own_rows * n_tensor
    in_rows, widths, local = in_weight.shape
    out_cols = down_weight.shape[2]
    n_mlp = widths - 3
    attn_width, mlp_width = 3 * local, n_mlp * local

    in_attn = in_weight[:, :3].astype(bf16).reshape(in_rows, attn_width)
    in_mlp = in_weight[:, 3:].astype(bf16).reshape(in_rows, mlp_width)
    down_low = down_weight.astype(bf16).reshape(widths_down(down_weight), out_cols)

    centered = block_input - jnp.mean(block_input, axis=-1, keepdims=True)
    inv_scale = lax.rsqrt(jnp.mean(centered * centered, axis=-1, keepdims=True) + norm_eps)
    xhat = centered * inv_scale
    begin, position, live = layout(seq_lengths[0], group)
    own_live = lax.dynamic_slice_in_dim(live, lax.axis_index("tensor") * own_rows, own_rows)
    cot_live = out_grad * own_live[:, None]
    cot_low = cot_live.astype(bf16)

    xhat_all, xhat_last = line_gather(xhat.astype(bf16), "tensor")
    attn_pieces = cube_gather(in_attn, "dp")
    in_mlp = after(in_mlp, attn_pieces[0][min(2, n_dp - 1)])
    mlp_pieces = cube_gather(in_mlp, "dp")
    small = lax.all_gather(
        jnp.concatenate([column_bias.astype(bf16).reshape(-1), vector_params.astype(bf16).reshape(-1)]),
        "dp",
        axis=0,
    )
    n_bias = column_bias.size
    bias_vals = (
        small[:, :n_bias].reshape((n_dp,) + column_bias.shape).transpose(1, 0, 2).reshape(widths, local)
    ).astype(f32)
    vector_vals = (
        small[:, n_bias:].reshape((n_dp,) + vector_params.shape).transpose(1, 0, 2).reshape(3, model)
    ).astype(f32)
    gain, shift, out_bias = vector_vals[0], vector_vals[1], vector_vals[2]

    cot_low = after(cot_low, *xhat_last)
    cot_all, _ = line_gather(cot_low, "tensor")
    down_low = after(down_low, mlp_pieces[0][min(2, n_dp - 1)])
    down_pieces = cube_gather(down_low, "dp")

    w_attn = cube_assemble(attn_pieces, "dp", 0)
    w_mlp = cube_assemble(mlp_pieces, "dp", 0)
    w_down = cube_assemble(down_pieces, "dp", 1)

    tables = rotary_tables(position)
    begin_col = begin[:, None]
    normed = (xhat_all.astype(f32) * gain + shift).astype(bf16)

    bias_flat = bias_vals.reshape(-1)
    proj_attn = mm(normed, w_attn) + bias_flat[:attn_width]
    attended, q_low, k_low, v_low, lse = attend_forward(
        proj_attn[:, :local],
        proj_attn[:, local : 2 * local],
        proj_attn[:, 2 * local :],
        tables,
        begin_col,
    )
    pre = mm(normed, w_mlp) + bias_flat[attn_width:]
    hidden, gelu_pull = jax.vjp(partial(jax.nn.gelu, approximate=True), pre)
    hidden = hidden.astype(bf16)
    out_part = (mm(attended, w_down[:local]) + mm(hidden, w_down[local:])).astype(bf16)
    mixed = line_scatter(out_part, "tensor")
    block_out = block_input + (mixed + out_bias)

    attn_grad = dot_t(cot_all, w_down[:local]).astype(bf16)
    pre_grad = gelu_pull(dot_t(cot_all, w_down[local:]))[0].astype(bf16)

    keep_masks = list(range(0, n_dp, 2))
    send_masks = [m + 1 for m in keep_masks]
    cot_send = columns_of(cot_all, "dp", send_masks, out_cols)
    cot_keep = columns_of(cot_all, "dp", keep_masks, out_cols)
    normed_send = columns_of(normed, "dp", send_masks, in_rows)
    normed_keep = columns_of(normed, "dp", keep_masks, in_rows)

    def down_part(cot):
        parts = jnp.concatenate([dot_s(attended, cot).astype(bf16), dot_s(hidden, cot).astype(bf16)], axis=0)
        return parts.reshape(parts.shape[0], n_dp // 2, out_cols).transpose(1, 0, 2)

    def in_part(rows, grads):
        return dot_s(rows, grads).astype(bf16).reshape(n_dp // 2, in_rows, grads.shape[1])

    down_reduced = cube_scatter(down_part(cot_send), down_part(cot_keep), "dp")
    in_mlp_reduced = cube_scatter(in_part(normed_send, pre_grad), in_part(normed_keep, pre_grad), "dp")

    dq, dk, dv = attend_backward(q_low, k_low, v_low, attn_grad, lse, tables, begin_col)
    qkv_grad = jnp.concatenate([dq, dk, dv], axis=1)
    dh_part = dot_t(qkv_grad, w_attn) + dot_t(pre_grad, w_mlp)
    dh = line_scatter(dh_part.astype(bf16), "tensor")
    in_attn_reduced = cube_scatter(in_part(normed_send, qkv_grad), in_part(normed_keep, qkv_grad), "dp")

    bias_grad = jnp.concatenate(
        [jnp.sum(qkv_grad, axis=0, dtype=f32), jnp.sum(pre_grad, axis=0, dtype=f32)]
    ).reshape(widths, n_dp, column_bias.shape[1])
    gain_part = jnp.sum(dh_part * xhat_all.astype(f32), axis=0)
    shift_part = jnp.sum(dh_part, axis=0)
    outbias_part = jnp.sum(cot_low.astype(f32), axis=0)
    vector_grad = jnp.stack([gain_part, shift_part, outbias_part]).reshape(3, n_dp, vector_params.shape[1])
    small_grad = jnp.concatenate(
        [
            bias_grad.transpose(1, 0, 2).reshape(n_dp, -1),
            vector_grad.transpose(1, 0, 2).reshape(n_dp, -1),
        ],
        axis=1,
    )
    small_reduced = lax.psum_scatter(small_grad, "dp", scatter_dimension=0, tiled=True)[0]
    bias_reduced = small_reduced[:n_bias].reshape(column_bias.shape)
    vector_reduced = lax.psum(small_reduced[n_bias:], "tensor").reshape(vector_params.shape)

    dxhat = dh * gain
    input_grad = cot_live + inv_scale * (
        dxhat
        - jnp.mean(dxhat, axis=-1, keepdims=True)
        - xhat * jnp.mean(dxhat * xhat, axis=-1, keepdims=True)
    )

    in_reduced = jnp.concatenate(
        [
            in_attn_reduced.reshape(in_rows, 3, local),
            in_mlp_reduced.reshape(in_rows, n_mlp, local),
        ],
        axis=1,
    )
    down_reduced = down_reduced.reshape(down_weight.shape)
    in_new, in_one, in_two = adam_update(
        in_weight, in_first, in_second, in_reduced, rate_in, weight_decay
    )
    down_new, down_one, down_two = adam_update(
        down_weight, down_first, down_second, down_reduced, rate_down, weight_decay
    )
    bias_new, bias_one, bias_two = adam_update(
        column_bias, bias_first, bias_second, bias_reduced, rate_vector, 0.0
    )
    vector_new, vector_one, vector_two = adam_update(
        vector_params, vector_first, vector_second, vector_reduced, rate_vector, 0.0
    )
    return (
        block_out,
        input_grad,
        in_new,
        in_one,
        in_two,
        down_new,
        down_one,
        down_two,
        bias_new,
        bias_one,
        bias_two,
        vector_new,
        vector_one,
        vector_two,
    )


def widths_down(down_weight):
    return down_weight.shape[0] * down_weight.shape[1]


def solution(mesh):
    return jax.shard_map(
        per_device,
        mesh=mesh,
        in_specs=(
            P(("dp", "tensor"), None),
            P(("dp", "tensor"), None),
            P("dp", None),
            P("dp", None, "tensor"),
            P(None, "tensor", "dp"),
            P(None, ("tensor", "dp")),
            P(None, "dp"),
            P("dp", None, "tensor"),
            P("dp", None, "tensor"),
            P(None, "tensor", "dp"),
            P(None, "tensor", "dp"),
            P(None, ("tensor", "dp")),
            P(None, ("tensor", "dp")),
            P(None, "dp"),
            P(None, "dp"),
        ),
        out_specs=(
            P(("dp", "tensor"), None),
            P(("dp", "tensor"), None),
            P("dp", None, "tensor"),
            P("dp", None, "tensor"),
            P("dp", None, "tensor"),
            P(None, "tensor", "dp"),
            P(None, "tensor", "dp"),
            P(None, "tensor", "dp"),
            P(None, ("tensor", "dp")),
            P(None, ("tensor", "dp")),
            P(None, ("tensor", "dp")),
            P(None, "dp"),
            P(None, "dp"),
            P(None, "dp"),
        ),
        check_vma=False,
    )
```

```python
from functools import partial

import jax
import jax.numpy as jnp
from jax import lax
from jax.experimental import pallas as pl
from jax.experimental.pallas import tpu as pltpu
from jax.sharding import PartitionSpec as P

HEAD = 64
ROT = 32
STEP = 8
LANES = 128
QUERY_ROWS = 256

norm_eps = 1e-05
beta_first = 0.9
beta_second = 0.95
adam_eps = 1e-08
masked_score = -1000000000.0
rate_in = 0.02
rate_down = 0.05
rate_vector = 0.2
weight_decay = 0.1

bf16 = jnp.bfloat16
f32 = jnp.float32


def layout(lengths, group_size):
    seq_ends = jnp.cumsum(lengths)
    places = jnp.arange(group_size, dtype=jnp.int32)
    segment = jnp.sum((places[:, None] >= seq_ends[None, :]).astype(jnp.int32), axis=1)
    starts = jnp.concatenate([jnp.zeros((1,), jnp.int32), seq_ends])
    picked = segment[:, None] == jnp.arange(lengths.shape[0] + 1, dtype=jnp.int32)[None, :]
    seq_begin = jnp.sum(jnp.where(picked, starts[None, :], 0), axis=1)
    live_mask = (segment < lengths.shape[0]).astype(f32)
    return seq_begin, places - seq_begin, live_mask


def rotary_tables(position):
    half_rot = ROT // 2
    frequency = 10000.0 ** (-2.0 * jnp.arange(half_rot, dtype=f32) / ROT)
    angles = position.astype(f32)[:, None] * frequency[None, :]
    cosine, sine = jnp.cos(angles), jnp.sin(angles)
    rows = position.shape[0]
    none = jnp.zeros((rows, half_rot), f32)
    rest = jnp.zeros((rows, HEAD - ROT), f32)
    own = jnp.concatenate([cosine, cosine, rest + 1.0], axis=1)
    ahead = jnp.concatenate([-sine, none, rest], axis=1)
    behind = jnp.concatenate([none, sine, rest], axis=1)
    return tuple(jnp.concatenate([t] * (LANES // HEAD), axis=1) for t in (own, ahead, behind))


def attend_mask(begin, row_start, rows, stop):
    key_place = lax.broadcasted_iota(jnp.int32, (rows, stop), 1)
    query_place = row_start + lax.broadcasted_iota(jnp.int32, (rows, stop), 0)
    return (key_place <= query_place) & (key_place >= begin)


def head_lanes(rows, head):
    lane = lax.broadcasted_iota(jnp.int32, (rows, LANES), 1)
    return (lane >= head * HEAD) & (lane < (head + 1) * HEAD)


def dot_t(a, b):
    return lax.dot_general(a, b, (((1,), (1,)), ((), ())), preferred_element_type=f32)


def dot_n(a, b):
    return lax.dot_general(a, b, (((1,), (0,)), ((), ())), preferred_element_type=f32)


def dot_s(a, b):
    return lax.dot_general(a, b, (((0,), (0,)), ((), ())), preferred_element_type=f32)


def turn(x, own, ahead, behind, sign):
    half = ROT // 2
    return x * own + sign * (
        pltpu.roll(x, LANES - half, 1) * ahead + pltpu.roll(x, half, 1) * behind
    )


def attend_backward_kernel(q_in, k_in, v_in, grad, lse, own, ahead, behind, begin, dq, dk, dv, k_sum, v_sum):
    total = q_in.shape[0]
    rows = min(QUERY_ROWS, total)
    k_sum[...] = jnp.zeros_like(k_sum)
    v_sum[...] = jnp.zeros_like(v_sum)
    scale = HEAD ** (-0.5)
    for start in range(0, total, rows):
        stop = start + rows
        place = pl.ds(start, rows)
        allowed = attend_mask(begin[place, :], start, rows, stop)
        q_sum = jnp.zeros((rows, LANES), f32)
        for head in range(LANES // HEAD):
            mine = head_lanes(rows, head)
            query = jnp.where(mine, q_in[place, :], jnp.zeros((rows, LANES), bf16)) * scale
            query = query.astype(bf16)
            cot = jnp.where(mine, grad[place, :], jnp.zeros((rows, LANES), bf16))
            scores = dot_t(query, k_in[:stop, :]) - lse[place, head * HEAD : head * HEAD + 1]
            probs = jnp.where(allowed, jnp.exp(scores), 0.0)
            prob_grad = dot_t(cot, v_in[:stop, :])
            mean = jnp.sum(probs * prob_grad, axis=1, keepdims=True)
            score_grad = (probs * (prob_grad - mean)).astype(bf16)
            q_step = dot_n(score_grad, k_in[:stop, :])
            q_sum = jnp.where(mine, q_step * scale, q_sum)
            k_sum[:stop, :] += dot_s(score_grad, query)
            v_sum[:stop, :] += dot_s(probs.astype(bf16), cot)
        dq[place, :] = turn(
            q_sum, own[place, :], ahead[place, :], behind[place, :], -1.0
        ).astype(bf16)
    dk[...] = turn(k_sum[...], own[...], ahead[...], behind[...], -1.0).astype(bf16)
    dv[...] = v_sum[...].astype(bf16)


def attend_backward(q, k, v, grad, lse, tables, begin):
    total, width = q.shape
    tile = pl.BlockSpec((total, LANES), lambda p: (0, p))
    fixed = pl.BlockSpec((total, LANES), lambda p: (0, 0))
    return pl.pallas_call(
        attend_backward_kernel,
        grid=(width // LANES,),
        in_specs=[tile] * 5 + [fixed] * 3 + [pl.BlockSpec((total, 1), lambda p: (0, 0))],
        out_specs=[tile] * 3,
        out_shape=[jax.ShapeDtypeStruct((total, width), bf16)] * 3,
        scratch_shapes=[pltpu.VMEM((total, LANES), f32)] * 2,
        compiler_params=pltpu.CompilerParams(vmem_limit_bytes=48 << 20),
        cost_estimate=pl.CostEstimate(
            flops=20 * total * total * width, bytes_accessed=20 * total * width, transcendentals=0
        ),
    )(q, k, v, grad, lse, *tables, begin)


def low_bit(mask):
    return mask & -mask


def high_bit(mask):
    return 1 << (mask.bit_length() - 1)


def gelu_and_slope(a):
    root = (2.0 / 3.141592653589793) ** 0.5
    square = a * a
    t = jnp.tanh(root * a * (1.0 + 0.044715 * square))
    half = 0.5 * (1.0 + t)
    return a * half, half + 0.5 * a * (1.0 - t * t) * (root * (1.0 + 3.0 * 0.044715 * square))


class Plan:
    def __init__(self, n_dp, n_line, rows, model, in_rows, local, n_mlp, out_cols):
        self.n_dp, self.n_line = n_dp, n_line
        self.rows, self.model = rows, model
        self.group = rows * n_line
        self.in_rows, self.local, self.n_mlp, self.out_cols = in_rows, local, n_mlp, out_cols
        self.attn, self.mlp = 3 * local, n_mlp * local
        self.down = (1 + n_mlp) * local
        self.bias_cols = local // n_dp
        self.bits = [1 << b for b in range(1, n_dp.bit_length() - 1)]
        even = range(2, n_dp, 2)
        self.single = [m for m in even if m.bit_count() == 1]
        self.several = sorted((m for m in even if m.bit_count() > 1), key=lambda m: m.bit_count())
        self.odd = list(range(1, n_dp, 2))

    def hop(self, mask, half):
        if mask & 1:
            return 1
        return high_bit(mask) if half == 0 else low_bit(mask)

    def onward(self, mask, half):
        if mask & 1:
            return []
        masks = [mask | 1] if self.n_dp > 1 else []
        return masks + [
            mask | b for b in self.bits if not mask & b and self.hop(mask | b, half) == b
        ]


def forward_kernel(
    plan,
    xhat_in, cot_in, wa_in, wm_in, wd_in, small_in, own, ahead, behind, begin,
    wa_out, wm_out, wd_out, xhat_out, normed_out, cot_out, q_out, k_out, v_out, att_out, lse_out,
    hidden_out, da_out, do_out, part_out,
    wa, wm, wd, small, xs, ns, cs, q, k, v, att, lse, hidden, slope, do,
    own_sem, out_sem, w_send, w_recv, up_send, up_recv, down_send, down_recv,
):
    n, line = plan.n_dp, plan.n_line
    me, place = lax.axis_index("dp"), lax.axis_index("tensor")
    rows, local = plan.rows, plan.local

    def owner(mask):
        index = me
        for b in [1] + plan.bits:
            if mask & b:
                index = index + b - 2 * b * lax.rem(index // b, 2)
        return index

    def slot(flow, index, half):
        if flow < 2:
            step = plan.in_rows // 2
            at = pl.multiple_of(index * plan.in_rows + half * step, step)
            return (wa, wm)[flow].at[pl.ds(at, step), :]
        if flow == 2:
            step = plan.down // 2
            at = pl.multiple_of(index * plan.out_cols, plan.out_cols)
            return wd.at[pl.ds(half * step, step), pl.ds(at, plan.out_cols)]
        return small.at[index]

    def halves(flow):
        return (0,) if flow == 3 else (0, 1)

    def w_copy(flow, mask, half):
        hop = plan.hop(mask, half)
        piece = slot(flow, owner(mask ^ hop), half)
        at = flow * 2 * n + 2 * mask + half
        return pltpu.make_async_remote_copy(
            src_ref=piece, dst_ref=piece, send_sem=w_send.at[at], recv_sem=w_recv.at[at],
            device_id={"dp": owner(hop)}, device_id_type=pl.DeviceIdType.MESH,
        )

    def w_start(flow, mask=0):
        for half in halves(flow):
            for target in plan.onward(mask, half):
                w_copy(flow, target, half).start()

    def w_arrive(flow, masks):
        for mask in masks:
            for half in halves(flow):
                piece = slot(flow, owner(mask), half)
                at = flow * 2 * n + 2 * mask + half
                pltpu.make_async_remote_copy(
                    src_ref=piece, dst_ref=piece, send_sem=w_send.at[at], recv_sem=w_recv.at[at],
                    device_id={"dp": owner(plan.hop(mask, half))}, device_id_type=pl.DeviceIdType.MESH,
                ).wait_recv()
                for target in plan.onward(mask, half):
                    w_copy(flow, target, half).start()

    def chunk(flow, index):
        return (xs, cs)[flow].at[pl.ds(pl.multiple_of(index * rows, rows), rows), :]

    def z_copy(flow, step, up):
        piece = chunk(flow, place - (step - 1) if up else place + (step - 1))
        at = flow * line + step
        return pltpu.make_async_remote_copy(
            src_ref=piece, dst_ref=piece,
            send_sem=(up_send if up else down_send).at[at],
            recv_sem=(up_recv if up else down_recv).at[at],
            device_id={"tensor": place + 1 if up else place - 1}, device_id_type=pl.DeviceIdType.MESH,
        )

    def sends(step, up):
        if up:
            return (place < line - 1) & (place >= step - 1)
        return (place > 0) & (place + step - 1 <= line - 1)

    def z_start(flow, step):
        for up in (True, False):
            @pl.when(sends(step, up))
            def _():
                z_copy(flow, step, up).start()

    def z_arrive(flow, step):
        for up in (True, False):
            @pl.when(place >= step if up else place + step <= line - 1)
            def _():
                piece = chunk(flow, place - step if up else place + step)
                at = flow * line + step
                pltpu.make_async_remote_copy(
                    src_ref=piece, dst_ref=piece,
                    send_sem=(up_send if up else down_send).at[at],
                    recv_sem=(up_recv if up else down_recv).at[at],
                    device_id={"tensor": place - 1 if up else place + 1},
                    device_id_type=pl.DeviceIdType.MESH,
                ).wait_recv()
        if step + 1 < line:
            z_start(flow, step + 1)

    def z_sent(flow, step, up):
        @pl.when(sends(step, up))
        def _():
            z_copy(flow, step, up).wait_send()

    def cot_start(step):
        for up in (True, False):
            last = place == step - 1 if up else place == line - step
            @pl.when(last & sends(1, up))
            def _():
                z_copy(0, step, up).wait_send()
                z_copy(1, 1, up).start()

    def at_distance(step, fn):
        if step == 0:
            fn(place)
            return

        def side(j, carry):
            index = place - step + 2 * step * j

            @pl.when((index >= 0) & (index < line))
            def _():
                fn(index)
            return carry

        lax.fori_loop(0, 2, side, 0)

    def span(index):
        return pl.ds(pl.multiple_of(index * rows, rows), rows)

    outs = [
        (wa, wa_out), (wm, wm_out), (wd, wd_out), (xs, xhat_out), (ns, normed_out), (cs, cot_out),
        (q, q_out), (k, k_out), (v, v_out), (att, att_out), (lse, lse_out), (hidden, hidden_out),
        (slope, da_out), (do, do_out), (xs, part_out),
    ]

    def out_copy(j):
        return pltpu.make_async_copy(outs[j][0], outs[j][1], out_sem.at[j])

    def write(*which):
        for j in which:
            out_copy(j).start()

    loads = [
        pltpu.make_async_copy(xhat_in, chunk(0, place), own_sem.at[0]),
        pltpu.make_async_copy(wa_in, wa.at[pl.ds(pl.multiple_of(me * plan.in_rows, plan.in_rows), plan.in_rows), :], own_sem.at[1]),
        pltpu.make_async_copy(small_in, small.at[me], own_sem.at[2]),
        pltpu.make_async_copy(wm_in, wm.at[pl.ds(pl.multiple_of(me * plan.in_rows, plan.in_rows), plan.in_rows), :], own_sem.at[3]),
        pltpu.make_async_copy(wd_in, wd.at[:, pl.ds(pl.multiple_of(me * plan.out_cols, plan.out_cols), plan.out_cols)], own_sem.at[4]),
        pltpu.make_async_copy(cot_in, chunk(1, place), own_sem.at[5]),
    ]
    for load in loads:
        load.start()
    barrier = pltpu.get_barrier_semaphore()
    for b in [1] + plan.bits if n > 1 else []:
        pl.semaphore_signal(barrier, inc=1, device_id={"dp": owner(b)}, device_id_type=pl.DeviceIdType.MESH)

    @pl.when(place < line - 1)
    def _():
        pl.semaphore_signal(barrier, inc=1, device_id={"tensor": place + 1}, device_id_type=pl.DeviceIdType.MESH)

    @pl.when(place > 0)
    def _():
        pl.semaphore_signal(barrier, inc=1, device_id={"tensor": place - 1}, device_id_type=pl.DeviceIdType.MESH)

    beside = (place + line - 1) // line + (2 * line - 2 - place) // line
    pl.semaphore_wait(barrier, (1 + len(plan.bits) if n > 1 else 0) + beside)

    def normalize_rows(index):
        at = span(index)
        gain = jnp.concatenate([small[o, 0:1, LANES:] for o in range(n)], axis=1).astype(f32)
        shift = jnp.concatenate([small[o, 1:2, LANES:] for o in range(n)], axis=1).astype(f32)
        ns[at, :] = (xs[at, :].astype(f32) * gain + shift).astype(bf16)

    def bias_row(r, first, width):
        per = LANES // plan.bias_cols
        groups = []
        for g in range(first // LANES, (first + width) // LANES):
            total = small[g * per, r : r + 1, :LANES].astype(f32)
            for o in range(1, per):
                total = total + small[g * per + o, r : r + 1, :LANES].astype(f32)
            groups.append(total)
        return jnp.concatenate(groups, axis=1)

    def attn_rows(index):
        at = span(index)
        normalize_rows(index)
        for r, target in enumerate((q, k, v)):
            proj = dot_n(ns[at, :], wa[:, r * local : (r + 1) * local]) + bias_row(r, 0, local)
            if r == 2:
                target[at, :] = proj.astype(bf16)
            else:
                for g in range(0, local, LANES):
                    target[at, g : g + LANES] = turn(
                        proj[:, g : g + LANES], own[at, :], ahead[at, :], behind[at, :], 1.0
                    ).astype(bf16)

    def mlp_rows(index):
        at = span(index)
        for r in range(plan.n_mlp):
            cols = slice(r * local, (r + 1) * local)
            pre = dot_n(ns[at, :], wm[:, cols]) + bias_row(3 + r, 0, local)
            value, grad = gelu_and_slope(pre)
            hidden[at, cols] = value.astype(bf16)
            slope[at, cols] = grad.astype(bf16)

    def attend(pair, carry):
        total = plan.group
        block = min(QUERY_ROWS, total)
        lanes = pl.ds(pl.multiple_of(pair * LANES, LANES), LANES)
        for start in range(0, total, block):
            stop = start + block
            here = pl.ds(start, block)
            allowed = attend_mask(begin[here, :], start, block, stop)
            query = q[here, lanes]
            results, sums = [], []
            for head in range(LANES // HEAD):
                mine = head_lanes(block, head)
                chosen = jnp.where(mine, query, jnp.zeros_like(query)) * HEAD ** (-0.5)
                scores = jnp.where(allowed, dot_t(chosen.astype(bf16), k[:stop, lanes]), masked_score)
                top = jnp.max(scores, axis=1, keepdims=True)
                weights = jnp.exp(scores - top)
                total_weight = jnp.sum(weights, axis=1, keepdims=True)
                results.append(dot_n(weights.astype(bf16), v[:stop, lanes]) / total_weight)
                sums.append(top + jnp.log(total_weight))
            first = head_lanes(block, 0)
            att[here, lanes] = jnp.where(first, results[0], results[1]).astype(bf16)
            lse[here, lanes] = jnp.where(first, sums[0], sums[1])
        return carry

    tile = min(512, plan.model)
    tall = min(512, plan.group)

    def out_tile(j, carry):
        cols = pl.ds(pl.multiple_of(lax.rem(j, plan.model // tile) * tile, tile), tile)
        at = pl.ds(pl.multiple_of((j // (plan.model // tile)) * tall, tall), tall)
        total = dot_n(att[at, :], wd[:local, cols]) + dot_n(hidden[at, :], wd[local:, cols])
        xs[at, cols] = total.astype(bf16)
        return carry

    def back_rows(index):
        at = span(index)
        do[at, :] = dot_t(cs[at, :], wd[:local, :]).astype(bf16)
        for r in range(plan.n_mlp):
            cols = slice(r * local, (r + 1) * local)
            grad = dot_t(cs[at, :], wd[(1 + r) * local : (2 + r) * local, :])
            slope[at, cols] = (grad * slope[at, cols].astype(f32)).astype(bf16)

    loads[0].wait()
    z_start(0, 1)
    loads[2].wait()
    w_start(3)
    loads[1].wait()
    w_start(0)
    loads[3].wait()
    loads[4].wait()
    loads[5].wait()
    w_arrive(0, plan.single)
    w_start(1)
    w_arrive(3, plan.single)
    if line > 1:
        z_arrive(0, 1)
        cot_start(1)
    w_arrive(3, plan.several)
    w_arrive(0, plan.several)
    w_arrive(3, plan.odd)
    w_arrive(0, plan.odd)
    write(0)
    at_distance(0, attn_rows)
    if line > 2:
        at_distance(1, attn_rows)
    w_arrive(1, plan.single)
    w_start(2)
    for step in range(2, line - 1):
        z_arrive(0, step)
        cot_start(step)
        at_distance(step, attn_rows)
    w_arrive(1, plan.several)
    w_arrive(1, plan.odd)
    write(1)
    near = max(line - 2, 0)
    lax.fori_loop(
        jnp.maximum(place - near, 0), jnp.minimum(place + near, line - 1) + 1,
        lambda c, carry: (mlp_rows(c), carry)[1], 0,
    )
    if line > 1:
        if line > 2:
            z_arrive(0, line - 1)
            cot_start(line - 1)
        at_distance(line - 1, lambda c: (attn_rows(c), mlp_rows(c))[0])
    write(3, 4, 6, 7, 8, 11)
    pairs = local // LANES
    lax.fori_loop(0, pairs // 2, attend, 0)
    w_arrive(2, plan.single)
    lax.fori_loop(pairs // 2, pairs, attend, 0)
    write(9, 10)
    if line > 1:
        z_arrive(1, 1)
    w_arrive(2, plan.several)
    w_arrive(2, plan.odd)
    write(2)
    out_copy(3).wait()
    for step in range(1, line):
        for up in (True, False):
            left = place != step - 1 if up else place != line - step
            @pl.when(left & sends(step, up))
            def _():
                z_copy(0, step, up).wait_send()
    lax.fori_loop(0, (plan.model // tile) * (plan.group // tall), out_tile, 0)
    write(14)
    at_distance(0, back_rows)
    if line > 1:
        at_distance(1, back_rows)
    for step in range(2, line):
        z_arrive(1, step)
        at_distance(step, back_rows)
    write(5, 12, 13)

    for flow in range(4):
        for mask in range(1, n):
            for half in halves(flow):
                w_copy(flow, mask, half).wait_send()
    for step in range(1, line):
        for up in (True, False):
            z_sent(1, step, up)
    for j in range(len(outs)):
        if j != 3:
            out_copy(j).wait()


def forward(plan, xhat, cot, wa, wm, wd, small, tables, begin):
    any_space = pl.BlockSpec(memory_space=pl.ANY)
    vmem = pl.BlockSpec(memory_space=pltpu.VMEM)
    n, line, group, model, local = plan.n_dp, plan.n_line, plan.group, plan.model, plan.local
    low = lambda *shape: jax.ShapeDtypeStruct(shape, bf16)
    out_shape = [
        low(model, plan.attn), low(model, plan.mlp), low(plan.down, model),
        low(group, model), low(group, model), low(group, model),
        low(group, local), low(group, local), low(group, local), low(group, local),
        jax.ShapeDtypeStruct((group, local), f32),
        low(group, plan.mlp), low(group, plan.mlp), low(group, local), low(group, model),
    ]
    scratch = lambda s: pltpu.VMEM(s.shape, s.dtype)
    dma = pltpu.SemaphoreType.DMA
    return pl.pallas_call(
        partial(forward_kernel, plan),
        in_specs=[any_space] * 6 + [vmem] * 4,
        out_specs=[any_space] * 15,
        out_shape=out_shape,
        scratch_shapes=[scratch(s) for s in out_shape[:3]]
        + [pltpu.VMEM((n, 16, LANES + plan.out_cols), bf16)]
        + [scratch(s) for s in out_shape[3:14]]
        + [dma((6,)), dma((15,)), dma((8 * n,)), dma((8 * n,))]
        + [dma((2 * line,))] * 4,
        compiler_params=pltpu.CompilerParams(
            collective_id=0, has_side_effects=True, vmem_limit_bytes=63 << 20
        ),
        cost_estimate=pl.CostEstimate(flops=60 * 10**9, bytes_accessed=80 << 20, transcendentals=0),
    )(xhat, cot, wa, wm, wd, small, *tables, begin)


def after(value, *others):
    return lax.optimization_barrier((value,) + others)[0]


def line_scatter(partials, axis):
    n = lax.axis_size(axis)
    me = lax.axis_index(axis)
    rows = partials.shape[0] // n

    def part(owner):
        owner = jnp.clip(owner, 0, n - 1)
        return lax.dynamic_slice_in_dim(partials, owner * rows, rows, 0)

    up = down = None
    for step in range(n - 1):
        to_up = part(me + n - 1 - step)
        to_down = part(me - n + 1 + step)
        if step:
            to_up = (to_up.astype(f32) + up.astype(f32)).astype(bf16)
            to_down = (to_down.astype(f32) + down.astype(f32)).astype(bf16)
        up = lax.ppermute(to_up, axis, [(j, j + 1) for j in range(0, min(step, n - 2) + 1)])
        down = lax.ppermute(to_down, axis, [(j, j - 1) for j in range(n - 1 - step, n)])
    return part(me).astype(f32) + up.astype(f32) + down.astype(f32)


def flip(value, axis, bit):
    return lax.ppermute(value, axis, [(j, j ^ bit) for j in range(lax.axis_size(axis))])


def cube_scatter(send, keep, axis):
    n = lax.axis_size(axis)
    got = flip(send, axis, 1)
    total = {2 * j: (keep[j].astype(f32) + got[j].astype(f32)).astype(bf16) for j in range(n // 2)}
    half = keep.shape[1] // 2
    bits = [1 << b for b in range(1, n.bit_length() - 1)]
    results = []
    for rows, order in ((slice(0, half), bits), (slice(half, None), bits[::-1])):
        held = {m: t[rows] for m, t in total.items()}
        for bit in order:
            away = [m for m in sorted(held) if m & bit]
            came = flip(jnp.stack([held[m] for m in away]), axis, bit)
            held = {
                m ^ bit: held[m ^ bit].astype(f32) + came[j].astype(f32) for j, m in enumerate(away)
            }
            if bit != order[-1]:
                held = {m: t.astype(bf16) for m, t in held.items()}
        results.append(held[0].astype(f32))
    return jnp.concatenate(results, axis=0)


def adam_update(weight, moment_one, moment_two, gradient, step_rate, decay_factor):
    first_new = beta_first * moment_one + (1.0 - beta_first) * gradient
    second_new = beta_second * moment_two + (1.0 - beta_second) * gradient * gradient
    corrected = first_new / (1.0 - beta_first**STEP)
    spread = jnp.sqrt(second_new / (1.0 - beta_second**STEP))
    return (
        weight - step_rate * (corrected / (spread + adam_eps) + decay_factor * weight),
        first_new,
        second_new,
    )


def mm(a, b):
    return jnp.dot(a, b, preferred_element_type=f32)


def columns_of(full, axis, masks, step):
    me = lax.axis_index(axis)
    return jnp.concatenate(
        [
            lax.dynamic_slice_in_dim(full, jnp.bitwise_xor(me, m) * step, step, 1)
            for m in masks
        ],
        axis=1,
    )


def per_device(
    block_input,
    out_grad,
    seq_lengths,
    in_weight,
    down_weight,
    column_bias,
    vector_params,
    in_first,
    in_second,
    down_first,
    down_second,
    bias_first,
    bias_second,
    vector_first,
    vector_second,
):
    n_dp = lax.axis_size("dp")
    n_tensor = lax.axis_size("tensor")
    own_rows, model = block_input.shape
    group = own_rows * n_tensor
    in_rows, widths, local = in_weight.shape
    out_cols = down_weight.shape[2]
    n_mlp = widths - 3
    attn_width, mlp_width = 3 * local, n_mlp * local

    in_attn = in_weight[:, :3].astype(bf16).reshape(in_rows, attn_width)
    in_mlp = in_weight[:, 3:].astype(bf16).reshape(in_rows, mlp_width)
    down_low = down_weight.astype(bf16).reshape(widths_down(down_weight), out_cols)

    centered = block_input - jnp.mean(block_input, axis=-1, keepdims=True)
    inv_scale = lax.rsqrt(jnp.mean(centered * centered, axis=-1, keepdims=True) + norm_eps)
    xhat = centered * inv_scale
    begin, position, live = layout(seq_lengths[0], group)
    own_live = lax.dynamic_slice_in_dim(live, lax.axis_index("tensor") * own_rows, own_rows)
    cot_live = out_grad * own_live[:, None]
    cot_low = cot_live.astype(bf16)

    me = lax.axis_index("dp")
    plan = Plan(n_dp, n_tensor, own_rows, model, in_rows, local, n_mlp, out_cols)
    n_bias = column_bias.size
    lane = lax.rem(me, LANES // plan.bias_cols) * plan.bias_cols
    bias_tile = lax.dynamic_update_slice(
        jnp.zeros((16, LANES), bf16), column_bias.astype(bf16), (0, lane)
    )
    small = jnp.concatenate([bias_tile, jnp.pad(vector_params.astype(bf16), ((0, 13), (0, 0)))], axis=1)
    tables = rotary_tables(position)
    begin_col = begin[:, None]
    (
        w_attn, w_mlp, w_down, xhat_all, normed, cot_all, q_low, k_low, v_low, attended, lse,
        hidden, pre_grad, attn_grad, out_part,
    ) = forward(plan, xhat.astype(bf16), cot_low, in_attn, in_mlp, down_low, small, tables, begin_col)
    vector_vals = lax.all_gather(vector_params.astype(bf16), "dp", axis=1, tiled=True).astype(f32)
    gain, out_bias = vector_vals[0], vector_vals[2]
    mixed = line_scatter(out_part, "tensor")
    block_out = block_input + (mixed + out_bias)

    keep_masks = list(range(0, n_dp, 2))
    send_masks = [m + 1 for m in keep_masks]
    cot_send = columns_of(cot_all, "dp", send_masks, out_cols)
    cot_keep = columns_of(cot_all, "dp", keep_masks, out_cols)
    normed_send = columns_of(normed, "dp", send_masks, in_rows)
    normed_keep = columns_of(normed, "dp", keep_masks, in_rows)

    def down_part(cot):
        parts = jnp.concatenate([dot_s(attended, cot).astype(bf16), dot_s(hidden, cot).astype(bf16)], axis=0)
        return parts.reshape(parts.shape[0], n_dp // 2, out_cols).transpose(1, 0, 2)

    def in_part(rows, grads):
        return dot_s(rows, grads).astype(bf16).reshape(n_dp // 2, in_rows, grads.shape[1])

    down_reduced = cube_scatter(down_part(cot_send), down_part(cot_keep), "dp")
    in_mlp_reduced = cube_scatter(in_part(normed_send, pre_grad), in_part(normed_keep, pre_grad), "dp")

    dq, dk, dv = attend_backward(q_low, k_low, v_low, attn_grad, lse, tables, begin_col)
    qkv_grad = jnp.concatenate([dq, dk, dv], axis=1)
    dh_part = dot_t(qkv_grad, w_attn) + dot_t(pre_grad, w_mlp)
    dh = line_scatter(dh_part.astype(bf16), "tensor")
    in_attn_reduced = cube_scatter(in_part(normed_send, qkv_grad), in_part(normed_keep, qkv_grad), "dp")

    bias_grad = jnp.concatenate(
        [jnp.sum(qkv_grad, axis=0, dtype=f32), jnp.sum(pre_grad, axis=0, dtype=f32)]
    ).reshape(widths, n_dp, column_bias.shape[1])
    gain_part = jnp.sum(dh_part * xhat_all.astype(f32), axis=0)
    shift_part = jnp.sum(dh_part, axis=0)
    outbias_part = jnp.sum(cot_low.astype(f32), axis=0)
    vector_grad = jnp.stack([gain_part, shift_part, outbias_part]).reshape(3, n_dp, vector_params.shape[1])
    small_grad = jnp.concatenate(
        [
            bias_grad.transpose(1, 0, 2).reshape(n_dp, -1),
            vector_grad.transpose(1, 0, 2).reshape(n_dp, -1),
        ],
        axis=1,
    )
    small_reduced = lax.psum_scatter(small_grad, "dp", scatter_dimension=0, tiled=True)[0]
    bias_reduced = small_reduced[:n_bias].reshape(column_bias.shape)
    vector_reduced = lax.psum(small_reduced[n_bias:], "tensor").reshape(vector_params.shape)

    dxhat = dh * gain
    input_grad = cot_live + inv_scale * (
        dxhat
        - jnp.mean(dxhat, axis=-1, keepdims=True)
        - xhat * jnp.mean(dxhat * xhat, axis=-1, keepdims=True)
    )

    in_reduced = jnp.concatenate(
        [
            in_attn_reduced.reshape(in_rows, 3, local),
            in_mlp_reduced.reshape(in_rows, n_mlp, local),
        ],
        axis=1,
    )
    down_reduced = down_reduced.reshape(down_weight.shape)
    in_new, in_one, in_two = adam_update(
        in_weight, in_first, in_second, in_reduced, rate_in, weight_decay
    )
    down_new, down_one, down_two = adam_update(
        down_weight, down_first, down_second, down_reduced, rate_down, weight_decay
    )
    bias_new, bias_one, bias_two = adam_update(
        column_bias, bias_first, bias_second, bias_reduced, rate_vector, 0.0
    )
    vector_new, vector_one, vector_two = adam_update(
        vector_params, vector_first, vector_second, vector_reduced, rate_vector, 0.0
    )
    return (
        block_out,
        input_grad,
        in_new,
        in_one,
        in_two,
        down_new,
        down_one,
        down_two,
        bias_new,
        bias_one,
        bias_two,
        vector_new,
        vector_one,
        vector_two,
    )


def widths_down(down_weight):
    return down_weight.shape[0] * down_weight.shape[1]


def solution(mesh):
    return jax.shard_map(
        per_device,
        mesh=mesh,
        in_specs=(
            P(("dp", "tensor"), None),
            P(("dp", "tensor"), None),
            P("dp", None),
            P("dp", None, "tensor"),
            P(None, "tensor", "dp"),
            P(None, ("tensor", "dp")),
            P(None, "dp"),
            P("dp", None, "tensor"),
            P("dp", None, "tensor"),
            P(None, "tensor", "dp"),
            P(None, "tensor", "dp"),
            P(None, ("tensor", "dp")),
            P(None, ("tensor", "dp")),
            P(None, "dp"),
            P(None, "dp"),
        ),
        out_specs=(
            P(("dp", "tensor"), None),
            P(("dp", "tensor"), None),
            P("dp", None, "tensor"),
            P("dp", None, "tensor"),
            P("dp", None, "tensor"),
            P(None, "tensor", "dp"),
            P(None, "tensor", "dp"),
            P(None, "tensor", "dp"),
            P(None, ("tensor", "dp")),
            P(None, ("tensor", "dp")),
            P(None, ("tensor", "dp")),
            P(None, "dp"),
            P(None, "dp"),
            P(None, "dp"),
        ),
        check_vma=False,
    )
```

```python
from functools import partial

import jax
import jax.numpy as jnp
from jax import lax
from jax.experimental import pallas as pl
from jax.experimental.pallas import tpu as pltpu
from jax.sharding import PartitionSpec as P

HEAD = 64
ROT = 32
STEP = 8
LANES = 128
QUERY_ROWS = 256

norm_eps = 1e-05
beta_first = 0.9
beta_second = 0.95
adam_eps = 1e-08
masked_score = -1000000000.0
rate_in = 0.02
rate_down = 0.05
rate_vector = 0.2
weight_decay = 0.1

bf16 = jnp.bfloat16
f32 = jnp.float32


def layout(lengths, group_size):
    seq_ends = jnp.cumsum(lengths)
    places = jnp.arange(group_size, dtype=jnp.int32)
    segment = jnp.sum((places[:, None] >= seq_ends[None, :]).astype(jnp.int32), axis=1)
    starts = jnp.concatenate([jnp.zeros((1,), jnp.int32), seq_ends])
    picked = segment[:, None] == jnp.arange(lengths.shape[0] + 1, dtype=jnp.int32)[None, :]
    seq_begin = jnp.sum(jnp.where(picked, starts[None, :], 0), axis=1)
    live_mask = (segment < lengths.shape[0]).astype(f32)
    return seq_begin, places - seq_begin, live_mask


def rotary_tables(position):
    half_rot = ROT // 2
    frequency = 10000.0 ** (-2.0 * jnp.arange(half_rot, dtype=f32) / ROT)
    angles = position.astype(f32)[:, None] * frequency[None, :]
    cosine, sine = jnp.cos(angles), jnp.sin(angles)
    rows = position.shape[0]
    none = jnp.zeros((rows, half_rot), f32)
    rest = jnp.zeros((rows, HEAD - ROT), f32)
    own = jnp.concatenate([cosine, cosine, rest + 1.0], axis=1)
    ahead = jnp.concatenate([-sine, none, rest], axis=1)
    behind = jnp.concatenate([none, sine, rest], axis=1)
    return tuple(jnp.concatenate([t] * (LANES // HEAD), axis=1) for t in (own, ahead, behind))


def attend_mask(begin, row_start, rows, stop):
    key_place = lax.broadcasted_iota(jnp.int32, (rows, stop), 1)
    query_place = row_start + lax.broadcasted_iota(jnp.int32, (rows, stop), 0)
    return (key_place <= query_place) & (key_place >= begin)


def head_lanes(rows, head):
    lane = lax.broadcasted_iota(jnp.int32, (rows, LANES), 1)
    return (lane >= head * HEAD) & (lane < (head + 1) * HEAD)


def dot_t(a, b):
    return lax.dot_general(a, b, (((1,), (1,)), ((), ())), preferred_element_type=f32)


def dot_n(a, b):
    return lax.dot_general(a, b, (((1,), (0,)), ((), ())), preferred_element_type=f32)


def dot_s(a, b):
    return lax.dot_general(a, b, (((0,), (0,)), ((), ())), preferred_element_type=f32)


def turn(x, own, ahead, behind, sign):
    half = ROT // 2
    return x * own + sign * (
        pltpu.roll(x, LANES - half, 1) * ahead + pltpu.roll(x, half, 1) * behind
    )


def low_bit(mask):
    return mask & -mask


def high_bit(mask):
    return 1 << (mask.bit_length() - 1)


def gelu_and_slope(a):
    root = (2.0 / 3.141592653589793) ** 0.5
    square = a * a
    t = jnp.tanh(root * a * (1.0 + 0.044715 * square))
    half = 0.5 * (1.0 + t)
    return a * half, half + 0.5 * a * (1.0 - t * t) * (root * (1.0 + 3.0 * 0.044715 * square))


class Plan:
    def __init__(self, n_dp, n_line, rows, model, in_rows, local, n_mlp, out_cols):
        self.n_dp, self.n_line = n_dp, n_line
        self.rows, self.model = rows, model
        self.group = rows * n_line
        self.in_rows, self.local, self.n_mlp, self.out_cols = in_rows, local, n_mlp, out_cols
        self.attn, self.mlp = 3 * local, n_mlp * local
        self.down = (1 + n_mlp) * local
        self.bias_cols = local // n_dp
        self.bits = [1 << b for b in range(1, n_dp.bit_length() - 1)]
        even = range(2, n_dp, 2)
        self.single = [m for m in even if m.bit_count() == 1]
        self.several = sorted((m for m in even if m.bit_count() > 1), key=lambda m: m.bit_count())
        self.odd = list(range(1, n_dp, 2))

    def hop(self, mask, half):
        if mask & 1:
            return 1
        return high_bit(mask) if half == 0 else low_bit(mask)

    def onward(self, mask, half):
        if mask & 1:
            return []
        masks = [mask | 1] if self.n_dp > 1 else []
        return masks + [
            mask | b for b in self.bits if not mask & b and self.hop(mask | b, half) == b
        ]


def forward_kernel(
    plan,
    xhat_in, cot_in, wa_in, wm_in, wd_in, small_in, own, ahead, behind, begin,
    wa_out, wm_out, small_out, xhat_out, sums_out, cot_out, q_out, k_out, v_out, att_out, lse_out,
    hidden_out, da_out, do_out, part_out,
    wa, wm, wd, small, xs, ns, sums, cs, q, k, v, att, lse, hidden, slope, do,
    own_sem, out_sem, w_send, w_recv, up_send, up_recv, down_send, down_recv,
):
    n, line = plan.n_dp, plan.n_line
    me, place = lax.axis_index("dp"), lax.axis_index("tensor")
    rows, local = plan.rows, plan.local

    def owner(mask):
        index = me
        for b in [1] + plan.bits:
            if mask & b:
                index = index + b - 2 * b * lax.rem(index // b, 2)
        return index

    def slot(flow, index, half):
        if flow < 2:
            step = plan.in_rows // 2
            at = pl.multiple_of(index * plan.in_rows + half * step, step)
            return (wa, wm)[flow].at[pl.ds(at, step), :]
        if flow == 2:
            step = plan.down // 2
            at = pl.multiple_of(index * plan.out_cols, plan.out_cols)
            return wd.at[pl.ds(half * step, step), pl.ds(at, plan.out_cols)]
        return small.at[index]

    def halves(flow):
        return (0,) if flow == 3 else (0, 1)

    def w_copy(flow, mask, half):
        hop = plan.hop(mask, half)
        piece = slot(flow, owner(mask ^ hop), half)
        at = flow * 2 * n + 2 * mask + half
        return pltpu.make_async_remote_copy(
            src_ref=piece, dst_ref=piece, send_sem=w_send.at[at], recv_sem=w_recv.at[at],
            device_id={"dp": owner(hop)}, device_id_type=pl.DeviceIdType.MESH,
        )

    def w_start(flow, mask=0):
        for half in halves(flow):
            for target in plan.onward(mask, half):
                w_copy(flow, target, half).start()

    def w_arrive(flow, masks):
        for mask in masks:
            for half in halves(flow):
                piece = slot(flow, owner(mask), half)
                at = flow * 2 * n + 2 * mask + half
                pltpu.make_async_remote_copy(
                    src_ref=piece, dst_ref=piece, send_sem=w_send.at[at], recv_sem=w_recv.at[at],
                    device_id={"dp": owner(plan.hop(mask, half))}, device_id_type=pl.DeviceIdType.MESH,
                ).wait_recv()
                for target in plan.onward(mask, half):
                    w_copy(flow, target, half).start()

    def chunk(flow, index):
        return (xs, cs)[flow].at[pl.ds(pl.multiple_of(index * rows, rows), rows), :]

    def z_copy(flow, step, up):
        piece = chunk(flow, place - (step - 1) if up else place + (step - 1))
        at = flow * line + step
        return pltpu.make_async_remote_copy(
            src_ref=piece, dst_ref=piece,
            send_sem=(up_send if up else down_send).at[at],
            recv_sem=(up_recv if up else down_recv).at[at],
            device_id={"tensor": place + 1 if up else place - 1}, device_id_type=pl.DeviceIdType.MESH,
        )

    def sends(step, up):
        if up:
            return (place < line - 1) & (place >= step - 1)
        return (place > 0) & (place + step - 1 <= line - 1)

    def z_start(flow, step):
        for up in (True, False):
            @pl.when(sends(step, up))
            def _():
                z_copy(flow, step, up).start()

    def z_arrive(flow, step):
        for up in (True, False):
            @pl.when(place >= step if up else place + step <= line - 1)
            def _():
                piece = chunk(flow, place - step if up else place + step)
                at = flow * line + step
                pltpu.make_async_remote_copy(
                    src_ref=piece, dst_ref=piece,
                    send_sem=(up_send if up else down_send).at[at],
                    recv_sem=(up_recv if up else down_recv).at[at],
                    device_id={"tensor": place - 1 if up else place + 1},
                    device_id_type=pl.DeviceIdType.MESH,
                ).wait_recv()
        if step + 1 < line:
            z_start(flow, step + 1)

    def z_sent(flow, step, up):
        @pl.when(sends(step, up))
        def _():
            z_copy(flow, step, up).wait_send()

    def cot_start(step):
        for up in (True, False):
            last = place == step - 1 if up else place == line - step
            @pl.when(last & sends(1, up))
            def _():
                z_copy(0, step, up).wait_send()
                z_copy(1, 1, up).start()

    def at_distance(step, fn):
        if step == 0:
            fn(place)
            return

        def side(j, carry):
            index = place - step + 2 * step * j

            @pl.when((index >= 0) & (index < line))
            def _():
                fn(index)
            return carry

        lax.fori_loop(0, 2, side, 0)

    def span(index):
        return pl.ds(pl.multiple_of(index * rows, rows), rows)

    outs = [
        (wa, wa_out), (wm, wm_out), (small, small_out), (xs, xhat_out), (sums, sums_out), (cs, cot_out),
        (q, q_out), (k, k_out), (v, v_out), (att, att_out), (lse, lse_out), (hidden, hidden_out),
        (slope, da_out), (do, do_out), (xs, part_out),
    ]

    def out_copy(j):
        return pltpu.make_async_copy(outs[j][0], outs[j][1], out_sem.at[j])

    def write(*which):
        for j in which:
            out_copy(j).start()

    loads = [
        pltpu.make_async_copy(xhat_in, chunk(0, place), own_sem.at[0]),
        pltpu.make_async_copy(wa_in, wa.at[pl.ds(pl.multiple_of(me * plan.in_rows, plan.in_rows), plan.in_rows), :], own_sem.at[1]),
        pltpu.make_async_copy(small_in, small.at[me], own_sem.at[2]),
        pltpu.make_async_copy(wm_in, wm.at[pl.ds(pl.multiple_of(me * plan.in_rows, plan.in_rows), plan.in_rows), :], own_sem.at[3]),
        pltpu.make_async_copy(wd_in, wd.at[:, pl.ds(pl.multiple_of(me * plan.out_cols, plan.out_cols), plan.out_cols)], own_sem.at[4]),
        pltpu.make_async_copy(cot_in, chunk(1, place), own_sem.at[5]),
    ]
    for load in loads:
        load.start()
    barrier = pltpu.get_barrier_semaphore()
    for b in [1] + plan.bits if n > 1 else []:
        pl.semaphore_signal(barrier, inc=1, device_id={"dp": owner(b)}, device_id_type=pl.DeviceIdType.MESH)

    @pl.when(place < line - 1)
    def _():
        pl.semaphore_signal(barrier, inc=1, device_id={"tensor": place + 1}, device_id_type=pl.DeviceIdType.MESH)

    @pl.when(place > 0)
    def _():
        pl.semaphore_signal(barrier, inc=1, device_id={"tensor": place - 1}, device_id_type=pl.DeviceIdType.MESH)

    beside = (place + line - 1) // line + (2 * line - 2 - place) // line
    pl.semaphore_wait(barrier, (1 + len(plan.bits) if n > 1 else 0) + beside)

    def normalize_rows(index):
        at = span(index)
        gain = jnp.concatenate([small[o, 0:1, LANES:] for o in range(n)], axis=1).astype(f32)
        shift = jnp.concatenate([small[o, 1:2, LANES:] for o in range(n)], axis=1).astype(f32)
        ns[at, :] = (xs[at, :].astype(f32) * gain + shift).astype(bf16)

    def bias_row(r, first, width):
        per = LANES // plan.bias_cols
        groups = []
        for g in range(first // LANES, (first + width) // LANES):
            total = small[g * per, r : r + 1, :LANES].astype(f32)
            for o in range(1, per):
                total = total + small[g * per + o, r : r + 1, :LANES].astype(f32)
            groups.append(total)
        return jnp.concatenate(groups, axis=1)

    def attn_rows(index):
        at = span(index)
        normalize_rows(index)
        for r, target in enumerate((q, k, v)):
            proj = dot_n(ns[at, :], wa[:, r * local : (r + 1) * local]) + bias_row(r, 0, local)
            if r == 2:
                target[at, :] = proj.astype(bf16)
            else:
                for g in range(0, local, LANES):
                    target[at, g : g + LANES] = turn(
                        proj[:, g : g + LANES], own[at, :], ahead[at, :], behind[at, :], 1.0
                    ).astype(bf16)

    def mlp_rows(index):
        at = span(index)
        for r in range(plan.n_mlp):
            cols = slice(r * local, (r + 1) * local)
            pre = dot_n(ns[at, :], wm[:, cols]) + bias_row(3 + r, 0, local)
            value, grad = gelu_and_slope(pre)
            hidden[at, cols] = value.astype(bf16)
            slope[at, cols] = grad.astype(bf16)

    def attend(pair, carry):
        total = plan.group
        block = min(QUERY_ROWS, total)
        lanes = pl.ds(pl.multiple_of(pair * LANES, LANES), LANES)
        for start in range(0, total, block):
            stop = start + block
            here = pl.ds(start, block)
            allowed = attend_mask(begin[here, :], start, block, stop)
            query = q[here, lanes]
            results, logs = [], []
            for head in range(LANES // HEAD):
                mine = head_lanes(block, head)
                chosen = jnp.where(mine, query, jnp.zeros_like(query)) * HEAD ** (-0.5)
                scores = jnp.where(allowed, dot_t(chosen.astype(bf16), k[:stop, lanes]), masked_score)
                top = jnp.max(scores, axis=1, keepdims=True)
                weights = jnp.exp(scores - top)
                total_weight = jnp.sum(weights, axis=1, keepdims=True)
                results.append(dot_n(weights.astype(bf16), v[:stop, lanes]) / total_weight)
                logs.append(top + jnp.log(total_weight))
            first = head_lanes(block, 0)
            att[here, lanes] = jnp.where(first, results[0], results[1]).astype(bf16)
            which = lax.broadcasted_iota(jnp.int32, (block, LANES), 1)
            held = lse[here, :]
            for head in range(LANES // HEAD):
                held = jnp.where(which == pair * (LANES // HEAD) + head, logs[head], held)
            lse[here, :] = held
        return carry

    tile = min(512, plan.model)
    tall = min(512, plan.group)

    def out_tile(j, carry):
        cols = pl.ds(pl.multiple_of(lax.rem(j, plan.model // tile) * tile, tile), tile)
        at = pl.ds(pl.multiple_of((j // (plan.model // tile)) * tall, tall), tall)
        total = dot_n(att[at, :], wd[:local, cols]) + dot_n(hidden[at, :], wd[local:, cols])
        xs[at, cols] = total.astype(bf16)
        return carry

    def back_rows(index):
        at = span(index)
        sums[0:1, :] += jnp.sum(cs[at, :].astype(f32), axis=0, keepdims=True)
        do[at, :] = dot_t(cs[at, :], wd[:local, :]).astype(bf16)
        for r in range(plan.n_mlp):
            cols = slice(r * local, (r + 1) * local)
            grad = dot_t(cs[at, :], wd[(1 + r) * local : (2 + r) * local, :])
            slope[at, cols] = (grad * slope[at, cols].astype(f32)).astype(bf16)

    loads[0].wait()
    z_start(0, 1)
    loads[2].wait()
    w_start(3)
    loads[1].wait()
    w_start(0)
    loads[3].wait()
    loads[4].wait()
    loads[5].wait()
    w_arrive(0, plan.single)
    w_start(1)
    w_arrive(3, plan.single)
    if line > 1:
        z_arrive(0, 1)
        cot_start(1)
    w_arrive(3, plan.several)
    w_arrive(0, plan.several)
    w_arrive(3, plan.odd)
    w_arrive(0, plan.odd)
    write(0, 2)
    sums[...] = jnp.zeros_like(sums)
    lse[...] = jnp.zeros_like(lse)
    at_distance(0, attn_rows)
    if line > 2:
        at_distance(1, attn_rows)
    w_arrive(1, plan.single)
    w_start(2)
    for step in range(2, line - 1):
        z_arrive(0, step)
        cot_start(step)
        at_distance(step, attn_rows)
    w_arrive(1, plan.several)
    w_arrive(1, plan.odd)
    write(1)
    near = max(line - 2, 0)
    lax.fori_loop(
        jnp.maximum(place - near, 0), jnp.minimum(place + near, line - 1) + 1,
        lambda c, carry: (mlp_rows(c), carry)[1], 0,
    )
    if line > 1:
        if line > 2:
            z_arrive(0, line - 1)
            cot_start(line - 1)
        at_distance(line - 1, lambda c: (attn_rows(c), mlp_rows(c))[0])
    write(3, 6, 7, 8, 11)
    pairs = local // LANES
    lax.fori_loop(0, pairs // 2, attend, 0)
    w_arrive(2, plan.single)
    lax.fori_loop(pairs // 2, pairs, attend, 0)
    write(9, 10)
    if line > 1:
        z_arrive(1, 1)
    w_arrive(2, plan.several)
    w_arrive(2, plan.odd)
    out_copy(3).wait()
    for step in range(1, line):
        for up in (True, False):
            left = place != step - 1 if up else place != line - step
            @pl.when(left & sends(step, up))
            def _():
                z_copy(0, step, up).wait_send()
    lax.fori_loop(0, (plan.model // tile) * (plan.group // tall), out_tile, 0)
    write(14)
    at_distance(0, back_rows)
    if line > 1:
        at_distance(1, back_rows)
    for step in range(2, line):
        z_arrive(1, step)
        at_distance(step, back_rows)
    write(4, 5, 12, 13)

    for flow in range(4):
        for mask in range(1, n):
            for half in halves(flow):
                w_copy(flow, mask, half).wait_send()
    for step in range(1, line):
        for up in (True, False):
            z_sent(1, step, up)
    for j in range(len(outs)):
        if j != 3:
            out_copy(j).wait()


def forward(plan, xhat, cot, wa, wm, wd, small, tables, begin):
    any_space = pl.BlockSpec(memory_space=pl.ANY)
    vmem = pl.BlockSpec(memory_space=pltpu.VMEM)
    n, line, group, model, local = plan.n_dp, plan.n_line, plan.group, plan.model, plan.local
    low = lambda *shape: jax.ShapeDtypeStruct(shape, bf16)
    out_shape = [
        low(model, plan.attn), low(model, plan.mlp), low(n, 16, LANES + plan.out_cols),
        low(group, model), jax.ShapeDtypeStruct((8, model), f32), low(group, model),
        low(group, local), low(group, local), low(group, local), low(group, local),
        jax.ShapeDtypeStruct((group, LANES), f32),
        low(group, plan.mlp), low(group, plan.mlp), low(group, local), low(group, model),
    ]
    scratch = lambda s: pltpu.VMEM(s.shape, s.dtype)
    dma = pltpu.SemaphoreType.DMA
    return pl.pallas_call(
        partial(forward_kernel, plan),
        in_specs=[any_space] * 6 + [vmem] * 4,
        out_specs=[any_space] * 15,
        out_shape=out_shape,
        scratch_shapes=[scratch(s) for s in out_shape[:2]]
        + [pltpu.VMEM((plan.down, model), bf16)]
        + [scratch(s) for s in out_shape[2:4]]
        + [pltpu.VMEM((group, model), bf16)]
        + [scratch(s) for s in out_shape[4:14]]
        + [dma((6,)), dma((15,)), dma((8 * n,)), dma((8 * n,))]
        + [dma((2 * line,))] * 4,
        compiler_params=pltpu.CompilerParams(
            collective_id=0, has_side_effects=True, vmem_limit_bytes=63 << 20
        ),
        cost_estimate=pl.CostEstimate(flops=60 * 10**9, bytes_accessed=80 << 20, transcendentals=0),
    )(xhat, cot, wa, wm, wd, small, *tables, begin)


def backward_kernel(
    plan,
    xhat_in, cot_in, att_in, hidden_in, da_in, do_in, q_in, k_in, v_in, part_in, wa_in, wm_in,
    lse, sums_in, own, ahead, behind, begin,
    down_out, in_out, small_out, part_out, rows_out, dh_out,
    turned, stage, og, da, qkv, do, k_sum, v_sum, sent, core_in, held, cube_in, up_in, down_in,
    w_tile, fin, dh_fin, small, small_in, shares,
    load_sem, stage_sem, tile_sem, fin_sem, dh_sem, core_send, core_recv, cube_send, cube_recv,
    up_send, up_recv, down_send, down_recv, small_send, small_recv, part_send, part_recv,
    share_send, share_recv, credit,
):
    n, line = plan.n_dp, plan.n_line
    me, place = lax.axis_index("dp"), lax.axis_index("tensor")
    rows, local, group, model, in_rows = plan.rows, plan.local, plan.group, plan.model, plan.in_rows
    MESH = pl.DeviceIdType.MESH
    half_rows, pairs_n, n_bits = in_rows // 2, n // 2, len(plan.bits)
    orders = (plan.bits, plan.bits[::-1])
    n_down, n_mlp = 1 + plan.n_mlp, plan.n_mlp
    flows = {"down": (n_down, 0, 0), "mlp": (n_mlp, n_down, 3), "attn": (3, 0, 0)}

    def owner(mask):
        index = me
        for b in [1] + plan.bits:
            if mask & b:
                index = index + b - 2 * b * lax.rem(index // b, 2)
        return index

    def peer(bit):
        return {"dp": owner(bit)}

    def position(mask, order):
        return sum((1 if mask & b else 0) << (n_bits - 1 - p) for p, b in enumerate(order))

    whole = [
        (att_in, og.at[:, pl.ds(0, local)]),
        (hidden_in, og.at[:, pl.ds(local, plan.mlp)]),
        (da_in, da),
        (q_in, qkv.at[:, pl.ds(0, local)]),
        (k_in, qkv.at[:, pl.ds(local, local)]),
        (v_in, qkv.at[:, pl.ds(2 * local, local)]),
        (do_in, do),
    ]
    for j, (a, b) in enumerate(whole):
        pltpu.make_async_copy(a, b, load_sem.at[j]).start()

    def loaded(*which):
        for j in which:
            pltpu.make_async_copy(whole[j][0], whole[j][1], load_sem.at[j]).wait()

    barrier = pltpu.get_barrier_semaphore()
    for b in [1] + plan.bits:
        pl.semaphore_signal(barrier, inc=1, device_id=peer(b), device_id_type=MESH)
    for d in range(1, line):
        pl.semaphore_signal(
            barrier, inc=1, device_id={"tensor": lax.rem(place + d, line)}, device_id_type=MESH
        )

    def part_copy(d, arriving):
        source = lax.rem(place + line - d, line) if arriving else place
        target = place if arriving else lax.rem(place + d, line)
        return pltpu.make_async_remote_copy(
            src_ref=part_in.at[pl.ds(pl.multiple_of(target * rows, rows), rows), :],
            dst_ref=part_out.at[source], send_sem=part_send.at[d], recv_sem=part_recv.at[d],
            device_id={"tensor": lax.rem(place + d, line)}, device_id_type=MESH,
        )

    def share_copy(d, arriving):
        source = lax.rem(place + line - d, line) if arriving else place
        return pltpu.make_async_remote_copy(
            src_ref=shares, dst_ref=rows_out.at[source],
            send_sem=share_send.at[d], recv_sem=share_recv.at[d],
            device_id={"tensor": lax.rem(place + d, line)}, device_id_type=MESH,
        )

    part_own = pltpu.make_async_copy(
        part_in.at[pl.ds(pl.multiple_of(place * rows, rows), rows), :], part_out.at[place], part_send.at[0]
    )
    share_own = pltpu.make_async_copy(shares, rows_out.at[place], share_send.at[0])

    def turn_columns(source, masks, first, started=False):
        def fetch(j):
            at = pl.multiple_of(owner(masks[j]) * in_rows, in_rows)
            return pltpu.make_async_copy(
                source.at[:, pl.ds(at, in_rows)], stage.at[j % 2], stage_sem.at[j % 2]
            )

        fetch(0).start()
        for j in range(len(masks)):
            if j + 1 < len(masks):
                fetch(j + 1).start()
            fetch(j).wait()
            turned[pl.ds((first + j) * in_rows, in_rows), :] = stage[j % 2].T

    def core_copy(name, t):
        return pltpu.make_async_remote_copy(
            src_ref=sent.at[lax.rem(t, 2)], dst_ref=core_in.at[t],
            send_sem=core_send.at[lax.rem(t, 2)], recv_sem=core_recv.at[t],
            device_id=peer(1), device_id_type=MESH,
        )

    def cube_copy(slot, half, phase):
        count = pairs_n >> (phase + 1)
        first = pairs_n - 2 * count
        at = half * n_bits + phase
        return pltpu.make_async_remote_copy(
            src_ref=held.at[slot, half, pl.ds(count, count)],
            dst_ref=cube_in.at[slot, half, pl.ds(first, count)],
            send_sem=cube_send.at[slot, at], recv_sem=cube_recv.at[slot, at],
            device_id=peer(orders[half][phase]), device_id_type=MESH,
        )

    def operand(name, t):
        source = {"down": og, "mlp": da, "attn": qkv}[name]
        return source[:, pl.ds(pl.multiple_of(t * local, local), local)]

    send_rows, keep_rows = pl.ds(0, pairs_n * in_rows), pl.ds(pairs_n * in_rows, pairs_n * in_rows)

    def send_core(name):
        tiles = flows[name][0]
        if name != "down":
            pl.semaphore_wait(credit.at[0], 1)

        def step(t, carry):
            @pl.when(t >= 2)
            def _():
                core_copy(name, t - 2).wait_send()
            sent[lax.rem(t, 2)] = dot_n(turned[send_rows, :], operand(name, t)).astype(bf16)
            core_copy(name, t).start()
            return carry

        lax.fori_loop(0, tiles, step, 0)
        for t in range(max(tiles - 2, 0), tiles):
            core_copy(name, t).wait_send()

    def keep_core(name):
        tiles, base, _ = flows[name]

        def step(t, carry):
            total = dot_n(turned[keep_rows, :], operand(name, t))
            core_copy(name, t).wait_recv()
            total = total + core_in[t].astype(f32)
            for j in range(pairs_n):
                for half in range(2):
                    at = j * in_rows + half * half_rows
                    held[base + t, half, position(2 * j, orders[half])] = total[at : at + half_rows].astype(bf16)
            for half in range(2):
                if n_bits:
                    cube_copy(base + t, half, 0).start()
            return carry

        lax.fori_loop(0, tiles, step, 0)
        if name != "attn":
            pl.semaphore_signal(credit.at[0], inc=1, device_id=peer(1), device_id_type=MESH)

    def cube_step(name, phase):
        tiles, base, result = flows[name]
        count = pairs_n >> (phase + 1)
        first = pairs_n - 2 * count
        target = down_out if name == "down" else in_out

        def fin_copy(t):
            return pltpu.make_async_copy(fin.at[lax.rem(t, 2)], target.at[result + t], fin_sem.at[lax.rem(t, 2)])

        def step(t, carry):
            slot = base + t
            if phase == n_bits - 1:
                @pl.when(t >= 2)
                def _():
                    fin_copy(t - 2).wait()
            for half in range(2):
                cube_copy(slot, half, phase).wait_recv()
                total = (
                    held[slot, half, 0:count].astype(f32)
                    + cube_in[slot, half, first : first + count].astype(f32)
                )
                if phase < n_bits - 1:
                    held[slot, half, 0:count] = total.astype(bf16)
                    cube_copy(slot, half, phase + 1).start()
                else:
                    fin[lax.rem(t, 2), half * half_rows : (half + 1) * half_rows, :] = total[0]
            if phase == n_bits - 1:
                fin_copy(t).start()
                if name != "down":
                    weight = w_tile[0 if name == "attn" else 1, 0:in_rows, pl.ds(pl.multiple_of(t * local, local), local)].astype(f32)
                    product = weight * fin[lax.rem(t, 2)]
                    extra = weight * small[n_bits + 1, pl.ds(result + t, 1), :]
                    for g in range(0, local, LANES):
                        shares[0] += product[:, g : g + LANES]
                        shares[1] += extra[:, g : g + LANES]
            return carry

        lax.fori_loop(0, tiles, step, 0)
        if phase == n_bits - 1:
            for t in range(max(tiles - 2, 0), tiles):
                fin_copy(t).wait()

    def cube_sent(name):
        tiles, base, _ = flows[name]

        def step(t, carry):
            for half in range(2):
                for phase in range(n_bits):
                    cube_copy(base + t, half, phase).wait_send()
            return carry

        lax.fori_loop(0, tiles, step, 0)

    def attend(pair, carry):
        block = min(QUERY_ROWS, group)
        scale = HEAD ** (-0.5)
        k_sum[...] = jnp.zeros_like(k_sum)
        v_sum[...] = jnp.zeros_like(v_sum)
        q_lanes, k_lanes, v_lanes = (
            pl.ds(pl.multiple_of(pair * LANES + r * local, LANES), LANES) for r in range(3)
        )
        lanes = q_lanes
        which = lax.broadcasted_iota(jnp.int32, (block, LANES), 1)
        for start in range(0, group, block):
            stop = start + block
            here = pl.ds(start, block)
            allowed = attend_mask(begin[here, :], start, block, stop)
            q_sum = jnp.zeros((block, LANES), f32)
            for head in range(LANES // HEAD):
                mine = head_lanes(block, head)
                query = jnp.where(mine, qkv[here, q_lanes], jnp.zeros((block, LANES), bf16)) * scale
                query = query.astype(bf16)
                cot = jnp.where(mine, do[here, lanes], jnp.zeros((block, LANES), bf16))
                level = jnp.sum(
                    jnp.where(which == pair * (LANES // HEAD) + head, lse[here, :], 0.0), axis=1, keepdims=True
                )
                scores = dot_t(query, qkv[:stop, k_lanes]) - level
                probs = jnp.where(allowed, jnp.exp(scores), 0.0)
                prob_grad = dot_t(cot, qkv[:stop, v_lanes])
                mean = jnp.sum(probs * prob_grad, axis=1, keepdims=True)
                score_grad = (probs * (prob_grad - mean)).astype(bf16)
                q_step = dot_n(score_grad, qkv[:stop, k_lanes])
                q_sum = jnp.where(mine, q_step * scale, q_sum)
                k_sum[:stop, :] += dot_s(score_grad, query)
                v_sum[:stop, :] += dot_s(probs.astype(bf16), cot)
            qkv[here, q_lanes] = turn(
                q_sum, own[here, :], ahead[here, :], behind[here, :], -1.0
            ).astype(bf16)
        qkv[:, k_lanes] = turn(k_sum[...], own[...], ahead[...], behind[...], -1.0).astype(bf16)
        qkv[:, v_lanes] = v_sum[...].astype(bf16)
        return carry

    width = min(256, model)
    d_tiles = model // width

    def tile_loads(t):
        at = pl.ds(pl.multiple_of(t * width, width), width)
        slot = lax.rem(t, 2)
        return (
            pltpu.make_async_copy(wa_in.at[at, :], w_tile.at[slot, pl.ds(0, width), pl.ds(0, plan.attn)], tile_sem.at[slot, 0]),
            pltpu.make_async_copy(wm_in.at[at, :], w_tile.at[slot, pl.ds(0, width), pl.ds(plan.attn, plan.mlp)], tile_sem.at[slot, 1]),
        )

    def line_copy(t, index, up, arriving=False):
        at = pl.ds(pl.multiple_of(index * rows, rows), rows)
        cols = pl.ds(pl.multiple_of(t * width, width), width)
        return pltpu.make_async_remote_copy(
            src_ref=og.at[at, cols],
            dst_ref=(up_in if up else down_in).at[t, index if up else line - 1 - index],
            send_sem=(up_send if up else down_send).at[t, index],
            recv_sem=(up_recv if up else down_recv).at[t, index],
            device_id={"tensor": place + 1 if up != arriving else place - 1}, device_id_type=MESH,
        )

    def line_first(t):
        for up in (True, False):
            @pl.when((place == 0) if up else (place == line - 1))
            def _():
                for step in range(line - 1):
                    line_copy(t, line - 1 - step if up else step, up).start()

    def line_pass(t, step):
        cols = pl.ds(pl.multiple_of(t * width, width), width)
        for up in (True, False):
            index = line - 1 - step if up else step
            at = pl.ds(index * rows, rows)
            hears = (place > 0) & (place < index) if up else (place < line - 1) & (place > index)

            @pl.when(hears)
            def _():
                line_copy(t, index, up, True).wait_recv()
                got = (up_in if up else down_in)[t, index if up else line - 1 - index]
                og[at, cols] = (og[at, cols].astype(f32) + got.astype(f32)).astype(bf16)
                line_copy(t, index, up).start()

    def line_last(t):
        cols = pl.ds(pl.multiple_of(t * width, width), width)
        at = pl.ds(pl.multiple_of(place * rows, rows), rows)
        slot = lax.rem(t, 2)

        @pl.when(t >= 2)
        def _():
            dh_copy(t - 2).wait()
        dh_fin[slot] = og[at, cols].astype(f32)
        for up in (True, False):
            @pl.when((place > 0) if up else (place < line - 1))
            def _():
                line_copy(t, place, up, True).wait_recv()
                buffer = up_in if up else down_in
                dh_fin[slot] += buffer[t, place if up else line - 1 - place].astype(f32)
        dh_copy(t).start()

    def dh_copy(t):
        cols = pl.ds(pl.multiple_of(t * width, width), width)
        return pltpu.make_async_copy(dh_fin.at[lax.rem(t, 2)], dh_out.at[:, cols], dh_sem.at[lax.rem(t, 2)])

    def line_sent(t):
        for index in range(line):
            for up in (True, False):
                goes = (place < index) if up else (place > index)

                @pl.when(goes)
                def _():
                    line_copy(t, index, up).wait_send()

    def dh_tile(t, carry):
        slot = lax.rem(t, 2)
        @pl.when(t + 1 < d_tiles)
        def _():
            for load in tile_loads(t + 1):
                load.start()
        for load in tile_loads(t):
            load.wait()
        total = dot_t(qkv[...], w_tile[slot, 0:width, : plan.attn]) + dot_t(da[...], w_tile[slot, 0:width, plan.attn :])
        og[:, pl.ds(pl.multiple_of(t * width, width), width)] = total.astype(bf16)
        line_first(t)
        return carry

    def small_copy(j):
        return pltpu.make_async_remote_copy(
            src_ref=small.at[j], dst_ref=small_in.at[j],
            send_sem=small_send.at[j], recv_sem=small_recv.at[j],
            device_id=peer(([1] + plan.bits)[j]), device_id_type=MESH,
        )

    def small_step(j):
        small_copy(j).wait_recv()
        small[j + 1] = small[j] + small_in[j]
        if j < n_bits:
            small_copy(j + 1).start()

    shares[...] = jnp.zeros_like(shares)
    small[0] = jnp.zeros_like(small[0])
    for load in tile_loads(0):
        load.start()
    send_masks, keep_masks = [2 * j + 1 for j in range(pairs_n)], [2 * j for j in range(pairs_n)]
    turn_columns(cot_in, send_masks, 0)
    pl.semaphore_wait(barrier, 1 + n_bits + line - 1)
    part_own.start()
    for d in range(1, line):
        part_copy(d, False).start()
    loaded(0, 1)
    send_core("down")
    turn_columns(cot_in, keep_masks, pairs_n)
    keep_core("down")
    loaded(2)
    turn_columns(xhat_in, send_masks, 0)
    send_core("mlp")
    turn_columns(xhat_in, keep_masks, pairs_n)
    keep_core("mlp")
    loaded(3, 4, 5, 6)
    pairs = local // LANES
    lax.fori_loop(0, pairs // 2, attend, 0)
    for phase in range(n_bits - 1):
        cube_step("down", phase)
    lax.fori_loop(pairs // 2, pairs, attend, 0)
    for r in range(3 + n_mlp):
        block = qkv[:, r * local : (r + 1) * local] if r < 3 else da[:, (r - 3) * local : (r - 2) * local]
        small[0, r : r + 1, :] = jnp.sum(block.astype(f32), axis=0, keepdims=True)
    for r in range(model // local):
        small[0, 8 + r : 9 + r, :] = sums_in[0:1, r * local : (r + 1) * local]
    small_copy(0).start()
    lax.fori_loop(0, d_tiles, dh_tile, 0)
    for phase in range(n_bits - 1):
        cube_step("mlp", phase)
    small_step(0)
    cube_step("down", n_bits - 1)
    cube_sent("down")
    for b in plan.bits:
        pl.semaphore_signal(credit.at[1], inc=1, device_id=peer(b), device_id_type=MESH)
    small_step(1)
    send_core("attn")
    pl.semaphore_wait(credit.at[1], n_bits)
    keep_core("attn")
    for j in range(2, n_bits + 1):
        small_step(j)
    own_rows = pl.ds(pl.multiple_of(me * in_rows, in_rows), in_rows)
    weights = [
        pltpu.make_async_copy(wa_in.at[own_rows, :], w_tile.at[0, pl.ds(0, in_rows), pl.ds(0, plan.attn)], tile_sem.at[0, 0]),
        pltpu.make_async_copy(wm_in.at[own_rows, :], w_tile.at[1, pl.ds(0, in_rows), pl.ds(0, plan.mlp)], tile_sem.at[1, 0]),
    ]
    for w in weights:
        w.start()

    def passes(first, stop):
        def step(t, carry):
            for s in range(line - 1):
                line_pass(t, s)
            return carry
        lax.fori_loop(first, stop, step, 0)

    passes(0, d_tiles // 2)
    for w in weights:
        w.wait()
    cube_step("mlp", n_bits - 1)
    passes(d_tiles // 2, d_tiles)
    for phase in range(n_bits):
        cube_step("attn", phase)
    share_own.start()
    for d in range(1, line):
        share_copy(d, False).start()

    def last(t, carry):
        line_last(t)
        return carry

    lax.fori_loop(0, d_tiles, last, 0)
    for t in range(max(d_tiles - 2, 0), d_tiles):
        dh_copy(t).wait()
    small_done = pltpu.make_async_copy(small.at[n_bits + 1], small_out, load_sem.at[0])
    small_done.start()
    cube_sent("mlp")
    cube_sent("attn")

    def sent_all(t, carry):
        line_sent(t)
        return carry

    lax.fori_loop(0, d_tiles, sent_all, 0)
    for j in range(n_bits + 1):
        small_copy(j).wait_send()
    part_own.wait()
    share_own.wait()
    for d in range(1, line):
        part_copy(d, False).wait_send()
        part_copy(d, True).wait_recv()
        share_copy(d, False).wait_send()
        share_copy(d, True).wait_recv()
    small_done.wait()


def backward(plan, xhat, cot, att, hidden, da, do, q, k, v, part, wa, wm, lse, sums, tables, begin):
    any_space = pl.BlockSpec(memory_space=pl.ANY)
    vmem = pl.BlockSpec(memory_space=pltpu.VMEM)
    n, line, group, model, local = plan.n_dp, plan.n_line, plan.group, plan.model, plan.local
    rows, in_rows, n_bits, pairs_n = plan.rows, plan.in_rows, len(plan.bits), n // 2
    n_down = 1 + plan.n_mlp
    small_rows = 8 + -(-(model // local) // 8) * 8
    width = min(256, model)
    d_tiles = model // width
    low = lambda *shape: pltpu.VMEM(shape, bf16)
    full = lambda *shape: pltpu.VMEM(shape, f32)
    dma = pltpu.SemaphoreType.DMA
    out = lambda dtype, *shape: jax.ShapeDtypeStruct(shape, dtype)
    slots = n_down + plan.n_mlp
    return pl.pallas_call(
        partial(backward_kernel, plan),
        in_specs=[any_space] * 12 + [vmem] * 6,
        out_specs=[any_space] * 6,
        out_shape=[
            out(f32, n_down, in_rows, local), out(f32, 3 + plan.n_mlp, in_rows, local),
            out(f32, small_rows, local), out(bf16, line, rows, model),
            out(f32, line, 2, in_rows, LANES), out(f32, rows, model),
        ],
        scratch_shapes=[
            low(n * in_rows, group), low(2, group, in_rows), low(group, plan.down), low(group, plan.mlp),
            low(group, plan.attn), low(group, local), full(group, LANES), full(group, LANES),
            low(2, pairs_n * in_rows, local), low(n_down, pairs_n * in_rows, local),
            low(slots, 2, pairs_n, in_rows // 2, local), low(slots, 2, max(pairs_n - 1, 1), in_rows // 2, local),
            low(d_tiles, line, rows, width), low(d_tiles, line, rows, width),
            low(2, max(width, in_rows), plan.attn + plan.mlp), full(2, in_rows, local), full(2, rows, width),
            full(n_bits + 2, small_rows, local), full(n_bits + 1, small_rows, local), full(2, in_rows, LANES),
            dma((7,)), dma((2,)), dma((2, 2)), dma((2,)), dma((2,)), dma((2,)), dma((n_down,)),
            dma((slots, max(2 * n_bits, 1))), dma((slots, max(2 * n_bits, 1))),
            dma((d_tiles, line)), dma((d_tiles, line)), dma((d_tiles, line)), dma((d_tiles, line)),
            dma((n_bits + 1,)), dma((n_bits + 1,)), dma((line,)), dma((line,)), dma((line,)), dma((line,)),
            pltpu.SemaphoreType.REGULAR((2,)),
        ],
        compiler_params=pltpu.CompilerParams(
            collective_id=1, has_side_effects=True, vmem_limit_bytes=63 << 20
        ),
        cost_estimate=pl.CostEstimate(flops=80 * 10**9, bytes_accessed=80 << 20, transcendentals=0),
    )(xhat, cot, att, hidden, da, do, q, k, v, part, wa, wm, lse, sums, *tables, begin)


def adam_update(weight, moment_one, moment_two, gradient, step_rate, decay_factor):
    first_new = beta_first * moment_one + (1.0 - beta_first) * gradient
    second_new = beta_second * moment_two + (1.0 - beta_second) * gradient * gradient
    corrected = first_new / (1.0 - beta_first**STEP)
    spread = jnp.sqrt(second_new / (1.0 - beta_second**STEP))
    return (
        weight - step_rate * (corrected / (spread + adam_eps) + decay_factor * weight),
        first_new,
        second_new,
    )


def per_device(
    block_input,
    out_grad,
    seq_lengths,
    in_weight,
    down_weight,
    column_bias,
    vector_params,
    in_first,
    in_second,
    down_first,
    down_second,
    bias_first,
    bias_second,
    vector_first,
    vector_second,
):
    n_dp = lax.axis_size("dp")
    n_tensor = lax.axis_size("tensor")
    own_rows, model = block_input.shape
    group = own_rows * n_tensor
    in_rows, widths, local = in_weight.shape
    out_cols = down_weight.shape[2]
    n_mlp = widths - 3
    attn_width, mlp_width = 3 * local, n_mlp * local

    in_attn = in_weight[:, :3].astype(bf16).reshape(in_rows, attn_width)
    in_mlp = in_weight[:, 3:].astype(bf16).reshape(in_rows, mlp_width)
    down_low = down_weight.astype(bf16).reshape(widths_down(down_weight), out_cols)

    centered = block_input - jnp.mean(block_input, axis=-1, keepdims=True)
    inv_scale = lax.rsqrt(jnp.mean(centered * centered, axis=-1, keepdims=True) + norm_eps)
    xhat = centered * inv_scale
    begin, position, live = layout(seq_lengths[0], group)
    own_live = lax.dynamic_slice_in_dim(live, lax.axis_index("tensor") * own_rows, own_rows)
    cot_live = out_grad * own_live[:, None]
    cot_low = cot_live.astype(bf16)

    me = lax.axis_index("dp")
    plan = Plan(n_dp, n_tensor, own_rows, model, in_rows, local, n_mlp, out_cols)
    lane = lax.rem(me, LANES // plan.bias_cols) * plan.bias_cols
    bias_tile = lax.dynamic_update_slice(
        jnp.zeros((16, LANES), bf16), column_bias.astype(bf16), (0, lane)
    )
    small = jnp.concatenate([bias_tile, jnp.pad(vector_params.astype(bf16), ((0, 13), (0, 0)))], axis=1)
    tables = rotary_tables(position)
    begin_col = begin[:, None]
    (
        w_attn, w_mlp, vectors, xhat_all, cot_sums, cot_all, q_low, k_low, v_low, attended, lse,
        hidden, pre_grad, attn_grad, out_part,
    ) = forward(plan, xhat.astype(bf16), cot_low, in_attn, in_mlp, down_low, small, tables, begin_col)
    down_grad, in_grad, small_grad, parts, shares, dh = backward(
        plan, xhat_all, cot_all, attended, hidden, pre_grad, attn_grad, q_low, k_low, v_low, out_part,
        w_attn, w_mlp, lse, cot_sums, tables, begin_col,
    )
    vector_vals = vectors[:, :3, LANES:].transpose(1, 0, 2).reshape(3, model).astype(f32)
    gain, out_bias = vector_vals[0], vector_vals[2]
    block_out = block_input + (jnp.sum(parts.astype(f32), axis=0) + out_bias)

    dxhat = dh * gain
    input_grad = cot_live + inv_scale * (
        dxhat
        - jnp.mean(dxhat, axis=-1, keepdims=True)
        - xhat * jnp.mean(dxhat * xhat, axis=-1, keepdims=True)
    )

    bias_full = small_grad[:widths]
    own_vectors = vector_params.astype(bf16).astype(f32)
    in_reduced = (
        in_grad * own_vectors[0][None, :, None] + own_vectors[1][None, :, None] * bias_full[:, None, :]
    ).transpose(1, 0, 2)
    down_reduced = down_grad.transpose(0, 2, 1)
    bias_reduced = lax.dynamic_slice_in_dim(bias_full, me * plan.bias_cols, plan.bias_cols, 1)
    out_sums = small_grad[8 : 8 + model // local].reshape(-1)
    vector_reduced = jnp.stack(
        [
            jnp.sum(shares[:, 0], axis=(0, 2)),
            jnp.sum(shares[:, 1], axis=(0, 2)),
            lax.dynamic_slice_in_dim(out_sums, me * out_cols, out_cols, 0),
        ]
    )

    in_new, in_one, in_two = adam_update(
        in_weight, in_first, in_second, in_reduced, rate_in, weight_decay
    )
    down_new, down_one, down_two = adam_update(
        down_weight, down_first, down_second, down_reduced, rate_down, weight_decay
    )
    bias_new, bias_one, bias_two = adam_update(
        column_bias, bias_first, bias_second, bias_reduced, rate_vector, 0.0
    )
    vector_new, vector_one, vector_two = adam_update(
        vector_params, vector_first, vector_second, vector_reduced, rate_vector, 0.0
    )
    return (
        block_out,
        input_grad,
        in_new,
        in_one,
        in_two,
        down_new,
        down_one,
        down_two,
        bias_new,
        bias_one,
        bias_two,
        vector_new,
        vector_one,
        vector_two,
    )


def widths_down(down_weight):
    return down_weight.shape[0] * down_weight.shape[1]


def solution(mesh):
    return jax.shard_map(
        per_device,
        mesh=mesh,
        in_specs=(
            P(("dp", "tensor"), None),
            P(("dp", "tensor"), None),
            P("dp", None),
            P("dp", None, "tensor"),
            P(None, "tensor", "dp"),
            P(None, ("tensor", "dp")),
            P(None, "dp"),
            P("dp", None, "tensor"),
            P("dp", None, "tensor"),
            P(None, "tensor", "dp"),
            P(None, "tensor", "dp"),
            P(None, ("tensor", "dp")),
            P(None, ("tensor", "dp")),
            P(None, "dp"),
            P(None, "dp"),
        ),
        out_specs=(
            P(("dp", "tensor"), None),
            P(("dp", "tensor"), None),
            P("dp", None, "tensor"),
            P("dp", None, "tensor"),
            P("dp", None, "tensor"),
            P(None, "tensor", "dp"),
            P(None, "tensor", "dp"),
            P(None, "tensor", "dp"),
            P(None, ("tensor", "dp")),
            P(None, ("tensor", "dp")),
            P(None, ("tensor", "dp")),
            P(None, "dp"),
            P(None, "dp"),
            P(None, "dp"),
        ),
        check_vma=False,
    )
```

```python
from functools import partial

import jax
import jax.numpy as jnp
import numpy as np
from jax import lax
from jax.experimental import pallas as pl
from jax.experimental.pallas import tpu as pltpu
from jax.sharding import PartitionSpec as P

HEAD = 64
ROT = 32
STEP = 8
LANES = 128
QUERY_ROWS = 256

norm_eps = 1e-05
beta_first = 0.9
beta_second = 0.95
adam_eps = 1e-08
masked_score = -1000000000.0
rate_in = 0.02
rate_down = 0.05
rate_vector = 0.2
weight_decay = 0.1

bf16 = jnp.bfloat16
f32 = jnp.float32


def angle_tables(rows):
    half_rot = ROT // 2
    frequency = 10000.0 ** (-2.0 * (np.arange(LANES) % half_rot) / ROT)
    angles = np.arange(rows)[:, None] * frequency[None, :]
    return np.cos(angles).astype(np.float32), np.sin(angles).astype(np.float32)


def ends_of(lengths):
    ends = [jnp.int32(0)]
    for j in range(lengths.shape[1]):
        ends.append(ends[-1] + lengths[0, j])
    return ends


def begins_of(lengths, start, rows):
    places = start + lax.broadcasted_iota(jnp.int32, (rows, 1), 0)
    begin = jnp.zeros((rows, 1), jnp.int32)
    for end in ends_of(lengths)[1:]:
        begin = jnp.where(places >= end, end, begin)
    return begin


def attend_mask(begin, row_start, rows, stop):
    key_place = lax.broadcasted_iota(jnp.int32, (rows, stop), 1)
    query_place = row_start + lax.broadcasted_iota(jnp.int32, (rows, stop), 0)
    return (key_place <= query_place) & (key_place >= begin)


def head_lanes(rows, head):
    lane = lax.broadcasted_iota(jnp.int32, (rows, LANES), 1)
    return (lane >= head * HEAD) & (lane < (head + 1) * HEAD)


def dot_t(a, b):
    return lax.dot_general(a, b, (((1,), (1,)), ((), ())), preferred_element_type=f32)


def dot_n(a, b):
    return lax.dot_general(a, b, (((1,), (0,)), ((), ())), preferred_element_type=f32)


def dot_s(a, b):
    return lax.dot_general(a, b, (((0,), (0,)), ((), ())), preferred_element_type=f32)


def turn(x, own, ahead, behind, sign):
    half = ROT // 2
    return x * own + sign * (
        pltpu.roll(x, LANES - half, 1) * ahead + pltpu.roll(x, half, 1) * behind
    )


def low_bit(mask):
    return mask & -mask


def high_bit(mask):
    return 1 << (mask.bit_length() - 1)


def gelu_and_slope(a):
    root = (2.0 / 3.141592653589793) ** 0.5
    square = a * a
    t = jnp.tanh(root * a * (1.0 + 0.044715 * square))
    half = 0.5 * (1.0 + t)
    return a * half, half + 0.5 * a * (1.0 - t * t) * (root * (1.0 + 3.0 * 0.044715 * square))


class LineSum:
    def __init__(self, place, line, source, landing, sems):
        self.place, self.line, self.source, self.landing = place, line, source, landing
        self.up_send, self.up_recv, self.down_send, self.down_recv = sems

    def copy(self, t, index, up, arriving=False):
        place = self.place
        slot = index - 1 if up else self.line - 2 - index
        return pltpu.make_async_remote_copy(
            src_ref=self.source(t, index),
            dst_ref=self.landing(t, slot, up),
            send_sem=(self.up_send if up else self.down_send).at[t, slot],
            recv_sem=(self.up_recv if up else self.down_recv).at[t, slot],
            device_id={"tensor": place + 1 if up != arriving else place - 1},
            device_id_type=pl.DeviceIdType.MESH,
        )

    def got(self, t, index, up):
        return self.landing(t, index - 1 if up else self.line - 2 - index, up)[...].astype(f32)

    def first(self, t):
        for up in (True, False):
            @pl.when((self.place == 0) if up else (self.place == self.line - 1))
            def _():
                for step in range(self.line - 1):
                    self.copy(t, self.line - 1 - step if up else step, up).start()

    def hand_on(self, t, up):
        place, line = self.place, self.line
        for step in range(line - 1):
            index = line - 1 - step if up else step
            hears = (place > 0) & (place < index) if up else (place < line - 1) & (place > index)

            @pl.when(hears)
            def _():
                self.copy(t, index, up, True).wait_recv()
                mine = self.source(t, index)
                mine[...] = (mine[...].astype(f32) + self.got(t, index, up)).astype(bf16)
                self.copy(t, index, up).start()

    def last(self, t, target):
        place, line = self.place, self.line
        target[...] = self.source(t, place)[...].astype(f32)
        for up in (True, False):
            @pl.when((place > 0) if up else (place < line - 1))
            def _():
                self.copy(t, place, up, True).wait_recv()
                target[...] += self.got(t, place, up)

    def sent(self, t):
        for index in range(self.line):
            for up in (True, False):
                @pl.when((self.place < index) if up else (self.place > index))
                def _():
                    self.copy(t, index, up).wait_send()


class Plan:
    def __init__(self, n_dp, n_line, rows, model, in_rows, local, n_mlp, out_cols):
        self.n_dp, self.n_line = n_dp, n_line
        self.rows, self.model = rows, model
        self.group = rows * n_line
        self.in_rows, self.local, self.n_mlp, self.out_cols = in_rows, local, n_mlp, out_cols
        self.attn, self.mlp = 3 * local, n_mlp * local
        self.down = (1 + n_mlp) * local
        self.bias_cols = local // n_dp
        self.width = min(256, model // 4)
        self.d_tiles = model // self.width
        self.early = 3 * self.d_tiles // 4
        self.bits = [1 << b for b in range(1, n_dp.bit_length() - 1)]
        even = range(2, n_dp, 2)
        self.single = [m for m in even if m.bit_count() == 1]
        self.several = sorted((m for m in even if m.bit_count() > 1), key=lambda m: m.bit_count())
        self.odd = list(range(1, n_dp, 2))

    def hop(self, mask, half):
        if mask & 1:
            return 1
        return high_bit(mask) if half == 0 else low_bit(mask)

    def onward(self, mask, half):
        if mask & 1:
            return []
        masks = [mask | 1] if self.n_dp > 1 else []
        return masks + [
            mask | b for b in self.bits if not mask & b and self.hop(mask | b, half) == b
        ]


def forward_kernel(
    plan,
    x_in, out_grad_in, w_in, wd_in, small_in, lengths, place_cos, place_sin,
    wa_out, wm_out, small_out, xhat_out, sums_out, cot_out, q_out, k_out, v_out, att_out, lse_out,
    hidden_out, da_out, do_out, part_out, own_out, ahead_out, behind_out, stats_out, mixed_out,
    wa, wm, wd, small, xs, ns, sums, cs, q, k, v, att, lse, hidden, slope, do,
    own, ahead, behind, stats, wide, block, tall_block,
    own_sem, block_sem, out_sem, w_send, w_recv, up_send, up_recv, down_send, down_recv,
    sum_up_send, sum_up_recv, sum_down_send, sum_down_recv, ready,
):
    n, line = plan.n_dp, plan.n_line
    me, place = lax.axis_index("dp"), lax.axis_index("tensor")
    rows, local, model = plan.rows, plan.local, plan.model

    def owner(mask):
        index = me
        for b in [1] + plan.bits:
            if mask & b:
                index = index + b - 2 * b * lax.rem(index // b, 2)
        return index

    def slot(flow, index, half):
        if flow < 2:
            step = plan.in_rows // 2
            at = pl.multiple_of(index * plan.in_rows + half * step, step)
            return (wa, wm)[flow].at[pl.ds(at, step), :]
        if flow == 2:
            step = plan.down // 2
            at = pl.multiple_of(index * plan.out_cols, plan.out_cols)
            return wd.at[pl.ds(half * step, step), pl.ds(at, plan.out_cols)]
        return small.at[index]

    def halves(flow):
        return (0,) if flow == 3 else (0, 1)

    def w_copy(flow, mask, half):
        hop = plan.hop(mask, half)
        piece = slot(flow, owner(mask ^ hop), half)
        at = flow * 2 * n + 2 * mask + half
        return pltpu.make_async_remote_copy(
            src_ref=piece, dst_ref=piece, send_sem=w_send.at[at], recv_sem=w_recv.at[at],
            device_id={"dp": owner(hop)}, device_id_type=pl.DeviceIdType.MESH,
        )

    def w_start(flow, mask=0):
        for half in halves(flow):
            for target in plan.onward(mask, half):
                w_copy(flow, target, half).start()

    def w_arrive(flow, masks):
        for mask in masks:
            for half in halves(flow):
                piece = slot(flow, owner(mask), half)
                at = flow * 2 * n + 2 * mask + half
                pltpu.make_async_remote_copy(
                    src_ref=piece, dst_ref=piece, send_sem=w_send.at[at], recv_sem=w_recv.at[at],
                    device_id={"dp": owner(plan.hop(mask, half))}, device_id_type=pl.DeviceIdType.MESH,
                ).wait_recv()
                for target in plan.onward(mask, half):
                    w_copy(flow, target, half).start()

    def chunk(flow, index):
        return (xs, cs)[flow].at[pl.ds(pl.multiple_of(index * rows, rows), rows), :]

    def z_copy(flow, step, up):
        piece = chunk(flow, place - (step - 1) if up else place + (step - 1))
        at = flow * line + step
        return pltpu.make_async_remote_copy(
            src_ref=piece, dst_ref=piece,
            send_sem=(up_send if up else down_send).at[at],
            recv_sem=(up_recv if up else down_recv).at[at],
            device_id={"tensor": place + 1 if up else place - 1}, device_id_type=pl.DeviceIdType.MESH,
        )

    def sends(step, up):
        if up:
            return (place < line - 1) & (place >= step - 1)
        return (place > 0) & (place + step - 1 <= line - 1)

    def z_start(flow, step):
        for up in (True, False):
            @pl.when(sends(step, up))
            def _():
                z_copy(flow, step, up).start()

    def z_arrive(flow, step):
        for up in (True, False):
            @pl.when(place >= step if up else place + step <= line - 1)
            def _():
                piece = chunk(flow, place - step if up else place + step)
                at = flow * line + step
                pltpu.make_async_remote_copy(
                    src_ref=piece, dst_ref=piece,
                    send_sem=(up_send if up else down_send).at[at],
                    recv_sem=(up_recv if up else down_recv).at[at],
                    device_id={"tensor": place - 1 if up else place + 1},
                    device_id_type=pl.DeviceIdType.MESH,
                ).wait_recv()
        if step + 1 < line:
            z_start(flow, step + 1)

    def z_sent(flow, step, up):
        @pl.when(sends(step, up))
        def _():
            z_copy(flow, step, up).wait_send()

    def cot_start(step):
        for up in (True, False):
            last = place == step - 1 if up else place == line - step
            @pl.when(last & sends(1, up))
            def _():
                z_copy(0, step, up).wait_send()
                z_copy(1, 1, up).start()

    def at_distance(step, fn):
        if step == 0:
            fn(place)
            return

        def side(j, carry):
            index = place - step + 2 * step * j

            @pl.when((index >= 0) & (index < line))
            def _():
                fn(index)
            return carry

        lax.fori_loop(0, 2, side, 0)

    def span(index):
        return pl.ds(pl.multiple_of(index * rows, rows), rows)

    early = plan.early * plan.width
    outs = [
        (wa, wa_out), (wm, wm_out), (small, small_out), (xs, xhat_out), (sums, sums_out), (cs, cot_out),
        (q, q_out), (k, k_out), (v, v_out), (att, att_out), (lse, lse_out), (hidden, hidden_out),
        (slope, da_out), (do, do_out), (xs.at[:, pl.ds(early, model - early)], part_out),
        (own, own_out), (ahead, ahead_out), (behind, behind_out), (stats, stats_out),
        (wide.at[:, pl.ds(0, early)], mixed_out),
    ]

    def out_copy(j):
        return pltpu.make_async_copy(outs[j][0], outs[j][1], out_sem.at[j])

    def write(*which):
        for j in which:
            out_copy(j).start()

    w_rows = pl.ds(pl.multiple_of(me * plan.in_rows, plan.in_rows), plan.in_rows)
    w_cols = pl.ds(pl.multiple_of(me * plan.out_cols, plan.out_cols), plan.out_cols)
    small_load = pltpu.make_async_copy(small_in, small.at[me], own_sem.at[2])

    def in_load(r):
        return pltpu.make_async_copy(w_in.at[r], block.at[r % 2], block_sem.at[0, r % 2])

    def down_load(r):
        return pltpu.make_async_copy(wd_in.at[r], tall_block.at[r % 2], block_sem.at[1, r % 2])

    def round_in(first, stop, target, shift):
        for r in range(first, stop):
            in_load(r).wait()
            target[w_rows, (r - shift) * local : (r - shift + 1) * local] = block[r % 2].astype(bf16)
            if r + 2 < 3 + plan.n_mlp:
                in_load(r + 2).start()

    def round_down():
        for r in range(1 + plan.n_mlp):
            down_load(r).wait()
            wd[r * local : (r + 1) * local, w_cols] = tall_block[r % 2].astype(bf16)
            if r + 2 < 1 + plan.n_mlp:
                down_load(r + 2).start()

    x_load = pltpu.make_async_copy(x_in, wide, own_sem.at[0])
    cot_load = pltpu.make_async_copy(out_grad_in, wide, own_sem.at[1])
    x_load.start()
    small_load.start()
    in_load(0).start()
    in_load(1).start()
    down_load(0).start()
    down_load(1).start()
    barrier = pltpu.get_barrier_semaphore()
    for b in [1] + plan.bits if n > 1 else []:
        pl.semaphore_signal(barrier, inc=1, device_id={"dp": owner(b)}, device_id_type=pl.DeviceIdType.MESH)

    @pl.when(place < line - 1)
    def _():
        pl.semaphore_signal(barrier, inc=1, device_id={"tensor": place + 1}, device_id_type=pl.DeviceIdType.MESH)

    @pl.when(place > 0)
    def _():
        pl.semaphore_signal(barrier, inc=1, device_id={"tensor": place - 1}, device_id_type=pl.DeviceIdType.MESH)

    beside = (place + line - 1) // line + (2 * line - 2 - place) // line
    pl.semaphore_wait(barrier, (1 + len(plan.bits) if n > 1 else 0) + beside)

    def normalize_rows(index):
        at = span(index)
        gain = jnp.concatenate([small[o, 0:1, LANES:] for o in range(n)], axis=1).astype(f32)
        shift = jnp.concatenate([small[o, 1:2, LANES:] for o in range(n)], axis=1).astype(f32)
        ns[...] = (xs[at, :].astype(f32) * gain + shift).astype(bf16)

    def bias_row(r, first, width):
        per = LANES // plan.bias_cols
        groups = []
        for g in range(first // LANES, (first + width) // LANES):
            total = small[g * per, r : r + 1, :LANES].astype(f32)
            for o in range(1, per):
                total = total + small[g * per + o, r : r + 1, :LANES].astype(f32)
            groups.append(total)
        return jnp.concatenate(groups, axis=1)

    def attn_rows(index):
        at = span(index)
        normalize_rows(index)
        for r, target in enumerate((q, k, v)):
            proj = dot_n(ns[...], wa[:, r * local : (r + 1) * local]) + bias_row(r, 0, local)
            if r == 2:
                target[at, :] = proj.astype(bf16)
            else:
                for g in range(0, local, LANES):
                    target[at, g : g + LANES] = turn(
                        proj[:, g : g + LANES], own[at, :], ahead[at, :], behind[at, :], 1.0
                    ).astype(bf16)

    def mlp_rows(index):
        at = span(index)
        normalize_rows(index)
        for r in range(plan.n_mlp):
            cols = slice(r * local, (r + 1) * local)
            pre = dot_n(ns[...], wm[:, cols]) + bias_row(3 + r, 0, local)
            value, grad = gelu_and_slope(pre)
            hidden[at, cols] = value.astype(bf16)
            slope[at, cols] = grad.astype(bf16)

    def attend(pair, carry):
        total = plan.group
        block = min(QUERY_ROWS, total)
        lanes = pl.ds(pl.multiple_of(pair * LANES, LANES), LANES)
        for start in range(0, total, block):
            stop = start + block
            here = pl.ds(start, block)
            allowed = attend_mask(begins_of(lengths, start, block), start, block, stop)
            query = q[here, lanes]
            results, logs = [], []
            for head in range(LANES // HEAD):
                mine = head_lanes(block, head)
                chosen = jnp.where(mine, query, jnp.zeros_like(query)) * HEAD ** (-0.5)
                scores = jnp.where(allowed, dot_t(chosen.astype(bf16), k[:stop, lanes]), masked_score)
                top = jnp.max(scores, axis=1, keepdims=True)
                weights = jnp.exp(scores - top)
                total_weight = jnp.sum(weights, axis=1, keepdims=True)
                results.append(dot_n(weights.astype(bf16), v[:stop, lanes]) / total_weight)
                logs.append(top + jnp.log(total_weight))
            first = head_lanes(block, 0)
            att[here, lanes] = jnp.where(first, results[0], results[1]).astype(bf16)
            which = lax.broadcasted_iota(jnp.int32, (block, LANES), 1)
            held = lse[here, :]
            for head in range(LANES // HEAD):
                held = jnp.where(which == pair * (LANES // HEAD) + head, logs[head], held)
            lse[here, :] = held
        return carry

    width = plan.width
    tall = min(512, plan.group)

    def out_tile(t):
        cols = pl.ds(pl.multiple_of(t * width, width), width)

        def part(j, carry):
            at = pl.ds(pl.multiple_of(j * tall, tall), tall)
            total = dot_n(att[at, :], wd[:local, cols]) + dot_n(hidden[at, :], wd[local:, cols])
            xs[at, cols] = total.astype(bf16)
            return carry

        lax.fori_loop(0, plan.group // tall, part, 0)

    def tile_source(t, index):
        return xs.at[span(index), pl.ds(pl.multiple_of(t * width, width), width)]

    def tile_landing(t, slot, up):
        at = slot * rows + (0 if up else (line - 1) * rows)
        return wm.at[pl.ds(pl.multiple_of(at, rows), rows), pl.ds(pl.multiple_of(t * width, width), width)]

    out_sum = LineSum(
        place, line, tile_source, tile_landing, (sum_up_send, sum_up_recv, sum_down_send, sum_down_recv)
    )

    def early_tiles(fn):
        lax.fori_loop(0, plan.early, lambda t, carry: (fn(t), carry)[1], 0)

    def back_rows(index):
        at = span(index)
        sums[0:1, :] += jnp.sum(cs[at, :].astype(f32), axis=0, keepdims=True)
        do[at, :] = dot_t(cs[at, :], wd[:local, :]).astype(bf16)
        for r in range(plan.n_mlp):
            cols = slice(r * local, (r + 1) * local)
            grad = dot_t(cs[at, :], wd[(1 + r) * local : (2 + r) * local, :])
            slope[at, cols] = (grad * slope[at, cols].astype(f32)).astype(bf16)

    def normalize_own():
        x_load.wait()
        value = wide[...]
        mean = jnp.mean(value, axis=1, keepdims=True)
        centered = value - mean
        scale = lax.rsqrt(jnp.mean(centered * centered, axis=1, keepdims=True) + norm_eps)
        xs[span(place), :] = (centered * scale).astype(bf16)
        stats[0] = jnp.broadcast_to(mean, (rows, LANES))
        stats[1] = jnp.broadcast_to(scale, (rows, LANES))
        cot_load.start()

    def mask_cot():
        cot_load.wait()
        places = place * rows + lax.broadcasted_iota(jnp.int32, (rows, 1), 0)
        cs[span(place), :] = jnp.where(places < ends_of(lengths)[-1], wide[...], 0.0).astype(bf16)

    def make_tables():
        block_rows = min(QUERY_ROWS, plan.group)
        ends = ends_of(lengths)
        for start in range(0, plan.group, block_rows):
            at = pl.ds(start, block_rows)
            places = start + lax.broadcasted_iota(jnp.int32, (block_rows, LANES), 0)
            begin_cos, begin_sin = place_cos[0:1, :], place_sin[0:1, :]
            for end in ends[1:]:
                row = pl.ds(jnp.minimum(end, plan.group - 1), 1)
                begin_cos = jnp.where(places >= end, place_cos[row, :], begin_cos)
                begin_sin = jnp.where(places >= end, place_sin[row, :], begin_sin)
            cosine = place_cos[at, :] * begin_cos + place_sin[at, :] * begin_sin
            sine = place_sin[at, :] * begin_cos - place_cos[at, :] * begin_sin
            lane = lax.rem(lax.broadcasted_iota(jnp.int32, (block_rows, LANES), 1), HEAD)
            own[at, :] = jnp.where(lane < ROT, cosine, 1.0)
            ahead[at, :] = jnp.where(lane < ROT // 2, -sine, 0.0)
            behind[at, :] = jnp.where((lane >= ROT // 2) & (lane < ROT), sine, 0.0)

    normalize_own()
    z_start(0, 1)
    small_load.wait()
    w_start(3)
    round_in(0, 3, wa, 0)
    w_start(0)
    round_in(3, 3 + plan.n_mlp, wm, 3)
    mask_cot()
    round_down()
    make_tables()
    sums[...] = jnp.zeros_like(sums)
    lse[...] = jnp.zeros_like(lse)
    write(15, 16, 17, 18)
    w_arrive(0, plan.single)
    w_start(1)
    w_arrive(3, plan.single)
    z_arrive(0, 1)
    cot_start(1)
    w_arrive(3, plan.several)
    w_arrive(0, plan.several)
    w_arrive(3, plan.odd)
    w_arrive(0, plan.odd)
    write(0, 2)
    at_distance(0, attn_rows)
    if line > 2:
        at_distance(1, attn_rows)
    w_arrive(1, plan.single)
    w_start(2)
    for step in range(2, line - 1):
        z_arrive(0, step)
        cot_start(step)
        at_distance(step, attn_rows)
    w_arrive(1, plan.several)
    w_arrive(1, plan.odd)
    write(1)
    near = max(line - 2, 0)
    lax.fori_loop(
        jnp.maximum(place - near, 0), jnp.minimum(place + near, line - 1) + 1,
        lambda c, carry: (mlp_rows(c), carry)[1], 0,
    )
    if line > 2:
        z_arrive(0, line - 1)
        cot_start(line - 1)
    at_distance(line - 1, lambda c: (attn_rows(c), mlp_rows(c))[0])
    write(3, 6, 7, 8, 11)
    pairs = local // LANES
    lax.fori_loop(0, pairs // 2, attend, 0)
    w_arrive(2, plan.single)
    out_copy(1).wait()
    for mask in range(1, n):
        for half in halves(1):
            w_copy(1, mask, half).wait_send()

    @pl.when(place < line - 1)
    def _():
        pl.semaphore_signal(ready, inc=1, device_id={"tensor": place + 1}, device_id_type=pl.DeviceIdType.MESH)

    @pl.when(place > 0)
    def _():
        pl.semaphore_signal(ready, inc=1, device_id={"tensor": place - 1}, device_id_type=pl.DeviceIdType.MESH)

    lax.fori_loop(pairs // 2, pairs, attend, 0)
    write(9, 10)
    z_arrive(1, 1)
    w_arrive(2, plan.several)
    out_copy(3).wait()
    for step in range(1, line):
        for up in (True, False):
            left = place != step - 1 if up else place != line - step
            @pl.when(left & sends(step, up))
            def _():
                z_copy(0, step, up).wait_send()
    pl.semaphore_wait(ready, beside)
    w_arrive(2, plan.odd)

    def first_tile(t):
        out_tile(t)
        out_sum.first(t)

    early_tiles(first_tile)
    lax.fori_loop(plan.early, plan.d_tiles, lambda t, carry: (out_tile(t), carry)[1], 0)
    write(14)
    at_distance(0, back_rows)
    if line > 2:
        at_distance(1, back_rows)
    for step in range(2, line - 1):
        z_arrive(1, step)
        at_distance(step, back_rows)

    def running(near_end):
        for up in (True, False):
            now = (place < line // 2) if up == near_end else (place >= line // 2)

            @pl.when(now)
            def _():
                for step in range(1, line):
                    z_sent(1, step, up)
                early_tiles(lambda t: out_sum.hand_on(t, up))

    running(True)
    if line > 2:
        z_arrive(1, line - 1)
    running(False)
    at_distance(line - 1, back_rows)
    write(4, 5, 12, 13)
    early_tiles(lambda t: out_sum.last(t, wide.at[:, pl.ds(pl.multiple_of(t * width, width), width)]))
    write(19)

    early_tiles(out_sum.sent)
    for flow in (0, 2, 3):
        for mask in range(1, n):
            for half in halves(flow):
                w_copy(flow, mask, half).wait_send()
    for j in range(len(outs)):
        if j not in (1, 3):
            out_copy(j).wait()


def forward(plan, x, out_grad, w, wd, small, lengths):
    any_space = pl.BlockSpec(memory_space=pl.ANY)
    vmem = pl.BlockSpec(memory_space=pltpu.VMEM)
    n, line, group, model, local, rows = (
        plan.n_dp, plan.n_line, plan.group, plan.model, plan.local, plan.rows
    )
    low = lambda *shape: jax.ShapeDtypeStruct(shape, bf16)
    full = lambda *shape: jax.ShapeDtypeStruct(shape, f32)
    early = plan.early * plan.width
    out_shape = [
        low(model, plan.attn), low(model, plan.mlp), low(n, 16, LANES + plan.out_cols),
        low(group, model), full(8, model), low(group, model),
        low(group, local), low(group, local), low(group, local), low(group, local),
        full(group, LANES),
        low(group, plan.mlp), low(group, plan.mlp), low(group, local), low(group, model - early),
        full(group, LANES), full(group, LANES), full(group, LANES), full(2, rows, LANES), full(rows, early),
    ]
    scratch = lambda s: pltpu.VMEM(s.shape, s.dtype)
    dma = pltpu.SemaphoreType.DMA
    return pl.pallas_call(
        partial(forward_kernel, plan),
        in_specs=[any_space] * 5 + [pl.BlockSpec(memory_space=pltpu.SMEM)] + [vmem] * 2,
        out_specs=[any_space] * 20,
        out_shape=out_shape,
        scratch_shapes=[scratch(s) for s in out_shape[:2]]
        + [pltpu.VMEM((plan.down, model), bf16)]
        + [scratch(s) for s in out_shape[2:4]]
        + [pltpu.VMEM((rows, model), bf16)]
        + [scratch(s) for s in out_shape[4:14]]
        + [scratch(s) for s in out_shape[15:19]]
        + [pltpu.VMEM((rows, model), f32), pltpu.VMEM((2,) + w.shape[1:], f32), pltpu.VMEM((2,) + wd.shape[1:], f32)]
        + [dma((3,)), dma((2, 2)), dma((20,)), dma((8 * n,)), dma((8 * n,))]
        + [dma((2 * line,))] * 4
        + [dma((plan.early, max(line - 1, 1)))] * 4
        + [pltpu.SemaphoreType.REGULAR],
        compiler_params=pltpu.CompilerParams(
            collective_id=0, has_side_effects=True, vmem_limit_bytes=63 << 20
        ),
        cost_estimate=pl.CostEstimate(flops=60 * 10**9, bytes_accessed=80 << 20, transcendentals=0),
    )(x, out_grad, w, wd, small, lengths, *angle_tables(group))


def backward_kernel(
    plan,
    xhat_in, cot_in, att_in, hidden_in, da_in, do_in, q_in, k_in, v_in, part_in, wa_in, wm_in,
    lse, sums_in, own, ahead, behind, lengths,
    down_out, in_out, small_out, mixed_out, rows_out, dh_out,
    turned, stage, og, da, qkv, do, k_sum, v_sum, sent, core_in, held, cube_in, up_in, down_in,
    part, part_up, part_down, w_tile, fin, fin_turned, dh_fin, small, small_in, shares,
    load_sem, stage_sem, tile_sem, fin_sem, dh_sem, core_send, core_recv, cube_send, cube_recv,
    up_send, up_recv, down_send, down_recv, part_up_send, part_up_recv, part_down_send, part_down_recv,
    small_send, small_recv, share_send, share_recv, credit,
):
    n, line = plan.n_dp, plan.n_line
    me, place = lax.axis_index("dp"), lax.axis_index("tensor")
    rows, local, group, model, in_rows = plan.rows, plan.local, plan.group, plan.model, plan.in_rows
    MESH = pl.DeviceIdType.MESH
    half_rows, pairs_n, n_bits = in_rows // 2, n // 2, len(plan.bits)
    orders = (plan.bits, plan.bits[::-1])
    n_down, n_mlp = 1 + plan.n_mlp, plan.n_mlp
    flows = {"down": (n_down, 0, 0), "mlp": (n_mlp, n_down, 3), "attn": (3, 0, 0)}

    def owner(mask):
        index = me
        for b in [1] + plan.bits:
            if mask & b:
                index = index + b - 2 * b * lax.rem(index // b, 2)
        return index

    def peer(bit):
        return {"dp": owner(bit)}

    def position(mask, order):
        return sum((1 if mask & b else 0) << (n_bits - 1 - p) for p, b in enumerate(order))

    whole = [
        (att_in, og.at[:, pl.ds(0, local)]),
        (hidden_in, og.at[:, pl.ds(local, plan.mlp)]),
        (da_in, da),
        (q_in, qkv.at[:, pl.ds(0, local)]),
        (k_in, qkv.at[:, pl.ds(local, local)]),
        (v_in, qkv.at[:, pl.ds(2 * local, local)]),
        (do_in, do),
        (part_in, part),
    ]
    for j, (a, b) in enumerate(whole):
        pltpu.make_async_copy(a, b, load_sem.at[j]).start()

    def loaded(*which):
        for j in which:
            pltpu.make_async_copy(whole[j][0], whole[j][1], load_sem.at[j]).wait()

    barrier = pltpu.get_barrier_semaphore()
    for b in [1] + plan.bits:
        pl.semaphore_signal(barrier, inc=1, device_id=peer(b), device_id_type=MESH)
    for d in range(1, line):
        pl.semaphore_signal(
            barrier, inc=1, device_id={"tensor": lax.rem(place + d, line)}, device_id_type=MESH
        )

    def share_copy(d, arriving):
        source = lax.rem(place + line - d, line) if arriving else place
        return pltpu.make_async_remote_copy(
            src_ref=shares, dst_ref=rows_out.at[source],
            send_sem=share_send.at[d], recv_sem=share_recv.at[d],
            device_id={"tensor": lax.rem(place + d, line)}, device_id_type=MESH,
        )

    share_own = pltpu.make_async_copy(shares, rows_out.at[place], share_send.at[0])

    def turn_columns(source, masks, first, started=False):
        def fetch(j):
            at = pl.multiple_of(owner(masks[j]) * in_rows, in_rows)
            return pltpu.make_async_copy(
                source.at[:, pl.ds(at, in_rows)], stage.at[j % 2], stage_sem.at[j % 2]
            )

        fetch(0).start()
        for j in range(len(masks)):
            if j + 1 < len(masks):
                fetch(j + 1).start()
            fetch(j).wait()
            turned[pl.ds((first + j) * in_rows, in_rows), :] = stage[j % 2].T

    def core_copy(name, t):
        return pltpu.make_async_remote_copy(
            src_ref=sent.at[lax.rem(t, 2)], dst_ref=core_in.at[t],
            send_sem=core_send.at[lax.rem(t, 2)], recv_sem=core_recv.at[t],
            device_id=peer(1), device_id_type=MESH,
        )

    def cube_copy(slot, half, phase):
        count = pairs_n >> (phase + 1)
        first = pairs_n - 2 * count
        at = half * n_bits + phase
        return pltpu.make_async_remote_copy(
            src_ref=held.at[slot, half, pl.ds(count, count)],
            dst_ref=cube_in.at[slot, half, pl.ds(first, count)],
            send_sem=cube_send.at[slot, at], recv_sem=cube_recv.at[slot, at],
            device_id=peer(orders[half][phase]), device_id_type=MESH,
        )

    def operand(name, t):
        source = {"down": og, "mlp": da, "attn": qkv}[name]
        return source[:, pl.ds(pl.multiple_of(t * local, local), local)]

    piece = min(2, pairs_n) * in_rows

    def send_core(name):
        tiles = flows[name][0]
        if name != "down":
            pl.semaphore_wait(credit.at[0], 1)

        def step(t, carry):
            @pl.when(t >= 2)
            def _():
                core_copy(name, t - 2).wait_send()
            for at in range(0, pairs_n * in_rows, piece):
                sent[lax.rem(t, 2), at : at + piece, :] = dot_n(
                    turned[at : at + piece, :], operand(name, t)
                ).astype(bf16)
            core_copy(name, t).start()
            return carry

        lax.fori_loop(0, tiles, step, 0)
        for t in range(max(tiles - 2, 0), tiles):
            core_copy(name, t).wait_send()

    def keep_core(name):
        tiles, base, _ = flows[name]

        def step(t, carry):
            core_copy(name, t).wait_recv()
            for first in range(0, pairs_n * in_rows, piece):
                kept = pairs_n * in_rows + first
                total = dot_n(turned[kept : kept + piece, :], operand(name, t))
                total = total + core_in[t, first : first + piece, :].astype(f32)
                for at in range(0, piece, half_rows):
                    j, half = divmod((first + at) // half_rows, 2)
                    held[base + t, half, position(2 * j, orders[half])] = total[at : at + half_rows].astype(bf16)
            for half in range(2):
                if n_bits:
                    cube_copy(base + t, half, 0).start()
            return carry

        lax.fori_loop(0, tiles, step, 0)
        if name != "attn":
            pl.semaphore_signal(credit.at[0], inc=1, device_id=peer(1), device_id_type=MESH)

    def cube_step(name, phase):
        tiles, base, result = flows[name]
        count = pairs_n >> (phase + 1)
        first = pairs_n - 2 * count
        target, depth = (down_out, 1) if name == "down" else (in_out, 2)

        def fin_copy(t):
            source = fin_turned if name == "down" else fin.at[lax.rem(t, 2)]
            return pltpu.make_async_copy(source, target.at[result + t], fin_sem.at[lax.rem(t, 2)])

        def step(t, carry):
            slot = base + t
            if phase == n_bits - 1:
                @pl.when(t >= depth)
                def _():
                    fin_copy(t - depth).wait()
            for half in range(2):
                cube_copy(slot, half, phase).wait_recv()
                total = (
                    held[slot, half, 0:count].astype(f32)
                    + cube_in[slot, half, first : first + count].astype(f32)
                )
                if phase < n_bits - 1:
                    held[slot, half, 0:count] = total.astype(bf16)
                    cube_copy(slot, half, phase + 1).start()
                else:
                    fin[lax.rem(t, 2), half * half_rows : (half + 1) * half_rows, :] = total[0]
            if phase == n_bits - 1:
                if name == "down":
                    fin_turned[...] = fin[lax.rem(t, 2)].T
                fin_copy(t).start()
                if name != "down":
                    weight = w_tile[0 if name == "attn" else 1, 0:in_rows, pl.ds(pl.multiple_of(t * local, local), local)].astype(f32)
                    product = weight * fin[lax.rem(t, 2)]
                    extra = weight * small[n_bits + 1, pl.ds(result + t, 1), :]
                    for g in range(0, local, LANES):
                        shares[0] += product[:, g : g + LANES]
                        shares[1] += extra[:, g : g + LANES]
            return carry

        lax.fori_loop(0, tiles, step, 0)
        if phase == n_bits - 1:
            for t in range(max(tiles - depth, 0), tiles):
                fin_copy(t).wait()

    def cube_sent(name):
        tiles, base, _ = flows[name]

        def step(t, carry):
            for half in range(2):
                for phase in range(n_bits):
                    cube_copy(base + t, half, phase).wait_send()
            return carry

        lax.fori_loop(0, tiles, step, 0)

    def attend(pair, carry):
        block = min(QUERY_ROWS, group)
        scale = HEAD ** (-0.5)
        k_sum[...] = jnp.zeros_like(k_sum)
        v_sum[...] = jnp.zeros_like(v_sum)
        q_lanes, k_lanes, v_lanes = (
            pl.ds(pl.multiple_of(pair * LANES + r * local, LANES), LANES) for r in range(3)
        )
        lanes = q_lanes
        which = lax.broadcasted_iota(jnp.int32, (block, LANES), 1)
        for start in range(0, group, block):
            stop = start + block
            here = pl.ds(start, block)
            allowed = attend_mask(begins_of(lengths, start, block), start, block, stop)
            q_sum = jnp.zeros((block, LANES), f32)
            for head in range(LANES // HEAD):
                mine = head_lanes(block, head)
                query = jnp.where(mine, qkv[here, q_lanes], jnp.zeros((block, LANES), bf16)) * scale
                query = query.astype(bf16)
                cot = jnp.where(mine, do[here, lanes], jnp.zeros((block, LANES), bf16))
                level = jnp.sum(
                    jnp.where(which == pair * (LANES // HEAD) + head, lse[here, :], 0.0), axis=1, keepdims=True
                )
                scores = dot_t(query, qkv[:stop, k_lanes]) - level
                probs = jnp.where(allowed, jnp.exp(scores), 0.0)
                prob_grad = dot_t(cot, qkv[:stop, v_lanes])
                mean = jnp.sum(probs * prob_grad, axis=1, keepdims=True)
                score_grad = (probs * (prob_grad - mean)).astype(bf16)
                q_step = dot_n(score_grad, qkv[:stop, k_lanes])
                q_sum = jnp.where(mine, q_step * scale, q_sum)
                k_sum[:stop, :] += dot_s(score_grad, query)
                v_sum[:stop, :] += dot_s(probs.astype(bf16), cot)
            qkv[here, q_lanes] = turn(
                q_sum, own[here, :], ahead[here, :], behind[here, :], -1.0
            ).astype(bf16)
        qkv[:, k_lanes] = turn(k_sum[...], own[...], ahead[...], behind[...], -1.0).astype(bf16)
        qkv[:, v_lanes] = v_sum[...].astype(bf16)
        return carry

    width, d_tiles = plan.width, plan.d_tiles

    def tile_loads(t):
        at = pl.ds(pl.multiple_of(t * width, width), width)
        slot = lax.rem(t, 2)
        return (
            pltpu.make_async_copy(wa_in.at[at, :], w_tile.at[slot, pl.ds(0, width), pl.ds(0, plan.attn)], tile_sem.at[slot, 0]),
            pltpu.make_async_copy(wm_in.at[at, :], w_tile.at[slot, pl.ds(0, width), pl.ds(plan.attn, plan.mlp)], tile_sem.at[slot, 1]),
        )

    def tile_of(buffer):
        def source(t, index):
            return buffer.at[
                pl.ds(pl.multiple_of(index * rows, rows), rows),
                pl.ds(pl.multiple_of(t * width, width), width),
            ]
        return source

    dh_sum = LineSum(
        place, line, tile_of(og), lambda t, slot, up: (up_in if up else down_in).at[t, slot],
        (up_send, up_recv, down_send, down_recv),
    )
    late = d_tiles - plan.early
    out_sum = LineSum(
        place, line, tile_of(part), lambda t, slot, up: (part_up if up else part_down).at[t, slot],
        (part_up_send, part_up_recv, part_down_send, part_down_recv),
    )

    def sum_copy(target, t):
        cols = pl.ds(pl.multiple_of(t * width, width), width)
        return pltpu.make_async_copy(dh_fin.at[lax.rem(t, 2)], target.at[:, cols], dh_sem.at[lax.rem(t, 2)])

    def finish(flow, target, count):
        def step(t):
            @pl.when(t >= 2)
            def _():
                sum_copy(target, t - 2).wait()
            flow.last(t, dh_fin.at[lax.rem(t, 2)])
            sum_copy(target, t).start()

        tiles(0, count, step)
        for t in range(max(count - 2, 0), count):
            sum_copy(target, t).wait()

    def tiles(first, stop, fn):
        lax.fori_loop(first, stop, lambda t, carry: (fn(t), carry)[1], 0)

    def hand_on(flow):
        def step(t):
            for up in (True, False):
                flow.hand_on(t, up)
        return step

    def dh_tile(t):
        slot = lax.rem(t, 2)
        @pl.when(t + 1 < d_tiles)
        def _():
            for load in tile_loads(t + 1):
                load.start()
        for load in tile_loads(t):
            load.wait()
        total = dot_t(qkv[...], w_tile[slot, 0:width, : plan.attn]) + dot_t(da[...], w_tile[slot, 0:width, plan.attn :])
        og[:, pl.ds(pl.multiple_of(t * width, width), width)] = total.astype(bf16)
        dh_sum.first(t)

    def small_copy(j):
        return pltpu.make_async_remote_copy(
            src_ref=small.at[j], dst_ref=small_in.at[j],
            send_sem=small_send.at[j], recv_sem=small_recv.at[j],
            device_id=peer(([1] + plan.bits)[j]), device_id_type=MESH,
        )

    def small_step(j):
        small_copy(j).wait_recv()
        small[j + 1] = small[j] + small_in[j]
        if j < n_bits:
            small_copy(j + 1).start()

    shares[...] = jnp.zeros_like(shares)
    small[0] = jnp.zeros_like(small[0])
    for load in tile_loads(0):
        load.start()
    send_masks, keep_masks = [2 * j + 1 for j in range(pairs_n)], [2 * j for j in range(pairs_n)]
    turn_columns(cot_in, send_masks, 0)
    pl.semaphore_wait(barrier, 1 + n_bits + line - 1)
    loaded(7)
    tiles(0, late, out_sum.first)
    loaded(0, 1)
    send_core("down")
    turn_columns(cot_in, keep_masks, pairs_n)
    keep_core("down")
    loaded(2, 3, 4, 5, 6)
    pairs = local // LANES
    lax.fori_loop(0, pairs // 2, attend, 0)
    tiles(0, late, hand_on(out_sum))
    lax.fori_loop(pairs // 2, pairs, attend, 0)
    for r in range(3 + n_mlp):
        block = qkv[:, r * local : (r + 1) * local] if r < 3 else da[:, (r - 3) * local : (r - 2) * local]
        small[0, r : r + 1, :] = jnp.sum(block.astype(f32), axis=0, keepdims=True)
    for r in range(model // local):
        small[0, 8 + r : 9 + r, :] = sums_in[0:1, r * local : (r + 1) * local]
    small_copy(0).start()
    some = min(3, d_tiles)
    tiles(0, some, dh_tile)
    for phase in range(n_bits - 1):
        cube_step("down", phase)
    turn_columns(xhat_in, send_masks, 0)
    send_core("mlp")
    turn_columns(xhat_in, keep_masks, pairs_n)
    keep_core("mlp")
    finish(out_sum, mixed_out, late)
    tiles(some, d_tiles, dh_tile)
    tiles(0, d_tiles // 4, hand_on(dh_sum))
    small_step(0)
    cube_step("down", n_bits - 1)
    cube_sent("down")
    for b in plan.bits:
        pl.semaphore_signal(credit.at[1], inc=1, device_id=peer(b), device_id_type=MESH)
    small_step(1)
    send_core("attn")
    pl.semaphore_wait(credit.at[1], n_bits)
    keep_core("attn")
    for j in range(2, n_bits + 1):
        small_step(j)
    own_rows = pl.ds(pl.multiple_of(me * in_rows, in_rows), in_rows)
    weights = [
        pltpu.make_async_copy(wa_in.at[own_rows, :], w_tile.at[0, pl.ds(0, in_rows), pl.ds(0, plan.attn)], tile_sem.at[0, 0]),
        pltpu.make_async_copy(wm_in.at[own_rows, :], w_tile.at[1, pl.ds(0, in_rows), pl.ds(0, plan.mlp)], tile_sem.at[1, 0]),
    ]
    for w in weights:
        w.start()
    tiles(d_tiles // 4, d_tiles // 2, hand_on(dh_sum))
    for phase in range(n_bits - 1):
        cube_step("mlp", phase)
    tiles(d_tiles // 2, 3 * d_tiles // 4, hand_on(dh_sum))
    for w in weights:
        w.wait()
    cube_step("mlp", n_bits - 1)
    tiles(3 * d_tiles // 4, d_tiles, hand_on(dh_sum))
    for phase in range(n_bits):
        cube_step("attn", phase)
    share_own.start()
    for d in range(1, line):
        share_copy(d, False).start()
    finish(dh_sum, dh_out, d_tiles)
    small_done = pltpu.make_async_copy(small.at[n_bits + 1], small_out, load_sem.at[0])
    small_done.start()
    cube_sent("mlp")
    cube_sent("attn")
    tiles(0, d_tiles, dh_sum.sent)
    tiles(0, late, out_sum.sent)
    for j in range(n_bits + 1):
        small_copy(j).wait_send()
    share_own.wait()
    for d in range(1, line):
        share_copy(d, False).wait_send()
        share_copy(d, True).wait_recv()
    small_done.wait()


def backward(plan, xhat, cot, att, hidden, da, do, q, k, v, part, wa, wm, lse, sums, tables, lengths):
    any_space = pl.BlockSpec(memory_space=pl.ANY)
    vmem = pl.BlockSpec(memory_space=pltpu.VMEM)
    n, line, group, model, local = plan.n_dp, plan.n_line, plan.group, plan.model, plan.local
    rows, in_rows, n_bits, pairs_n = plan.rows, plan.in_rows, len(plan.bits), n // 2
    n_down = 1 + plan.n_mlp
    small_rows = 8 + -(-(model // local) // 8) * 8
    width, d_tiles, steps = plan.width, plan.d_tiles, max(line - 1, 1)
    late = d_tiles - plan.early
    low = lambda *shape: pltpu.VMEM(shape, bf16)
    full = lambda *shape: pltpu.VMEM(shape, f32)
    dma = pltpu.SemaphoreType.DMA
    out = lambda dtype, *shape: jax.ShapeDtypeStruct(shape, dtype)
    slots = n_down + plan.n_mlp
    return pl.pallas_call(
        partial(backward_kernel, plan),
        in_specs=[any_space] * 12 + [vmem] * 5 + [pl.BlockSpec(memory_space=pltpu.SMEM)],
        out_specs=[any_space] * 6,
        out_shape=[
            out(f32, n_down, local, in_rows), out(f32, 3 + plan.n_mlp, in_rows, local),
            out(f32, small_rows, local), out(f32, rows, late * width),
            out(f32, line, 2, in_rows, LANES), out(f32, rows, model),
        ],
        scratch_shapes=[
            low(n * in_rows, group), low(2, group, in_rows), low(group, plan.down), low(group, plan.mlp),
            low(group, plan.attn), low(group, local), full(group, LANES), full(group, LANES),
            low(2, pairs_n * in_rows, local), low(n_down, pairs_n * in_rows, local),
            low(slots, 2, pairs_n, in_rows // 2, local), low(slots, 2, max(pairs_n - 1, 1), in_rows // 2, local),
            low(d_tiles, steps, rows, width), low(d_tiles, steps, rows, width),
            low(group, late * width), low(late, steps, rows, width), low(late, steps, rows, width),
            low(2, max(width, in_rows), plan.attn + plan.mlp), full(2, in_rows, local), full(local, in_rows), full(2, rows, width),
            full(n_bits + 2, small_rows, local), full(n_bits + 1, small_rows, local), full(2, in_rows, LANES),
            dma((8,)), dma((2,)), dma((2, 2)), dma((2,)), dma((2,)), dma((2,)), dma((n_down,)),
            dma((slots, max(2 * n_bits, 1))), dma((slots, max(2 * n_bits, 1))),
            dma((d_tiles, steps)), dma((d_tiles, steps)), dma((d_tiles, steps)), dma((d_tiles, steps)),
            dma((late, steps)), dma((late, steps)), dma((late, steps)), dma((late, steps)),
            dma((n_bits + 1,)), dma((n_bits + 1,)), dma((line,)), dma((line,)),
            pltpu.SemaphoreType.REGULAR((2,)),
        ],
        compiler_params=pltpu.CompilerParams(
            collective_id=1, has_side_effects=True, vmem_limit_bytes=63 << 20
        ),
        cost_estimate=pl.CostEstimate(flops=80 * 10**9, bytes_accessed=80 << 20, transcendentals=0),
    )(xhat, cot, att, hidden, da, do, q, k, v, part, wa, wm, lse, sums, *tables, lengths)


def adam_update(weight, moment_one, moment_two, gradient, step_rate, decay_factor):
    first_new = beta_first * moment_one + (1.0 - beta_first) * gradient
    second_new = beta_second * moment_two + (1.0 - beta_second) * gradient * gradient
    corrected = first_new / (1.0 - beta_first**STEP)
    spread = jnp.sqrt(second_new / (1.0 - beta_second**STEP))
    return (
        weight - step_rate * (corrected / (spread + adam_eps) + decay_factor * weight),
        first_new,
        second_new,
    )


def per_device(
    block_input,
    out_grad,
    seq_lengths,
    in_weight,
    down_weight,
    column_bias,
    vector_params,
    in_first,
    in_second,
    down_first,
    down_second,
    bias_first,
    bias_second,
    vector_first,
    vector_second,
):
    n_dp = lax.axis_size("dp")
    n_tensor = lax.axis_size("tensor")
    own_rows, model = block_input.shape
    group = own_rows * n_tensor
    in_rows, widths, local = in_weight.shape
    out_cols = down_weight.shape[2]
    n_mlp = widths - 3
    attn_width, mlp_width = 3 * local, n_mlp * local

    me = lax.axis_index("dp")
    plan = Plan(n_dp, n_tensor, own_rows, model, in_rows, local, n_mlp, out_cols)
    share = LANES // plan.bias_cols
    lane = lax.broadcasted_iota(jnp.int32, (widths, LANES), 1) // plan.bias_cols
    bias_tile = jnp.where(lane == lax.rem(me, share), jnp.tile(column_bias, (1, share)), 0.0)
    small = jnp.concatenate(
        [jnp.pad(bias_tile, ((0, 16 - widths), (0, 0))), jnp.pad(vector_params, ((0, 13), (0, 0)))], axis=1
    ).astype(bf16)
    (
        w_attn, w_mlp, vectors, xhat_all, cot_sums, cot_all, q_low, k_low, v_low, attended, lse,
        hidden, pre_grad, attn_grad, out_part, own, ahead, behind, stats, mixed_early,
    ) = forward(plan, block_input, out_grad, in_weight.transpose(1, 0, 2), down_weight, small, seq_lengths)
    down_grad, in_grad, small_grad, mixed_late, shares, dh = backward(
        plan, xhat_all, cot_all, attended, hidden, pre_grad, attn_grad, q_low, k_low, v_low, out_part,
        w_attn, w_mlp, lse, cot_sums, (own, ahead, behind), seq_lengths,
    )
    vector_vals = vectors[:, :3, LANES:].transpose(1, 0, 2).reshape(3, model).astype(f32)
    gain, out_bias = vector_vals[0], vector_vals[2]
    block_out = block_input + (jnp.concatenate([mixed_early, mixed_late], axis=1) + out_bias)
    mean, inv_scale = stats[0, :, :1], stats[1, :, :1]
    xhat = (block_input - mean) * inv_scale
    places = lax.axis_index("tensor") * own_rows + lax.broadcasted_iota(jnp.int32, (own_rows, 1), 0)
    cot_live = jnp.where(places < jnp.sum(seq_lengths), out_grad, 0.0)

    dxhat = dh * gain
    input_grad = cot_live + inv_scale * (
        dxhat
        - jnp.mean(dxhat, axis=-1, keepdims=True)
        - xhat * jnp.mean(dxhat * xhat, axis=-1, keepdims=True)
    )

    bias_full = small_grad[:widths]
    own_vectors = vector_params.astype(bf16).astype(f32)
    in_reduced = (
        in_grad * own_vectors[0][None, :, None] + own_vectors[1][None, :, None] * bias_full[:, None, :]
    ).transpose(1, 0, 2)
    down_reduced = down_grad
    bias_reduced = lax.dynamic_slice_in_dim(bias_full, me * plan.bias_cols, plan.bias_cols, 1)
    out_sums = small_grad[8 : 8 + model // local].reshape(-1)
    vector_reduced = jnp.stack(
        [
            jnp.sum(shares[:, 0], axis=(0, 2)),
            jnp.sum(shares[:, 1], axis=(0, 2)),
            lax.dynamic_slice_in_dim(out_sums, me * out_cols, out_cols, 0),
        ]
    )

    in_new, in_one, in_two = adam_update(
        in_weight, in_first, in_second, in_reduced, rate_in, weight_decay
    )
    down_new, down_one, down_two = adam_update(
        down_weight, down_first, down_second, down_reduced, rate_down, weight_decay
    )
    bias_new, bias_one, bias_two = adam_update(
        column_bias, bias_first, bias_second, bias_reduced, rate_vector, 0.0
    )
    vector_new, vector_one, vector_two = adam_update(
        vector_params, vector_first, vector_second, vector_reduced, rate_vector, 0.0
    )
    return (
        block_out,
        input_grad,
        in_new,
        in_one,
        in_two,
        down_new,
        down_one,
        down_two,
        bias_new,
        bias_one,
        bias_two,
        vector_new,
        vector_one,
        vector_two,
    )


def widths_down(down_weight):
    return down_weight.shape[0] * down_weight.shape[1]


def solution(mesh):
    return jax.shard_map(
        per_device,
        mesh=mesh,
        in_specs=(
            P(("dp", "tensor"), None),
            P(("dp", "tensor"), None),
            P("dp", None),
            P("dp", None, "tensor"),
            P(None, "tensor", "dp"),
            P(None, ("tensor", "dp")),
            P(None, "dp"),
            P("dp", None, "tensor"),
            P("dp", None, "tensor"),
            P(None, "tensor", "dp"),
            P(None, "tensor", "dp"),
            P(None, ("tensor", "dp")),
            P(None, ("tensor", "dp")),
            P(None, "dp"),
            P(None, "dp"),
        ),
        out_specs=(
            P(("dp", "tensor"), None),
            P(("dp", "tensor"), None),
            P("dp", None, "tensor"),
            P("dp", None, "tensor"),
            P("dp", None, "tensor"),
            P(None, "tensor", "dp"),
            P(None, "tensor", "dp"),
            P(None, "tensor", "dp"),
            P(None, ("tensor", "dp")),
            P(None, ("tensor", "dp")),
            P(None, ("tensor", "dp")),
            P(None, "dp"),
            P(None, "dp"),
            P(None, "dp"),
        ),
        check_vma=False,
    )
```

```python
from functools import partial

import jax
import jax.numpy as jnp
import numpy as np
from jax import lax
from jax.experimental import pallas as pl
from jax.experimental.pallas import tpu as pltpu
from jax.sharding import PartitionSpec as P

HEAD = 64
ROT = 32
STEP = 8
LANES = 128
QUERY_ROWS = 256

norm_eps = 1e-05
beta_first = 0.9
beta_second = 0.95
adam_eps = 1e-08
masked_score = -1000000000.0
rate_in = 0.02
rate_down = 0.05
rate_vector = 0.2
weight_decay = 0.1

bf16 = jnp.bfloat16
f32 = jnp.float32


def angle_tables(rows):
    half_rot = ROT // 2
    frequency = 10000.0 ** (-2.0 * (np.arange(LANES) % half_rot) / ROT)
    angles = np.arange(rows)[:, None] * frequency[None, :]
    return np.cos(angles).astype(np.float32), np.sin(angles).astype(np.float32)


def ends_of(lengths):
    ends = [jnp.int32(0)]
    for j in range(lengths.shape[1]):
        ends.append(ends[-1] + lengths[0, j])
    return ends


def begins_of(lengths, start, rows):
    places = start + lax.broadcasted_iota(jnp.int32, (rows, 1), 0)
    begin = jnp.zeros((rows, 1), jnp.int32)
    for end in ends_of(lengths)[1:]:
        begin = jnp.where(places >= end, end, begin)
    return begin


def attend_mask(begin, row_start, rows, stop):
    key_place = lax.broadcasted_iota(jnp.int32, (rows, stop), 1)
    query_place = row_start + lax.broadcasted_iota(jnp.int32, (rows, stop), 0)
    return (key_place <= query_place) & (key_place >= begin)


def head_lanes(rows, head):
    lane = lax.broadcasted_iota(jnp.int32, (rows, LANES), 1)
    return (lane >= head * HEAD) & (lane < (head + 1) * HEAD)


def dot_t(a, b):
    return lax.dot_general(a, b, (((1,), (1,)), ((), ())), preferred_element_type=f32)


def dot_n(a, b):
    return lax.dot_general(a, b, (((1,), (0,)), ((), ())), preferred_element_type=f32)


def dot_s(a, b):
    return lax.dot_general(a, b, (((0,), (0,)), ((), ())), preferred_element_type=f32)


def turn(x, own, ahead, behind, sign):
    half = ROT // 2
    return x * own + sign * (
        pltpu.roll(x, LANES - half, 1) * ahead + pltpu.roll(x, half, 1) * behind
    )


def low_bit(mask):
    return mask & -mask


def high_bit(mask):
    return 1 << (mask.bit_length() - 1)


def gelu_and_slope(a):
    root = (2.0 / 3.141592653589793) ** 0.5
    square = a * a
    t = jnp.tanh(root * a * (1.0 + 0.044715 * square))
    half = 0.5 * (1.0 + t)
    return a * half, half + 0.5 * a * (1.0 - t * t) * (root * (1.0 + 3.0 * 0.044715 * square))


class LineSum:
    def __init__(self, place, line, source, landing, sems):
        self.place, self.line, self.source, self.landing = place, line, source, landing
        self.up_send, self.up_recv, self.down_send, self.down_recv = sems

    def copy(self, t, index, up, arriving=False):
        place = self.place
        slot = index - 1 if up else self.line - 2 - index
        return pltpu.make_async_remote_copy(
            src_ref=self.source(t, index),
            dst_ref=self.landing(t, slot, up),
            send_sem=(self.up_send if up else self.down_send).at[t, slot],
            recv_sem=(self.up_recv if up else self.down_recv).at[t, slot],
            device_id={"tensor": place + 1 if up != arriving else place - 1},
            device_id_type=pl.DeviceIdType.MESH,
        )

    def got(self, t, index, up):
        return self.landing(t, index - 1 if up else self.line - 2 - index, up)[...].astype(f32)

    def first(self, t):
        for up in (True, False):
            @pl.when((self.place == 0) if up else (self.place == self.line - 1))
            def _():
                for step in range(self.line - 1):
                    self.copy(t, self.line - 1 - step if up else step, up).start()

    def hand_on(self, t, up):
        place, line = self.place, self.line
        for step in range(line - 1):
            index = line - 1 - step if up else step
            hears = (place > 0) & (place < index) if up else (place < line - 1) & (place > index)

            @pl.when(hears)
            def _():
                self.copy(t, index, up, True).wait_recv()
                mine = self.source(t, index)
                mine[...] = (mine[...].astype(f32) + self.got(t, index, up)).astype(bf16)
                self.copy(t, index, up).start()

    def both_ways(self, first, stop, count, lag=2):
        def step(t, carry):
            for up in (True, False):
                far = 2 * self.place // self.line
                index = t - lag * (far if up else 1 - far)

                @pl.when((index >= 0) & (index < count))
                def _():
                    self.hand_on(index, up)
            return carry

        lax.fori_loop(first, stop + (lag if stop == count else 0), step, 0)

    def last(self, t, target):
        place, line = self.place, self.line
        target[...] = self.source(t, place)[...].astype(f32)
        for up in (True, False):
            @pl.when((place > 0) if up else (place < line - 1))
            def _():
                self.copy(t, place, up, True).wait_recv()
                target[...] += self.got(t, place, up)

    def sent(self, t):
        for index in range(self.line):
            for up in (True, False):
                @pl.when((self.place < index) if up else (self.place > index))
                def _():
                    self.copy(t, index, up).wait_send()


class Plan:
    def __init__(self, n_dp, n_line, rows, model, in_rows, local, n_mlp, out_cols):
        self.n_dp, self.n_line = n_dp, n_line
        self.rows, self.model = rows, model
        self.group = rows * n_line
        self.in_rows, self.local, self.n_mlp, self.out_cols = in_rows, local, n_mlp, out_cols
        self.attn, self.mlp = 3 * local, n_mlp * local
        self.down = (1 + n_mlp) * local
        self.bias_cols = local // n_dp
        self.width = out_cols
        self.d_tiles = model // out_cols
        self.early = 3 * self.d_tiles // 4
        self.bits = [1 << b for b in range(1, n_dp.bit_length() - 1)]
        even = range(2, n_dp, 2)
        self.single = [m for m in even if m.bit_count() == 1]
        self.several = sorted((m for m in even if m.bit_count() > 1), key=lambda m: m.bit_count())
        self.odd = list(range(1, n_dp, 2))

    def hop(self, mask, half):
        if mask & 1:
            return 1
        return high_bit(mask) if half == 0 else low_bit(mask)

    def onward(self, mask, half):
        if mask & 1:
            return []
        masks = [mask | 1] if self.n_dp > 1 else []
        return masks + [
            mask | b for b in self.bits if not mask & b and self.hop(mask | b, half) == b
        ]


def forward_kernel(
    plan,
    x_in, out_grad_in, w_in, wd_in, small_in, lengths, place_cos, place_sin,
    wa_out, wm_out, small_out, xhat_out, sums_out, cot_out, q_out, k_out, v_out, att_out, lse_out,
    hidden_out, da_out, do_out, part_out, own_out, ahead_out, behind_out, stats_out, mixed_out,
    wa, wm, wd, small, xs, ns, sums, cs, q, k, v, att, lse, hidden, slope, do,
    own, ahead, behind, stats, land_up, land_down, wide, mixed, block, tall_block,
    mixed_sem, own_sem, block_sem, out_sem, w_send, w_recv, up_send, up_recv, down_send, down_recv,
    sum_up_send, sum_up_recv, sum_down_send, sum_down_recv,
):
    n, line = plan.n_dp, plan.n_line
    me, place = lax.axis_index("dp"), lax.axis_index("tensor")
    rows, local, model, width = plan.rows, plan.local, plan.model, plan.width

    def owner(mask):
        index = me
        for b in [1] + plan.bits:
            if mask & b:
                index = index + b - 2 * b * lax.rem(index // b, 2)
        return index

    def slot(flow, index, half):
        if flow < 2:
            step = plan.in_rows // 2
            at = pl.multiple_of(index * plan.in_rows + half * step, step)
            return (wa, wm)[flow].at[pl.ds(at, step), :]
        if flow == 2:
            step = plan.down // 2
            return wd.at[index, pl.ds(half * step, step), :]
        return small.at[index]

    def halves(flow):
        return (0,) if flow == 3 else (0, 1)

    def w_copy(flow, mask, half):
        hop = plan.hop(mask, half)
        piece = slot(flow, owner(mask ^ hop), half)
        at = flow * 2 * n + 2 * mask + half
        return pltpu.make_async_remote_copy(
            src_ref=piece, dst_ref=piece, send_sem=w_send.at[at], recv_sem=w_recv.at[at],
            device_id={"dp": owner(hop)}, device_id_type=pl.DeviceIdType.MESH,
        )

    def w_start(flow, mask=0):
        for half in halves(flow):
            for target in plan.onward(mask, half):
                w_copy(flow, target, half).start()

    def w_arrive(flow, masks):
        for mask in masks:
            for half in halves(flow):
                piece = slot(flow, owner(mask), half)
                at = flow * 2 * n + 2 * mask + half
                pltpu.make_async_remote_copy(
                    src_ref=piece, dst_ref=piece, send_sem=w_send.at[at], recv_sem=w_recv.at[at],
                    device_id={"dp": owner(plan.hop(mask, half))}, device_id_type=pl.DeviceIdType.MESH,
                ).wait_recv()
                for target in plan.onward(mask, half):
                    w_copy(flow, target, half).start()

    def chunk(flow, index):
        return (xs, cs)[flow].at[:, pl.ds(pl.multiple_of(index * rows, rows), rows), :]

    def z_copy(flow, step, up):
        piece = chunk(flow, place - (step - 1) if up else place + (step - 1))
        at = flow * line + step
        return pltpu.make_async_remote_copy(
            src_ref=piece, dst_ref=piece,
            send_sem=(up_send if up else down_send).at[at],
            recv_sem=(up_recv if up else down_recv).at[at],
            device_id={"tensor": place + 1 if up else place - 1}, device_id_type=pl.DeviceIdType.MESH,
        )

    def sends(step, up):
        if up:
            return (place < line - 1) & (place >= step - 1)
        return (place > 0) & (place + step - 1 <= line - 1)

    def z_start(flow, step):
        for up in (True, False):
            @pl.when(sends(step, up))
            def _():
                z_copy(flow, step, up).start()

    def z_arrive(flow, step):
        for up in (True, False):
            @pl.when(place >= step if up else place + step <= line - 1)
            def _():
                piece = chunk(flow, place - step if up else place + step)
                at = flow * line + step
                pltpu.make_async_remote_copy(
                    src_ref=piece, dst_ref=piece,
                    send_sem=(up_send if up else down_send).at[at],
                    recv_sem=(up_recv if up else down_recv).at[at],
                    device_id={"tensor": place - 1 if up else place + 1},
                    device_id_type=pl.DeviceIdType.MESH,
                ).wait_recv()
        if step + 1 < line:
            z_start(flow, step + 1)

    def z_sent(flow, step, up):
        @pl.when(sends(step, up))
        def _():
            z_copy(flow, step, up).wait_send()

    def cot_start(step):
        for up in (True, False):
            last = place == step - 1 if up else place == line - step
            @pl.when(last & sends(1, up))
            def _():
                z_copy(0, step, up).wait_send()
                z_copy(1, 1, up).start()

    def at_distance(step, fn):
        if step == 0:
            fn(place)
            return

        def side(j, carry):
            index = place - step + 2 * step * j

            @pl.when((index >= 0) & (index < line))
            def _():
                fn(index)
            return carry

        lax.fori_loop(0, 2, side, 0)

    def span(index):
        return pl.ds(pl.multiple_of(index * rows, rows), rows)

    outs = [
        (wa, wa_out), (wm, wm_out), (small, small_out), (xs, xhat_out), (sums, sums_out), (cs, cot_out),
        (q, q_out), (k, k_out), (v, v_out), (att, att_out), (lse, lse_out), (hidden, hidden_out),
        (slope, da_out), (do, do_out), (xs.at[pl.ds(plan.early, plan.d_tiles - plan.early)], part_out),
        (own, own_out), (ahead, ahead_out), (behind, behind_out), (stats, stats_out),
    ]

    def out_copy(j):
        return pltpu.make_async_copy(outs[j][0], outs[j][1], out_sem.at[j])

    def write(*which):
        for j in which:
            out_copy(j).start()

    w_rows = pl.ds(pl.multiple_of(me * plan.in_rows, plan.in_rows), plan.in_rows)
    small_load = pltpu.make_async_copy(small_in, small.at[me], own_sem.at[2])

    half_rows, half_cols = plan.in_rows // 2, local // 2

    def in_load(i):
        return pltpu.make_async_copy(
            w_in.at[i // 2, pl.ds(i % 2 * half_rows, half_rows), :], block.at[i % 2], block_sem.at[0, i % 2]
        )

    def down_load(i):
        return pltpu.make_async_copy(
            wd_in.at[i // 2, pl.ds(i % 2 * half_cols, half_cols), :], tall_block.at[i % 2], block_sem.at[1, i % 2]
        )

    def round_in(first, stop, target):
        for i in range(2 * first, 2 * stop):
            r, half = divmod(i, 2)
            in_load(i).wait()
            to = pl.ds(pl.multiple_of(me * plan.in_rows + half * half_rows, half_rows), half_rows)
            target[to, (r - first) * local : (r - first + 1) * local] = block[half].astype(bf16)
            if i + 2 < 2 * (3 + plan.n_mlp):
                in_load(i + 2).start()

    def round_down():
        for i in range(2 * (1 + plan.n_mlp)):
            down_load(i).wait()
            wd[me, i * half_cols : (i + 1) * half_cols, :] = tall_block[i % 2].astype(bf16)
            if i + 2 < 2 * (1 + plan.n_mlp):
                down_load(i + 2).start()

    strip_rows = min(64, rows)
    strip_count = rows // strip_rows

    def row_load(j):
        source = x_in if j < strip_count else out_grad_in
        first = j % strip_count * strip_rows
        return pltpu.make_async_copy(
            source.at[pl.ds(first, strip_rows), :], wide.at[j % 2], own_sem.at[j % 2]
        )

    row_load(0).start()
    row_load(1).start()
    small_load.start()
    in_load(0).start()
    in_load(1).start()
    down_load(0).start()
    down_load(1).start()
    table_loads = [
        pltpu.make_async_copy(place_cos, own, own_sem.at[3]), pltpu.make_async_copy(place_sin, ahead, own_sem.at[4])
    ]
    for load in table_loads:
        load.start()
    barrier = pltpu.get_barrier_semaphore()
    for b in [1] + plan.bits if n > 1 else []:
        pl.semaphore_signal(barrier, inc=1, device_id={"dp": owner(b)}, device_id_type=pl.DeviceIdType.MESH)

    @pl.when(place < line - 1)
    def _():
        pl.semaphore_signal(barrier, inc=1, device_id={"tensor": place + 1}, device_id_type=pl.DeviceIdType.MESH)

    @pl.when(place > 0)
    def _():
        pl.semaphore_signal(barrier, inc=1, device_id={"tensor": place - 1}, device_id_type=pl.DeviceIdType.MESH)

    beside = (place + line - 1) // line + (2 * line - 2 - place) // line
    pl.semaphore_wait(barrier, (1 + len(plan.bits) if n > 1 else 0) + beside)

    def normalize_rows(index):
        at = span(index)
        for o in range(n):
            gain, shift = small[o, 0:1, LANES:].astype(f32), small[o, 1:2, LANES:].astype(f32)
            ns[:, o * width : (o + 1) * width] = (xs[o, at, :].astype(f32) * gain + shift).astype(bf16)

    def bias_row(r, first, width):
        per = LANES // plan.bias_cols
        groups = []
        for g in range(first // LANES, (first + width) // LANES):
            total = small[g * per, r : r + 1, :LANES].astype(f32)
            for o in range(1, per):
                total = total + small[g * per + o, r : r + 1, :LANES].astype(f32)
            groups.append(total)
        return jnp.concatenate(groups, axis=1)

    def attn_rows(index):
        at = span(index)
        normalize_rows(index)
        for r, target in enumerate((q, k, v)):
            proj = dot_n(ns[...], wa[:, r * local : (r + 1) * local]) + bias_row(r, 0, local)
            if r == 2:
                target[at, :] = proj.astype(bf16)
            else:
                for g in range(0, local, LANES):
                    target[at, g : g + LANES] = turn(
                        proj[:, g : g + LANES], own[at, :], ahead[at, :], behind[at, :], 1.0
                    ).astype(bf16)

    def mlp_rows(index):
        at = span(index)
        normalize_rows(index)
        for r in range(plan.n_mlp):
            cols = slice(r * local, (r + 1) * local)
            pre = dot_n(ns[...], wm[:, cols]) + bias_row(3 + r, 0, local)
            value, grad = gelu_and_slope(pre)
            hidden[at, cols] = value.astype(bf16)
            slope[at, cols] = grad.astype(bf16)

    def attend(pair, carry):
        total = plan.group
        block = min(QUERY_ROWS, total)
        lanes = pl.ds(pl.multiple_of(pair * LANES, LANES), LANES)
        for start in range(0, total, block):
            stop = start + block
            here = pl.ds(start, block)
            allowed = attend_mask(begins_of(lengths, start, block), start, block, stop)
            query = q[here, lanes]
            results, logs = [], []
            for head in range(LANES // HEAD):
                mine = head_lanes(block, head)
                chosen = jnp.where(mine, query, jnp.zeros_like(query)) * HEAD ** (-0.5)
                scores = jnp.where(allowed, dot_t(chosen.astype(bf16), k[:stop, lanes]), masked_score)
                top = jnp.max(scores, axis=1, keepdims=True)
                weights = jnp.exp(scores - top)
                total_weight = jnp.sum(weights, axis=1, keepdims=True)
                results.append(dot_n(weights.astype(bf16), v[:stop, lanes]) / total_weight)
                logs.append(top + jnp.log(total_weight))
            first = head_lanes(block, 0)
            att[here, lanes] = jnp.where(first, results[0], results[1]).astype(bf16)
            which = lax.broadcasted_iota(jnp.int32, (block, LANES), 1)
            held = lse[here, :]
            for head in range(LANES // HEAD):
                held = jnp.where(which == pair * (LANES // HEAD) + head, logs[head], held)
            lse[here, :] = held
        return carry

    tall = min(512, plan.group)

    def out_tile(t):
        def part(j, carry):
            at = pl.ds(pl.multiple_of(j * tall, tall), tall)
            total = dot_n(att[at, :], wd[t, :local, :]) + dot_n(hidden[at, :], wd[t, local:, :])
            xs[t, at, :] = total.astype(bf16)
            return carry

        lax.fori_loop(0, plan.group // tall, part, 0)

    def tile_source(t, index):
        return xs.at[t, span(index), :]

    def tile_landing(t, slot, up):
        return (land_up if up else land_down).at[t, slot]

    out_sum = LineSum(
        place, line, tile_source, tile_landing, (sum_up_send, sum_up_recv, sum_down_send, sum_down_recv)
    )

    def early_tiles(fn):
        lax.fori_loop(0, plan.early, lambda t, carry: (fn(t), carry)[1], 0)

    def back_rows(index):
        at = span(index)
        for o in range(n):
            sums[0:1, o * width : (o + 1) * width] += jnp.sum(cs[o, at, :].astype(f32), axis=0, keepdims=True)
        for r in range(1 + plan.n_mlp):
            grad = dot_t(cs[0, at, :], wd[0, r * local : (r + 1) * local, :])
            for o in range(1, n):
                grad = grad + dot_t(cs[o, at, :], wd[o, r * local : (r + 1) * local, :])
            if r == 0:
                do[at, :] = grad.astype(bf16)
            else:
                cols = slice((r - 1) * local, r * local)
                slope[at, cols] = (grad * slope[at, cols].astype(f32)).astype(bf16)

    def normalize_own():
        for j in range(strip_count):
            row_load(j).wait()
            at = slice(j * strip_rows, (j + 1) * strip_rows)
            value = wide[j % 2]
            mean = jnp.mean(value, axis=1, keepdims=True)
            centered = value - mean
            scale = lax.rsqrt(jnp.mean(centered * centered, axis=1, keepdims=True) + norm_eps)
            normed = (centered * scale).astype(bf16)
            to = pl.ds(pl.multiple_of(place * rows + j * strip_rows, strip_rows), strip_rows)
            for o in range(n):
                xs[o, to, :] = normed[:, o * width : (o + 1) * width]
            stats[0, at, :] = jnp.broadcast_to(mean, (strip_rows, LANES))
            stats[1, at, :] = jnp.broadcast_to(scale, (strip_rows, LANES))
            if j + 2 < 2 * strip_count:
                row_load(j + 2).start()

    def mask_cot():
        for j in range(strip_count, 2 * strip_count):
            row_load(j).wait()
            first = place * rows + (j - strip_count) * strip_rows
            places = first + lax.broadcasted_iota(jnp.int32, (strip_rows, 1), 0)
            masked = jnp.where(places < ends_of(lengths)[-1], wide[j % 2], 0.0).astype(bf16)
            to = pl.ds(pl.multiple_of(first, strip_rows), strip_rows)
            for o in range(n):
                cs[o, to, :] = masked[:, o * width : (o + 1) * width]
            if j + 2 < 2 * strip_count:
                row_load(j + 2).start()

    def make_tables():
        for load in table_loads:
            load.wait()
        block_rows = min(QUERY_ROWS, plan.group)
        ends = ends_of(lengths)
        at_ends = [pl.ds(jnp.minimum(end, plan.group - 1), 1) for end in ends]
        cosines, sines = [own[row, :] for row in at_ends], [ahead[row, :] for row in at_ends]
        for start in range(0, plan.group, block_rows):
            at = pl.ds(start, block_rows)
            places = start + lax.broadcasted_iota(jnp.int32, (block_rows, LANES), 0)
            begin_cos, begin_sin = cosines[0], sines[0]
            for end, end_cos, end_sin in zip(ends[1:], cosines[1:], sines[1:]):
                begin_cos = jnp.where(places >= end, end_cos, begin_cos)
                begin_sin = jnp.where(places >= end, end_sin, begin_sin)
            place_c, place_s = own[at, :], ahead[at, :]
            cosine = place_c * begin_cos + place_s * begin_sin
            sine = place_s * begin_cos - place_c * begin_sin
            lane = lax.rem(lax.broadcasted_iota(jnp.int32, (block_rows, LANES), 1), HEAD)
            own[at, :] = jnp.where(lane < ROT, cosine, 1.0)
            ahead[at, :] = jnp.where(lane < ROT // 2, -sine, 0.0)
            behind[at, :] = jnp.where((lane >= ROT // 2) & (lane < ROT), sine, 0.0)

    def mixed_copy(t):
        cols = pl.ds(pl.multiple_of(t * width, width), width)
        return pltpu.make_async_copy(mixed.at[lax.rem(t, 2)], mixed_out.at[:, cols], mixed_sem.at[lax.rem(t, 2)])

    def finish_tile(t):
        @pl.when(t >= 2)
        def _():
            mixed_copy(t - 2).wait()
        out_sum.last(t, mixed.at[lax.rem(t, 2)])
        mixed_copy(t).start()

    normalize_own()
    z_start(0, 1)
    small_load.wait()
    w_start(3)
    round_in(0, 3, wa)
    w_start(0)
    round_in(3, 3 + plan.n_mlp, wm)
    mask_cot()
    round_down()
    make_tables()
    sums[...] = jnp.zeros_like(sums)
    lse[...] = jnp.zeros_like(lse)
    write(15, 16, 17, 18)
    w_arrive(0, plan.single)
    w_start(1)
    w_arrive(3, plan.single)
    z_arrive(0, 1)
    cot_start(1)
    w_arrive(3, plan.several)
    w_arrive(0, plan.several)
    w_arrive(3, plan.odd)
    w_arrive(0, plan.odd)
    write(0, 2)
    at_distance(0, attn_rows)
    if line > 2:
        at_distance(1, attn_rows)
    w_arrive(1, plan.single)
    w_start(2)
    for step in range(2, line - 1):
        z_arrive(0, step)
        cot_start(step)
        at_distance(step, attn_rows)
    w_arrive(1, plan.several)
    w_arrive(1, plan.odd)
    write(1)
    near = max(line - 2, 0)
    lax.fori_loop(
        jnp.maximum(place - near, 0), jnp.minimum(place + near, line - 1) + 1,
        lambda c, carry: (mlp_rows(c), carry)[1], 0,
    )
    if line > 2:
        z_arrive(0, line - 1)
        cot_start(line - 1)
    at_distance(line - 1, lambda c: (attn_rows(c), mlp_rows(c))[0])
    write(3, 6, 7, 8, 11)
    pairs = local // LANES
    lax.fori_loop(0, pairs // 2, attend, 0)
    w_arrive(2, plan.single)
    lax.fori_loop(pairs // 2, pairs, attend, 0)
    write(9, 10)
    z_arrive(1, 1)
    w_arrive(2, plan.several)
    out_copy(3).wait()
    for step in range(1, line):
        for up in (True, False):
            left = place != step - 1 if up else place != line - step
            @pl.when(left & sends(step, up))
            def _():
                z_copy(0, step, up).wait_send()
    w_arrive(2, plan.odd)

    def first_tile(t):
        out_tile(t)
        out_sum.first(t)

    early_tiles(first_tile)
    lax.fori_loop(plan.early, plan.d_tiles, lambda t, carry: (out_tile(t), carry)[1], 0)
    write(14)
    at_distance(0, back_rows)
    if line > 2:
        at_distance(1, back_rows)
    for step in range(2, line - 1):
        z_arrive(1, step)
        at_distance(step, back_rows)

    def running(near_end):
        for up in (True, False):
            now = (place < line // 2) if up == near_end else (place >= line // 2)

            @pl.when(now)
            def _():
                for step in range(1, line):
                    z_sent(1, step, up)
                early_tiles(lambda t: out_sum.hand_on(t, up))

    running(True)
    if line > 2:
        z_arrive(1, line - 1)
    running(False)
    at_distance(line - 1, back_rows)
    write(4, 5, 12, 13)
    early_tiles(finish_tile)
    for t in range(max(plan.early - 2, 0), plan.early):
        mixed_copy(t).wait()

    early_tiles(out_sum.sent)
    for flow in range(4):
        for mask in range(1, n):
            for half in halves(flow):
                w_copy(flow, mask, half).wait_send()
    for j in range(len(outs)):
        if j != 3:
            out_copy(j).wait()


def forward(plan, x, out_grad, w, wd, small, lengths):
    any_space = pl.BlockSpec(memory_space=pl.ANY)
    n, line, group, model, local, rows = (
        plan.n_dp, plan.n_line, plan.group, plan.model, plan.local, plan.rows
    )
    low = lambda *shape: jax.ShapeDtypeStruct(shape, bf16)
    full = lambda *shape: jax.ShapeDtypeStruct(shape, f32)
    early = plan.early * plan.width
    out_shape = [
        low(model, plan.attn), low(model, plan.mlp), low(n, 16, LANES + plan.out_cols),
        low(n, group, plan.width), full(8, model), low(n, group, plan.width),
        low(group, local), low(group, local), low(group, local), low(group, local),
        full(group, LANES),
        low(group, plan.mlp), low(group, plan.mlp), low(group, local),
        low(plan.d_tiles - plan.early, group, plan.width),
        full(group, LANES), full(group, LANES), full(group, LANES), full(2, rows, LANES), full(rows, early),
    ]
    scratch = lambda s: pltpu.VMEM(s.shape, s.dtype)
    dma = pltpu.SemaphoreType.DMA
    return pl.pallas_call(
        partial(forward_kernel, plan),
        in_specs=[any_space] * 5 + [pl.BlockSpec(memory_space=pltpu.SMEM)] + [any_space] * 2,
        out_specs=[any_space] * 20,
        out_shape=out_shape,
        scratch_shapes=[scratch(s) for s in out_shape[:2]]
        + [pltpu.VMEM((n, plan.down, plan.out_cols), bf16)]
        + [scratch(s) for s in out_shape[2:4]]
        + [pltpu.VMEM((rows, model), bf16)]
        + [scratch(s) for s in out_shape[4:14]]
        + [scratch(s) for s in out_shape[15:19]]
        + [pltpu.VMEM((plan.early, max(line - 1, 1), rows, plan.width), bf16)] * 2
        + [
            pltpu.VMEM((2, min(64, rows), model), f32), pltpu.VMEM((2, rows, plan.width), f32),
            pltpu.VMEM((2, plan.in_rows // 2, local), f32), pltpu.VMEM((2, local // 2, plan.out_cols), f32),
        ]
        + [dma((2,)), dma((5,)), dma((2, 2)), dma((19,)), dma((8 * n,)), dma((8 * n,))]
        + [dma((2 * line,))] * 4
        + [dma((plan.early, max(line - 1, 1)))] * 4,
        compiler_params=pltpu.CompilerParams(
            collective_id=0, has_side_effects=True, vmem_limit_bytes=63 << 20
        ),
        cost_estimate=pl.CostEstimate(flops=60 * 10**9, bytes_accessed=80 << 20, transcendentals=0),
    )(x, out_grad, w, wd, small, lengths, *angle_tables(group))


def backward_kernel(
    plan,
    xhat_in, cot_in, att_in, hidden_in, da_in, do_in, q_in, k_in, v_in, part_in, wa_in, wm_in,
    lse, sums_in, own, ahead, behind, lengths,
    down_out, in_out, small_out, mixed_out, rows_out, dh_out,
    turned, stage, og, da, qkv, do, k_sum, v_sum, sent, core_in, held, cube_in, up_in, down_in,
    part, part_up, part_down, w_tile, fin, fin_turned, dh_fin, small, small_in, shares,
    load_sem, stage_sem, tile_sem, fin_sem, dh_sem, core_send, core_recv, cube_send, cube_recv,
    up_send, up_recv, down_send, down_recv, part_up_send, part_up_recv, part_down_send, part_down_recv,
    small_send, small_recv, share_send, share_recv, credit,
):
    n, line = plan.n_dp, plan.n_line
    me, place = lax.axis_index("dp"), lax.axis_index("tensor")
    rows, local, group, model, in_rows = plan.rows, plan.local, plan.group, plan.model, plan.in_rows
    MESH = pl.DeviceIdType.MESH
    half_rows, pairs_n, n_bits = in_rows // 2, n // 2, len(plan.bits)
    orders = (plan.bits, plan.bits[::-1])
    n_down, n_mlp = 1 + plan.n_mlp, plan.n_mlp
    flows = {"down": (n_down, 0, 0), "mlp": (n_mlp, n_down, 3), "attn": (3, 0, 0)}

    def owner(mask):
        index = me
        for b in [1] + plan.bits:
            if mask & b:
                index = index + b - 2 * b * lax.rem(index // b, 2)
        return index

    def peer(bit):
        return {"dp": owner(bit)}

    def position(mask, order):
        return sum((1 if mask & b else 0) << (n_bits - 1 - p) for p, b in enumerate(order))

    width, d_tiles = plan.width, plan.d_tiles
    sub = local // width

    def strip(source, j):
        return source.at[:, pl.ds(j * width, width)]

    whole = [
        (da_in, da),
        (q_in, qkv.at[:, pl.ds(0, local)]),
        (k_in, qkv.at[:, pl.ds(local, local)]),
        (v_in, qkv.at[:, pl.ds(2 * local, local)]),
        (do_in, do),
        (part_in, part),
    ]
    whole = whole + [
        (strip(att_in, j) if j < sub else strip(hidden_in, j - sub), og.at[j]) for j in range(n_down * sub)
    ]
    strips = range(6, len(whole))
    for j, (a, b) in enumerate(whole):
        pltpu.make_async_copy(a, b, load_sem.at[j]).start()

    def loaded(*which):
        for j in which:
            pltpu.make_async_copy(whole[j][0], whole[j][1], load_sem.at[j]).wait()

    barrier = pltpu.get_barrier_semaphore()
    for b in [1] + plan.bits:
        pl.semaphore_signal(barrier, inc=1, device_id=peer(b), device_id_type=MESH)
    for d in range(1, line):
        pl.semaphore_signal(
            barrier, inc=1, device_id={"tensor": lax.rem(place + d, line)}, device_id_type=MESH
        )

    def share_copy(d, arriving):
        source = lax.rem(place + line - d, line) if arriving else place
        return pltpu.make_async_remote_copy(
            src_ref=shares, dst_ref=rows_out.at[source],
            send_sem=share_send.at[d], recv_sem=share_recv.at[d],
            device_id={"tensor": lax.rem(place + d, line)}, device_id_type=MESH,
        )

    share_own = pltpu.make_async_copy(shares, rows_out.at[place], share_send.at[0])

    def turn_columns(source, masks):
        def fetch(j):
            return pltpu.make_async_copy(source.at[owner(masks[j])], stage.at[j % 2], stage_sem.at[j % 2])

        fetch(0).start()
        for j in range(len(masks)):
            if j + 1 < len(masks):
                fetch(j + 1).start()
            fetch(j).wait()
            turned[pl.ds(j * in_rows, in_rows), :] = stage[j % 2].T

    def core_copy(name, t):
        return pltpu.make_async_remote_copy(
            src_ref=sent.at[lax.rem(t, 2)], dst_ref=core_in.at[t],
            send_sem=core_send.at[lax.rem(t, 2)], recv_sem=core_recv.at[t],
            device_id=peer(1), device_id_type=MESH,
        )

    def cube_copy(slot, half, phase):
        count = pairs_n >> (phase + 1)
        first = pairs_n - 2 * count
        at = half * n_bits + phase
        return pltpu.make_async_remote_copy(
            src_ref=held.at[slot, half, pl.ds(count, count)],
            dst_ref=cube_in.at[slot, half, pl.ds(first, count)],
            send_sem=cube_send.at[slot, at], recv_sem=cube_recv.at[slot, at],
            device_id=peer(orders[half][phase]), device_id_type=MESH,
        )

    def product(name, at, count, t):
        if name == "down":
            return [dot_n(turned[at : at + count, :], og[t * sub + j]) for j in range(sub)]
        source = da if name == "mlp" else qkv
        return [dot_n(turned[at : at + count, :], source[:, pl.ds(pl.multiple_of(t * local, local), local)])]

    piece = min(2, pairs_n) * in_rows

    def send_core(name, t):
        @pl.when(t >= 2)
        def _():
            core_copy(name, t - 2).wait_send()
        for at in range(0, pairs_n * in_rows, piece):
            strips_of = product(name, at, piece, t)
            step = local // len(strips_of)
            for j, value in enumerate(strips_of):
                sent[lax.rem(t, 2), at : at + piece, j * step : (j + 1) * step] = value.astype(bf16)
        core_copy(name, t).start()

    def keep_core(name, t):
        base = flows[name][1]
        core_copy(name, t).wait_recv()
        for first in range(0, pairs_n * in_rows, piece):
            strips_of = product(name, pairs_n * in_rows + first, piece, t)
            step = local // len(strips_of)
            for i, value in enumerate(strips_of):
                cols = slice(i * step, (i + 1) * step)
                total = value + core_in[t, first : first + piece, cols].astype(f32)
                for at in range(0, piece, half_rows):
                    j, half = divmod((first + at) // half_rows, 2)
                    held[base + t, half, position(2 * j, orders[half]), :, cols] = total[at : at + half_rows].astype(bf16)
        for half in range(2):
            if n_bits:
                cube_copy(base + t, half, 0).start()

    def scatter(name):
        tiles_n = flows[name][0]
        if name != "down":
            pl.semaphore_wait(credit.at[0], 1)
        if name == "attn":
            pl.semaphore_wait(credit.at[1], n_bits)

        def step(t, carry):
            @pl.when(t < tiles_n)
            def _():
                send_core(name, t)

            @pl.when(t >= 1)
            def _():
                keep_core(name, t - 1)
            return carry

        lax.fori_loop(0, tiles_n + 1, step, 0)
        for t in range(max(tiles_n - 2, 0), tiles_n):
            core_copy(name, t).wait_send()
        if name != "attn":
            pl.semaphore_signal(credit.at[0], inc=1, device_id=peer(1), device_id_type=MESH)

    def cube_step(name, phase):
        tiles, base, result = flows[name]
        count = pairs_n >> (phase + 1)
        first = pairs_n - 2 * count
        target, depth = (down_out, 1) if name == "down" else (in_out, 2)

        def fin_copy(t):
            source = fin_turned if name == "down" else fin.at[lax.rem(t, 2)]
            return pltpu.make_async_copy(source, target.at[result + t], fin_sem.at[lax.rem(t, 2)])

        def step(t, carry):
            slot = base + t
            if phase == n_bits - 1:
                @pl.when(t >= depth)
                def _():
                    fin_copy(t - depth).wait()
            for half in range(2):
                cube_copy(slot, half, phase).wait_recv()
                total = (
                    held[slot, half, 0:count].astype(f32)
                    + cube_in[slot, half, first : first + count].astype(f32)
                )
                if phase < n_bits - 1:
                    held[slot, half, 0:count] = total.astype(bf16)
                    cube_copy(slot, half, phase + 1).start()
                else:
                    fin[lax.rem(t, 2), half * half_rows : (half + 1) * half_rows, :] = total[0]
            if phase == n_bits - 1:
                if name == "down":
                    fin_turned[...] = fin[lax.rem(t, 2)].T
                fin_copy(t).start()
                if name != "down":
                    weight = w_tile[0 if name == "attn" else 1, 0:in_rows, pl.ds(pl.multiple_of(t * local, local), local)].astype(f32)
                    product = weight * fin[lax.rem(t, 2)]
                    extra = weight * small[n_bits + 1, pl.ds(result + t, 1), :]
                    for g in range(0, local, LANES):
                        shares[0] += product[:, g : g + LANES]
                        shares[1] += extra[:, g : g + LANES]
            return carry

        lax.fori_loop(0, tiles, step, 0)
        if phase == n_bits - 1:
            for t in range(max(tiles - depth, 0), tiles):
                fin_copy(t).wait()

    def cube_sent(name):
        tiles, base, _ = flows[name]

        def step(t, carry):
            for half in range(2):
                for phase in range(n_bits):
                    cube_copy(base + t, half, phase).wait_send()
            return carry

        lax.fori_loop(0, tiles, step, 0)

    def attend(pair, carry):
        block = min(QUERY_ROWS, group)
        scale = HEAD ** (-0.5)
        k_sum[...] = jnp.zeros_like(k_sum)
        v_sum[...] = jnp.zeros_like(v_sum)
        q_lanes, k_lanes, v_lanes = (
            pl.ds(pl.multiple_of(pair * LANES + r * local, LANES), LANES) for r in range(3)
        )
        lanes = q_lanes
        which = lax.broadcasted_iota(jnp.int32, (block, LANES), 1)
        for start in range(0, group, block):
            stop = start + block
            here = pl.ds(start, block)
            allowed = attend_mask(begins_of(lengths, start, block), start, block, stop)
            q_sum = jnp.zeros((block, LANES), f32)
            for head in range(LANES // HEAD):
                mine = head_lanes(block, head)
                query = jnp.where(mine, qkv[here, q_lanes], jnp.zeros((block, LANES), bf16)) * scale
                query = query.astype(bf16)
                cot = jnp.where(mine, do[here, lanes], jnp.zeros((block, LANES), bf16))
                level = jnp.sum(
                    jnp.where(which == pair * (LANES // HEAD) + head, lse[here, :], 0.0), axis=1, keepdims=True
                )
                scores = dot_t(query, qkv[:stop, k_lanes]) - level
                probs = jnp.where(allowed, jnp.exp(scores), 0.0)
                prob_grad = dot_t(cot, qkv[:stop, v_lanes])
                mean = jnp.sum(probs * prob_grad, axis=1, keepdims=True)
                score_grad = (probs * (prob_grad - mean)).astype(bf16)
                q_step = dot_n(score_grad, qkv[:stop, k_lanes])
                q_sum = jnp.where(mine, q_step * scale, q_sum)
                k_sum[:stop, :] += dot_s(score_grad, query)
                v_sum[:stop, :] += dot_s(probs.astype(bf16), cot)
            qkv[here, q_lanes] = turn(
                q_sum, own[here, :], ahead[here, :], behind[here, :], -1.0
            ).astype(bf16)
        qkv[:, k_lanes] = turn(k_sum[...], own[...], ahead[...], behind[...], -1.0).astype(bf16)
        qkv[:, v_lanes] = v_sum[...].astype(bf16)
        return carry

    def tile_loads(t):
        at = pl.ds(pl.multiple_of(t * width, width), width)
        slot = lax.rem(t, 2)
        return (
            pltpu.make_async_copy(wa_in.at[at, :], w_tile.at[slot, pl.ds(0, width), pl.ds(0, plan.attn)], tile_sem.at[slot, 0]),
            pltpu.make_async_copy(wm_in.at[at, :], w_tile.at[slot, pl.ds(0, width), pl.ds(plan.attn, plan.mlp)], tile_sem.at[slot, 1]),
        )

    def tile_of(buffer):
        def source(t, index):
            return buffer.at[t, pl.ds(pl.multiple_of(index * rows, rows), rows), :]
        return source

    dh_sum = LineSum(
        place, line, tile_of(og), lambda t, slot, up: (up_in if up else down_in).at[t, slot],
        (up_send, up_recv, down_send, down_recv),
    )
    late = d_tiles - plan.early
    out_sum = LineSum(
        place, line, tile_of(part), lambda t, slot, up: (part_up if up else part_down).at[t, slot],
        (part_up_send, part_up_recv, part_down_send, part_down_recv),
    )

    def sum_copy(target, t):
        cols = pl.ds(pl.multiple_of(t * width, width), width)
        return pltpu.make_async_copy(dh_fin.at[lax.rem(t, 2)], target.at[:, cols], dh_sem.at[lax.rem(t, 2)])

    def finish(flow, target, count):
        def step(t):
            @pl.when(t >= 2)
            def _():
                sum_copy(target, t - 2).wait()
            flow.last(t, dh_fin.at[lax.rem(t, 2)])
            sum_copy(target, t).start()

        tiles(0, count, step)
        for t in range(max(count - 2, 0), count):
            sum_copy(target, t).wait()

    def tiles(first, stop, fn):
        lax.fori_loop(first, stop, lambda t, carry: (fn(t), carry)[1], 0)

    def dh_tile(t):
        slot = lax.rem(t, 2)
        @pl.when(t + 1 < d_tiles)
        def _():
            for load in tile_loads(t + 1):
                load.start()
        for load in tile_loads(t):
            load.wait()
        total = dot_t(qkv[...], w_tile[slot, 0:width, : plan.attn]) + dot_t(da[...], w_tile[slot, 0:width, plan.attn :])
        og[t] = total.astype(bf16)
        dh_sum.first(t)

    def small_copy(j):
        return pltpu.make_async_remote_copy(
            src_ref=small.at[j], dst_ref=small_in.at[j],
            send_sem=small_send.at[j], recv_sem=small_recv.at[j],
            device_id=peer(([1] + plan.bits)[j]), device_id_type=MESH,
        )

    def small_step(j):
        small_copy(j).wait_recv()
        small[j + 1] = small[j] + small_in[j]
        if j < n_bits:
            small_copy(j + 1).start()

    shares[...] = jnp.zeros_like(shares)
    small[0] = jnp.zeros_like(small[0])
    for load in tile_loads(0):
        load.start()
    masks = [2 * j + 1 for j in range(pairs_n)] + [2 * j for j in range(pairs_n)]
    turn_columns(cot_in, masks)
    pl.semaphore_wait(barrier, 1 + n_bits + line - 1)
    loaded(5)
    tiles(0, late, out_sum.first)
    loaded(*strips)
    scatter("down")
    loaded(0, 1, 2, 3, 4)
    pairs = local // LANES
    lax.fori_loop(0, pairs // 2, attend, 0)
    out_sum.both_ways(0, late, late)
    lax.fori_loop(pairs // 2, pairs, attend, 0)
    for r in range(3 + n_mlp):
        block = qkv[:, r * local : (r + 1) * local] if r < 3 else da[:, (r - 3) * local : (r - 2) * local]
        small[0, r : r + 1, :] = jnp.sum(block.astype(f32), axis=0, keepdims=True)
    for r in range(model // local):
        small[0, 8 + r : 9 + r, :] = sums_in[0:1, r * local : (r + 1) * local]
    small_copy(0).start()
    some = min(3, d_tiles)
    tiles(0, some, dh_tile)
    for phase in range(n_bits - 1):
        cube_step("down", phase)
    turn_columns(xhat_in, masks)
    scatter("mlp")
    finish(out_sum, mixed_out, late)
    tiles(some, d_tiles, dh_tile)
    dh_sum.both_ways(0, d_tiles // 4, d_tiles)
    small_step(0)
    cube_step("down", n_bits - 1)
    cube_sent("down")
    for b in plan.bits:
        pl.semaphore_signal(credit.at[1], inc=1, device_id=peer(b), device_id_type=MESH)
    small_step(1)
    scatter("attn")
    for j in range(2, n_bits + 1):
        small_step(j)
    own_rows = pl.ds(pl.multiple_of(me * in_rows, in_rows), in_rows)
    weights = [
        pltpu.make_async_copy(wa_in.at[own_rows, :], w_tile.at[0, pl.ds(0, in_rows), pl.ds(0, plan.attn)], tile_sem.at[0, 0]),
        pltpu.make_async_copy(wm_in.at[own_rows, :], w_tile.at[1, pl.ds(0, in_rows), pl.ds(0, plan.mlp)], tile_sem.at[1, 0]),
    ]
    for w in weights:
        w.start()
    dh_sum.both_ways(d_tiles // 4, d_tiles // 2, d_tiles)
    for phase in range(n_bits - 1):
        cube_step("mlp", phase)
    dh_sum.both_ways(d_tiles // 2, 3 * d_tiles // 4, d_tiles)
    for w in weights:
        w.wait()
    cube_step("mlp", n_bits - 1)
    dh_sum.both_ways(3 * d_tiles // 4, d_tiles, d_tiles)
    for phase in range(n_bits):
        cube_step("attn", phase)
    share_own.start()
    for d in range(1, line):
        share_copy(d, False).start()
    finish(dh_sum, dh_out, d_tiles)
    small_done = pltpu.make_async_copy(small.at[n_bits + 1], small_out, load_sem.at[0])
    small_done.start()
    cube_sent("mlp")
    cube_sent("attn")
    tiles(0, d_tiles, dh_sum.sent)
    tiles(0, late, out_sum.sent)
    for j in range(n_bits + 1):
        small_copy(j).wait_send()
    share_own.wait()
    for d in range(1, line):
        share_copy(d, False).wait_send()
        share_copy(d, True).wait_recv()
    small_done.wait()


def backward(plan, xhat, cot, att, hidden, da, do, q, k, v, part, wa, wm, lse, sums, tables, lengths):
    any_space = pl.BlockSpec(memory_space=pl.ANY)
    vmem = pl.BlockSpec(memory_space=pltpu.VMEM)
    n, line, group, model, local = plan.n_dp, plan.n_line, plan.group, plan.model, plan.local
    rows, in_rows, n_bits, pairs_n = plan.rows, plan.in_rows, len(plan.bits), n // 2
    n_down = 1 + plan.n_mlp
    small_rows = 8 + -(-(model // local) // 8) * 8
    width, d_tiles, steps = plan.width, plan.d_tiles, max(line - 1, 1)
    late = d_tiles - plan.early
    low = lambda *shape: pltpu.VMEM(shape, bf16)
    full = lambda *shape: pltpu.VMEM(shape, f32)
    dma = pltpu.SemaphoreType.DMA
    out = lambda dtype, *shape: jax.ShapeDtypeStruct(shape, dtype)
    slots = n_down + plan.n_mlp
    return pl.pallas_call(
        partial(backward_kernel, plan),
        in_specs=[any_space] * 12 + [vmem] * 5 + [pl.BlockSpec(memory_space=pltpu.SMEM)],
        out_specs=[any_space] * 6,
        out_shape=[
            out(f32, n_down, local, in_rows), out(f32, 3 + plan.n_mlp, in_rows, local),
            out(f32, small_rows, local), out(f32, rows, late * width),
            out(f32, line, 2, in_rows, LANES), out(f32, rows, model),
        ],
        scratch_shapes=[
            low(n * in_rows, group), low(2, group, in_rows),
            low(max(d_tiles, plan.down // width), group, width), low(group, plan.mlp),
            low(group, plan.attn), low(group, local), full(group, LANES), full(group, LANES),
            low(2, pairs_n * in_rows, local), low(n_down, pairs_n * in_rows, local),
            low(slots, 2, pairs_n, in_rows // 2, local), low(slots, 2, max(pairs_n - 1, 1), in_rows // 2, local),
            low(d_tiles, steps, rows, width), low(d_tiles, steps, rows, width),
            low(late, group, width), low(late, steps, rows, width), low(late, steps, rows, width),
            low(2, max(width, in_rows), plan.attn + plan.mlp), full(2, in_rows, local), full(local, in_rows), full(2, rows, width),
            full(n_bits + 2, small_rows, local), full(n_bits + 1, small_rows, local), full(2, in_rows, LANES),
            dma((6 + plan.down // width,)), dma((2,)), dma((2, 2)), dma((2,)), dma((2,)), dma((2,)), dma((n_down,)),
            dma((slots, max(2 * n_bits, 1))), dma((slots, max(2 * n_bits, 1))),
            dma((d_tiles, steps)), dma((d_tiles, steps)), dma((d_tiles, steps)), dma((d_tiles, steps)),
            dma((late, steps)), dma((late, steps)), dma((late, steps)), dma((late, steps)),
            dma((n_bits + 1,)), dma((n_bits + 1,)), dma((line,)), dma((line,)),
            pltpu.SemaphoreType.REGULAR((2,)),
        ],
        compiler_params=pltpu.CompilerParams(
            collective_id=1, has_side_effects=True, vmem_limit_bytes=63 << 20
        ),
        cost_estimate=pl.CostEstimate(flops=80 * 10**9, bytes_accessed=80 << 20, transcendentals=0),
    )(xhat, cot, att, hidden, da, do, q, k, v, part, wa, wm, lse, sums, *tables, lengths)


def adam_update(weight, moment_one, moment_two, gradient, step_rate, decay_factor):
    first_new = beta_first * moment_one + (1.0 - beta_first) * gradient
    second_new = beta_second * moment_two + (1.0 - beta_second) * gradient * gradient
    corrected = first_new / (1.0 - beta_first**STEP)
    spread = jnp.sqrt(second_new / (1.0 - beta_second**STEP))
    return (
        weight - step_rate * (corrected / (spread + adam_eps) + decay_factor * weight),
        first_new,
        second_new,
    )


def per_device(
    block_input,
    out_grad,
    seq_lengths,
    in_weight,
    down_weight,
    column_bias,
    vector_params,
    in_first,
    in_second,
    down_first,
    down_second,
    bias_first,
    bias_second,
    vector_first,
    vector_second,
):
    n_dp = lax.axis_size("dp")
    n_tensor = lax.axis_size("tensor")
    own_rows, model = block_input.shape
    group = own_rows * n_tensor
    in_rows, widths, local = in_weight.shape
    out_cols = down_weight.shape[2]
    n_mlp = widths - 3
    attn_width, mlp_width = 3 * local, n_mlp * local

    me = lax.axis_index("dp")
    plan = Plan(n_dp, n_tensor, own_rows, model, in_rows, local, n_mlp, out_cols)
    share = LANES // plan.bias_cols
    lane = lax.broadcasted_iota(jnp.int32, (widths, LANES), 1) // plan.bias_cols
    bias_tile = jnp.where(lane == lax.rem(me, share), jnp.tile(column_bias, (1, share)), 0.0)
    small = jnp.concatenate(
        [jnp.pad(bias_tile, ((0, 16 - widths), (0, 0))), jnp.pad(vector_params, ((0, 13), (0, 0)))], axis=1
    ).astype(bf16)
    (
        w_attn, w_mlp, vectors, xhat_all, cot_sums, cot_all, q_low, k_low, v_low, attended, lse,
        hidden, pre_grad, attn_grad, out_part, own, ahead, behind, stats, mixed_early,
    ) = forward(plan, block_input, out_grad, in_weight.transpose(1, 0, 2), down_weight, small, seq_lengths)
    down_grad, in_grad, small_grad, mixed_late, shares, dh = backward(
        plan, xhat_all, cot_all, attended, hidden, pre_grad, attn_grad, q_low, k_low, v_low, out_part,
        w_attn, w_mlp, lse, cot_sums, (own, ahead, behind), seq_lengths,
    )
    vector_vals = vectors[:, :3, LANES:].transpose(1, 0, 2).reshape(3, model).astype(f32)
    gain, out_bias = vector_vals[0], vector_vals[2]
    block_out = block_input + (jnp.concatenate([mixed_early, mixed_late], axis=1) + out_bias)
    mean, inv_scale = stats[0, :, :1], stats[1, :, :1]
    xhat = (block_input - mean) * inv_scale
    places = lax.axis_index("tensor") * own_rows + lax.broadcasted_iota(jnp.int32, (own_rows, 1), 0)
    cot_live = jnp.where(places < jnp.sum(seq_lengths), out_grad, 0.0)

    dxhat = dh * gain
    input_grad = cot_live + inv_scale * (
        dxhat
        - jnp.mean(dxhat, axis=-1, keepdims=True)
        - xhat * jnp.mean(dxhat * xhat, axis=-1, keepdims=True)
    )

    bias_full = small_grad[:widths]
    own_vectors = vector_params.astype(bf16).astype(f32)
    in_reduced = (
        in_grad * own_vectors[0][None, :, None] + own_vectors[1][None, :, None] * bias_full[:, None, :]
    ).transpose(1, 0, 2)
    down_reduced = down_grad
    bias_reduced = lax.dynamic_slice_in_dim(bias_full, me * plan.bias_cols, plan.bias_cols, 1)
    out_sums = small_grad[8 : 8 + model // local].reshape(-1)
    vector_reduced = jnp.stack(
        [
            jnp.sum(shares[:, 0], axis=(0, 2)),
            jnp.sum(shares[:, 1], axis=(0, 2)),
            lax.dynamic_slice_in_dim(out_sums, me * out_cols, out_cols, 0),
        ]
    )

    in_new, in_one, in_two = adam_update(
        in_weight, in_first, in_second, in_reduced, rate_in, weight_decay
    )
    down_new, down_one, down_two = adam_update(
        down_weight, down_first, down_second, down_reduced, rate_down, weight_decay
    )
    bias_new, bias_one, bias_two = adam_update(
        column_bias, bias_first, bias_second, bias_reduced, rate_vector, 0.0
    )
    vector_new, vector_one, vector_two = adam_update(
        vector_params, vector_first, vector_second, vector_reduced, rate_vector, 0.0
    )
    return (
        block_out,
        input_grad,
        in_new,
        in_one,
        in_two,
        down_new,
        down_one,
        down_two,
        bias_new,
        bias_one,
        bias_two,
        vector_new,
        vector_one,
        vector_two,
    )


def widths_down(down_weight):
    return down_weight.shape[0] * down_weight.shape[1]


def solution(mesh):
    return jax.shard_map(
        per_device,
        mesh=mesh,
        in_specs=(
            P(("dp", "tensor"), None),
            P(("dp", "tensor"), None),
            P("dp", None),
            P("dp", None, "tensor"),
            P(None, "tensor", "dp"),
            P(None, ("tensor", "dp")),
            P(None, "dp"),
            P("dp", None, "tensor"),
            P("dp", None, "tensor"),
            P(None, "tensor", "dp"),
            P(None, "tensor", "dp"),
            P(None, ("tensor", "dp")),
            P(None, ("tensor", "dp")),
            P(None, "dp"),
            P(None, "dp"),
        ),
        out_specs=(
            P(("dp", "tensor"), None),
            P(("dp", "tensor"), None),
            P("dp", None, "tensor"),
            P("dp", None, "tensor"),
            P("dp", None, "tensor"),
            P(None, "tensor", "dp"),
            P(None, "tensor", "dp"),
            P(None, "tensor", "dp"),
            P(None, ("tensor", "dp")),
            P(None, ("tensor", "dp")),
            P(None, ("tensor", "dp")),
            P(None, "dp"),
            P(None, "dp"),
            P(None, "dp"),
        ),
        check_vma=False,
    )
```

```python
from functools import partial

import jax
import jax.numpy as jnp
import numpy as np
from jax import lax
from jax.experimental import pallas as pl
from jax.experimental.pallas import tpu as pltpu
from jax.sharding import PartitionSpec as P

HEAD = 64
ROT = 32
STEP = 8
LANES = 128
QUERY_ROWS = 256

norm_eps = 1e-05
beta_first = 0.9
beta_second = 0.95
adam_eps = 1e-08
masked_score = -1000000000.0
rate_in = 0.02
rate_down = 0.05
rate_vector = 0.2
weight_decay = 0.1

bf16 = jnp.bfloat16
f32 = jnp.float32


def angle_tables(rows):
    half_rot = ROT // 2
    frequency = 10000.0 ** (-2.0 * (np.arange(LANES) % half_rot) / ROT)
    angles = np.arange(rows)[:, None] * frequency[None, :]
    return np.cos(angles).astype(np.float32), np.sin(angles).astype(np.float32)


def ends_of(lengths):
    ends = [jnp.int32(0)]
    for j in range(lengths.shape[1]):
        ends.append(ends[-1] + lengths[0, j])
    return ends


def begins_of(lengths, start, rows):
    places = start + lax.broadcasted_iota(jnp.int32, (rows, 1), 0)
    begin = jnp.zeros((rows, 1), jnp.int32)
    for end in ends_of(lengths)[1:]:
        begin = jnp.where(places >= end, end, begin)
    return begin


def attend_mask(begin, row_start, rows, stop):
    key_place = lax.broadcasted_iota(jnp.int32, (rows, stop), 1)
    query_place = row_start + lax.broadcasted_iota(jnp.int32, (rows, stop), 0)
    return (key_place <= query_place) & (key_place >= begin)


def head_lanes(rows, head):
    lane = lax.broadcasted_iota(jnp.int32, (rows, LANES), 1)
    return (lane >= head * HEAD) & (lane < (head + 1) * HEAD)


def dot_t(a, b):
    return lax.dot_general(a, b, (((1,), (1,)), ((), ())), preferred_element_type=f32)


def dot_n(a, b):
    return lax.dot_general(a, b, (((1,), (0,)), ((), ())), preferred_element_type=f32)


def dot_s(a, b):
    return lax.dot_general(a, b, (((0,), (0,)), ((), ())), preferred_element_type=f32)


def turn(x, own, ahead, behind, sign):
    half = ROT // 2
    return x * own + sign * (
        pltpu.roll(x, LANES - half, 1) * ahead + pltpu.roll(x, half, 1) * behind
    )


def low_bit(mask):
    return mask & -mask


def high_bit(mask):
    return 1 << (mask.bit_length() - 1)


def gelu_and_slope(a):
    root = (2.0 / 3.141592653589793) ** 0.5
    square = a * a
    t = jnp.tanh(root * a * (1.0 + 0.044715 * square))
    half = 0.5 * (1.0 + t)
    return a * half, half + 0.5 * a * (1.0 - t * t) * (root * (1.0 + 3.0 * 0.044715 * square))


class LineSum:
    def __init__(self, place, line, source, landing, sems):
        self.place, self.line, self.source, self.landing = place, line, source, landing
        self.up_send, self.up_recv, self.down_send, self.down_recv = sems

    def copy(self, t, index, up, arriving=False):
        place = self.place
        slot = self.slot(index, up)
        return pltpu.make_async_remote_copy(
            src_ref=self.source(t, index),
            dst_ref=self.landing(t, slot),
            send_sem=(self.up_send if up else self.down_send).at[t, slot],
            recv_sem=(self.up_recv if up else self.down_recv).at[t, slot],
            device_id={"tensor": place + 1 if up != arriving else place - 1},
            device_id_type=pl.DeviceIdType.MESH,
        )

    def got(self, t, index, up):
        return self.landing(t, self.slot(index, up))[...].astype(f32)

    def slot(self, index, up):
        return index - 1 if up else lax.rem(self.line - 1 + index, self.line + 1)

    def first(self, t):
        for up in (True, False):
            @pl.when((self.place == 0) if up else (self.place == self.line - 1))
            def _():
                for step in range(self.line - 1):
                    self.copy(t, self.line - 1 - step if up else step, up).start()

    def hand_on(self, t, up):
        place, line = self.place, self.line
        for step in range(line - 1):
            index = line - 1 - step if up else step
            hears = (place > 0) & (place < index) if up else (place < line - 1) & (place > index)

            @pl.when(hears)
            def _():
                self.copy(t, index, up, True).wait_recv()
                mine = self.source(t, index)
                mine[...] = (mine[...].astype(f32) + self.got(t, index, up)).astype(bf16)
                self.copy(t, index, up).start()

    def both_ways(self, first, stop, count, lag=2):
        def step(t, carry):
            for up in (True, False):
                far = 2 * self.place // self.line
                index = t - lag * (far if up else 1 - far)

                @pl.when((index >= 0) & (index < count))
                def _():
                    self.hand_on(index, up)
            return carry

        lax.fori_loop(first, stop + (lag if stop == count else 0), step, 0)

    def last(self, t, target):
        place, line = self.place, self.line
        target[...] = self.source(t, place)[...].astype(f32)
        for up in (True, False):
            @pl.when((place > 0) if up else (place < line - 1))
            def _():
                self.copy(t, place, up, True).wait_recv()
                target[...] += self.got(t, place, up)

    def sent(self, t):
        for index in range(self.line):
            for up in (True, False):
                @pl.when((self.place < index) if up else (self.place > index))
                def _():
                    self.copy(t, index, up).wait_send()


class Plan:
    def __init__(self, n_dp, n_line, rows, model, in_rows, local, n_mlp, out_cols):
        self.n_dp, self.n_line = n_dp, n_line
        self.rows, self.model = rows, model
        self.group = rows * n_line
        self.in_rows, self.local, self.n_mlp, self.out_cols = in_rows, local, n_mlp, out_cols
        self.attn, self.mlp = 3 * local, n_mlp * local
        self.down = (1 + n_mlp) * local
        self.bias_cols = local // n_dp
        self.width = out_cols
        self.d_tiles = model // out_cols
        self.bits = [1 << b for b in range(1, n_dp.bit_length() - 1)]
        even = range(2, n_dp, 2)
        self.single = [m for m in even if m.bit_count() == 1]
        self.several = sorted((m for m in even if m.bit_count() > 1), key=lambda m: m.bit_count())
        self.odd = list(range(1, n_dp, 2))

    def hop(self, mask, half):
        if mask & 1:
            return 1
        return high_bit(mask) if half == 0 else low_bit(mask)

    def onward(self, mask, half):
        if mask & 1:
            return []
        masks = [mask | 1] if self.n_dp > 1 else []
        return masks + [
            mask | b for b in self.bits if not mask & b and self.hop(mask | b, half) == b
        ]


def forward_kernel(
    plan,
    x_in, out_grad_in, w_in, wd_in, small_in, lengths, place_cos, place_sin,
    wa_out, wm_out, small_out, xhat_out, sums_out, cot_out, q_out, k_out, v_out, att_out,
    hidden_out, da_out, dh_out, stats_out, mixed_out,
    wa, wm, wd, small, xs, ns, sums, cs, q, k, v, att, lse, hidden, slope, k_sum, v_sum,
    own, ahead, behind, stats, land, wide, mixed, block, tall_block,
    mixed_sem, own_sem, block_sem, out_sem, w_send, w_recv, up_send, up_recv, down_send, down_recv,
    sum_up_send, sum_up_recv, sum_down_send, sum_down_recv,
):
    n, line = plan.n_dp, plan.n_line
    me, place = lax.axis_index("dp"), lax.axis_index("tensor")
    rows, local, model, width = plan.rows, plan.local, plan.model, plan.width

    def owner(mask):
        index = me
        for b in [1] + plan.bits:
            if mask & b:
                index = index + b - 2 * b * lax.rem(index // b, 2)
        return index

    def slot(flow, index, half):
        if flow < 2:
            step = plan.in_rows // 2
            at = pl.multiple_of(index * plan.in_rows + half * step, step)
            return (wa, wm)[flow].at[pl.ds(at, step), :]
        if flow == 2:
            step = plan.down // 2
            return wd.at[index, pl.ds(half * step, step), :]
        return small.at[index]

    def halves(flow):
        return (0,) if flow == 3 else (0, 1)

    def w_copy(flow, mask, half):
        hop = plan.hop(mask, half)
        piece = slot(flow, owner(mask ^ hop), half)
        at = flow * 2 * n + 2 * mask + half
        return pltpu.make_async_remote_copy(
            src_ref=piece, dst_ref=piece, send_sem=w_send.at[at], recv_sem=w_recv.at[at],
            device_id={"dp": owner(hop)}, device_id_type=pl.DeviceIdType.MESH,
        )

    def w_start(flow, mask=0):
        for half in halves(flow):
            for target in plan.onward(mask, half):
                w_copy(flow, target, half).start()

    def w_arrive(flow, masks):
        for mask in masks:
            for half in halves(flow):
                piece = slot(flow, owner(mask), half)
                at = flow * 2 * n + 2 * mask + half
                pltpu.make_async_remote_copy(
                    src_ref=piece, dst_ref=piece, send_sem=w_send.at[at], recv_sem=w_recv.at[at],
                    device_id={"dp": owner(plan.hop(mask, half))}, device_id_type=pl.DeviceIdType.MESH,
                ).wait_recv()
                for target in plan.onward(mask, half):
                    w_copy(flow, target, half).start()

    def chunk(flow, index):
        return (xs, cs)[flow].at[:, pl.ds(pl.multiple_of(index * rows, rows), rows), :]

    def z_copy(flow, step, up):
        piece = chunk(flow, place - (step - 1) if up else place + (step - 1))
        at = flow * line + step
        return pltpu.make_async_remote_copy(
            src_ref=piece, dst_ref=piece,
            send_sem=(up_send if up else down_send).at[at],
            recv_sem=(up_recv if up else down_recv).at[at],
            device_id={"tensor": place + 1 if up else place - 1}, device_id_type=pl.DeviceIdType.MESH,
        )

    def sends(step, up):
        if up:
            return (place < line - 1) & (place >= step - 1)
        return (place > 0) & (place + step - 1 <= line - 1)

    def z_start(flow, step):
        for up in (True, False):
            @pl.when(sends(step, up))
            def _():
                z_copy(flow, step, up).start()

    def z_arrive(flow, step):
        for up in (True, False):
            @pl.when(place >= step if up else place + step <= line - 1)
            def _():
                piece = chunk(flow, place - step if up else place + step)
                at = flow * line + step
                pltpu.make_async_remote_copy(
                    src_ref=piece, dst_ref=piece,
                    send_sem=(up_send if up else down_send).at[at],
                    recv_sem=(up_recv if up else down_recv).at[at],
                    device_id={"tensor": place - 1 if up else place + 1},
                    device_id_type=pl.DeviceIdType.MESH,
                ).wait_recv()
        if step + 1 < line:
            z_start(flow, step + 1)

    def z_sent(flow, step, up):
        @pl.when(sends(step, up))
        def _():
            z_copy(flow, step, up).wait_send()

    def cot_start(step):
        for up in (True, False):
            last = place == step - 1 if up else place == line - step
            @pl.when(last & sends(1, up))
            def _():
                z_copy(0, step, up).wait_send()
                z_copy(1, 1, up).start()

    def at_distance(step, fn):
        if step == 0:
            fn(place)
            return

        def side(j, carry):
            index = place - step + 2 * step * j

            @pl.when((index >= 0) & (index < line))
            def _():
                fn(index)
            return carry

        lax.fori_loop(0, 2, side, 0)

    def span(index):
        return pl.ds(pl.multiple_of(index * rows, rows), rows)

    outs = [
        (wa, wa_out), (wm, wm_out), (small, small_out), (xs, xhat_out), (sums, sums_out), (cs, cot_out),
        (q, q_out), (k, k_out), (v, v_out), (att, att_out), (hidden, hidden_out),
        (slope, da_out), (cs, dh_out), (stats, stats_out),
    ]

    def out_copy(j):
        return pltpu.make_async_copy(outs[j][0], outs[j][1], out_sem.at[j])

    def write(*which):
        for j in which:
            out_copy(j).start()

    w_rows = pl.ds(pl.multiple_of(me * plan.in_rows, plan.in_rows), plan.in_rows)
    small_load = pltpu.make_async_copy(small_in, small.at[me], own_sem.at[2])

    some_rows, some_cols = plan.in_rows // 4, local // 4

    def in_load(i):
        return pltpu.make_async_copy(
            w_in.at[i // 4, pl.ds(i % 4 * some_rows, some_rows), :], block.at[i % 2], block_sem.at[0, i % 2]
        )

    def down_load(i):
        return pltpu.make_async_copy(
            wd_in.at[i // 4, pl.ds(i % 4 * some_cols, some_cols), :], tall_block.at[i % 2], block_sem.at[1, i % 2]
        )

    def round_in(first, stop, target):
        for i in range(4 * first, 4 * stop):
            r, part = divmod(i, 4)
            in_load(i).wait()
            to = pl.ds(pl.multiple_of(me * plan.in_rows + part * some_rows, some_rows), some_rows)
            target[to, (r - first) * local : (r - first + 1) * local] = block[i % 2].astype(bf16)
            if i + 2 < 4 * (3 + plan.n_mlp):
                in_load(i + 2).start()

    def round_down():
        for i in range(4 * (1 + plan.n_mlp)):
            down_load(i).wait()
            wd[me, i * some_cols : (i + 1) * some_cols, :] = tall_block[i % 2].astype(bf16)
            if i + 2 < 4 * (1 + plan.n_mlp):
                down_load(i + 2).start()

    strip_rows = min(32, rows)
    strip_count = rows // strip_rows

    def row_load(j):
        source = x_in if j < strip_count else out_grad_in
        first = j % strip_count * strip_rows
        return pltpu.make_async_copy(
            source.at[pl.ds(first, strip_rows), :], wide.at[j % 2], own_sem.at[j % 2]
        )

    row_load(0).start()
    row_load(1).start()
    small_load.start()
    in_load(0).start()
    in_load(1).start()
    down_load(0).start()
    down_load(1).start()
    table_loads = [
        pltpu.make_async_copy(place_cos, own, own_sem.at[3]), pltpu.make_async_copy(place_sin, ahead, own_sem.at[4])
    ]
    for load in table_loads:
        load.start()
    barrier = pltpu.get_barrier_semaphore()
    for b in [1] + plan.bits if n > 1 else []:
        pl.semaphore_signal(barrier, inc=1, device_id={"dp": owner(b)}, device_id_type=pl.DeviceIdType.MESH)

    @pl.when(place < line - 1)
    def _():
        pl.semaphore_signal(barrier, inc=1, device_id={"tensor": place + 1}, device_id_type=pl.DeviceIdType.MESH)

    @pl.when(place > 0)
    def _():
        pl.semaphore_signal(barrier, inc=1, device_id={"tensor": place - 1}, device_id_type=pl.DeviceIdType.MESH)

    beside = (place + line - 1) // line + (2 * line - 2 - place) // line
    pl.semaphore_wait(barrier, (1 + len(plan.bits) if n > 1 else 0) + beside)

    def normalize_rows(index):
        at = span(index)
        for o in range(n):
            gain, shift = small[o, 0:1, LANES:].astype(f32), small[o, 1:2, LANES:].astype(f32)
            ns[:, o * width : (o + 1) * width] = (xs[o, at, :].astype(f32) * gain + shift).astype(bf16)

    def bias_row(r, first, width):
        per = LANES // plan.bias_cols
        groups = []
        for g in range(first // LANES, (first + width) // LANES):
            total = small[g * per, r : r + 1, :LANES].astype(f32)
            for o in range(1, per):
                total = total + small[g * per + o, r : r + 1, :LANES].astype(f32)
            groups.append(total)
        return jnp.concatenate(groups, axis=1)

    def attn_rows(index):
        at = span(index)
        normalize_rows(index)
        for r, target in enumerate((q, k, v)):
            proj = dot_n(ns[...], wa[:, r * local : (r + 1) * local]) + bias_row(r, 0, local)
            if r == 2:
                target[at, :] = proj.astype(bf16)
            else:
                for g in range(0, local, LANES):
                    target[at, g : g + LANES] = turn(
                        proj[:, g : g + LANES], own[at, :], ahead[at, :], behind[at, :], 1.0
                    ).astype(bf16)

    def mlp_rows(index):
        at = span(index)
        normalize_rows(index)
        for r in range(plan.n_mlp):
            cols = slice(r * local, (r + 1) * local)
            pre = dot_n(ns[...], wm[:, cols]) + bias_row(3 + r, 0, local)
            value, grad = gelu_and_slope(pre)
            hidden[at, cols] = value.astype(bf16)
            slope[at, cols] = grad.astype(bf16)

    def attend(pair, carry):
        total = plan.group
        block = min(QUERY_ROWS, total)
        lanes = pl.ds(pl.multiple_of(pair * LANES, LANES), LANES)
        for start in range(0, total, block):
            stop = start + block
            here = pl.ds(start, block)
            allowed = attend_mask(begins_of(lengths, start, block), start, block, stop)
            query = q[here, lanes]
            results, logs = [], []
            for head in range(LANES // HEAD):
                mine = head_lanes(block, head)
                chosen = jnp.where(mine, query, jnp.zeros_like(query)) * HEAD ** (-0.5)
                scores = jnp.where(allowed, dot_t(chosen.astype(bf16), k[:stop, lanes]), masked_score)
                top = jnp.max(scores, axis=1, keepdims=True)
                weights = jnp.exp(scores - top)
                total_weight = jnp.sum(weights, axis=1, keepdims=True)
                results.append(dot_n(weights.astype(bf16), v[:stop, lanes]) / total_weight)
                logs.append(top + jnp.log(total_weight))
            first = head_lanes(block, 0)
            att[here, lanes] = jnp.where(first, results[0], results[1]).astype(bf16)
            which = lax.broadcasted_iota(jnp.int32, (block, LANES), 1)
            held = lse[here, :]
            for head in range(LANES // HEAD):
                held = jnp.where(which == pair * (LANES // HEAD) + head, logs[head], held)
            lse[here, :] = held
        return carry

    tall = min(512, plan.group)

    def out_tile(t):
        def part(j, carry):
            at = pl.ds(pl.multiple_of(j * tall, tall), tall)
            total = dot_n(att[at, :], wd[t, :local, :]) + dot_n(hidden[at, :], wd[t, local:, :])
            xs[t, at, :] = total.astype(bf16)
            return carry

        lax.fori_loop(0, plan.group // tall, part, 0)

    def tile_source(t, index):
        return xs.at[t, span(index), :]

    def tile_landing(t, slot):
        return land.at[t, slot]

    out_sum = LineSum(
        place, line, tile_source, tile_landing, (sum_up_send, sum_up_recv, sum_down_send, sum_down_recv)
    )

    def all_tiles(fn):
        lax.fori_loop(0, plan.d_tiles, lambda t, carry: (fn(t), carry)[1], 0)

    def back_rows(index):
        at = span(index)
        for o in range(n):
            sums[0:1, o * width : (o + 1) * width] += jnp.sum(cs[o, at, :].astype(f32), axis=0, keepdims=True)
        for r in range(1 + plan.n_mlp):
            grad = dot_t(cs[0, at, :], wd[0, r * local : (r + 1) * local, :])
            for o in range(1, n):
                grad = grad + dot_t(cs[o, at, :], wd[o, r * local : (r + 1) * local, :])
            if r == 0:
                att[at, :] = grad.astype(bf16)
            else:
                cols = slice((r - 1) * local, r * local)
                slope[at, cols] = (grad * slope[at, cols].astype(f32)).astype(bf16)

    def attend_back(pair, carry):
        block = min(QUERY_ROWS, plan.group)
        scale = HEAD ** (-0.5)
        k_sum[...] = jnp.zeros_like(k_sum)
        v_sum[...] = jnp.zeros_like(v_sum)
        lanes = pl.ds(pl.multiple_of(pair * LANES, LANES), LANES)
        which = lax.broadcasted_iota(jnp.int32, (block, LANES), 1)
        for start in range(0, plan.group, block):
            stop = start + block
            here = pl.ds(start, block)
            allowed = attend_mask(begins_of(lengths, start, block), start, block, stop)
            q_sum = jnp.zeros((block, LANES), f32)
            for head in range(LANES // HEAD):
                mine = head_lanes(block, head)
                query = jnp.where(mine, q[here, lanes], jnp.zeros((block, LANES), bf16)) * scale
                query = query.astype(bf16)
                cot = jnp.where(mine, att[here, lanes], jnp.zeros((block, LANES), bf16))
                level = jnp.sum(
                    jnp.where(which == pair * (LANES // HEAD) + head, lse[here, :], 0.0), axis=1, keepdims=True
                )
                scores = dot_t(query, k[:stop, lanes]) - level
                probs = jnp.where(allowed, jnp.exp(scores), 0.0)
                prob_grad = dot_t(cot, v[:stop, lanes])
                mean = jnp.sum(probs * prob_grad, axis=1, keepdims=True)
                score_grad = (probs * (prob_grad - mean)).astype(bf16)
                q_step = dot_n(score_grad, k[:stop, lanes])
                q_sum = jnp.where(mine, q_step * scale, q_sum)
                k_sum[:stop, :] += dot_s(score_grad, query)
                v_sum[:stop, :] += dot_s(probs.astype(bf16), cot)
            q[here, lanes] = turn(
                q_sum, own[here, :], ahead[here, :], behind[here, :], -1.0
            ).astype(bf16)
        k[:, lanes] = turn(k_sum[...], own[...], ahead[...], behind[...], -1.0).astype(bf16)
        v[:, lanes] = v_sum[...].astype(bf16)
        return carry

    def dh_tile(t):
        at = pl.ds(pl.multiple_of(t * width, width), width)
        total = dot_t(slope[...], wm[at, :])
        for r, grad in enumerate((q, k, v)):
            total = total + dot_t(grad[...], wa[at, r * local : (r + 1) * local])
        cs[t] = total.astype(bf16)

    def normalize_own():
        for j in range(strip_count):
            row_load(j).wait()
            at = slice(j * strip_rows, (j + 1) * strip_rows)
            value = wide[j % 2]
            mean = jnp.mean(value, axis=1, keepdims=True)
            centered = value - mean
            scale = lax.rsqrt(jnp.mean(centered * centered, axis=1, keepdims=True) + norm_eps)
            normed = (centered * scale).astype(bf16)
            to = pl.ds(pl.multiple_of(place * rows + j * strip_rows, strip_rows), strip_rows)
            for o in range(n):
                xs[o, to, :] = normed[:, o * width : (o + 1) * width]
            stats[0, at, :] = jnp.broadcast_to(mean, (strip_rows, LANES))
            stats[1, at, :] = jnp.broadcast_to(scale, (strip_rows, LANES))
            if j + 2 < 2 * strip_count:
                row_load(j + 2).start()

    def mask_cot():
        for j in range(strip_count, 2 * strip_count):
            row_load(j).wait()
            first = place * rows + (j - strip_count) * strip_rows
            places = first + lax.broadcasted_iota(jnp.int32, (strip_rows, 1), 0)
            masked = jnp.where(places < ends_of(lengths)[-1], wide[j % 2], 0.0).astype(bf16)
            to = pl.ds(pl.multiple_of(first, strip_rows), strip_rows)
            for o in range(n):
                cs[o, to, :] = masked[:, o * width : (o + 1) * width]
            if j + 2 < 2 * strip_count:
                row_load(j + 2).start()

    def make_tables():
        for load in table_loads:
            load.wait()
        block_rows = min(QUERY_ROWS, plan.group)
        ends = ends_of(lengths)
        at_ends = [pl.ds(jnp.minimum(end, plan.group - 1), 1) for end in ends]
        cosines, sines = [own[row, :] for row in at_ends], [ahead[row, :] for row in at_ends]
        for start in range(0, plan.group, block_rows):
            at = pl.ds(start, block_rows)
            places = start + lax.broadcasted_iota(jnp.int32, (block_rows, LANES), 0)
            begin_cos, begin_sin = cosines[0], sines[0]
            for end, end_cos, end_sin in zip(ends[1:], cosines[1:], sines[1:]):
                begin_cos = jnp.where(places >= end, end_cos, begin_cos)
                begin_sin = jnp.where(places >= end, end_sin, begin_sin)
            place_c, place_s = own[at, :], ahead[at, :]
            cosine = place_c * begin_cos + place_s * begin_sin
            sine = place_s * begin_cos - place_c * begin_sin
            lane = lax.rem(lax.broadcasted_iota(jnp.int32, (block_rows, LANES), 1), HEAD)
            own[at, :] = jnp.where(lane < ROT, cosine, 1.0)
            ahead[at, :] = jnp.where(lane < ROT // 2, -sine, 0.0)
            behind[at, :] = jnp.where((lane >= ROT // 2) & (lane < ROT), sine, 0.0)

    def mixed_copy(t):
        cols = pl.ds(pl.multiple_of(t * width, width), width)
        return pltpu.make_async_copy(mixed.at[lax.rem(t, 2)], mixed_out.at[:, cols], mixed_sem.at[lax.rem(t, 2)])

    def finish_tile(t):
        @pl.when(t >= 2)
        def _():
            mixed_copy(t - 2).wait()
        out_sum.last(t, mixed.at[lax.rem(t, 2)])
        mixed_copy(t).start()

    small_load.wait()
    w_start(3)
    round_in(0, 3, wa)
    w_start(0)
    normalize_own()
    z_start(0, 1)
    round_in(3, 3 + plan.n_mlp, wm)
    mask_cot()
    round_down()
    make_tables()
    sums[...] = jnp.zeros_like(sums)
    lse[...] = jnp.zeros_like(lse)
    write(13)
    w_arrive(0, plan.single)
    w_start(1)
    w_arrive(3, plan.single)
    z_arrive(0, 1)
    cot_start(1)
    w_arrive(3, plan.several)
    w_arrive(0, plan.several)
    w_arrive(3, plan.odd)
    w_arrive(0, plan.odd)
    write(0, 2)
    at_distance(0, attn_rows)
    if line > 2:
        at_distance(1, attn_rows)
    w_arrive(1, plan.single)
    w_start(2)
    for step in range(2, line - 1):
        z_arrive(0, step)
        cot_start(step)
        at_distance(step, attn_rows)
    w_arrive(1, plan.several)
    w_arrive(1, plan.odd)
    write(1)
    near = max(line - 2, 0)
    lax.fori_loop(
        jnp.maximum(place - near, 0), jnp.minimum(place + near, line - 1) + 1,
        lambda c, carry: (mlp_rows(c), carry)[1], 0,
    )
    if line > 2:
        z_arrive(0, line - 1)
        cot_start(line - 1)
    at_distance(line - 1, lambda c: (attn_rows(c), mlp_rows(c))[0])
    write(3, 10)
    pairs = local // LANES
    lax.fori_loop(0, pairs // 2, attend, 0)
    w_arrive(2, plan.single)
    lax.fori_loop(pairs // 2, pairs, attend, 0)
    write(9)
    z_arrive(1, 1)
    w_arrive(2, plan.several)
    out_copy(3).wait()
    for step in range(1, line):
        for up in (True, False):
            left = place != step - 1 if up else place != line - step
            @pl.when(left & sends(step, up))
            def _():
                z_copy(0, step, up).wait_send()
    w_arrive(2, plan.odd)

    def first_tile(t):
        out_tile(t)
        out_sum.first(t)

    all_tiles(first_tile)
    out_copy(9).wait()
    at_distance(0, back_rows)
    if line > 2:
        at_distance(1, back_rows)
    for step in range(2, line - 1):
        z_arrive(1, step)
        at_distance(step, back_rows)

    def running(near_end):
        for up in (True, False):
            now = (place < line // 2) if up == near_end else (place >= line // 2)

            @pl.when(now)
            def _():
                for step in range(1, line):
                    z_sent(1, step, up)
                all_tiles(lambda t: out_sum.hand_on(t, up))

    running(True)
    if line > 2:
        z_arrive(1, line - 1)
    running(False)
    at_distance(line - 1, back_rows)
    write(4, 5, 11)
    lax.fori_loop(0, pairs, attend_back, 0)
    write(6, 7, 8)
    out_copy(5).wait()
    all_tiles(dh_tile)
    write(12)
    all_tiles(finish_tile)
    for t in range(max(plan.d_tiles - 2, 0), plan.d_tiles):
        mixed_copy(t).wait()

    all_tiles(out_sum.sent)
    for flow in range(4):
        for mask in range(1, n):
            for half in halves(flow):
                w_copy(flow, mask, half).wait_send()
    for j in range(len(outs)):
        if j not in (3, 5, 9):
            out_copy(j).wait()


def forward(plan, x, out_grad, w, wd, small, lengths):
    any_space = pl.BlockSpec(memory_space=pl.ANY)
    n, line, group, model, local, rows = (
        plan.n_dp, plan.n_line, plan.group, plan.model, plan.local, plan.rows
    )
    low = lambda *shape: jax.ShapeDtypeStruct(shape, bf16)
    full = lambda *shape: jax.ShapeDtypeStruct(shape, f32)
    out_shape = [
        low(model, plan.attn), low(model, plan.mlp), low(n, 16, LANES + plan.out_cols),
        low(n, group, plan.width), full(8, model), low(n, group, plan.width),
        low(group, local), low(group, local), low(group, local), low(group, local),
        low(group, plan.mlp), low(group, plan.mlp), low(n, group, plan.width), full(2, rows, LANES),
        full(rows, model),
    ]
    scratch = lambda s: pltpu.VMEM(s.shape, s.dtype)
    dma = pltpu.SemaphoreType.DMA
    return pl.pallas_call(
        partial(forward_kernel, plan),
        in_specs=[any_space] * 5 + [pl.BlockSpec(memory_space=pltpu.SMEM)] + [any_space] * 2,
        out_specs=[any_space] * 15,
        out_shape=out_shape,
        scratch_shapes=[scratch(s) for s in out_shape[:2]]
        + [pltpu.VMEM((n, plan.down, plan.out_cols), bf16)]
        + [scratch(s) for s in out_shape[2:4]]
        + [pltpu.VMEM((rows, model), bf16)]
        + [scratch(s) for s in out_shape[4:10]]
        + [pltpu.VMEM((group, LANES), f32)]
        + [scratch(s) for s in out_shape[10:12]]
        + [pltpu.VMEM((group, LANES), f32)] * 5
        + [scratch(out_shape[13])]
        + [pltpu.VMEM((plan.d_tiles, line + 1, rows, plan.width), bf16)]
        + [
            pltpu.VMEM((2, min(32, rows), model), f32), pltpu.VMEM((2, rows, plan.width), f32),
            pltpu.VMEM((2, plan.in_rows // 4, local), f32), pltpu.VMEM((2, local // 4, plan.out_cols), f32),
        ]
        + [dma((2,)), dma((5,)), dma((2, 2)), dma((14,)), dma((8 * n,)), dma((8 * n,))]
        + [dma((2 * line,))] * 4
        + [dma((plan.d_tiles, line + 1))] * 4,
        compiler_params=pltpu.CompilerParams(
            collective_id=0, has_side_effects=True, vmem_limit_bytes=63 << 20
        ),
        cost_estimate=pl.CostEstimate(flops=60 * 10**9, bytes_accessed=80 << 20, transcendentals=0),
    )(x, out_grad, w, wd, small, lengths, *angle_tables(group))


def backward_kernel(
    plan,
    xhat_in, cot_in, att_in, hidden_in, da_in, q_in, k_in, v_in, dh_in, wa_in, wm_in, sums_in,
    down_out, in_out, small_out, rows_out, dh_out,
    turned, stage, og, da, qkv, dh, sent, core_in, held, cube_in, land,
    w_own, fin, fin_turned, dh_fin, small, small_in, shares,
    load_sem, stage_sem, fin_sem, dh_sem, core_send, core_recv, cube_send, cube_recv,
    up_send, up_recv, down_send, down_recv,
    small_send, small_recv, share_send, share_recv, credit,
):
    n, line = plan.n_dp, plan.n_line
    me, place = lax.axis_index("dp"), lax.axis_index("tensor")
    rows, local, group, model, in_rows = plan.rows, plan.local, plan.group, plan.model, plan.in_rows
    MESH = pl.DeviceIdType.MESH
    half_rows, pairs_n, n_bits = in_rows // 2, n // 2, len(plan.bits)
    orders = (plan.bits, plan.bits[::-1])
    n_down, n_mlp = 1 + plan.n_mlp, plan.n_mlp
    flows = {"down": (n_down, 0, 0), "mlp": (n_mlp, n_down, 3), "attn": (3, 0, 0)}

    def owner(mask):
        index = me
        for b in [1] + plan.bits:
            if mask & b:
                index = index + b - 2 * b * lax.rem(index // b, 2)
        return index

    def peer(bit):
        return {"dp": owner(bit)}

    def position(mask, order):
        return sum((1 if mask & b else 0) << (n_bits - 1 - p) for p, b in enumerate(order))

    width, d_tiles = plan.width, plan.d_tiles
    sub = local // width
    own_rows = pl.ds(pl.multiple_of(me * in_rows, in_rows), in_rows)

    def strip(source, j):
        return source.at[:, pl.ds(j * width, width)]

    whole = [
        (da_in, da),
        (q_in, qkv.at[:, pl.ds(0, local)]),
        (k_in, qkv.at[:, pl.ds(local, local)]),
        (v_in, qkv.at[:, pl.ds(2 * local, local)]),
        (dh_in, dh),
        (wa_in.at[own_rows, :], w_own.at[:, pl.ds(0, plan.attn)]),
        (wm_in.at[own_rows, :], w_own.at[:, pl.ds(plan.attn, plan.mlp)]),
    ]
    whole = whole + [
        (strip(att_in, j) if j < sub else strip(hidden_in, j - sub), og.at[j]) for j in range(n_down * sub)
    ]
    strips = range(7, len(whole))
    for j, (a, b) in enumerate(whole):
        pltpu.make_async_copy(a, b, load_sem.at[j]).start()

    def loaded(*which):
        for j in which:
            pltpu.make_async_copy(whole[j][0], whole[j][1], load_sem.at[j]).wait()

    barrier = pltpu.get_barrier_semaphore()
    for b in [1] + plan.bits:
        pl.semaphore_signal(barrier, inc=1, device_id=peer(b), device_id_type=MESH)
    for d in range(1, line):
        pl.semaphore_signal(
            barrier, inc=1, device_id={"tensor": lax.rem(place + d, line)}, device_id_type=MESH
        )

    def share_copy(d, arriving):
        source = lax.rem(place + line - d, line) if arriving else place
        return pltpu.make_async_remote_copy(
            src_ref=shares, dst_ref=rows_out.at[source],
            send_sem=share_send.at[d], recv_sem=share_recv.at[d],
            device_id={"tensor": lax.rem(place + d, line)}, device_id_type=MESH,
        )

    share_own = pltpu.make_async_copy(shares, rows_out.at[place], share_send.at[0])

    def turn_columns(source, masks):
        def fetch(j):
            return pltpu.make_async_copy(source.at[owner(masks[j])], stage.at[j % 2], stage_sem.at[j % 2])

        fetch(0).start()
        for j in range(len(masks)):
            if j + 1 < len(masks):
                fetch(j + 1).start()
            fetch(j).wait()
            turned[pl.ds(j * in_rows, in_rows), :] = stage[j % 2].T

    def core_copy(name, t):
        return pltpu.make_async_remote_copy(
            src_ref=sent.at[lax.rem(t, 2)], dst_ref=core_in.at[t],
            send_sem=core_send.at[lax.rem(t, 2)], recv_sem=core_recv.at[t],
            device_id=peer(1), device_id_type=MESH,
        )

    def cube_copy(slot, half, phase):
        count = pairs_n >> (phase + 1)
        first = pairs_n - 2 * count
        at = half * n_bits + phase
        return pltpu.make_async_remote_copy(
            src_ref=held.at[slot, half, pl.ds(count, count)],
            dst_ref=cube_in.at[slot, half, pl.ds(first, count)],
            send_sem=cube_send.at[slot, at], recv_sem=cube_recv.at[slot, at],
            device_id=peer(orders[half][phase]), device_id_type=MESH,
        )

    def product(name, at, count, t):
        if name == "down":
            return [dot_n(turned[at : at + count, :], og[t * sub + j]) for j in range(sub)]
        source = da if name == "mlp" else qkv
        return [dot_n(turned[at : at + count, :], source[:, pl.ds(pl.multiple_of(t * local, local), local)])]

    piece = min(2, pairs_n) * in_rows

    def send_core(name, t):
        @pl.when(t >= 2)
        def _():
            core_copy(name, t - 2).wait_send()
        for at in range(0, pairs_n * in_rows, piece):
            strips_of = product(name, at, piece, t)
            step = local // len(strips_of)
            for j, value in enumerate(strips_of):
                sent[lax.rem(t, 2), at : at + piece, j * step : (j + 1) * step] = value.astype(bf16)
        core_copy(name, t).start()

    def keep_core(name, t):
        base = flows[name][1]
        core_copy(name, t).wait_recv()
        for first in range(0, pairs_n * in_rows, piece):
            strips_of = product(name, pairs_n * in_rows + first, piece, t)
            step = local // len(strips_of)
            for i, value in enumerate(strips_of):
                cols = slice(i * step, (i + 1) * step)
                total = value + core_in[t, first : first + piece, cols].astype(f32)
                for at in range(0, piece, half_rows):
                    j, half = divmod((first + at) // half_rows, 2)
                    held[base + t, half, position(2 * j, orders[half]), :, cols] = total[at : at + half_rows].astype(bf16)
        for half in range(2):
            if n_bits:
                cube_copy(base + t, half, 0).start()

    def scatter(name):
        tiles_n = flows[name][0]
        if name != "down":
            pl.semaphore_wait(credit.at[0], 1)
        if name == "attn":
            pl.semaphore_wait(credit.at[1], n_bits)

        def step(t, carry):
            @pl.when(t < tiles_n)
            def _():
                send_core(name, t)

            @pl.when(t >= 1)
            def _():
                keep_core(name, t - 1)
            return carry

        lax.fori_loop(0, tiles_n + 1, step, 0)
        for t in range(max(tiles_n - 2, 0), tiles_n):
            core_copy(name, t).wait_send()
        if name != "attn":
            pl.semaphore_signal(credit.at[0], inc=1, device_id=peer(1), device_id_type=MESH)

    def cube_step(name, phase):
        tiles, base, result = flows[name]
        count = pairs_n >> (phase + 1)
        first = pairs_n - 2 * count
        target, depth = (down_out, 1) if name == "down" else (in_out, 2)

        def fin_copy(t):
            source = fin_turned if name == "down" else fin.at[lax.rem(t, 2)]
            return pltpu.make_async_copy(source, target.at[result + t], fin_sem.at[lax.rem(t, 2)])

        def step(t, carry):
            slot = base + t
            if phase == n_bits - 1:
                @pl.when(t >= depth)
                def _():
                    fin_copy(t - depth).wait()
            for half in range(2):
                cube_copy(slot, half, phase).wait_recv()
                total = (
                    held[slot, half, 0:count].astype(f32)
                    + cube_in[slot, half, first : first + count].astype(f32)
                )
                if phase < n_bits - 1:
                    held[slot, half, 0:count] = total.astype(bf16)
                    cube_copy(slot, half, phase + 1).start()
                else:
                    fin[lax.rem(t, 2), half * half_rows : (half + 1) * half_rows, :] = total[0]
            if phase == n_bits - 1:
                if name == "down":
                    fin_turned[...] = fin[lax.rem(t, 2)].T
                fin_copy(t).start()
                if name != "down":
                    weight = w_own[:, pl.ds(pl.multiple_of((result + t) * local, local), local)].astype(f32)
                    product = weight * fin[lax.rem(t, 2)]
                    extra = weight * small[n_bits + 1, pl.ds(result + t, 1), :]
                    for g in range(0, local, LANES):
                        shares[0] += product[:, g : g + LANES]
                        shares[1] += extra[:, g : g + LANES]
            return carry

        lax.fori_loop(0, tiles, step, 0)
        if phase == n_bits - 1:
            for t in range(max(tiles - depth, 0), tiles):
                fin_copy(t).wait()

    def cube_sent(name):
        tiles, base, _ = flows[name]

        def step(t, carry):
            for half in range(2):
                for phase in range(n_bits):
                    cube_copy(base + t, half, phase).wait_send()
            return carry

        lax.fori_loop(0, tiles, step, 0)

    def tile_of(buffer):
        def source(t, index):
            return buffer.at[t, pl.ds(pl.multiple_of(index * rows, rows), rows), :]
        return source

    dh_sum = LineSum(
        place, line, tile_of(dh), lambda t, slot: land.at[t, slot],
        (up_send, up_recv, down_send, down_recv),
    )
    def sum_copy(target, t):
        cols = pl.ds(pl.multiple_of(t * width, width), width)
        return pltpu.make_async_copy(dh_fin.at[lax.rem(t, 2)], target.at[:, cols], dh_sem.at[lax.rem(t, 2)])

    def finish(flow, target, count):
        def step(t):
            @pl.when(t >= 2)
            def _():
                sum_copy(target, t - 2).wait()
            flow.last(t, dh_fin.at[lax.rem(t, 2)])
            sum_copy(target, t).start()

        tiles(0, count, step)
        for t in range(max(count - 2, 0), count):
            sum_copy(target, t).wait()

    def tiles(first, stop, fn):
        lax.fori_loop(first, stop, lambda t, carry: (fn(t), carry)[1], 0)

    def small_copy(j):
        return pltpu.make_async_remote_copy(
            src_ref=small.at[j], dst_ref=small_in.at[j],
            send_sem=small_send.at[j], recv_sem=small_recv.at[j],
            device_id=peer(([1] + plan.bits)[j]), device_id_type=MESH,
        )

    def small_step(j):
        small_copy(j).wait_recv()
        small[j + 1] = small[j] + small_in[j]
        if j < n_bits:
            small_copy(j + 1).start()

    shares[...] = jnp.zeros_like(shares)
    small[0] = jnp.zeros_like(small[0])
    masks = [2 * j + 1 for j in range(pairs_n)] + [2 * j for j in range(pairs_n)]
    pl.semaphore_wait(barrier, 1 + n_bits + line - 1)
    loaded(4)
    tiles(0, d_tiles, dh_sum.first)
    turn_columns(cot_in, masks)
    loaded(*strips)
    scatter("down")
    dh_sum.both_ways(0, d_tiles // 4, d_tiles)
    turn_columns(xhat_in, masks)
    loaded(0, 1, 2, 3)
    scatter("mlp")
    dh_sum.both_ways(d_tiles // 4, d_tiles // 2, d_tiles)
    for r in range(3 + n_mlp):
        block = qkv[:, r * local : (r + 1) * local] if r < 3 else da[:, (r - 3) * local : (r - 2) * local]
        small[0, r : r + 1, :] = jnp.sum(block.astype(f32), axis=0, keepdims=True)
    for r in range(model // local):
        small[0, 8 + r : 9 + r, :] = sums_in[0:1, r * local : (r + 1) * local]
    small_copy(0).start()
    for phase in range(n_bits - 1):
        cube_step("down", phase)
    small_step(0)
    dh_sum.both_ways(d_tiles // 2, 3 * d_tiles // 4, d_tiles)
    small_step(1)
    for phase in range(n_bits - 1):
        cube_step("mlp", phase)
    cube_step("down", n_bits - 1)
    cube_sent("down")
    for b in plan.bits:
        pl.semaphore_signal(credit.at[1], inc=1, device_id=peer(b), device_id_type=MESH)
    scatter("attn")
    for j in range(2, n_bits + 1):
        small_step(j)
    dh_sum.both_ways(3 * d_tiles // 4, d_tiles, d_tiles)
    loaded(5, 6)
    cube_step("mlp", n_bits - 1)
    finish(dh_sum, dh_out, d_tiles)
    for phase in range(n_bits):
        cube_step("attn", phase)
    share_own.start()
    for d in range(1, line):
        share_copy(d, False).start()
    small_done = pltpu.make_async_copy(small.at[n_bits + 1], small_out, load_sem.at[0])
    small_done.start()
    cube_sent("mlp")
    cube_sent("attn")
    tiles(0, d_tiles, dh_sum.sent)
    for j in range(n_bits + 1):
        small_copy(j).wait_send()
    share_own.wait()
    for d in range(1, line):
        share_copy(d, False).wait_send()
        share_copy(d, True).wait_recv()
    small_done.wait()


def backward(plan, xhat, cot, att, hidden, da, q, k, v, dh, wa, wm, sums):
    any_space = pl.BlockSpec(memory_space=pl.ANY)
    vmem = pl.BlockSpec(memory_space=pltpu.VMEM)
    n, line, group, model, local = plan.n_dp, plan.n_line, plan.group, plan.model, plan.local
    rows, in_rows, n_bits, pairs_n = plan.rows, plan.in_rows, len(plan.bits), n // 2
    n_down = 1 + plan.n_mlp
    small_rows = 8 + -(-(model // local) // 8) * 8
    width, d_tiles = plan.width, plan.d_tiles
    low = lambda *shape: pltpu.VMEM(shape, bf16)
    full = lambda *shape: pltpu.VMEM(shape, f32)
    dma = pltpu.SemaphoreType.DMA
    out = lambda dtype, *shape: jax.ShapeDtypeStruct(shape, dtype)
    slots = n_down + plan.n_mlp
    return pl.pallas_call(
        partial(backward_kernel, plan),
        in_specs=[any_space] * 11 + [vmem],
        out_specs=[any_space] * 5,
        out_shape=[
            out(f32, n_down, local, in_rows), out(f32, 3 + plan.n_mlp, in_rows, local),
            out(f32, small_rows, local),
            out(f32, line, 2, in_rows, LANES), out(f32, rows, model),
        ],
        scratch_shapes=[
            low(n * in_rows, group), low(2, group, in_rows),
            low(max(d_tiles, plan.down // width), group, width), low(group, plan.mlp),
            low(group, plan.attn), low(d_tiles, group, width),
            low(2, pairs_n * in_rows, local), low(n_down, pairs_n * in_rows, local),
            low(slots, 2, pairs_n, in_rows // 2, local), low(slots, 2, max(pairs_n - 1, 1), in_rows // 2, local),
            low(d_tiles, line + 1, rows, width),
            low(in_rows, plan.attn + plan.mlp), full(2, in_rows, local), full(local, in_rows), full(2, rows, width),
            full(n_bits + 2, small_rows, local), full(n_bits + 1, small_rows, local), full(2, in_rows, LANES),
            dma((7 + plan.down // width,)), dma((2,)), dma((2,)), dma((2,)), dma((2,)), dma((n_down,)),
            dma((slots, max(2 * n_bits, 1))), dma((slots, max(2 * n_bits, 1))),
            dma((d_tiles, line + 1)), dma((d_tiles, line + 1)), dma((d_tiles, line + 1)), dma((d_tiles, line + 1)),
            dma((n_bits + 1,)), dma((n_bits + 1,)), dma((line,)), dma((line,)),
            pltpu.SemaphoreType.REGULAR((2,)),
        ],
        compiler_params=pltpu.CompilerParams(
            collective_id=1, has_side_effects=True, vmem_limit_bytes=63 << 20
        ),
        cost_estimate=pl.CostEstimate(flops=80 * 10**9, bytes_accessed=80 << 20, transcendentals=0),
    )(xhat, cot, att, hidden, da, q, k, v, dh, wa, wm, sums)


def adam_update(weight, moment_one, moment_two, gradient, step_rate, decay_factor):
    first_new = beta_first * moment_one + (1.0 - beta_first) * gradient
    second_new = beta_second * moment_two + (1.0 - beta_second) * gradient * gradient
    corrected = first_new / (1.0 - beta_first**STEP)
    spread = jnp.sqrt(second_new / (1.0 - beta_second**STEP))
    return (
        weight - step_rate * (corrected / (spread + adam_eps) + decay_factor * weight),
        first_new,
        second_new,
    )


def per_device(
    block_input,
    out_grad,
    seq_lengths,
    in_weight,
    down_weight,
    column_bias,
    vector_params,
    in_first,
    in_second,
    down_first,
    down_second,
    bias_first,
    bias_second,
    vector_first,
    vector_second,
):
    n_dp = lax.axis_size("dp")
    n_tensor = lax.axis_size("tensor")
    own_rows, model = block_input.shape
    group = own_rows * n_tensor
    in_rows, widths, local = in_weight.shape
    out_cols = down_weight.shape[2]
    n_mlp = widths - 3
    attn_width, mlp_width = 3 * local, n_mlp * local

    me = lax.axis_index("dp")
    plan = Plan(n_dp, n_tensor, own_rows, model, in_rows, local, n_mlp, out_cols)
    share = LANES // plan.bias_cols
    lane = lax.broadcasted_iota(jnp.int32, (widths, LANES), 1) // plan.bias_cols
    bias_tile = jnp.where(lane == lax.rem(me, share), jnp.tile(column_bias, (1, share)), 0.0)
    small = jnp.concatenate(
        [jnp.pad(bias_tile, ((0, 16 - widths), (0, 0))), jnp.pad(vector_params, ((0, 13), (0, 0)))], axis=1
    ).astype(bf16)
    (
        w_attn, w_mlp, vectors, xhat_all, cot_sums, cot_all, q_grad, k_grad, v_grad, attended,
        hidden, pre_grad, dh_part, stats, mixed,
    ) = forward(plan, block_input, out_grad, in_weight.transpose(1, 0, 2), down_weight, small, seq_lengths)
    down_grad, in_grad, small_grad, shares, dh = backward(
        plan, xhat_all, cot_all, attended, hidden, pre_grad, q_grad, k_grad, v_grad, dh_part,
        w_attn, w_mlp, cot_sums,
    )
    vector_vals = vectors[:, :3, LANES:].transpose(1, 0, 2).reshape(3, model).astype(f32)
    gain, out_bias = vector_vals[0], vector_vals[2]
    block_out = block_input + (mixed + out_bias)
    mean, inv_scale = stats[0, :, :1], stats[1, :, :1]
    xhat = (block_input - mean) * inv_scale
    places = lax.axis_index("tensor") * own_rows + lax.broadcasted_iota(jnp.int32, (own_rows, 1), 0)
    cot_live = jnp.where(places < jnp.sum(seq_lengths), out_grad, 0.0)

    dxhat = dh * gain
    input_grad = cot_live + inv_scale * (
        dxhat
        - jnp.mean(dxhat, axis=-1, keepdims=True)
        - xhat * jnp.mean(dxhat * xhat, axis=-1, keepdims=True)
    )

    bias_full = small_grad[:widths]
    own_vectors = vector_params.astype(bf16).astype(f32)
    in_reduced = (
        in_grad * own_vectors[0][None, :, None] + own_vectors[1][None, :, None] * bias_full[:, None, :]
    ).transpose(1, 0, 2)
    down_reduced = down_grad
    bias_reduced = lax.dynamic_slice_in_dim(bias_full, me * plan.bias_cols, plan.bias_cols, 1)
    out_sums = small_grad[8 : 8 + model // local].reshape(-1)
    vector_reduced = jnp.stack(
        [
            jnp.sum(shares[:, 0], axis=(0, 2)),
            jnp.sum(shares[:, 1], axis=(0, 2)),
            lax.dynamic_slice_in_dim(out_sums, me * out_cols, out_cols, 0),
        ]
    )

    in_new, in_one, in_two = adam_update(
        in_weight, in_first, in_second, in_reduced, rate_in, weight_decay
    )
    down_new, down_one, down_two = adam_update(
        down_weight, down_first, down_second, down_reduced, rate_down, weight_decay
    )
    bias_new, bias_one, bias_two = adam_update(
        column_bias, bias_first, bias_second, bias_reduced, rate_vector, 0.0
    )
    vector_new, vector_one, vector_two = adam_update(
        vector_params, vector_first, vector_second, vector_reduced, rate_vector, 0.0
    )
    return (
        block_out,
        input_grad,
        in_new,
        in_one,
        in_two,
        down_new,
        down_one,
        down_two,
        bias_new,
        bias_one,
        bias_two,
        vector_new,
        vector_one,
        vector_two,
    )


def widths_down(down_weight):
    return down_weight.shape[0] * down_weight.shape[1]


def solution(mesh):
    return jax.shard_map(
        per_device,
        mesh=mesh,
        in_specs=(
            P(("dp", "tensor"), None),
            P(("dp", "tensor"), None),
            P("dp", None),
            P("dp", None, "tensor"),
            P(None, "tensor", "dp"),
            P(None, ("tensor", "dp")),
            P(None, "dp"),
            P("dp", None, "tensor"),
            P("dp", None, "tensor"),
            P(None, "tensor", "dp"),
            P(None, "tensor", "dp"),
            P(None, ("tensor", "dp")),
            P(None, ("tensor", "dp")),
            P(None, "dp"),
            P(None, "dp"),
        ),
        out_specs=(
            P(("dp", "tensor"), None),
            P(("dp", "tensor"), None),
            P("dp", None, "tensor"),
            P("dp", None, "tensor"),
            P("dp", None, "tensor"),
            P(None, "tensor", "dp"),
            P(None, "tensor", "dp"),
            P(None, "tensor", "dp"),
            P(None, ("tensor", "dp")),
            P(None, ("tensor", "dp")),
            P(None, ("tensor", "dp")),
            P(None, "dp"),
            P(None, "dp"),
            P(None, "dp"),
        ),
        check_vma=False,
    )
```

```python
from functools import partial

import jax
import jax.numpy as jnp
import numpy as np
from jax import lax
from jax.experimental import pallas as pl
from jax.experimental.pallas import tpu as pltpu
from jax.sharding import PartitionSpec as P

HEAD = 64
ROT = 32
STEP = 8
LANES = 128
QUERY_ROWS = 256

norm_eps = 1e-05
beta_first = 0.9
beta_second = 0.95
adam_eps = 1e-08
masked_score = -1000000000.0
rate_in = 0.02
rate_down = 0.05
rate_vector = 0.2
weight_decay = 0.1

bf16 = jnp.bfloat16
f32 = jnp.float32


def angle_tables(rows):
    half_rot = ROT // 2
    frequency = 10000.0 ** (-2.0 * (np.arange(LANES) % half_rot) / ROT)
    angles = np.arange(rows)[:, None] * frequency[None, :]
    return np.cos(angles).astype(np.float32), np.sin(angles).astype(np.float32)


def ends_of(lengths):
    ends = [jnp.int32(0)]
    for j in range(lengths.shape[1]):
        ends.append(ends[-1] + lengths[0, j])
    return ends


def begins_of(lengths, start, rows):
    places = start + lax.broadcasted_iota(jnp.int32, (rows, 1), 0)
    begin = jnp.zeros((rows, 1), jnp.int32)
    for end in ends_of(lengths)[1:]:
        begin = jnp.where(places >= end, end, begin)
    return begin


def attend_mask(begin, row_start, rows, stop):
    key_place = lax.broadcasted_iota(jnp.int32, (rows, stop), 1)
    query_place = row_start + lax.broadcasted_iota(jnp.int32, (rows, stop), 0)
    return (key_place <= query_place) & (key_place >= begin)


def head_lanes(rows, head):
    lane = lax.broadcasted_iota(jnp.int32, (rows, LANES), 1)
    return (lane >= head * HEAD) & (lane < (head + 1) * HEAD)


def dot_t(a, b):
    return lax.dot_general(a, b, (((1,), (1,)), ((), ())), preferred_element_type=f32)


def dot_n(a, b):
    return lax.dot_general(a, b, (((1,), (0,)), ((), ())), preferred_element_type=f32)


def dot_s(a, b):
    return lax.dot_general(a, b, (((0,), (0,)), ((), ())), preferred_element_type=f32)


def turn(x, own, sines, sign):
    half = ROT // 2
    lane = lax.rem(lax.broadcasted_iota(jnp.int32, x.shape, 1), HEAD)
    other = jnp.where(lane < half, pltpu.roll(x, LANES - half, 1), pltpu.roll(x, half, 1))
    return x * own + sign * (other * sines)


def low_bit(mask):
    return mask & -mask


def high_bit(mask):
    return 1 << (mask.bit_length() - 1)


def gelu_and_slope(a):
    root = (2.0 / 3.141592653589793) ** 0.5
    square = a * a
    t = jnp.tanh(root * a * (1.0 + 0.044715 * square))
    half = 0.5 * (1.0 + t)
    return a * half, half + 0.5 * a * (1.0 - t * t) * (root * (1.0 + 3.0 * 0.044715 * square))


class LineSum:
    def __init__(self, place, line, source, landing, sems):
        self.place, self.line, self.source, self.landing = place, line, source, landing
        self.up_send, self.up_recv, self.down_send, self.down_recv = sems

    def copy(self, t, index, up, arriving=False):
        place = self.place
        slot = self.slot(index, up)
        return pltpu.make_async_remote_copy(
            src_ref=self.source(t, index),
            dst_ref=self.landing(t, slot),
            send_sem=(self.up_send if up else self.down_send).at[t, slot],
            recv_sem=(self.up_recv if up else self.down_recv).at[t, slot],
            device_id={"tensor": place + 1 if up != arriving else place - 1},
            device_id_type=pl.DeviceIdType.MESH,
        )

    def got(self, t, index, up):
        return self.landing(t, self.slot(index, up))[...].astype(f32)

    def slot(self, index, up):
        return index - 1 if up else lax.rem(self.line - 1 + index, self.line + 1)

    def first(self, t):
        for up in (True, False):
            @pl.when((self.place == 0) if up else (self.place == self.line - 1))
            def _():
                for step in range(self.line - 1):
                    self.copy(t, self.line - 1 - step if up else step, up).start()

    def hand_on(self, t, up):
        place, line = self.place, self.line
        for step in range(line - 1):
            index = line - 1 - step if up else step
            hears = (place > 0) & (place < index) if up else (place < line - 1) & (place > index)

            @pl.when(hears)
            def _():
                self.copy(t, index, up, True).wait_recv()
                mine = self.source(t, index)
                mine[...] = (mine[...].astype(f32) + self.got(t, index, up)).astype(bf16)
                self.copy(t, index, up).start()

    def one_way(self, first, stop, near):
        def step(t, carry):
            for up in (True, False):
                far = 2 * self.place // self.line
                late = far if up else 1 - far

                @pl.when(late == (0 if near else 1))
                def _():
                    self.hand_on(t, up)
            return carry

        lax.fori_loop(first, stop, step, 0)

    def last(self, t, target):
        place, line = self.place, self.line
        target[...] = self.source(t, place)[...].astype(f32)
        for up in (True, False):
            @pl.when((place > 0) if up else (place < line - 1))
            def _():
                self.copy(t, place, up, True).wait_recv()
                target[...] += self.got(t, place, up)

    def sent(self, t):
        for index in range(self.line):
            for up in (True, False):
                @pl.when((self.place < index) if up else (self.place > index))
                def _():
                    self.copy(t, index, up).wait_send()


class Plan:
    def __init__(self, n_dp, n_line, rows, model, in_rows, local, n_mlp, out_cols):
        self.n_dp, self.n_line = n_dp, n_line
        self.rows, self.model = rows, model
        self.group = rows * n_line
        self.in_rows, self.local, self.n_mlp, self.out_cols = in_rows, local, n_mlp, out_cols
        self.attn, self.mlp = 3 * local, n_mlp * local
        self.down = (1 + n_mlp) * local
        self.bias_cols = local // n_dp
        self.width = out_cols
        self.d_tiles = model // out_cols
        self.bits = [1 << b for b in range(1, n_dp.bit_length() - 1)]
        even = range(2, n_dp, 2)
        self.single = [m for m in even if m.bit_count() == 1]
        self.several = sorted((m for m in even if m.bit_count() > 1), key=lambda m: m.bit_count())
        self.odd = list(range(1, n_dp, 2))

    def hop(self, mask, half):
        if mask & 1:
            return 1
        return high_bit(mask) if half == 0 else low_bit(mask)

    def onward(self, mask, half):
        if mask & 1:
            return []
        masks = [mask | 1] if self.n_dp > 1 else []
        return masks + [
            mask | b for b in self.bits if not mask & b and self.hop(mask | b, half) == b
        ]


def forward_kernel(
    plan,
    x_in, out_grad_in, w_in, wd_in, small_in, lengths, place_cos, place_sin,
    wa_out, wm_out, small_out, sums_out, stats_out, dh_out, tiles_out, xhat_out, cot_out, mixed_out,
    wa, wm, wd, small, xs, ns, sums, cs, q, k, v, att, lse, hidden, slope, k_sum, v_sum,
    own, sines, stats, land, wide, mixed,
    turn_sem, mixed_sem, own_sem, block_sem, out_sem, w_send, w_recv, up_send, up_recv, down_send, down_recv,
    sum_up_send, sum_up_recv, sum_down_send, sum_down_recv,
):
    n, line = plan.n_dp, plan.n_line
    me, place = lax.axis_index("dp"), lax.axis_index("tensor")
    rows, local, model, width = plan.rows, plan.local, plan.model, plan.width

    def owner(mask):
        index = me
        for b in [1] + plan.bits:
            if mask & b:
                index = index + b - 2 * b * lax.rem(index // b, 2)
        return index

    def slot(flow, index, half):
        if flow < 2:
            step = plan.in_rows // 2
            at = pl.multiple_of(index * plan.in_rows + half * step, step)
            return (wa, wm)[flow].at[pl.ds(at, step), :]
        if flow == 2:
            step = plan.down // 2
            return wd.at[index, pl.ds(half * step, step), :]
        return small.at[index]

    def halves(flow):
        return (0,) if flow == 3 else (0, 1)

    def w_copy(flow, mask, half):
        hop = plan.hop(mask, half)
        piece = slot(flow, owner(mask ^ hop), half)
        at = flow * 2 * n + 2 * mask + half
        return pltpu.make_async_remote_copy(
            src_ref=piece, dst_ref=piece, send_sem=w_send.at[at], recv_sem=w_recv.at[at],
            device_id={"dp": owner(hop)}, device_id_type=pl.DeviceIdType.MESH,
        )

    def w_start(flow, mask=0):
        for half in halves(flow):
            for target in plan.onward(mask, half):
                w_copy(flow, target, half).start()

    def w_arrive(flow, masks):
        for mask in masks:
            for half in halves(flow):
                piece = slot(flow, owner(mask), half)
                at = flow * 2 * n + 2 * mask + half
                pltpu.make_async_remote_copy(
                    src_ref=piece, dst_ref=piece, send_sem=w_send.at[at], recv_sem=w_recv.at[at],
                    device_id={"dp": owner(plan.hop(mask, half))}, device_id_type=pl.DeviceIdType.MESH,
                ).wait_recv()
                for target in plan.onward(mask, half):
                    w_copy(flow, target, half).start()

    def chunk(flow, index):
        return (xs, cs)[flow].at[:, pl.ds(pl.multiple_of(index * rows, rows), rows), :]

    def z_copy(flow, step, up):
        piece = chunk(flow, place - (step - 1) if up else place + (step - 1))
        at = flow * line + step
        return pltpu.make_async_remote_copy(
            src_ref=piece, dst_ref=piece,
            send_sem=(up_send if up else down_send).at[at],
            recv_sem=(up_recv if up else down_recv).at[at],
            device_id={"tensor": place + 1 if up else place - 1}, device_id_type=pl.DeviceIdType.MESH,
        )

    def sends(step, up):
        if up:
            return (place < line - 1) & (place >= step - 1)
        return (place > 0) & (place + step - 1 <= line - 1)

    def z_start(flow, step):
        for up in (True, False):
            @pl.when(sends(step, up))
            def _():
                z_copy(flow, step, up).start()

    def z_arrive(flow, step):
        for up in (True, False):
            @pl.when(place >= step if up else place + step <= line - 1)
            def _():
                piece = chunk(flow, place - step if up else place + step)
                at = flow * line + step
                pltpu.make_async_remote_copy(
                    src_ref=piece, dst_ref=piece,
                    send_sem=(up_send if up else down_send).at[at],
                    recv_sem=(up_recv if up else down_recv).at[at],
                    device_id={"tensor": place - 1 if up else place + 1},
                    device_id_type=pl.DeviceIdType.MESH,
                ).wait_recv()
        if step + 1 < line:
            z_start(flow, step + 1)

    def z_sent(flow, step, up):
        @pl.when(sends(step, up))
        def _():
            z_copy(flow, step, up).wait_send()

    def cot_start(step):
        for up in (True, False):
            last = place == step - 1 if up else place == line - step
            @pl.when(last & sends(1, up))
            def _():
                z_copy(0, step, up).wait_send()
                z_copy(1, 1, up).start()

    def at_distance(step, fn):
        if step == 0:
            fn(place)
            return

        def side(j, carry):
            index = place - step + 2 * step * j

            @pl.when((index >= 0) & (index < line))
            def _():
                fn(index)
            return carry

        lax.fori_loop(0, 2, side, 0)

    def span(index):
        return pl.ds(pl.multiple_of(index * rows, rows), rows)

    outs = [
        (wa, wa_out), (wm, wm_out), (small, small_out), (sums, sums_out), (stats, stats_out), (cs, dh_out),
        (att, tiles_out.at[0]),
    ]
    for first, source in ((1, hidden), (1 + plan.n_mlp, slope)):
        outs = outs + [
            (source.at[:, pl.ds(r * local, local)], tiles_out.at[first + r]) for r in range(plan.n_mlp)
        ]
    outs = outs + [(source, tiles_out.at[1 + 2 * plan.n_mlp + r]) for r, source in enumerate((q, k, v))]
    hidden_at, da_at, qkv_at = (
        range(7, 7 + plan.n_mlp), range(7 + plan.n_mlp, 7 + 2 * plan.n_mlp), range(7 + 2 * plan.n_mlp, 10 + 2 * plan.n_mlp)
    )

    def out_copy(j):
        return pltpu.make_async_copy(outs[j][0], outs[j][1], out_sem.at[j])

    def write(*which):
        for j in which:
            out_copy(j).start()

    w_rows = pl.ds(pl.multiple_of(me * plan.in_rows, plan.in_rows), plan.in_rows)
    small_load = pltpu.make_async_copy(small_in, small.at[me], own_sem.at[2])

    stages = (k_sum, v_sum)

    def block_copies(i):
        source = w_in.at[i] if i < 3 + plan.n_mlp else wd_in.at[i - 3 - plan.n_mlp]
        height, wide_cols = source.shape
        strip = min(LANES, wide_cols)
        return [
            (
                g, strip, height,
                pltpu.make_async_copy(
                    source.at[:, pl.ds(g * strip, strip)],
                    stages[i % 2].at[pl.ds(g * height, height), pl.ds(0, strip)],
                    block_sem.at[i % 2, g],
                ),
            )
            for g in range(wide_cols // strip)
        ]

    def block_start(i):
        if i < 4 + 2 * plan.n_mlp:
            for part in block_copies(i):
                part[3].start()

    def round_blocks(first, stop, store):
        for i in range(first, stop):
            for g, strip, height, copy in block_copies(i):
                copy.wait()
                store(i - first, g * strip, strip, stages[i % 2][g * height : (g + 1) * height, :strip].astype(bf16))
            block_start(i + 2)

    def round_in(first, stop, target):
        def store(r, at, strip, value):
            target[w_rows, r * local + at : r * local + at + strip] = value

        round_blocks(first, stop, store)

    def round_down():
        def store(r, at, strip, value):
            wd[me, r * local : (r + 1) * local, at : at + strip] = value

        round_blocks(3 + plan.n_mlp, 4 + 2 * plan.n_mlp, store)

    strip_rows = min(32, rows)
    strip_count = rows // strip_rows

    def row_load(j):
        source = x_in if j < strip_count else out_grad_in
        first = j % strip_count * strip_rows
        return pltpu.make_async_copy(
            source.at[pl.ds(first, strip_rows), :], wide.at[j % 2], own_sem.at[j % 2]
        )

    row_load(0).start()
    row_load(1).start()
    small_load.start()
    block_start(0)
    block_start(1)
    table_loads = [
        pltpu.make_async_copy(place_cos, own, own_sem.at[3]), pltpu.make_async_copy(place_sin, sines, own_sem.at[4])
    ]
    for load in table_loads:
        load.start()
    barrier = pltpu.get_barrier_semaphore()
    for b in [1] + plan.bits if n > 1 else []:
        pl.semaphore_signal(barrier, inc=1, device_id={"dp": owner(b)}, device_id_type=pl.DeviceIdType.MESH)

    @pl.when(place < line - 1)
    def _():
        pl.semaphore_signal(barrier, inc=1, device_id={"tensor": place + 1}, device_id_type=pl.DeviceIdType.MESH)

    @pl.when(place > 0)
    def _():
        pl.semaphore_signal(barrier, inc=1, device_id={"tensor": place - 1}, device_id_type=pl.DeviceIdType.MESH)

    beside = (place + line - 1) // line + (2 * line - 2 - place) // line
    pl.semaphore_wait(barrier, (1 + len(plan.bits) if n > 1 else 0) + beside)

    def normalize_rows(index):
        at = span(index)
        for o in range(n):
            gain, shift = small[o, 0:1, LANES:].astype(f32), small[o, 1:2, LANES:].astype(f32)
            ns[0:rows, o * width : (o + 1) * width] = (xs[o, at, :].astype(f32) * gain + shift).astype(bf16)

    def bias_row(r, first, width):
        per = LANES // plan.bias_cols
        groups = []
        for g in range(first // LANES, (first + width) // LANES):
            total = small[g * per, r : r + 1, :LANES].astype(f32)
            for o in range(1, per):
                total = total + small[g * per + o, r : r + 1, :LANES].astype(f32)
            groups.append(total)
        return jnp.concatenate(groups, axis=1)

    def turn_rows(source, target, index):
        def staged(o):
            return ns.at[pl.ds(0, width), pl.ds(o % 2 * rows, rows)]

        def copy(o):
            return pltpu.make_async_copy(staged(o), target.at[o, :, span(index)], turn_sem.at[o % 2])

        for o in range(n):
            if o >= 2:
                copy(o - 2).wait()
            staged(o)[...] = source[o, span(index), :].T
            copy(o).start()
        for o in range(max(n - 2, 0), n):
            copy(o).wait()

    def attn_rows(index):
        at = span(index)
        turn_rows(xs, xhat_out, index)
        normalize_rows(index)
        for r, target in enumerate((q, k, v)):
            proj = dot_n(ns[0:rows, :], wa[:, r * local : (r + 1) * local]) + bias_row(r, 0, local)
            if r == 2:
                target[at, :] = proj.astype(bf16)
            else:
                for g in range(0, local, LANES):
                    target[at, g : g + LANES] = turn(
                        proj[:, g : g + LANES], own[at, :], sines[at, :], 1.0
                    ).astype(bf16)

    def mlp_rows(index):
        at = span(index)
        normalize_rows(index)
        for r in range(plan.n_mlp):
            cols = slice(r * local, (r + 1) * local)
            pre = dot_n(ns[0:rows, :], wm[:, cols]) + bias_row(3 + r, 0, local)
            value, grad = gelu_and_slope(pre)
            hidden[at, cols] = value.astype(bf16)
            slope[at, cols] = grad.astype(bf16)

    def attend(pair, carry):
        total = plan.group
        block = min(QUERY_ROWS, total)
        lanes = pl.ds(pl.multiple_of(pair * LANES, LANES), LANES)
        for start in range(0, total, block):
            stop = start + block
            here = pl.ds(start, block)
            allowed = attend_mask(begins_of(lengths, start, block), start, block, stop)
            query = q[here, lanes]
            results, logs = [], []
            for head in range(LANES // HEAD):
                mine = head_lanes(block, head)
                chosen = jnp.where(mine, query, jnp.zeros_like(query)) * HEAD ** (-0.5)
                scores = jnp.where(allowed, dot_t(chosen.astype(bf16), k[:stop, lanes]), masked_score)
                top = jnp.max(scores, axis=1, keepdims=True)
                weights = jnp.exp(scores - top)
                total_weight = jnp.sum(weights, axis=1, keepdims=True)
                results.append(dot_n(weights.astype(bf16), v[:stop, lanes]) / total_weight)
                logs.append(top + jnp.log(total_weight))
            first = head_lanes(block, 0)
            att[here, lanes] = jnp.where(first, results[0], results[1]).astype(bf16)
            which = lax.broadcasted_iota(jnp.int32, (block, LANES), 1)
            held = lse[here, :]
            for head in range(LANES // HEAD):
                held = jnp.where(which == pair * (LANES // HEAD) + head, logs[head], held)
            lse[here, :] = held
        return carry

    tall = min(512, plan.group)

    def out_tile(t):
        def part(j, carry):
            at = pl.ds(pl.multiple_of(j * tall, tall), tall)
            total = dot_n(att[at, :], wd[t, :local, :]) + dot_n(hidden[at, :], wd[t, local:, :])
            xs[t, at, :] = total.astype(bf16)
            return carry

        lax.fori_loop(0, plan.group // tall, part, 0)

    def tile_source(t, index):
        return xs.at[t, span(index), :]

    def tile_landing(t, slot):
        return land.at[t, slot]

    out_sum = LineSum(
        place, line, tile_source, tile_landing, (sum_up_send, sum_up_recv, sum_down_send, sum_down_recv)
    )

    def all_tiles(fn):
        lax.fori_loop(0, plan.d_tiles, lambda t, carry: (fn(t), carry)[1], 0)

    def back_rows(index):
        at = span(index)
        turn_rows(cs, cot_out, index)
        for o in range(n):
            sums[0:1, o * width : (o + 1) * width] += jnp.sum(cs[o, at, :].astype(f32), axis=0, keepdims=True)
        for r in range(1 + plan.n_mlp):
            grad = dot_t(cs[0, at, :], wd[0, r * local : (r + 1) * local, :])
            for o in range(1, n):
                grad = grad + dot_t(cs[o, at, :], wd[o, r * local : (r + 1) * local, :])
            if r == 0:
                att[at, :] = grad.astype(bf16)
            else:
                cols = slice((r - 1) * local, r * local)
                slope[at, cols] = (grad * slope[at, cols].astype(f32)).astype(bf16)

    def attend_back(pair, carry):
        block = min(QUERY_ROWS, plan.group)
        scale = HEAD ** (-0.5)
        k_sum[...] = jnp.zeros_like(k_sum)
        v_sum[...] = jnp.zeros_like(v_sum)
        lanes = pl.ds(pl.multiple_of(pair * LANES, LANES), LANES)
        which = lax.broadcasted_iota(jnp.int32, (block, LANES), 1)
        for start in range(0, plan.group, block):
            stop = start + block
            here = pl.ds(start, block)
            allowed = attend_mask(begins_of(lengths, start, block), start, block, stop)
            q_sum = jnp.zeros((block, LANES), f32)
            for head in range(LANES // HEAD):
                mine = head_lanes(block, head)
                query = jnp.where(mine, q[here, lanes], jnp.zeros((block, LANES), bf16)) * scale
                query = query.astype(bf16)
                cot = jnp.where(mine, att[here, lanes], jnp.zeros((block, LANES), bf16))
                level = jnp.sum(
                    jnp.where(which == pair * (LANES // HEAD) + head, lse[here, :], 0.0), axis=1, keepdims=True
                )
                scores = dot_t(query, k[:stop, lanes]) - level
                probs = jnp.where(allowed, jnp.exp(scores), 0.0)
                prob_grad = dot_t(cot, v[:stop, lanes])
                mean = jnp.sum(probs * prob_grad, axis=1, keepdims=True)
                score_grad = (probs * (prob_grad - mean)).astype(bf16)
                q_step = dot_n(score_grad, k[:stop, lanes])
                q_sum = jnp.where(mine, q_step * scale, q_sum)
                k_sum[:stop, :] += dot_s(score_grad, query)
                v_sum[:stop, :] += dot_s(probs.astype(bf16), cot)
            q[here, lanes] = turn(
                q_sum, own[here, :], sines[here, :], -1.0
            ).astype(bf16)
        k[:, lanes] = turn(k_sum[...], own[...], sines[...], -1.0).astype(bf16)
        v[:, lanes] = v_sum[...].astype(bf16)
        return carry

    def dh_tile(t):
        at = pl.ds(pl.multiple_of(t * width, width), width)
        total = dot_t(slope[...], wm[at, :])
        for r, grad in enumerate((q, k, v)):
            total = total + dot_t(grad[...], wa[at, r * local : (r + 1) * local])
        cs[t] = total.astype(bf16)

    def normalize_own():
        for j in range(strip_count):
            row_load(j).wait()
            at = slice(j * strip_rows, (j + 1) * strip_rows)
            value = wide[j % 2]
            mean = jnp.mean(value, axis=1, keepdims=True)
            centered = value - mean
            scale = lax.rsqrt(jnp.mean(centered * centered, axis=1, keepdims=True) + norm_eps)
            normed = (centered * scale).astype(bf16)
            to = pl.ds(pl.multiple_of(place * rows + j * strip_rows, strip_rows), strip_rows)
            for o in range(n):
                xs[o, to, :] = normed[:, o * width : (o + 1) * width]
            first = lax.broadcasted_iota(jnp.int32, (strip_rows, LANES), 1) == 0
            stats[at, :] = jnp.where(first, mean, scale)
            if j + 2 < 2 * strip_count:
                row_load(j + 2).start()

    def mask_cot():
        for j in range(strip_count, 2 * strip_count):
            row_load(j).wait()
            first = place * rows + (j - strip_count) * strip_rows
            places = first + lax.broadcasted_iota(jnp.int32, (strip_rows, 1), 0)
            masked = jnp.where(places < ends_of(lengths)[-1], wide[j % 2], 0.0).astype(bf16)
            to = pl.ds(pl.multiple_of(first, strip_rows), strip_rows)
            for o in range(n):
                cs[o, to, :] = masked[:, o * width : (o + 1) * width]
            if j + 2 < 2 * strip_count:
                row_load(j + 2).start()

    def make_tables():
        for load in table_loads:
            load.wait()
        block_rows = min(QUERY_ROWS, plan.group)
        ends = ends_of(lengths)
        at_ends = [pl.ds(jnp.minimum(end, plan.group - 1), 1) for end in ends]
        end_cosines, end_sines = [own[row, :] for row in at_ends], [sines[row, :] for row in at_ends]
        for start in range(0, plan.group, block_rows):
            at = pl.ds(start, block_rows)
            places = start + lax.broadcasted_iota(jnp.int32, (block_rows, LANES), 0)
            begin_cos, begin_sin = end_cosines[0], end_sines[0]
            for end, end_cos, end_sin in zip(ends[1:], end_cosines[1:], end_sines[1:]):
                begin_cos = jnp.where(places >= end, end_cos, begin_cos)
                begin_sin = jnp.where(places >= end, end_sin, begin_sin)
            place_c, place_s = own[at, :], sines[at, :]
            cosine = place_c * begin_cos + place_s * begin_sin
            sine = place_s * begin_cos - place_c * begin_sin
            lane = lax.rem(lax.broadcasted_iota(jnp.int32, (block_rows, LANES), 1), HEAD)
            own[at, :] = jnp.where(lane < ROT, cosine, 1.0)
            sines[at, :] = jnp.where(lane < ROT // 2, -sine, jnp.where(lane < ROT, sine, 0.0))

    def mixed_copy(t):
        cols = pl.ds(pl.multiple_of(t * width, width), width)
        return pltpu.make_async_copy(mixed.at[lax.rem(t, 2)], mixed_out.at[:, cols], mixed_sem.at[lax.rem(t, 2)])

    def finish_tile(t):
        @pl.when(t >= 2)
        def _():
            mixed_copy(t - 2).wait()
        out_sum.last(t, mixed.at[lax.rem(t, 2)])
        mixed_copy(t).start()

    small_load.wait()
    w_start(3)
    round_in(0, 3, wa)
    w_start(0)
    normalize_own()
    z_start(0, 1)
    round_in(3, 3 + plan.n_mlp, wm)
    mask_cot()
    round_down()
    make_tables()
    sums[...] = jnp.zeros_like(sums)
    lse[...] = jnp.zeros_like(lse)
    write(4)
    w_arrive(0, plan.single)
    w_start(1)
    w_arrive(3, plan.single)
    z_arrive(0, 1)
    cot_start(1)
    w_arrive(3, plan.several)
    w_arrive(0, plan.several)
    w_arrive(3, plan.odd)
    w_arrive(0, plan.odd)
    write(0, 2)
    at_distance(0, attn_rows)
    if line > 2:
        at_distance(1, attn_rows)
    w_arrive(1, plan.single)
    w_start(2)
    for step in range(2, line - 1):
        z_arrive(0, step)
        cot_start(step)
        at_distance(step, attn_rows)
    w_arrive(1, plan.several)
    w_arrive(1, plan.odd)
    write(1)
    near = max(line - 2, 0)
    lax.fori_loop(
        jnp.maximum(place - near, 0), jnp.minimum(place + near, line - 1) + 1,
        lambda c, carry: (mlp_rows(c), carry)[1], 0,
    )
    if line > 2:
        z_arrive(0, line - 1)
        cot_start(line - 1)
    at_distance(line - 1, lambda c: (attn_rows(c), mlp_rows(c))[0])
    write(*hidden_at)
    pairs = local // LANES
    lax.fori_loop(0, pairs // 2, attend, 0)
    w_arrive(2, plan.single)
    lax.fori_loop(pairs // 2, pairs, attend, 0)
    write(6)
    z_arrive(1, 1)
    w_arrive(2, plan.several)
    for step in range(1, line):
        for up in (True, False):
            left = place != step - 1 if up else place != line - step
            @pl.when(left & sends(step, up))
            def _():
                z_copy(0, step, up).wait_send()
    w_arrive(2, plan.odd)

    def first_tile(t):
        out_tile(t)
        out_sum.first(t)

    all_tiles(first_tile)
    out_copy(6).wait()
    at_distance(0, back_rows)
    if line > 2:
        at_distance(1, back_rows)
    for step in range(2, line - 1):
        z_arrive(1, step)
        at_distance(step, back_rows)

    def settle(near):
        for up in (True, False):
            now = (place < line // 2) if up == near else (place >= line // 2)

            @pl.when(now)
            def _():
                for step in range(1, line):
                    z_sent(1, step, up)

    quarter, count = plan.d_tiles // 4, plan.d_tiles
    settle(True)
    out_sum.one_way(0, quarter, True)
    if line > 2:
        z_arrive(1, line - 1)
    at_distance(line - 1, back_rows)
    write(3, *da_at)
    settle(False)
    lax.fori_loop(0, pairs // 2, attend_back, 0)
    out_sum.one_way(quarter, 2 * quarter, True)
    out_sum.one_way(0, quarter, False)
    lax.fori_loop(pairs // 2, pairs, attend_back, 0)
    write(*qkv_at)
    out_sum.one_way(2 * quarter, 3 * quarter, True)
    out_sum.one_way(quarter, 2 * quarter, False)
    all_tiles(dh_tile)
    write(5)
    out_sum.one_way(3 * quarter, count, True)
    out_sum.one_way(2 * quarter, count, False)
    all_tiles(finish_tile)
    for t in range(max(count - 2, 0), count):
        mixed_copy(t).wait()

    all_tiles(out_sum.sent)
    for flow in range(4):
        for mask in range(1, n):
            for half in halves(flow):
                w_copy(flow, mask, half).wait_send()
    for j in range(len(outs)):
        if j != 6:
            out_copy(j).wait()


def forward(plan, x, out_grad, w, wd, small, lengths):
    any_space = pl.BlockSpec(memory_space=pl.ANY)
    n, line, group, model, local, rows = (
        plan.n_dp, plan.n_line, plan.group, plan.model, plan.local, plan.rows
    )
    low = lambda *shape: jax.ShapeDtypeStruct(shape, bf16)
    full = lambda *shape: jax.ShapeDtypeStruct(shape, f32)
    tiles = 4 + 2 * plan.n_mlp
    out_shape = [
        low(model, plan.attn), low(model, plan.mlp), low(n, 16, LANES + plan.out_cols),
        full(8, model), full(rows, LANES), low(n, group, plan.width), low(tiles, group, local),
        low(n, plan.width, group), low(n, plan.width, group), full(rows, model),
    ]
    act = pltpu.VMEM((n, group, plan.width), bf16)
    head = pltpu.VMEM((group, local), bf16)
    hide = pltpu.VMEM((group, plan.mlp), bf16)
    lane = pltpu.VMEM((group, LANES), f32)
    scratch = lambda s: pltpu.VMEM(s.shape, s.dtype)
    dma = pltpu.SemaphoreType.DMA
    return pl.pallas_call(
        partial(forward_kernel, plan),
        in_specs=[any_space] * 5 + [pl.BlockSpec(memory_space=pltpu.SMEM)] + [any_space] * 2,
        out_specs=[any_space] * 10,
        out_shape=out_shape,
        scratch_shapes=[scratch(s) for s in out_shape[:2]]
        + [pltpu.VMEM((n, plan.down, plan.out_cols), bf16), scratch(out_shape[2]), act]
        + [pltpu.VMEM((max(rows, plan.width), model), bf16), scratch(out_shape[3]), act, head, head, head, head, lane]
        + [hide, hide] + [lane] * 4 + [scratch(out_shape[4])]
        + [pltpu.VMEM((plan.d_tiles, line + 1, rows, plan.width), bf16)]
        + [
            pltpu.VMEM((2, min(32, rows), model), f32), pltpu.VMEM((2, rows, plan.width), f32),
        ]
        + [dma((2,)), dma((2,)), dma((5,)), dma((2, 4)), dma((6 + tiles,)), dma((8 * n,)), dma((8 * n,))]
        + [dma((2 * line,))] * 4
        + [dma((plan.d_tiles, line + 1))] * 4,
        compiler_params=pltpu.CompilerParams(
            collective_id=0, has_side_effects=True, vmem_limit_bytes=63 << 20
        ),
        cost_estimate=pl.CostEstimate(flops=60 * 10**9, bytes_accessed=80 << 20, transcendentals=0),
    )(x, out_grad, w, wd, small, lengths, *angle_tables(group))


def backward_kernel(
    plan,
    xhat_in, cot_in, tiles_in, dh_in, wa_in, wm_in, sums_in,
    down_out, in_out, small_out, rows_out, dh_out,
    turned, operand, dh, sent, core_in, held, cube_in, land,
    w_own, fin, fin_turned, dh_fin, small, small_in, shares,
    load_sem, turn_sem, operand_sem, fin_sem, dh_sem, core_send, core_recv, cube_send, cube_recv,
    up_send, up_recv, down_send, down_recv,
    small_send, small_recv, share_send, share_recv, credit,
):
    n, line = plan.n_dp, plan.n_line
    me, place = lax.axis_index("dp"), lax.axis_index("tensor")
    rows, local, group, model, in_rows = plan.rows, plan.local, plan.group, plan.model, plan.in_rows
    MESH = pl.DeviceIdType.MESH
    half_rows, pairs_n, n_bits = in_rows // 2, n // 2, len(plan.bits)
    orders = (plan.bits, plan.bits[::-1])
    n_down, n_mlp = 1 + plan.n_mlp, plan.n_mlp
    def owner(mask):
        index = me
        for b in [1] + plan.bits:
            if mask & b:
                index = index + b - 2 * b * lax.rem(index // b, 2)
        return index

    def peer(bit):
        return {"dp": owner(bit)}

    def position(mask, order):
        return sum((1 if mask & b else 0) << (n_bits - 1 - p) for p, b in enumerate(order))

    width, d_tiles = plan.width, plan.d_tiles
    own_rows = pl.ds(pl.multiple_of(me * in_rows, in_rows), in_rows)

    whole = [
        (dh_in, dh),
        (wa_in.at[own_rows, :], w_own.at[:, pl.ds(0, plan.attn)]),
        (wm_in.at[own_rows, :], w_own.at[:, pl.ds(plan.attn, plan.mlp)]),
    ]
    for j, (a, b) in enumerate(whole):
        pltpu.make_async_copy(a, b, load_sem.at[j]).start()

    def loaded(*which):
        for j in which:
            pltpu.make_async_copy(whole[j][0], whole[j][1], load_sem.at[j]).wait()

    barrier = pltpu.get_barrier_semaphore()
    for b in [1] + plan.bits:
        pl.semaphore_signal(barrier, inc=1, device_id=peer(b), device_id_type=MESH)
    for d in range(1, line):
        pl.semaphore_signal(
            barrier, inc=1, device_id={"tensor": lax.rem(place + d, line)}, device_id_type=MESH
        )

    def share_copy(d, arriving):
        source = lax.rem(place + line - d, line) if arriving else place
        return pltpu.make_async_remote_copy(
            src_ref=shares, dst_ref=rows_out.at[source],
            send_sem=share_send.at[d], recv_sem=share_recv.at[d],
            device_id={"tensor": lax.rem(place + d, line)}, device_id_type=MESH,
        )

    share_own = pltpu.make_async_copy(shares, rows_out.at[place], share_send.at[0])

    masks = [2 * j + 1 for j in range(pairs_n)] + [2 * j for j in range(pairs_n)]

    def turned_copy(source, j):
        return pltpu.make_async_copy(
            source.at[owner(masks[j])], turned.at[pl.ds(j * in_rows, in_rows), :], turn_sem.at[j]
        )

    def turned_start(source):
        for j in range(n):
            turned_copy(source, j).start()

    def turned_wait(source):
        for j in range(n):
            turned_copy(source, j).wait()

    tiles_n = n_down + n_mlp + 3

    def operand_copy(t):
        slot = lax.rem(t, 3)
        return pltpu.make_async_copy(tiles_in.at[t], operand.at[slot], operand_sem.at[slot])

    def core_copy(t, base):
        return pltpu.make_async_remote_copy(
            src_ref=sent.at[lax.rem(t, 2)], dst_ref=core_in.at[t - base],
            send_sem=core_send.at[lax.rem(t, 2)], recv_sem=core_recv.at[t - base],
            device_id=peer(1), device_id_type=MESH,
        )

    def cube_copy(slot, half, phase):
        count = pairs_n >> (phase + 1)
        first = pairs_n - 2 * count
        at = half * n_bits + phase
        return pltpu.make_async_remote_copy(
            src_ref=held.at[slot, half, pl.ds(count, count)],
            dst_ref=cube_in.at[slot, half, pl.ds(first, count)],
            send_sem=cube_send.at[slot, at], recv_sem=cube_recv.at[slot, at],
            device_id=peer(orders[half][phase]), device_id_type=MESH,
        )

    piece = min(2, pairs_n) * in_rows

    def send_core(t, base):
        @pl.when(t >= base + 2)
        def _():
            core_copy(t - 2, base).wait_send()
        slot = lax.rem(t, 3)
        for at in range(0, pairs_n * in_rows, piece):
            sent[lax.rem(t, 2), at : at + piece, :] = dot_n(turned[at : at + piece, :], operand[slot]).astype(bf16)
        core_copy(t, base).start()
        if base:
            row = lax.rem(t - base + 3, n_mlp + 3)
            small[0, pl.ds(row, 1), :] = jnp.sum(operand[slot].astype(f32), axis=0, keepdims=True)

    def keep_core(t, base):
        core_copy(t, base).wait_recv()
        for first in range(0, pairs_n * in_rows, piece):
            kept = pairs_n * in_rows + first
            total = dot_n(turned[kept : kept + piece, :], operand[lax.rem(t, 3)])
            total = total + core_in[t - base, first : first + piece, :].astype(f32)
            for at in range(0, piece, half_rows):
                j, half = divmod((first + at) // half_rows, 2)
                held[t, half, position(2 * j, orders[half])] = total[at : at + half_rows].astype(bf16)
        for half in range(2):
            if n_bits:
                cube_copy(t, half, 0).start()

    def scatter(base, stop):
        def step(t, carry):
            operand_copy(t).wait()

            @pl.when(t + 1 < tiles_n)
            def _():
                operand_copy(t + 1).start()
            send_core(t, base)

            @pl.when(t >= base + 1)
            def _():
                keep_core(t - 1, base)
            return carry

        lax.fori_loop(base, stop, step, 0)
        keep_core(stop - 1, base)
        for t in range(max(stop - 2, base), stop):
            core_copy(t, base).wait_send()

    def cube_step(base, stop, phase):
        count = pairs_n >> (phase + 1)
        first = pairs_n - 2 * count
        down = base == 0
        depth = 1 if down else 2

        def result(t):
            return t if down else lax.rem(t - n_down + 3, n_mlp + 3)

        def fin_copy(t):
            source = fin_turned if down else fin.at[lax.rem(t, 2)]
            target = down_out if down else in_out
            return pltpu.make_async_copy(source, target.at[result(t)], fin_sem.at[lax.rem(t, 2)])

        def step(t, carry):
            slot = t
            if phase == n_bits - 1:
                @pl.when(t >= base + depth)
                def _():
                    fin_copy(t - depth).wait()
            for half in range(2):
                cube_copy(slot, half, phase).wait_recv()
                total = (
                    held[slot, half, 0:count].astype(f32)
                    + cube_in[slot, half, first : first + count].astype(f32)
                )
                if phase < n_bits - 1:
                    held[slot, half, 0:count] = total.astype(bf16)
                    cube_copy(slot, half, phase + 1).start()
                else:
                    fin[lax.rem(t, 2), half * half_rows : (half + 1) * half_rows, :] = total[0]
            if phase == n_bits - 1:
                if down:
                    fin_turned[...] = fin[lax.rem(t, 2)].T
                fin_copy(t).start()
                if not down:
                    weight = w_own[:, pl.ds(pl.multiple_of(result(t) * local, local), local)].astype(f32)
                    product = weight * fin[lax.rem(t, 2)]
                    extra = weight * small[n_bits + 1, pl.ds(result(t), 1), :]
                    for g in range(0, local, LANES):
                        shares[0] += product[:, g : g + LANES]
                        shares[1] += extra[:, g : g + LANES]
            return carry

        lax.fori_loop(base, stop, step, 0)
        if phase == n_bits - 1:
            for t in range(max(stop - depth, base), stop):
                fin_copy(t).wait()

    def cube_sent(t):
        for half in range(2):
            for phase in range(n_bits):
                cube_copy(t, half, phase).wait_send()

    def tile_of(buffer):
        def source(t, index):
            return buffer.at[t, pl.ds(pl.multiple_of(index * rows, rows), rows), :]
        return source

    dh_sum = LineSum(
        place, line, tile_of(dh), lambda t, slot: land.at[t, slot],
        (up_send, up_recv, down_send, down_recv),
    )
    def sum_copy(target, t):
        cols = pl.ds(pl.multiple_of(t * width, width), width)
        return pltpu.make_async_copy(dh_fin.at[lax.rem(t, 2)], target.at[:, cols], dh_sem.at[lax.rem(t, 2)])

    def finish(flow, target, count):
        def step(t):
            @pl.when(t >= 2)
            def _():
                sum_copy(target, t - 2).wait()
            flow.last(t, dh_fin.at[lax.rem(t, 2)])
            sum_copy(target, t).start()

        tiles(0, count, step)
        for t in range(max(count - 2, 0), count):
            sum_copy(target, t).wait()

    def tiles(first, stop, fn):
        lax.fori_loop(first, stop, lambda t, carry: (fn(t), carry)[1], 0)

    def small_copy(j):
        return pltpu.make_async_remote_copy(
            src_ref=small.at[j], dst_ref=small_in.at[j],
            send_sem=small_send.at[j], recv_sem=small_recv.at[j],
            device_id=peer(([1] + plan.bits)[j]), device_id_type=MESH,
        )

    def small_step(j):
        small_copy(j).wait_recv()
        small[j + 1] = small[j] + small_in[j]
        if j < n_bits:
            small_copy(j + 1).start()

    turned_start(cot_in)
    operand_copy(0).start()
    shares[...] = jnp.zeros_like(shares)
    small[0] = jnp.zeros_like(small[0])
    for r in range(model // local):
        small[0, 8 + r : 9 + r, :] = sums_in[0:1, r * local : (r + 1) * local]
    pl.semaphore_wait(barrier, 1 + n_bits + line - 1)
    loaded(0)
    tiles(0, d_tiles, dh_sum.first)
    turned_wait(cot_in)
    quarter = d_tiles // 4
    scatter(0, n_down)
    pl.semaphore_signal(credit, inc=1, device_id=peer(1), device_id_type=MESH)
    turned_start(xhat_in)
    dh_sum.one_way(0, quarter, True)
    turned_wait(xhat_in)
    pl.semaphore_wait(credit, 1)
    scatter(n_down, tiles_n)
    small_copy(0).start()
    dh_sum.one_way(quarter, 2 * quarter, True)
    dh_sum.one_way(0, quarter, False)
    for phase in range(n_bits - 1):
        cube_step(0, n_down, phase)
    small_step(0)
    dh_sum.one_way(2 * quarter, 3 * quarter, True)
    dh_sum.one_way(quarter, 2 * quarter, False)
    for j in range(1, n_bits + 1):
        small_step(j)
    loaded(1, 2)
    for phase in range(n_bits - 1):
        cube_step(n_down, n_down + n_mlp, phase)
    dh_sum.one_way(3 * quarter, d_tiles, True)
    dh_sum.one_way(2 * quarter, 3 * quarter, False)
    cube_step(0, n_down, n_bits - 1)
    dh_sum.one_way(3 * quarter, d_tiles, False)
    for phase in range(n_bits - 1):
        cube_step(n_down + n_mlp, tiles_n, phase)
    finish(dh_sum, dh_out, d_tiles)
    cube_step(n_down, n_down + n_mlp, n_bits - 1)
    cube_step(n_down + n_mlp, tiles_n, n_bits - 1)
    share_own.start()
    for d in range(1, line):
        share_copy(d, False).start()
    small_done = pltpu.make_async_copy(small.at[n_bits + 1], small_out, load_sem.at[0])
    small_done.start()
    tiles(0, tiles_n, cube_sent)
    tiles(0, d_tiles, dh_sum.sent)
    for j in range(n_bits + 1):
        small_copy(j).wait_send()
    share_own.wait()
    for d in range(1, line):
        share_copy(d, False).wait_send()
        share_copy(d, True).wait_recv()
    small_done.wait()


def backward(plan, xhat, cot, tiles, dh, wa, wm, sums):
    any_space = pl.BlockSpec(memory_space=pl.ANY)
    vmem = pl.BlockSpec(memory_space=pltpu.VMEM)
    n, line, group, model, local = plan.n_dp, plan.n_line, plan.group, plan.model, plan.local
    rows, in_rows, n_bits, pairs_n = plan.rows, plan.in_rows, len(plan.bits), n // 2
    n_down = 1 + plan.n_mlp
    small_rows = 8 + -(-(model // local) // 8) * 8
    width, d_tiles = plan.width, plan.d_tiles
    low = lambda *shape: pltpu.VMEM(shape, bf16)
    full = lambda *shape: pltpu.VMEM(shape, f32)
    dma = pltpu.SemaphoreType.DMA
    out = lambda dtype, *shape: jax.ShapeDtypeStruct(shape, dtype)
    slots = n_down + plan.n_mlp + 3
    return pl.pallas_call(
        partial(backward_kernel, plan),
        in_specs=[any_space] * 6 + [vmem],
        out_specs=[any_space] * 5,
        out_shape=[
            out(f32, n_down, local, in_rows), out(f32, 3 + plan.n_mlp, in_rows, local),
            out(f32, small_rows, local),
            out(f32, line, 2, in_rows, LANES), out(f32, rows, model),
        ],
        scratch_shapes=[
            low(n * in_rows, group), low(3, group, local), low(d_tiles, group, width),
            low(2, pairs_n * in_rows, local), low(3 + plan.n_mlp, pairs_n * in_rows, local),
            low(slots, 2, pairs_n, in_rows // 2, local), low(slots, 2, max(pairs_n - 1, 1), in_rows // 2, local),
            low(d_tiles, line + 1, rows, width),
            low(in_rows, plan.attn + plan.mlp), full(2, in_rows, local), full(local, in_rows), full(2, rows, width),
            full(n_bits + 2, small_rows, local), full(n_bits + 1, small_rows, local), full(2, in_rows, LANES),
            dma((3,)), dma((n,)), dma((3,)), dma((2,)), dma((2,)), dma((2,)), dma((3 + plan.n_mlp,)),
            dma((slots, max(2 * n_bits, 1))), dma((slots, max(2 * n_bits, 1))),
            dma((d_tiles, line + 1)), dma((d_tiles, line + 1)), dma((d_tiles, line + 1)), dma((d_tiles, line + 1)),
            dma((n_bits + 1,)), dma((n_bits + 1,)), dma((line,)), dma((line,)),
            pltpu.SemaphoreType.REGULAR,
        ],
        compiler_params=pltpu.CompilerParams(
            collective_id=1, has_side_effects=True, vmem_limit_bytes=63 << 20
        ),
        cost_estimate=pl.CostEstimate(flops=80 * 10**9, bytes_accessed=80 << 20, transcendentals=0),
    )(xhat, cot, tiles, dh, wa, wm, sums)


def adam_update(weight, moment_one, moment_two, gradient, step_rate, decay_factor):
    first_new = beta_first * moment_one + (1.0 - beta_first) * gradient
    second_new = beta_second * moment_two + (1.0 - beta_second) * gradient * gradient
    corrected = first_new / (1.0 - beta_first**STEP)
    spread = jnp.sqrt(second_new / (1.0 - beta_second**STEP))
    return (
        weight - step_rate * (corrected / (spread + adam_eps) + decay_factor * weight),
        first_new,
        second_new,
    )


def per_device(
    block_input,
    out_grad,
    seq_lengths,
    in_weight,
    down_weight,
    column_bias,
    vector_params,
    in_first,
    in_second,
    down_first,
    down_second,
    bias_first,
    bias_second,
    vector_first,
    vector_second,
):
    n_dp = lax.axis_size("dp")
    n_tensor = lax.axis_size("tensor")
    own_rows, model = block_input.shape
    group = own_rows * n_tensor
    in_rows, widths, local = in_weight.shape
    out_cols = down_weight.shape[2]
    n_mlp = widths - 3
    attn_width, mlp_width = 3 * local, n_mlp * local

    me = lax.axis_index("dp")
    plan = Plan(n_dp, n_tensor, own_rows, model, in_rows, local, n_mlp, out_cols)
    share = LANES // plan.bias_cols
    lane = lax.broadcasted_iota(jnp.int32, (widths, LANES), 1) // plan.bias_cols
    bias_tile = jnp.where(lane == lax.rem(me, share), jnp.tile(column_bias, (1, share)), 0.0)
    small = jnp.concatenate(
        [jnp.pad(bias_tile, ((0, 16 - widths), (0, 0))), jnp.pad(vector_params, ((0, 13), (0, 0)))], axis=1
    ).astype(bf16)
    (
        w_attn, w_mlp, vectors, cot_sums, stats, dh_part, tiles, xhat_turned, cot_turned, mixed,
    ) = forward(plan, block_input, out_grad, in_weight.transpose(1, 0, 2), down_weight, small, seq_lengths)
    down_grad, in_grad, small_grad, shares, dh = backward(
        plan, xhat_turned, cot_turned, tiles, dh_part, w_attn, w_mlp, cot_sums
    )
    vector_vals = vectors[:, :3, LANES:].transpose(1, 0, 2).reshape(3, model).astype(f32)
    gain, out_bias = vector_vals[0], vector_vals[2]
    block_out = block_input + (mixed + out_bias)
    mean, inv_scale = stats[:, :1], stats[:, 1:2]
    xhat = (block_input - mean) * inv_scale
    places = lax.axis_index("tensor") * own_rows + lax.broadcasted_iota(jnp.int32, (own_rows, 1), 0)
    cot_live = jnp.where(places < jnp.sum(seq_lengths), out_grad, 0.0)

    dxhat = dh * gain
    input_grad = cot_live + inv_scale * (
        dxhat
        - jnp.mean(dxhat, axis=-1, keepdims=True)
        - xhat * jnp.mean(dxhat * xhat, axis=-1, keepdims=True)
    )

    bias_full = small_grad[:widths]
    own_vectors = vector_params.astype(bf16).astype(f32)
    in_reduced = (
        in_grad * own_vectors[0][None, :, None] + own_vectors[1][None, :, None] * bias_full[:, None, :]
    ).transpose(1, 0, 2)
    down_reduced = down_grad
    bias_reduced = lax.dynamic_slice_in_dim(bias_full, me * plan.bias_cols, plan.bias_cols, 1)
    out_sums = small_grad[8 : 8 + model // local].reshape(-1)
    vector_reduced = jnp.stack(
        [
            jnp.sum(shares[:, 0], axis=(0, 2)),
            jnp.sum(shares[:, 1], axis=(0, 2)),
            lax.dynamic_slice_in_dim(out_sums, me * out_cols, out_cols, 0),
        ]
    )

    in_new, in_one, in_two = adam_update(
        in_weight, in_first, in_second, in_reduced, rate_in, weight_decay
    )
    down_new, down_one, down_two = adam_update(
        down_weight, down_first, down_second, down_reduced, rate_down, weight_decay
    )
    bias_new, bias_one, bias_two = adam_update(
        column_bias, bias_first, bias_second, bias_reduced, rate_vector, 0.0
    )
    vector_new, vector_one, vector_two = adam_update(
        vector_params, vector_first, vector_second, vector_reduced, rate_vector, 0.0
    )
    return (
        block_out,
        input_grad,
        in_new,
        in_one,
        in_two,
        down_new,
        down_one,
        down_two,
        bias_new,
        bias_one,
        bias_two,
        vector_new,
        vector_one,
        vector_two,
    )


def widths_down(down_weight):
    return down_weight.shape[0] * down_weight.shape[1]


def solution(mesh):
    return jax.shard_map(
        per_device,
        mesh=mesh,
        in_specs=(
            P(("dp", "tensor"), None),
            P(("dp", "tensor"), None),
            P("dp", None),
            P("dp", None, "tensor"),
            P(None, "tensor", "dp"),
            P(None, ("tensor", "dp")),
            P(None, "dp"),
            P("dp", None, "tensor"),
            P("dp", None, "tensor"),
            P(None, "tensor", "dp"),
            P(None, "tensor", "dp"),
            P(None, ("tensor", "dp")),
            P(None, ("tensor", "dp")),
            P(None, "dp"),
            P(None, "dp"),
        ),
        out_specs=(
            P(("dp", "tensor"), None),
            P(("dp", "tensor"), None),
            P("dp", None, "tensor"),
            P("dp", None, "tensor"),
            P("dp", None, "tensor"),
            P(None, "tensor", "dp"),
            P(None, "tensor", "dp"),
            P(None, "tensor", "dp"),
            P(None, ("tensor", "dp")),
            P(None, ("tensor", "dp")),
            P(None, ("tensor", "dp")),
            P(None, "dp"),
            P(None, "dp"),
            P(None, "dp"),
        ),
        check_vma=False,
    )
```

```python
from functools import partial

import jax
import jax.numpy as jnp
import numpy as np
from jax import lax
from jax.experimental import pallas as pl
from jax.experimental.pallas import tpu as pltpu
from jax.sharding import PartitionSpec as P

HEAD = 64
ROT = 32
STEP = 8
LANES = 128
QUERY_ROWS = 256

norm_eps = 1e-05
beta_first = 0.9
beta_second = 0.95
adam_eps = 1e-08
masked_score = -1000000000.0
rate_in = 0.02
rate_down = 0.05
rate_vector = 0.2
weight_decay = 0.1

bf16 = jnp.bfloat16
f32 = jnp.float32


def angle_tables(rows):
    half_rot = ROT // 2
    frequency = 10000.0 ** (-2.0 * (np.arange(LANES) % half_rot) / ROT)
    angles = np.arange(rows)[:, None] * frequency[None, :]
    return np.cos(angles).astype(np.float32), np.sin(angles).astype(np.float32)


def ends_of(lengths):
    ends = [jnp.int32(0)]
    for j in range(lengths.shape[1]):
        ends.append(ends[-1] + lengths[0, j])
    return ends


def begins_of(lengths, start, rows):
    places = start + lax.broadcasted_iota(jnp.int32, (rows, 1), 0)
    begin = jnp.zeros((rows, 1), jnp.int32)
    for end in ends_of(lengths)[1:]:
        begin = jnp.where(places >= end, end, begin)
    return begin


def attend_mask(begin, row_start, rows, stop):
    key_place = lax.broadcasted_iota(jnp.int32, (rows, stop), 1)
    query_place = row_start + lax.broadcasted_iota(jnp.int32, (rows, stop), 0)
    return (key_place <= query_place) & (key_place >= begin)


def head_lanes(rows, head):
    lane = lax.broadcasted_iota(jnp.int32, (rows, LANES), 1)
    return (lane >= head * HEAD) & (lane < (head + 1) * HEAD)


def dot_t(a, b):
    return lax.dot_general(a, b, (((1,), (1,)), ((), ())), preferred_element_type=f32)


def dot_n(a, b):
    return lax.dot_general(a, b, (((1,), (0,)), ((), ())), preferred_element_type=f32)


def dot_s(a, b):
    return lax.dot_general(a, b, (((0,), (0,)), ((), ())), preferred_element_type=f32)


def turn(x, own, sines, sign):
    half = ROT // 2
    lane = lax.rem(lax.broadcasted_iota(jnp.int32, x.shape, 1), HEAD)
    other = jnp.where(lane < half, pltpu.roll(x, LANES - half, 1), pltpu.roll(x, half, 1))
    return x * own + sign * (other * sines)


def low_bit(mask):
    return mask & -mask


def high_bit(mask):
    return 1 << (mask.bit_length() - 1)


def gelu_and_slope(a):
    root = (2.0 / 3.141592653589793) ** 0.5
    square = a * a
    t = jnp.tanh(root * a * (1.0 + 0.044715 * square))
    half = 0.5 * (1.0 + t)
    return a * half, half + 0.5 * a * (1.0 - t * t) * (root * (1.0 + 3.0 * 0.044715 * square))


class LineSum:
    def __init__(self, place, line, source, landing, sems):
        self.place, self.line, self.source, self.landing = place, line, source, landing
        self.up_send, self.up_recv, self.down_send, self.down_recv = sems

    def copy(self, t, index, up, arriving=False):
        place = self.place
        slot = self.slot(index, up)
        return pltpu.make_async_remote_copy(
            src_ref=self.source(t, index),
            dst_ref=self.landing(t, slot),
            send_sem=(self.up_send if up else self.down_send).at[t, slot],
            recv_sem=(self.up_recv if up else self.down_recv).at[t, slot],
            device_id={"tensor": place + 1 if up != arriving else place - 1},
            device_id_type=pl.DeviceIdType.MESH,
        )

    def got(self, t, index, up):
        return self.landing(t, self.slot(index, up))[...].astype(f32)

    def slot(self, index, up):
        return index - 1 if up else lax.rem(self.line - 1 + index, self.line + 1)

    def first(self, t):
        for up in (True, False):
            @pl.when((self.place == 0) if up else (self.place == self.line - 1))
            def _():
                for step in range(self.line - 1):
                    self.copy(t, self.line - 1 - step if up else step, up).start()

    def hand_on(self, t, up):
        place, line = self.place, self.line
        for step in range(line - 1):
            index = line - 1 - step if up else step
            hears = (place > 0) & (place < index) if up else (place < line - 1) & (place > index)

            @pl.when(hears)
            def _():
                self.copy(t, index, up, True).wait_recv()
                mine = self.source(t, index)
                mine[...] = (mine[...].astype(f32) + self.got(t, index, up)).astype(bf16)
                self.copy(t, index, up).start()

    def one_way(self, first, stop, near):
        def step(t, carry):
            for up in (True, False):
                far = 2 * self.place // self.line
                late = far if up else 1 - far

                @pl.when(late == (0 if near else 1))
                def _():
                    self.hand_on(t, up)
            return carry

        lax.fori_loop(first, stop, step, 0)

    def last(self, t, target):
        place, line = self.place, self.line
        target[...] = self.source(t, place)[...].astype(f32)
        for up in (True, False):
            @pl.when((place > 0) if up else (place < line - 1))
            def _():
                self.copy(t, place, up, True).wait_recv()
                target[...] += self.got(t, place, up)

    def sent(self, t):
        for index in range(self.line):
            for up in (True, False):
                @pl.when((self.place < index) if up else (self.place > index))
                def _():
                    self.copy(t, index, up).wait_send()


class Plan:
    def __init__(self, n_dp, n_line, rows, model, in_rows, local, n_mlp, out_cols):
        self.n_dp, self.n_line = n_dp, n_line
        self.rows, self.model = rows, model
        self.group = rows * n_line
        self.in_rows, self.local, self.n_mlp, self.out_cols = in_rows, local, n_mlp, out_cols
        self.attn, self.mlp = 3 * local, n_mlp * local
        self.down = (1 + n_mlp) * local
        self.bias_cols = local // n_dp
        self.width = out_cols
        self.d_tiles = model // out_cols
        self.bits = [1 << b for b in range(1, n_dp.bit_length() - 1)]
        even = range(2, n_dp, 2)
        self.single = [m for m in even if m.bit_count() == 1]
        self.several = sorted((m for m in even if m.bit_count() > 1), key=lambda m: m.bit_count())
        self.odd = list(range(1, n_dp, 2))

    def hop(self, mask, half):
        if mask & 1:
            return 1
        return high_bit(mask) if half == 0 else low_bit(mask)

    def onward(self, mask, half):
        if mask & 1:
            return []
        masks = [mask | 1] if self.n_dp > 1 else []
        return masks + [
            mask | b for b in self.bits if not mask & b and self.hop(mask | b, half) == b
        ]


def forward_kernel(
    plan,
    x_in, out_grad_in, w_in, wd_in, small_in, lengths, place_cos, place_sin,
    wa_out, wm_out, small_out, sums_out, stats_out, dh_out, tiles_out, xhat_out, cot_out, mixed_out,
    wa, wm, wd, small, xs, ns, sums, cs, q, k, v, att, lse, hidden, slope, k_sum, v_sum,
    own, sines, stats, land, wide, mixed,
    turn_sem, mixed_sem, own_sem, block_sem, out_sem, w_send, w_recv, up_send, up_recv, down_send, down_recv,
    sum_up_send, sum_up_recv, sum_down_send, sum_down_recv,
):
    n, line = plan.n_dp, plan.n_line
    me, place = lax.axis_index("dp"), lax.axis_index("tensor")
    rows, local, model, width = plan.rows, plan.local, plan.model, plan.width

    def owner(mask):
        index = me
        for b in [1] + plan.bits:
            if mask & b:
                index = index + b - 2 * b * lax.rem(index // b, 2)
        return index

    def owner_of(j):
        index = 0
        for b in [1] + plan.bits:
            index = index + b * lax.rem(me // b + j // b, 2)
        return index

    def slot(flow, index, half):
        if flow < 2:
            step = plan.in_rows // 2
            at = pl.multiple_of(index * plan.in_rows + half * step, step)
            return (wa, wm)[flow].at[pl.ds(at, step), :]
        if flow == 2:
            step = plan.down // 2
            return wd.at[index, pl.ds(half * step, step), :]
        return small.at[index]

    def halves(flow):
        return (0,) if flow == 3 else (0, 1)

    def w_copy(flow, mask, half):
        hop = plan.hop(mask, half)
        piece = slot(flow, owner(mask ^ hop), half)
        at = flow * 2 * n + 2 * mask + half
        return pltpu.make_async_remote_copy(
            src_ref=piece, dst_ref=piece, send_sem=w_send.at[at], recv_sem=w_recv.at[at],
            device_id={"dp": owner(hop)}, device_id_type=pl.DeviceIdType.MESH,
        )

    def w_start(flow, mask=0):
        for half in halves(flow):
            for target in plan.onward(mask, half):
                w_copy(flow, target, half).start()

    def w_arrive(flow, masks):
        for mask in masks:
            for half in halves(flow):
                piece = slot(flow, owner(mask), half)
                at = flow * 2 * n + 2 * mask + half
                pltpu.make_async_remote_copy(
                    src_ref=piece, dst_ref=piece, send_sem=w_send.at[at], recv_sem=w_recv.at[at],
                    device_id={"dp": owner(plan.hop(mask, half))}, device_id_type=pl.DeviceIdType.MESH,
                ).wait_recv()
                for target in plan.onward(mask, half):
                    w_copy(flow, target, half).start()

    def chunk(flow, index):
        return (xs, cs)[flow].at[:, pl.ds(pl.multiple_of(index * rows, rows), rows), :]

    def z_copy(flow, step, up):
        piece = chunk(flow, place - (step - 1) if up else place + (step - 1))
        at = flow * line + step
        return pltpu.make_async_remote_copy(
            src_ref=piece, dst_ref=piece,
            send_sem=(up_send if up else down_send).at[at],
            recv_sem=(up_recv if up else down_recv).at[at],
            device_id={"tensor": place + 1 if up else place - 1}, device_id_type=pl.DeviceIdType.MESH,
        )

    def sends(step, up):
        if up:
            return (place < line - 1) & (place >= step - 1)
        return (place > 0) & (place + step - 1 <= line - 1)

    def z_start(flow, step):
        for up in (True, False):
            @pl.when(sends(step, up))
            def _():
                z_copy(flow, step, up).start()

    def z_arrive(flow, step):
        for up in (True, False):
            @pl.when(place >= step if up else place + step <= line - 1)
            def _():
                piece = chunk(flow, place - step if up else place + step)
                at = flow * line + step
                pltpu.make_async_remote_copy(
                    src_ref=piece, dst_ref=piece,
                    send_sem=(up_send if up else down_send).at[at],
                    recv_sem=(up_recv if up else down_recv).at[at],
                    device_id={"tensor": place - 1 if up else place + 1},
                    device_id_type=pl.DeviceIdType.MESH,
                ).wait_recv()
        if step + 1 < line:
            z_start(flow, step + 1)

    def z_sent(flow, step, up):
        @pl.when(sends(step, up))
        def _():
            z_copy(flow, step, up).wait_send()

    def cot_start(step):
        for up in (True, False):
            last = place == step - 1 if up else place == line - step
            @pl.when(last & sends(1, up))
            def _():
                z_copy(0, step, up).wait_send()
                z_copy(1, 1, up).start()

    def at_distance(step, fn):
        if step == 0:
            fn(place)
            return

        def side(j, carry):
            index = place - step + 2 * step * j

            @pl.when((index >= 0) & (index < line))
            def _():
                fn(index)
            return carry

        lax.fori_loop(0, 2, side, 0)

    def span(index):
        return pl.ds(pl.multiple_of(index * rows, rows), rows)

    outs = [
        (wa, wa_out), (wm, wm_out), (small, small_out), (sums, sums_out), (stats, stats_out), (cs, dh_out),
        (att, tiles_out.at[0]),
    ]
    for first, source in ((1, hidden), (1 + plan.n_mlp, slope)):
        outs = outs + [
            (source.at[:, pl.ds(r * local, local)], tiles_out.at[first + r]) for r in range(plan.n_mlp)
        ]
    outs = outs + [(source, tiles_out.at[1 + 2 * plan.n_mlp + r]) for r, source in enumerate((q, k, v))]
    hidden_at, da_at, qkv_at = (
        range(7, 7 + plan.n_mlp), range(7 + plan.n_mlp, 7 + 2 * plan.n_mlp), range(7 + 2 * plan.n_mlp, 10 + 2 * plan.n_mlp)
    )

    def out_copy(j):
        return pltpu.make_async_copy(outs[j][0], outs[j][1], out_sem.at[j])

    def write(*which):
        for j in which:
            out_copy(j).start()

    w_rows = pl.ds(pl.multiple_of(me * plan.in_rows, plan.in_rows), plan.in_rows)
    small_load = pltpu.make_async_copy(small_in, small.at[me], own_sem.at[2])

    stages = (k_sum, v_sum)

    def block_copies(i):
        source = w_in.at[i] if i < 3 + plan.n_mlp else wd_in.at[i - 3 - plan.n_mlp]
        height, wide_cols = source.shape
        strip = min(LANES, wide_cols)
        return [
            (
                g, strip, height,
                pltpu.make_async_copy(
                    source.at[:, pl.ds(g * strip, strip)],
                    stages[i % 2].at[pl.ds(g * height, height), pl.ds(0, strip)],
                    block_sem.at[i % 2, g],
                ),
            )
            for g in range(wide_cols // strip)
        ]

    def block_start(i):
        if i < 4 + 2 * plan.n_mlp:
            for part in block_copies(i):
                part[3].start()

    def round_blocks(first, stop, store):
        for i in range(first, stop):
            for g, strip, height, copy in block_copies(i):
                copy.wait()
                store(i - first, g * strip, strip, stages[i % 2][g * height : (g + 1) * height, :strip].astype(bf16))
            block_start(i + 2)

    def round_in(first, stop, target):
        def store(r, at, strip, value):
            target[w_rows, r * local + at : r * local + at + strip] = value

        round_blocks(first, stop, store)

    def round_down():
        def store(r, at, strip, value):
            wd[me, r * local : (r + 1) * local, at : at + strip] = value

        round_blocks(3 + plan.n_mlp, 4 + 2 * plan.n_mlp, store)

    strip_rows = min(32, rows)
    strip_count = rows // strip_rows

    def row_load(j):
        source = x_in if j < strip_count else out_grad_in
        first = j % strip_count * strip_rows
        return pltpu.make_async_copy(
            source.at[pl.ds(first, strip_rows), :], wide.at[j % 2], own_sem.at[j % 2]
        )

    row_load(0).start()
    row_load(1).start()
    small_load.start()
    block_start(0)
    block_start(1)
    table_loads = [
        pltpu.make_async_copy(place_cos, own, own_sem.at[3]), pltpu.make_async_copy(place_sin, sines, own_sem.at[4])
    ]
    for load in table_loads:
        load.start()
    barrier = pltpu.get_barrier_semaphore()
    for b in [1] + plan.bits if n > 1 else []:
        pl.semaphore_signal(barrier, inc=1, device_id={"dp": owner(b)}, device_id_type=pl.DeviceIdType.MESH)

    @pl.when(place < line - 1)
    def _():
        pl.semaphore_signal(barrier, inc=1, device_id={"tensor": place + 1}, device_id_type=pl.DeviceIdType.MESH)

    @pl.when(place > 0)
    def _():
        pl.semaphore_signal(barrier, inc=1, device_id={"tensor": place - 1}, device_id_type=pl.DeviceIdType.MESH)

    beside = (place + line - 1) // line + (2 * line - 2 - place) // line
    pl.semaphore_wait(barrier, (1 + len(plan.bits) if n > 1 else 0) + beside)

    def normalize_rows(index):
        at = span(index)
        for o in range(n):
            gain, shift = small[o, 0:1, LANES:].astype(f32), small[o, 1:2, LANES:].astype(f32)
            ns[0:rows, o * width : (o + 1) * width] = (xs[o, at, :].astype(f32) * gain + shift).astype(bf16)

    def bias_row(r, first, width):
        per = LANES // plan.bias_cols
        groups = []
        for g in range(first // LANES, (first + width) // LANES):
            total = small[g * per, r : r + 1, :LANES].astype(f32)
            for o in range(1, per):
                total = total + small[g * per + o, r : r + 1, :LANES].astype(f32)
            groups.append(total)
        return jnp.concatenate(groups, axis=1)

    def turn_rows(source, target, index):
        def staged(o):
            return ns.at[pl.ds(0, width), pl.ds(o % 2 * rows, rows)]

        def copy(o):
            return pltpu.make_async_copy(staged(o), target.at[o, :, span(index)], turn_sem.at[o % 2])

        for o in range(n):
            if o >= 2:
                copy(o - 2).wait()
            staged(o)[...] = source[o, span(index), :].T
            copy(o).start()
        for o in range(max(n - 2, 0), n):
            copy(o).wait()

    def attn_rows(index):
        at = span(index)
        turn_rows(xs, xhat_out, index)
        normalize_rows(index)
        for r, target in enumerate((q, k, v)):
            proj = dot_n(ns[0:rows, :], wa[:, r * local : (r + 1) * local]) + bias_row(r, 0, local)
            if r == 2:
                target[at, :] = proj.astype(bf16)
            else:
                for g in range(0, local, LANES):
                    target[at, g : g + LANES] = turn(
                        proj[:, g : g + LANES], own[at, :], sines[at, :], 1.0
                    ).astype(bf16)

    def mlp_rows(index):
        at = span(index)
        normalize_rows(index)
        for r in range(plan.n_mlp):
            cols = slice(r * local, (r + 1) * local)
            pre = dot_n(ns[0:rows, :], wm[:, cols]) + bias_row(3 + r, 0, local)
            value, grad = gelu_and_slope(pre)
            hidden[at, cols] = value.astype(bf16)
            slope[at, cols] = grad.astype(bf16)

    def attend(pair, carry):
        total = plan.group
        block = min(QUERY_ROWS, total)
        lanes = pl.ds(pl.multiple_of(pair * LANES, LANES), LANES)
        for start in range(0, total, block):
            stop = start + block
            here = pl.ds(start, block)
            allowed = attend_mask(begins_of(lengths, start, block), start, block, stop)
            query = q[here, lanes]
            results, logs = [], []
            for head in range(LANES // HEAD):
                mine = head_lanes(block, head)
                chosen = jnp.where(mine, query, jnp.zeros_like(query)) * HEAD ** (-0.5)
                scores = jnp.where(allowed, dot_t(chosen.astype(bf16), k[:stop, lanes]), masked_score)
                top = jnp.max(scores, axis=1, keepdims=True)
                weights = jnp.exp(scores - top)
                total_weight = jnp.sum(weights, axis=1, keepdims=True)
                results.append(dot_n(weights.astype(bf16), v[:stop, lanes]) / total_weight)
                logs.append(top + jnp.log(total_weight))
            first = head_lanes(block, 0)
            att[here, lanes] = jnp.where(first, results[0], results[1]).astype(bf16)
            which = lax.broadcasted_iota(jnp.int32, (block, LANES), 1)
            held = lse[here, :]
            for head in range(LANES // HEAD):
                held = jnp.where(which == pair * (LANES // HEAD) + head, logs[head], held)
            lse[here, :] = held
        return carry

    tall = min(512, plan.group)

    def out_tile(t):
        o = owner_of(t)

        def part(j, carry):
            at = pl.ds(pl.multiple_of(j * tall, tall), tall)
            total = dot_n(att[at, :], wd[o, :local, :]) + dot_n(hidden[at, :], wd[o, local:, :])
            xs[t, at, :] = total.astype(bf16)
            return carry

        lax.fori_loop(0, plan.group // tall, part, 0)

    def tile_source(t, index):
        return xs.at[t, span(index), :]

    def tile_landing(t, slot):
        return land.at[t, slot]

    out_sum = LineSum(
        place, line, tile_source, tile_landing, (sum_up_send, sum_up_recv, sum_down_send, sum_down_recv)
    )

    def all_tiles(fn):
        lax.fori_loop(0, plan.d_tiles, lambda t, carry: (fn(t), carry)[1], 0)

    def cot_rows(index):
        at = span(index)
        turn_rows(cs, cot_out, index)
        for o in range(n):
            sums[0:1, o * width : (o + 1) * width] += jnp.sum(cs[o, at, :].astype(f32), axis=0, keepdims=True)

    def back_rows(index):
        at = span(index)
        for r in range(1 + plan.n_mlp):
            grad = dot_t(cs[0, at, :], wd[0, r * local : (r + 1) * local, :])
            for o in range(1, n):
                grad = grad + dot_t(cs[o, at, :], wd[o, r * local : (r + 1) * local, :])
            if r == 0:
                att[at, :] = grad.astype(bf16)
            else:
                cols = slice((r - 1) * local, r * local)
                slope[at, cols] = (grad * slope[at, cols].astype(f32)).astype(bf16)

    def attend_back(pair, carry):
        block = min(QUERY_ROWS, plan.group)
        scale = HEAD ** (-0.5)
        k_sum[...] = jnp.zeros_like(k_sum)
        v_sum[...] = jnp.zeros_like(v_sum)
        lanes = pl.ds(pl.multiple_of(pair * LANES, LANES), LANES)
        which = lax.broadcasted_iota(jnp.int32, (block, LANES), 1)
        for start in range(0, plan.group, block):
            stop = start + block
            here = pl.ds(start, block)
            allowed = attend_mask(begins_of(lengths, start, block), start, block, stop)
            q_sum = jnp.zeros((block, LANES), f32)
            for head in range(LANES // HEAD):
                mine = head_lanes(block, head)
                query = jnp.where(mine, q[here, lanes], jnp.zeros((block, LANES), bf16)) * scale
                query = query.astype(bf16)
                cot = jnp.where(mine, att[here, lanes], jnp.zeros((block, LANES), bf16))
                level = jnp.sum(
                    jnp.where(which == pair * (LANES // HEAD) + head, lse[here, :], 0.0), axis=1, keepdims=True
                )
                scores = dot_t(query, k[:stop, lanes]) - level
                probs = jnp.where(allowed, jnp.exp(scores), 0.0)
                prob_grad = dot_t(cot, v[:stop, lanes])
                mean = jnp.sum(probs * prob_grad, axis=1, keepdims=True)
                score_grad = (probs * (prob_grad - mean)).astype(bf16)
                q_step = dot_n(score_grad, k[:stop, lanes])
                q_sum = jnp.where(mine, q_step * scale, q_sum)
                k_sum[:stop, :] += dot_s(score_grad, query)
                v_sum[:stop, :] += dot_s(probs.astype(bf16), cot)
            q[here, lanes] = turn(
                q_sum, own[here, :], sines[here, :], -1.0
            ).astype(bf16)
        k[:, lanes] = turn(k_sum[...], own[...], sines[...], -1.0).astype(bf16)
        v[:, lanes] = v_sum[...].astype(bf16)
        return carry

    def dh_tile(t):
        at = pl.ds(pl.multiple_of(t * width, width), width)
        total = dot_t(slope[...], wm[at, :])
        for r, grad in enumerate((q, k, v)):
            total = total + dot_t(grad[...], wa[at, r * local : (r + 1) * local])
        cs[t] = total.astype(bf16)

    def normalize_own():
        for j in range(strip_count):
            row_load(j).wait()
            at = slice(j * strip_rows, (j + 1) * strip_rows)
            value = wide[j % 2]
            mean = jnp.mean(value, axis=1, keepdims=True)
            centered = value - mean
            scale = lax.rsqrt(jnp.mean(centered * centered, axis=1, keepdims=True) + norm_eps)
            normed = (centered * scale).astype(bf16)
            to = pl.ds(pl.multiple_of(place * rows + j * strip_rows, strip_rows), strip_rows)
            for o in range(n):
                xs[o, to, :] = normed[:, o * width : (o + 1) * width]
            first = lax.broadcasted_iota(jnp.int32, (strip_rows, LANES), 1) == 0
            stats[at, :] = jnp.where(first, mean, scale)
            if j + 2 < 2 * strip_count:
                row_load(j + 2).start()

    def mask_cot():
        for j in range(strip_count, 2 * strip_count):
            row_load(j).wait()
            first = place * rows + (j - strip_count) * strip_rows
            places = first + lax.broadcasted_iota(jnp.int32, (strip_rows, 1), 0)
            masked = jnp.where(places < ends_of(lengths)[-1], wide[j % 2], 0.0).astype(bf16)
            to = pl.ds(pl.multiple_of(first, strip_rows), strip_rows)
            for o in range(n):
                cs[o, to, :] = masked[:, o * width : (o + 1) * width]
            if j + 2 < 2 * strip_count:
                row_load(j + 2).start()

    def make_tables():
        for load in table_loads:
            load.wait()
        block_rows = min(QUERY_ROWS, plan.group)
        ends = ends_of(lengths)
        at_ends = [pl.ds(jnp.minimum(end, plan.group - 1), 1) for end in ends]
        end_cosines, end_sines = [own[row, :] for row in at_ends], [sines[row, :] for row in at_ends]
        for start in range(0, plan.group, block_rows):
            at = pl.ds(start, block_rows)
            places = start + lax.broadcasted_iota(jnp.int32, (block_rows, LANES), 0)
            begin_cos, begin_sin = end_cosines[0], end_sines[0]
            for end, end_cos, end_sin in zip(ends[1:], end_cosines[1:], end_sines[1:]):
                begin_cos = jnp.where(places >= end, end_cos, begin_cos)
                begin_sin = jnp.where(places >= end, end_sin, begin_sin)
            place_c, place_s = own[at, :], sines[at, :]
            cosine = place_c * begin_cos + place_s * begin_sin
            sine = place_s * begin_cos - place_c * begin_sin
            lane = lax.rem(lax.broadcasted_iota(jnp.int32, (block_rows, LANES), 1), HEAD)
            own[at, :] = jnp.where(lane < ROT, cosine, 1.0)
            sines[at, :] = jnp.where(lane < ROT // 2, -sine, jnp.where(lane < ROT, sine, 0.0))

    def mixed_copy(t):
        cols = pl.ds(pl.multiple_of(owner_of(t) * width, width), width)
        return pltpu.make_async_copy(mixed.at[lax.rem(t, 2)], mixed_out.at[:, cols], mixed_sem.at[lax.rem(t, 2)])

    def finish_tile(t):
        @pl.when(t >= 2)
        def _():
            mixed_copy(t - 2).wait()
        out_sum.last(t, mixed.at[lax.rem(t, 2)])
        mixed_copy(t).start()

    small_load.wait()
    w_start(3)
    round_in(0, 3, wa)
    w_start(0)
    normalize_own()
    z_start(0, 1)
    round_in(3, 3 + plan.n_mlp, wm)
    mask_cot()
    round_down()
    make_tables()
    sums[...] = jnp.zeros_like(sums)
    lse[...] = jnp.zeros_like(lse)
    write(4)
    w_arrive(0, plan.single)
    w_start(1)
    w_arrive(3, plan.single)
    z_arrive(0, 1)
    cot_start(1)
    w_arrive(3, plan.several)
    w_arrive(0, plan.several)
    w_arrive(3, plan.odd)
    w_arrive(0, plan.odd)
    write(0, 2)
    at_distance(0, cot_rows)
    at_distance(0, attn_rows)
    if line > 2:
        at_distance(1, attn_rows)
    w_arrive(1, plan.single)
    w_start(2)
    for step in range(2, line - 1):
        z_arrive(0, step)
        cot_start(step)
        at_distance(step, attn_rows)
    w_arrive(1, plan.several)
    w_arrive(1, plan.odd)
    write(1)
    near = max(line - 2, 0)
    lax.fori_loop(
        jnp.maximum(place - near, 0), jnp.minimum(place + near, line - 1) + 1,
        lambda c, carry: (mlp_rows(c), carry)[1], 0,
    )
    w_arrive(2, plan.single)
    if line > 2:
        z_arrive(0, line - 1)
        cot_start(line - 1)
    at_distance(line - 1, lambda c: (attn_rows(c), mlp_rows(c))[0])
    write(*hidden_at)
    pairs = local // LANES
    lax.fori_loop(0, pairs // 2, attend, 0)
    w_arrive(2, plan.several)
    z_arrive(1, 1)
    lax.fori_loop(pairs // 2, pairs, attend, 0)
    write(6)
    if line > 2:
        at_distance(1, cot_rows)
    for step in range(1, line):
        for up in (True, False):
            left = place != step - 1 if up else place != line - step
            @pl.when(left & sends(step, up))
            def _():
                z_copy(0, step, up).wait_send()

    def some_tiles(first, stop):
        def step(t, carry):
            out_tile(t)
            out_sum.first(t)
            return carry

        lax.fori_loop(first, stop, step, 0)

    split = min(6, n)
    w_arrive(2, [m for m in plan.odd if m < 2])
    some_tiles(0, min(2, n))
    w_arrive(2, [m for m in plan.odd if 2 <= m < split])
    some_tiles(min(2, n), split)
    w_arrive(2, [m for m in plan.odd if m >= split])
    some_tiles(split, n)
    out_copy(6).wait()
    at_distance(0, back_rows)
    if line > 2:
        at_distance(1, back_rows)
    for step in range(2, line - 1):
        z_arrive(1, step)
        at_distance(step, lambda c: (cot_rows(c), back_rows(c))[0])

    def settle(near):
        for up in (True, False):
            now = (place < line // 2) if up == near else (place >= line // 2)

            @pl.when(now)
            def _():
                for step in range(1, line):
                    z_sent(1, step, up)

    quarter, count = plan.d_tiles // 4, plan.d_tiles
    settle(True)
    out_sum.one_way(0, quarter, True)
    if line > 2:
        z_arrive(1, line - 1)
    at_distance(line - 1, lambda c: (cot_rows(c), back_rows(c))[0])
    write(3, *da_at)
    settle(False)
    lax.fori_loop(0, pairs // 2, attend_back, 0)
    out_sum.one_way(quarter, 2 * quarter, True)
    out_sum.one_way(0, quarter, False)
    lax.fori_loop(pairs // 2, pairs, attend_back, 0)
    write(*qkv_at)
    out_sum.one_way(2 * quarter, 3 * quarter, True)
    out_sum.one_way(quarter, 2 * quarter, False)
    all_tiles(dh_tile)
    write(5)
    out_sum.one_way(3 * quarter, count, True)
    out_sum.one_way(2 * quarter, count, False)
    all_tiles(finish_tile)
    for t in range(max(count - 2, 0), count):
        mixed_copy(t).wait()

    all_tiles(out_sum.sent)
    for flow in range(4):
        for mask in range(1, n):
            for half in halves(flow):
                w_copy(flow, mask, half).wait_send()
    for j in range(len(outs)):
        if j != 6:
            out_copy(j).wait()


def forward(plan, x, out_grad, w, wd, small, lengths):
    any_space = pl.BlockSpec(memory_space=pl.ANY)
    n, line, group, model, local, rows = (
        plan.n_dp, plan.n_line, plan.group, plan.model, plan.local, plan.rows
    )
    low = lambda *shape: jax.ShapeDtypeStruct(shape, bf16)
    full = lambda *shape: jax.ShapeDtypeStruct(shape, f32)
    tiles = 4 + 2 * plan.n_mlp
    out_shape = [
        low(model, plan.attn), low(model, plan.mlp), low(n, 16, LANES + plan.out_cols),
        full(8, model), full(rows, LANES), low(n, group, plan.width), low(tiles, group, local),
        low(n, plan.width, group), low(n, plan.width, group), full(rows, model),
    ]
    act = pltpu.VMEM((n, group, plan.width), bf16)
    head = pltpu.VMEM((group, local), bf16)
    hide = pltpu.VMEM((group, plan.mlp), bf16)
    lane = pltpu.VMEM((group, LANES), f32)
    scratch = lambda s: pltpu.VMEM(s.shape, s.dtype)
    dma = pltpu.SemaphoreType.DMA
    return pl.pallas_call(
        partial(forward_kernel, plan),
        in_specs=[any_space] * 5 + [pl.BlockSpec(memory_space=pltpu.SMEM)] + [any_space] * 2,
        out_specs=[any_space] * 10,
        out_shape=out_shape,
        scratch_shapes=[scratch(s) for s in out_shape[:2]]
        + [pltpu.VMEM((n, plan.down, plan.out_cols), bf16), scratch(out_shape[2]), act]
        + [pltpu.VMEM((max(rows, plan.width), model), bf16), scratch(out_shape[3]), act, head, head, head, head, lane]
        + [hide, hide] + [lane] * 4 + [scratch(out_shape[4])]
        + [pltpu.VMEM((plan.d_tiles, line + 1, rows, plan.width), bf16)]
        + [
            pltpu.VMEM((2, min(32, rows), model), f32), pltpu.VMEM((2, rows, plan.width), f32),
        ]
        + [dma((2,)), dma((2,)), dma((5,)), dma((2, 4)), dma((6 + tiles,)), dma((8 * n,)), dma((8 * n,))]
        + [dma((2 * line,))] * 4
        + [dma((plan.d_tiles, line + 1))] * 4,
        compiler_params=pltpu.CompilerParams(
            collective_id=0, has_side_effects=True, vmem_limit_bytes=63 << 20
        ),
        cost_estimate=pl.CostEstimate(flops=60 * 10**9, bytes_accessed=80 << 20, transcendentals=0),
    )(x, out_grad, w, wd, small, lengths, *angle_tables(group))


def backward_kernel(
    plan,
    xhat_in, cot_in, tiles_in, dh_in, wa_in, wm_in, sums_in,
    down_out, in_out, small_out, rows_out, dh_out,
    turned, operand, dh, sent, core_in, held, cube_in, land,
    w_own, fin, fin_turned, dh_fin, small, small_in, shares,
    load_sem, turn_sem, operand_sem, fin_sem, dh_sem, core_send, core_recv, cube_send, cube_recv,
    up_send, up_recv, down_send, down_recv,
    small_send, small_recv, share_send, share_recv, credit,
):
    n, line = plan.n_dp, plan.n_line
    me, place = lax.axis_index("dp"), lax.axis_index("tensor")
    rows, local, group, model, in_rows = plan.rows, plan.local, plan.group, plan.model, plan.in_rows
    MESH = pl.DeviceIdType.MESH
    half_rows, pairs_n, n_bits = in_rows // 2, n // 2, len(plan.bits)
    orders = (plan.bits, plan.bits[::-1])
    n_down, n_mlp = 1 + plan.n_mlp, plan.n_mlp
    def owner(mask):
        index = me
        for b in [1] + plan.bits:
            if mask & b:
                index = index + b - 2 * b * lax.rem(index // b, 2)
        return index

    def peer(bit):
        return {"dp": owner(bit)}

    def position(mask, order):
        return sum((1 if mask & b else 0) << (n_bits - 1 - p) for p, b in enumerate(order))

    width, d_tiles = plan.width, plan.d_tiles
    own_rows = pl.ds(pl.multiple_of(me * in_rows, in_rows), in_rows)

    whole = [
        (dh_in, dh),
        (wa_in.at[own_rows, :], w_own.at[:, pl.ds(0, plan.attn)]),
        (wm_in.at[own_rows, :], w_own.at[:, pl.ds(plan.attn, plan.mlp)]),
    ]
    for j, (a, b) in enumerate(whole):
        pltpu.make_async_copy(a, b, load_sem.at[j]).start()

    def loaded(*which):
        for j in which:
            pltpu.make_async_copy(whole[j][0], whole[j][1], load_sem.at[j]).wait()

    barrier = pltpu.get_barrier_semaphore()
    for b in [1] + plan.bits:
        pl.semaphore_signal(barrier, inc=1, device_id=peer(b), device_id_type=MESH)
    for d in range(1, line):
        pl.semaphore_signal(
            barrier, inc=1, device_id={"tensor": lax.rem(place + d, line)}, device_id_type=MESH
        )

    def share_copy(d, arriving):
        source = lax.rem(place + line - d, line) if arriving else place
        return pltpu.make_async_remote_copy(
            src_ref=shares, dst_ref=rows_out.at[source],
            send_sem=share_send.at[d], recv_sem=share_recv.at[d],
            device_id={"tensor": lax.rem(place + d, line)}, device_id_type=MESH,
        )

    share_own = pltpu.make_async_copy(shares, rows_out.at[place], share_send.at[0])

    masks = [2 * j + 1 for j in range(pairs_n)] + [2 * j for j in range(pairs_n)]

    def turned_copy(source, j):
        return pltpu.make_async_copy(
            source.at[owner(masks[j])], turned.at[pl.ds(j * in_rows, in_rows), :], turn_sem.at[j]
        )

    def turned_start(source):
        for j in range(n):
            turned_copy(source, j).start()

    def turned_wait(source):
        for j in range(n):
            turned_copy(source, j).wait()

    tiles_n = n_down + n_mlp + 3

    def operand_copy(t):
        slot = lax.rem(t, 3)
        return pltpu.make_async_copy(tiles_in.at[t], operand.at[slot], operand_sem.at[slot])

    def core_copy(t, base):
        return pltpu.make_async_remote_copy(
            src_ref=sent.at[lax.rem(t, 2)], dst_ref=core_in.at[t - base],
            send_sem=core_send.at[lax.rem(t, 2)], recv_sem=core_recv.at[t - base],
            device_id=peer(1), device_id_type=MESH,
        )

    def cube_copy(slot, half, phase):
        count = pairs_n >> (phase + 1)
        first = pairs_n - 2 * count
        at = half * n_bits + phase
        return pltpu.make_async_remote_copy(
            src_ref=held.at[slot, half, pl.ds(count, count)],
            dst_ref=cube_in.at[slot, half, pl.ds(first, count)],
            send_sem=cube_send.at[slot, at], recv_sem=cube_recv.at[slot, at],
            device_id=peer(orders[half][phase]), device_id_type=MESH,
        )

    piece = min(2, pairs_n) * in_rows

    def send_core(t, base):
        @pl.when(t >= base + 2)
        def _():
            core_copy(t - 2, base).wait_send()
        slot = lax.rem(t, 3)
        for at in range(0, pairs_n * in_rows, piece):
            sent[lax.rem(t, 2), at : at + piece, :] = dot_n(turned[at : at + piece, :], operand[slot]).astype(bf16)
        core_copy(t, base).start()
        if base:
            row = lax.rem(t - base + 3, n_mlp + 3)
            small[0, pl.ds(row, 1), :] = jnp.sum(operand[slot].astype(f32), axis=0, keepdims=True)

    def keep_core(t, base):
        core_copy(t, base).wait_recv()
        for first in range(0, pairs_n * in_rows, piece):
            kept = pairs_n * in_rows + first
            total = dot_n(turned[kept : kept + piece, :], operand[lax.rem(t, 3)])
            total = total + core_in[t - base, first : first + piece, :].astype(f32)
            for at in range(0, piece, half_rows):
                j, half = divmod((first + at) // half_rows, 2)
                held[t, half, position(2 * j, orders[half])] = total[at : at + half_rows].astype(bf16)
        for half in range(2):
            if n_bits:
                cube_copy(t, half, 0).start()

    def scatter(base, stop):
        def step(t, carry):
            operand_copy(t).wait()

            @pl.when(t + 1 < tiles_n)
            def _():
                operand_copy(t + 1).start()
            send_core(t, base)

            @pl.when(t >= base + 1)
            def _():
                keep_core(t - 1, base)
            return carry

        lax.fori_loop(base, stop, step, 0)
        keep_core(stop - 1, base)
        for t in range(max(stop - 2, base), stop):
            core_copy(t, base).wait_send()

    def cube_step(base, stop, phase):
        count = pairs_n >> (phase + 1)
        first = pairs_n - 2 * count
        down = base == 0
        depth = 1 if down else 2

        def result(t):
            return t if down else lax.rem(t - n_down + 3, n_mlp + 3)

        def fin_copy(t):
            source = fin_turned if down else fin.at[lax.rem(t, 2)]
            target = down_out if down else in_out
            return pltpu.make_async_copy(source, target.at[result(t)], fin_sem.at[lax.rem(t, 2)])

        def step(t, carry):
            slot = t
            if phase == n_bits - 1:
                @pl.when(t >= base + depth)
                def _():
                    fin_copy(t - depth).wait()
            for half in range(2):
                cube_copy(slot, half, phase).wait_recv()
                total = (
                    held[slot, half, 0:count].astype(f32)
                    + cube_in[slot, half, first : first + count].astype(f32)
                )
                if phase < n_bits - 1:
                    held[slot, half, 0:count] = total.astype(bf16)
                    cube_copy(slot, half, phase + 1).start()
                else:
                    fin[lax.rem(t, 2), half * half_rows : (half + 1) * half_rows, :] = total[0]
            if phase == n_bits - 1:
                if down:
                    fin_turned[...] = fin[lax.rem(t, 2)].T
                fin_copy(t).start()
                if not down:
                    weight = w_own[:, pl.ds(pl.multiple_of(result(t) * local, local), local)].astype(f32)
                    product = weight * fin[lax.rem(t, 2)]
                    extra = weight * small[n_bits + 1, pl.ds(result(t), 1), :]
                    for g in range(0, local, LANES):
                        shares[0] += product[:, g : g + LANES]
                        shares[1] += extra[:, g : g + LANES]
            return carry

        lax.fori_loop(base, stop, step, 0)
        if phase == n_bits - 1:
            for t in range(max(stop - depth, base), stop):
                fin_copy(t).wait()

    def cube_sent(t):
        for half in range(2):
            for phase in range(n_bits):
                cube_copy(t, half, phase).wait_send()

    def tile_of(buffer):
        def source(t, index):
            return buffer.at[t, pl.ds(pl.multiple_of(index * rows, rows), rows), :]
        return source

    dh_sum = LineSum(
        place, line, tile_of(dh), lambda t, slot: land.at[t, slot],
        (up_send, up_recv, down_send, down_recv),
    )
    def sum_copy(target, t):
        cols = pl.ds(pl.multiple_of(t * width, width), width)
        return pltpu.make_async_copy(dh_fin.at[lax.rem(t, 2)], target.at[:, cols], dh_sem.at[lax.rem(t, 2)])

    def finish(flow, target, count):
        def step(t):
            @pl.when(t >= 2)
            def _():
                sum_copy(target, t - 2).wait()
            flow.last(t, dh_fin.at[lax.rem(t, 2)])
            sum_copy(target, t).start()

        tiles(0, count, step)
        for t in range(max(count - 2, 0), count):
            sum_copy(target, t).wait()

    def tiles(first, stop, fn):
        lax.fori_loop(first, stop, lambda t, carry: (fn(t), carry)[1], 0)

    def small_copy(j):
        return pltpu.make_async_remote_copy(
            src_ref=small.at[j], dst_ref=small_in.at[j],
            send_sem=small_send.at[j], recv_sem=small_recv.at[j],
            device_id=peer(([1] + plan.bits)[j]), device_id_type=MESH,
        )

    def small_step(j):
        small_copy(j).wait_recv()
        small[j + 1] = small[j] + small_in[j]
        if j < n_bits:
            small_copy(j + 1).start()

    turned_start(cot_in)
    operand_copy(0).start()
    shares[...] = jnp.zeros_like(shares)
    small[0] = jnp.zeros_like(small[0])
    for r in range(model // local):
        small[0, 8 + r : 9 + r, :] = sums_in[0:1, r * local : (r + 1) * local]
    pl.semaphore_wait(barrier, 1 + n_bits + line - 1)
    loaded(0)
    tiles(0, d_tiles, dh_sum.first)
    turned_wait(cot_in)
    quarter = d_tiles // 4
    scatter(0, n_down)
    pl.semaphore_signal(credit, inc=1, device_id=peer(1), device_id_type=MESH)
    turned_start(xhat_in)
    dh_sum.one_way(0, quarter, True)
    turned_wait(xhat_in)
    pl.semaphore_wait(credit, 1)
    scatter(n_down, tiles_n)
    small_copy(0).start()
    dh_sum.one_way(quarter, 2 * quarter, True)
    dh_sum.one_way(0, quarter, False)
    for phase in range(n_bits - 1):
        cube_step(0, n_down, phase)
    small_step(0)
    dh_sum.one_way(2 * quarter, 3 * quarter, True)
    dh_sum.one_way(quarter, 2 * quarter, False)
    for j in range(1, n_bits + 1):
        small_step(j)
    loaded(1, 2)
    for phase in range(n_bits - 1):
        cube_step(n_down, n_down + n_mlp, phase)
    dh_sum.one_way(3 * quarter, d_tiles, True)
    dh_sum.one_way(2 * quarter, 3 * quarter, False)
    cube_step(0, n_down, n_bits - 1)
    dh_sum.one_way(3 * quarter, d_tiles, False)
    for phase in range(n_bits - 1):
        cube_step(n_down + n_mlp, tiles_n, phase)
    finish(dh_sum, dh_out, d_tiles)
    cube_step(n_down, n_down + n_mlp, n_bits - 1)
    cube_step(n_down + n_mlp, tiles_n, n_bits - 1)
    share_own.start()
    for d in range(1, line):
        share_copy(d, False).start()
    small_done = pltpu.make_async_copy(small.at[n_bits + 1], small_out, load_sem.at[0])
    small_done.start()
    tiles(0, tiles_n, cube_sent)
    tiles(0, d_tiles, dh_sum.sent)
    for j in range(n_bits + 1):
        small_copy(j).wait_send()
    share_own.wait()
    for d in range(1, line):
        share_copy(d, False).wait_send()
        share_copy(d, True).wait_recv()
    small_done.wait()


def backward(plan, xhat, cot, tiles, dh, wa, wm, sums):
    any_space = pl.BlockSpec(memory_space=pl.ANY)
    vmem = pl.BlockSpec(memory_space=pltpu.VMEM)
    n, line, group, model, local = plan.n_dp, plan.n_line, plan.group, plan.model, plan.local
    rows, in_rows, n_bits, pairs_n = plan.rows, plan.in_rows, len(plan.bits), n // 2
    n_down = 1 + plan.n_mlp
    small_rows = 8 + -(-(model // local) // 8) * 8
    width, d_tiles = plan.width, plan.d_tiles
    low = lambda *shape: pltpu.VMEM(shape, bf16)
    full = lambda *shape: pltpu.VMEM(shape, f32)
    dma = pltpu.SemaphoreType.DMA
    out = lambda dtype, *shape: jax.ShapeDtypeStruct(shape, dtype)
    slots = n_down + plan.n_mlp + 3
    return pl.pallas_call(
        partial(backward_kernel, plan),
        in_specs=[any_space] * 6 + [vmem],
        out_specs=[any_space] * 5,
        out_shape=[
            out(f32, n_down, local, in_rows), out(f32, 3 + plan.n_mlp, in_rows, local),
            out(f32, small_rows, local),
            out(f32, line, 2, in_rows, LANES), out(f32, rows, model),
        ],
        scratch_shapes=[
            low(n * in_rows, group), low(3, group, local), low(d_tiles, group, width),
            low(2, pairs_n * in_rows, local), low(3 + plan.n_mlp, pairs_n * in_rows, local),
            low(slots, 2, pairs_n, in_rows // 2, local), low(slots, 2, max(pairs_n - 1, 1), in_rows // 2, local),
            low(d_tiles, line + 1, rows, width),
            low(in_rows, plan.attn + plan.mlp), full(2, in_rows, local), full(local, in_rows), full(2, rows, width),
            full(n_bits + 2, small_rows, local), full(n_bits + 1, small_rows, local), full(2, in_rows, LANES),
            dma((3,)), dma((n,)), dma((3,)), dma((2,)), dma((2,)), dma((2,)), dma((3 + plan.n_mlp,)),
            dma((slots, max(2 * n_bits, 1))), dma((slots, max(2 * n_bits, 1))),
            dma((d_tiles, line + 1)), dma((d_tiles, line + 1)), dma((d_tiles, line + 1)), dma((d_tiles, line + 1)),
            dma((n_bits + 1,)), dma((n_bits + 1,)), dma((line,)), dma((line,)),
            pltpu.SemaphoreType.REGULAR,
        ],
        compiler_params=pltpu.CompilerParams(
            collective_id=1, has_side_effects=True, vmem_limit_bytes=63 << 20
        ),
        cost_estimate=pl.CostEstimate(flops=80 * 10**9, bytes_accessed=80 << 20, transcendentals=0),
    )(xhat, cot, tiles, dh, wa, wm, sums)


def adam_update(weight, moment_one, moment_two, gradient, step_rate, decay_factor):
    first_new = beta_first * moment_one + (1.0 - beta_first) * gradient
    second_new = beta_second * moment_two + (1.0 - beta_second) * gradient * gradient
    corrected = first_new / (1.0 - beta_first**STEP)
    spread = jnp.sqrt(second_new / (1.0 - beta_second**STEP))
    return (
        weight - step_rate * (corrected / (spread + adam_eps) + decay_factor * weight),
        first_new,
        second_new,
    )


def per_device(
    block_input,
    out_grad,
    seq_lengths,
    in_weight,
    down_weight,
    column_bias,
    vector_params,
    in_first,
    in_second,
    down_first,
    down_second,
    bias_first,
    bias_second,
    vector_first,
    vector_second,
):
    n_dp = lax.axis_size("dp")
    n_tensor = lax.axis_size("tensor")
    own_rows, model = block_input.shape
    group = own_rows * n_tensor
    in_rows, widths, local = in_weight.shape
    out_cols = down_weight.shape[2]
    n_mlp = widths - 3
    attn_width, mlp_width = 3 * local, n_mlp * local

    me = lax.axis_index("dp")
    plan = Plan(n_dp, n_tensor, own_rows, model, in_rows, local, n_mlp, out_cols)
    share = LANES // plan.bias_cols
    lane = lax.broadcasted_iota(jnp.int32, (widths, LANES), 1) // plan.bias_cols
    bias_tile = jnp.where(lane == lax.rem(me, share), jnp.tile(column_bias, (1, share)), 0.0)
    small = jnp.concatenate(
        [jnp.pad(bias_tile, ((0, 16 - widths), (0, 0))), jnp.pad(vector_params, ((0, 13), (0, 0)))], axis=1
    ).astype(bf16)
    (
        w_attn, w_mlp, vectors, cot_sums, stats, dh_part, tiles, xhat_turned, cot_turned, mixed,
    ) = forward(plan, block_input, out_grad, in_weight.transpose(1, 0, 2), down_weight, small, seq_lengths)
    down_grad, in_grad, small_grad, shares, dh = backward(
        plan, xhat_turned, cot_turned, tiles, dh_part, w_attn, w_mlp, cot_sums
    )
    vector_vals = vectors[:, :3, LANES:].transpose(1, 0, 2).reshape(3, model).astype(f32)
    gain, out_bias = vector_vals[0], vector_vals[2]
    block_out = block_input + (mixed + out_bias)
    mean, inv_scale = stats[:, :1], stats[:, 1:2]
    xhat = (block_input - mean) * inv_scale
    places = lax.axis_index("tensor") * own_rows + lax.broadcasted_iota(jnp.int32, (own_rows, 1), 0)
    cot_live = jnp.where(places < jnp.sum(seq_lengths), out_grad, 0.0)

    dxhat = dh * gain
    input_grad = cot_live + inv_scale * (
        dxhat
        - jnp.mean(dxhat, axis=-1, keepdims=True)
        - xhat * jnp.mean(dxhat * xhat, axis=-1, keepdims=True)
    )

    bias_full = small_grad[:widths]
    own_vectors = vector_params.astype(bf16).astype(f32)
    in_reduced = (
        in_grad * own_vectors[0][None, :, None] + own_vectors[1][None, :, None] * bias_full[:, None, :]
    ).transpose(1, 0, 2)
    down_reduced = down_grad
    bias_reduced = lax.dynamic_slice_in_dim(bias_full, me * plan.bias_cols, plan.bias_cols, 1)
    out_sums = small_grad[8 : 8 + model // local].reshape(-1)
    vector_reduced = jnp.stack(
        [
            jnp.sum(shares[:, 0], axis=(0, 2)),
            jnp.sum(shares[:, 1], axis=(0, 2)),
            lax.dynamic_slice_in_dim(out_sums, me * out_cols, out_cols, 0),
        ]
    )

    in_new, in_one, in_two = adam_update(
        in_weight, in_first, in_second, in_reduced, rate_in, weight_decay
    )
    down_new, down_one, down_two = adam_update(
        down_weight, down_first, down_second, down_reduced, rate_down, weight_decay
    )
    bias_new, bias_one, bias_two = adam_update(
        column_bias, bias_first, bias_second, bias_reduced, rate_vector, 0.0
    )
    vector_new, vector_one, vector_two = adam_update(
        vector_params, vector_first, vector_second, vector_reduced, rate_vector, 0.0
    )
    return (
        block_out,
        input_grad,
        in_new,
        in_one,
        in_two,
        down_new,
        down_one,
        down_two,
        bias_new,
        bias_one,
        bias_two,
        vector_new,
        vector_one,
        vector_two,
    )


def widths_down(down_weight):
    return down_weight.shape[0] * down_weight.shape[1]


def solution(mesh):
    return jax.shard_map(
        per_device,
        mesh=mesh,
        in_specs=(
            P(("dp", "tensor"), None),
            P(("dp", "tensor"), None),
            P("dp", None),
            P("dp", None, "tensor"),
            P(None, "tensor", "dp"),
            P(None, ("tensor", "dp")),
            P(None, "dp"),
            P("dp", None, "tensor"),
            P("dp", None, "tensor"),
            P(None, "tensor", "dp"),
            P(None, "tensor", "dp"),
            P(None, ("tensor", "dp")),
            P(None, ("tensor", "dp")),
            P(None, "dp"),
            P(None, "dp"),
        ),
        out_specs=(
            P(("dp", "tensor"), None),
            P(("dp", "tensor"), None),
            P("dp", None, "tensor"),
            P("dp", None, "tensor"),
            P("dp", None, "tensor"),
            P(None, "tensor", "dp"),
            P(None, "tensor", "dp"),
            P(None, "tensor", "dp"),
            P(None, ("tensor", "dp")),
            P(None, ("tensor", "dp")),
            P(None, ("tensor", "dp")),
            P(None, "dp"),
            P(None, "dp"),
            P(None, "dp"),
        ),
        check_vma=False,
    )
```

```python
from functools import partial

import jax
import jax.numpy as jnp
import numpy as np
from jax import lax
from jax.experimental import pallas as pl
from jax.experimental.pallas import tpu as pltpu
from jax.sharding import PartitionSpec as P

HEAD = 64
ROT = 32
STEP = 8
LANES = 128
QUERY_ROWS = 256

norm_eps = 1e-05
beta_first = 0.9
beta_second = 0.95
adam_eps = 1e-08
masked_score = -1000000000.0
rate_in = 0.02
rate_down = 0.05
rate_vector = 0.2
weight_decay = 0.1

bf16 = jnp.bfloat16
f32 = jnp.float32


def angle_tables(rows):
    half_rot = ROT // 2
    frequency = 10000.0 ** (-2.0 * (np.arange(LANES) % half_rot) / ROT)
    angles = np.arange(rows)[:, None] * frequency[None, :]
    return np.cos(angles).astype(np.float32), np.sin(angles).astype(np.float32)


def ends_of(lengths):
    ends = [jnp.int32(0)]
    for j in range(lengths.shape[1]):
        ends.append(ends[-1] + lengths[0, j])
    return ends


def begins_of(lengths, start, rows):
    places = start + lax.broadcasted_iota(jnp.int32, (rows, 1), 0)
    begin = jnp.zeros((rows, 1), jnp.int32)
    for end in ends_of(lengths)[1:]:
        begin = jnp.where(places >= end, end, begin)
    return begin


def attend_mask(begin, row_start, rows, stop):
    key_place = lax.broadcasted_iota(jnp.int32, (rows, stop), 1)
    query_place = row_start + lax.broadcasted_iota(jnp.int32, (rows, stop), 0)
    return (key_place <= query_place) & (key_place >= begin)


def head_lanes(rows, head):
    lane = lax.broadcasted_iota(jnp.int32, (rows, LANES), 1)
    return (lane >= head * HEAD) & (lane < (head + 1) * HEAD)


def dot_t(a, b):
    return lax.dot_general(a, b, (((1,), (1,)), ((), ())), preferred_element_type=f32)


def dot_n(a, b):
    return lax.dot_general(a, b, (((1,), (0,)), ((), ())), preferred_element_type=f32)


def dot_s(a, b):
    return lax.dot_general(a, b, (((0,), (0,)), ((), ())), preferred_element_type=f32)


def turn(x, own, sines, sign):
    half = ROT // 2
    lane = lax.rem(lax.broadcasted_iota(jnp.int32, x.shape, 1), HEAD)
    other = jnp.where(lane < half, pltpu.roll(x, LANES - half, 1), pltpu.roll(x, half, 1))
    return x * own + sign * (other * sines)


def low_bit(mask):
    return mask & -mask


def high_bit(mask):
    return 1 << (mask.bit_length() - 1)


def gelu_and_slope(a):
    root = (2.0 / 3.141592653589793) ** 0.5
    square = a * a
    t = jnp.tanh(root * a * (1.0 + 0.044715 * square))
    half = 0.5 * (1.0 + t)
    return a * half, half + 0.5 * a * (1.0 - t * t) * (root * (1.0 + 3.0 * 0.044715 * square))


class LineSum:
    depth, near_lag, far_lag = 2, 2, 5

    def __init__(self, place, line, count, source, landing, sems):
        self.place, self.line, self.count = place, line, count
        self.source, self.landing = source, landing
        self.done = 0
        self.up_send, self.up_recv, self.down_send, self.down_recv = sems

    def copy(self, t, index, up, arriving=False):
        place = self.place
        slot = self.slot(index, up)
        return pltpu.make_async_remote_copy(
            src_ref=self.source(t, index),
            dst_ref=self.landing(t, slot),
            send_sem=(self.up_send if up else self.down_send).at[t, slot],
            recv_sem=(self.up_recv if up else self.down_recv).at[t, slot],
            device_id={"tensor": place + 1 if up != arriving else place - 1},
            device_id_type=pl.DeviceIdType.MESH,
        )

    def got(self, t, index, up):
        return self.landing(t, self.slot(index, up))[...].astype(f32)

    def slot(self, index, up):
        return index - 1 if up else lax.rem(self.line - 1 + index, self.line + 1)

    def start_messages(self, t, up):
        for step in range(self.line - 1):
            self.copy(t, self.line - 1 - step if up else step, up).start()

    def wait_messages(self, t, up):
        for step in range(self.line - 1):
            self.copy(t, self.line - 1 - step if up else step, up).wait_send()

    def step(self, k):
        far_up = 2 * self.place // self.line
        for up in (True, False):
            end = (self.place == 0) if up else (self.place == self.line - 1)

            @pl.when(end & (k >= self.depth) & (k < self.count))
            def _():
                self.wait_messages(k - self.depth, up)

            @pl.when(end & (k < self.count))
            def _():
                self.start_messages(k, up)

            far = far_up if up else 1 - far_up
            t = k - self.near_lag - (self.far_lag - self.near_lag) * far

            @pl.when((t >= 0) & (t < self.count))
            def _():
                self.hand_on(t, up)

    def take(self, count):
        first = self.done
        self.done = min(first + count, self.count + self.far_lag)
        return first

    def advance(self, count):
        first = self.take(count)
        lax.fori_loop(first, self.done, lambda k, carry: (self.step(k), carry)[1], 0)

    def finish_steps(self):
        self.advance(self.count + self.far_lag)

    def hand_on(self, t, up):
        place, line = self.place, self.line
        for step in range(line - 1):
            index = line - 1 - step if up else step
            hears = (place > 0) & (place < index) if up else (place < line - 1) & (place > index)

            @pl.when(hears)
            def _():
                self.copy(t, index, up, True).wait_recv()
                mine = self.source(t, index)
                mine[...] = (mine[...].astype(f32) + self.got(t, index, up)).astype(bf16)
                self.copy(t, index, up).start()

    def last(self, t, target):
        place, line = self.place, self.line
        target[...] = self.source(t, place)[...].astype(f32)
        for up in (True, False):
            @pl.when((place > 0) if up else (place < line - 1))
            def _():
                self.copy(t, place, up, True).wait_recv()
                target[...] += self.got(t, place, up)

    def sent(self, t):
        line, place = self.line, self.place
        waited = t < self.count - self.depth
        for index in range(line):
            for up in (True, False):
                goes = (place < index) if up else (place > index)
                end = (place == 0) if up else (place == line - 1)

                @pl.when(goes & jnp.logical_not(end & waited))
                def _():
                    self.copy(t, index, up).wait_send()


class Plan:
    def __init__(self, n_dp, n_line, rows, model, in_rows, local, n_mlp, out_cols):
        self.n_dp, self.n_line = n_dp, n_line
        self.rows, self.model = rows, model
        self.group = rows * n_line
        self.in_rows, self.local, self.n_mlp, self.out_cols = in_rows, local, n_mlp, out_cols
        self.attn, self.mlp = 3 * local, n_mlp * local
        self.down = (1 + n_mlp) * local
        self.bias_cols = local // n_dp
        self.width = out_cols
        self.d_tiles = model // out_cols
        self.bits = [1 << b for b in range(1, n_dp.bit_length() - 1)]
        even = range(2, n_dp, 2)
        self.single = [m for m in even if m.bit_count() == 1]
        self.several = sorted((m for m in even if m.bit_count() > 1), key=lambda m: m.bit_count())
        self.odd = list(range(1, n_dp, 2))

    def hop(self, mask, half):
        if mask & 1:
            return 1
        return high_bit(mask) if half == 0 else low_bit(mask)

    def onward(self, mask, half):
        if mask & 1:
            return []
        masks = [mask | 1] if self.n_dp > 1 else []
        return masks + [
            mask | b for b in self.bits if not mask & b and self.hop(mask | b, half) == b
        ]


def forward_kernel(
    plan,
    x_in, out_grad_in, w_in, wd_in, small_in, lengths, place_cos, place_sin,
    wa_out, wm_out, small_out, sums_out, stats_out, dh_out, tiles_out, xhat_out, cot_out, mixed_out,
    wa, wm, wd, small, xs, ns, sums, cs, q, k, v, att, lse, hidden, slope, k_sum, v_sum,
    own, sines, stats, land, wide, mixed,
    turn_sem, mixed_sem, own_sem, block_sem, out_sem, w_send, w_recv, up_send, up_recv, down_send, down_recv,
    sum_up_send, sum_up_recv, sum_down_send, sum_down_recv,
):
    n, line = plan.n_dp, plan.n_line
    me, place = lax.axis_index("dp"), lax.axis_index("tensor")
    rows, local, model, width = plan.rows, plan.local, plan.model, plan.width

    def owner(mask):
        index = me
        for b in [1] + plan.bits:
            if mask & b:
                index = index + b - 2 * b * lax.rem(index // b, 2)
        return index

    def owner_of(j):
        index = 0
        for b in [1] + plan.bits:
            index = index + b * lax.rem(me // b + j // b, 2)
        return index

    def slot(flow, index, half):
        if flow < 2:
            step = plan.in_rows // 2
            at = pl.multiple_of(index * plan.in_rows + half * step, step)
            return (wa, wm)[flow].at[pl.ds(at, step), :]
        if flow == 2:
            step = plan.down // 2
            return wd.at[index, pl.ds(half * step, step), :]
        return small.at[index]

    def halves(flow):
        return (0,) if flow == 3 else (0, 1)

    def w_copy(flow, mask, half):
        hop = plan.hop(mask, half)
        piece = slot(flow, owner(mask ^ hop), half)
        at = flow * 2 * n + 2 * mask + half
        return pltpu.make_async_remote_copy(
            src_ref=piece, dst_ref=piece, send_sem=w_send.at[at], recv_sem=w_recv.at[at],
            device_id={"dp": owner(hop)}, device_id_type=pl.DeviceIdType.MESH,
        )

    def w_start(flow, mask=0):
        for half in halves(flow):
            for target in plan.onward(mask, half):
                w_copy(flow, target, half).start()

    def w_arrive(flow, masks):
        for mask in masks:
            for half in halves(flow):
                piece = slot(flow, owner(mask), half)
                at = flow * 2 * n + 2 * mask + half
                pltpu.make_async_remote_copy(
                    src_ref=piece, dst_ref=piece, send_sem=w_send.at[at], recv_sem=w_recv.at[at],
                    device_id={"dp": owner(plan.hop(mask, half))}, device_id_type=pl.DeviceIdType.MESH,
                ).wait_recv()
                for target in plan.onward(mask, half):
                    w_copy(flow, target, half).start()

    def chunk(flow, index):
        return (xs, cs)[flow].at[:, pl.ds(pl.multiple_of(index * rows, rows), rows), :]

    def z_copy(flow, step, up):
        piece = chunk(flow, place - (step - 1) if up else place + (step - 1))
        at = flow * line + step
        return pltpu.make_async_remote_copy(
            src_ref=piece, dst_ref=piece,
            send_sem=(up_send if up else down_send).at[at],
            recv_sem=(up_recv if up else down_recv).at[at],
            device_id={"tensor": place + 1 if up else place - 1}, device_id_type=pl.DeviceIdType.MESH,
        )

    def sends(step, up):
        if up:
            return (place < line - 1) & (place >= step - 1)
        return (place > 0) & (place + step - 1 <= line - 1)

    def z_start(flow, step):
        for up in (True, False):
            @pl.when(sends(step, up))
            def _():
                z_copy(flow, step, up).start()

    def z_arrive(flow, step):
        for up in (True, False):
            @pl.when(place >= step if up else place + step <= line - 1)
            def _():
                piece = chunk(flow, place - step if up else place + step)
                at = flow * line + step
                pltpu.make_async_remote_copy(
                    src_ref=piece, dst_ref=piece,
                    send_sem=(up_send if up else down_send).at[at],
                    recv_sem=(up_recv if up else down_recv).at[at],
                    device_id={"tensor": place - 1 if up else place + 1},
                    device_id_type=pl.DeviceIdType.MESH,
                ).wait_recv()
        if step + 1 < line:
            z_start(flow, step + 1)

    def z_sent(flow, step, up):
        @pl.when(sends(step, up))
        def _():
            z_copy(flow, step, up).wait_send()

    def cot_start(step):
        for up in (True, False):
            last = place == step - 1 if up else place == line - step
            @pl.when(last & sends(1, up))
            def _():
                z_copy(0, step, up).wait_send()
                z_copy(1, 1, up).start()

    def at_distance(step, fn):
        if step == 0:
            fn(place)
            return

        def side(j, carry):
            index = place - step + 2 * step * j

            @pl.when((index >= 0) & (index < line))
            def _():
                fn(index)
            return carry

        lax.fori_loop(0, 2, side, 0)

    def span(index):
        return pl.ds(pl.multiple_of(index * rows, rows), rows)

    outs = [
        (wa, wa_out), (wm, wm_out), (small, small_out), (sums, sums_out), (stats, stats_out), (cs, dh_out),
        (att, tiles_out.at[0]),
    ]
    for first, source in ((1, hidden), (1 + plan.n_mlp, slope)):
        outs = outs + [
            (source.at[:, pl.ds(r * local, local)], tiles_out.at[first + r]) for r in range(plan.n_mlp)
        ]
    outs = outs + [(source, tiles_out.at[1 + 2 * plan.n_mlp + r]) for r, source in enumerate((q, k, v))]
    hidden_at, da_at, qkv_at = (
        range(7, 7 + plan.n_mlp), range(7 + plan.n_mlp, 7 + 2 * plan.n_mlp), range(7 + 2 * plan.n_mlp, 10 + 2 * plan.n_mlp)
    )

    def out_copy(j):
        return pltpu.make_async_copy(outs[j][0], outs[j][1], out_sem.at[j])

    def write(*which):
        for j in which:
            out_copy(j).start()

    w_rows = pl.ds(pl.multiple_of(me * plan.in_rows, plan.in_rows), plan.in_rows)
    small_load = pltpu.make_async_copy(small_in, small.at[me], own_sem.at[2])

    stages = (k_sum, v_sum)

    def block_copies(i):
        source = w_in.at[i] if i < 3 + plan.n_mlp else wd_in.at[i - 3 - plan.n_mlp]
        height, wide_cols = source.shape
        strip = min(LANES, wide_cols)
        return [
            (
                g, strip, height,
                pltpu.make_async_copy(
                    source.at[:, pl.ds(g * strip, strip)],
                    stages[i % 2].at[pl.ds(g * height, height), pl.ds(0, strip)],
                    block_sem.at[i % 2, g],
                ),
            )
            for g in range(wide_cols // strip)
        ]

    def block_start(i):
        if i < 4 + 2 * plan.n_mlp:
            for part in block_copies(i):
                part[3].start()

    def round_blocks(first, stop, store):
        for i in range(first, stop):
            for g, strip, height, copy in block_copies(i):
                copy.wait()
                store(i - first, g * strip, strip, stages[i % 2][g * height : (g + 1) * height, :strip].astype(bf16))
            block_start(i + 2)

    def round_in(first, stop, target):
        def store(r, at, strip, value):
            target[w_rows, r * local + at : r * local + at + strip] = value

        round_blocks(first, stop, store)

    def round_down():
        def store(r, at, strip, value):
            wd[me, r * local : (r + 1) * local, at : at + strip] = value

        round_blocks(3 + plan.n_mlp, 4 + 2 * plan.n_mlp, store)

    strip_rows = min(32, rows)
    strip_count = rows // strip_rows

    def row_load(j):
        source = x_in if j < strip_count else out_grad_in
        first = j % strip_count * strip_rows
        return pltpu.make_async_copy(
            source.at[pl.ds(first, strip_rows), :], wide.at[j % 2], own_sem.at[j % 2]
        )

    row_load(0).start()
    row_load(1).start()
    small_load.start()
    block_start(0)
    block_start(1)
    table_loads = [
        pltpu.make_async_copy(place_cos, own, own_sem.at[3]), pltpu.make_async_copy(place_sin, sines, own_sem.at[4])
    ]
    for load in table_loads:
        load.start()
    barrier = pltpu.get_barrier_semaphore()
    for b in [1] + plan.bits if n > 1 else []:
        pl.semaphore_signal(barrier, inc=1, device_id={"dp": owner(b)}, device_id_type=pl.DeviceIdType.MESH)

    @pl.when(place < line - 1)
    def _():
        pl.semaphore_signal(barrier, inc=1, device_id={"tensor": place + 1}, device_id_type=pl.DeviceIdType.MESH)

    @pl.when(place > 0)
    def _():
        pl.semaphore_signal(barrier, inc=1, device_id={"tensor": place - 1}, device_id_type=pl.DeviceIdType.MESH)

    beside = (place + line - 1) // line + (2 * line - 2 - place) // line
    pl.semaphore_wait(barrier, (1 + len(plan.bits) if n > 1 else 0) + beside)

    def normalize_rows(index):
        at = span(index)
        for o in range(n):
            gain, shift = small[o, 0:1, LANES:].astype(f32), small[o, 1:2, LANES:].astype(f32)
            ns[0:rows, o * width : (o + 1) * width] = (xs[o, at, :].astype(f32) * gain + shift).astype(bf16)

    def bias_row(r, first, width):
        per = LANES // plan.bias_cols
        groups = []
        for g in range(first // LANES, (first + width) // LANES):
            total = small[g * per, r : r + 1, :LANES].astype(f32)
            for o in range(1, per):
                total = total + small[g * per + o, r : r + 1, :LANES].astype(f32)
            groups.append(total)
        return jnp.concatenate(groups, axis=1)

    def turn_rows(source, target, index):
        def staged(o):
            return ns.at[pl.ds(0, width), pl.ds(o % 2 * rows, rows)]

        def copy(o):
            return pltpu.make_async_copy(staged(o), target.at[o, :, span(index)], turn_sem.at[o % 2])

        for o in range(n):
            if o >= 2:
                copy(o - 2).wait()
            staged(o)[...] = source[o, span(index), :].T
            copy(o).start()
        for o in range(max(n - 2, 0), n):
            copy(o).wait()

    def attn_rows(index):
        at = span(index)
        turn_rows(xs, xhat_out, index)
        normalize_rows(index)
        for r, target in enumerate((q, k, v)):
            proj = dot_n(ns[0:rows, :], wa[:, r * local : (r + 1) * local]) + bias_row(r, 0, local)
            if r == 2:
                target[at, :] = proj.astype(bf16)
            else:
                for g in range(0, local, LANES):
                    target[at, g : g + LANES] = turn(
                        proj[:, g : g + LANES], own[at, :], sines[at, :], 1.0
                    ).astype(bf16)

    def mlp_rows(index):
        at = span(index)
        normalize_rows(index)
        for r in range(plan.n_mlp):
            cols = slice(r * local, (r + 1) * local)
            pre = dot_n(ns[0:rows, :], wm[:, cols]) + bias_row(3 + r, 0, local)
            value, grad = gelu_and_slope(pre)
            hidden[at, cols] = value.astype(bf16)
            slope[at, cols] = grad.astype(bf16)

    def attend(pair, carry):
        total = plan.group
        block = min(QUERY_ROWS, total)
        lanes = pl.ds(pl.multiple_of(pair * LANES, LANES), LANES)
        for start in range(0, total, block):
            stop = start + block
            here = pl.ds(start, block)
            allowed = attend_mask(begins_of(lengths, start, block), start, block, stop)
            query = q[here, lanes]
            results, logs = [], []
            for head in range(LANES // HEAD):
                mine = head_lanes(block, head)
                chosen = jnp.where(mine, query, jnp.zeros_like(query)) * HEAD ** (-0.5)
                scores = jnp.where(allowed, dot_t(chosen.astype(bf16), k[:stop, lanes]), masked_score)
                top = jnp.max(scores, axis=1, keepdims=True)
                weights = jnp.exp(scores - top)
                total_weight = jnp.sum(weights, axis=1, keepdims=True)
                results.append(dot_n(weights.astype(bf16), v[:stop, lanes]) / total_weight)
                logs.append(top + jnp.log(total_weight))
            first = head_lanes(block, 0)
            att[here, lanes] = jnp.where(first, results[0], results[1]).astype(bf16)
            which = lax.broadcasted_iota(jnp.int32, (block, LANES), 1)
            held = lse[here, :]
            for head in range(LANES // HEAD):
                held = jnp.where(which == pair * (LANES // HEAD) + head, logs[head], held)
            lse[here, :] = held
        return carry

    tall = min(512, plan.group)

    def out_tile(t):
        o = owner_of(t)

        def part(j, carry):
            at = pl.ds(pl.multiple_of(j * tall, tall), tall)
            total = dot_n(att[at, :], wd[o, :local, :]) + dot_n(hidden[at, :], wd[o, local:, :])
            xs[t, at, :] = total.astype(bf16)
            return carry

        lax.fori_loop(0, plan.group // tall, part, 0)

    def tile_source(t, index):
        return xs.at[t, span(index), :]

    def tile_landing(t, slot):
        return land.at[t, slot]

    out_sum = LineSum(
        place, line, plan.d_tiles, tile_source, tile_landing, (sum_up_send, sum_up_recv, sum_down_send, sum_down_recv)
    )

    def all_tiles(fn):
        lax.fori_loop(0, plan.d_tiles, lambda t, carry: (fn(t), carry)[1], 0)

    def cot_rows(index):
        at = span(index)
        turn_rows(cs, cot_out, index)
        for o in range(n):
            sums[0:1, o * width : (o + 1) * width] += jnp.sum(cs[o, at, :].astype(f32), axis=0, keepdims=True)

    def back_rows(index):
        at = span(index)
        for r in range(1 + plan.n_mlp):
            grad = dot_t(cs[0, at, :], wd[0, r * local : (r + 1) * local, :])
            for o in range(1, n):
                grad = grad + dot_t(cs[o, at, :], wd[o, r * local : (r + 1) * local, :])
            if r == 0:
                att[at, :] = grad.astype(bf16)
            else:
                cols = slice((r - 1) * local, r * local)
                slope[at, cols] = (grad * slope[at, cols].astype(f32)).astype(bf16)

    def attend_back(pair, carry):
        block = min(QUERY_ROWS, plan.group)
        scale = HEAD ** (-0.5)
        k_sum[...] = jnp.zeros_like(k_sum)
        v_sum[...] = jnp.zeros_like(v_sum)
        lanes = pl.ds(pl.multiple_of(pair * LANES, LANES), LANES)
        which = lax.broadcasted_iota(jnp.int32, (block, LANES), 1)
        for start in range(0, plan.group, block):
            stop = start + block
            here = pl.ds(start, block)
            allowed = attend_mask(begins_of(lengths, start, block), start, block, stop)
            q_sum = jnp.zeros((block, LANES), f32)
            for head in range(LANES // HEAD):
                mine = head_lanes(block, head)
                query = jnp.where(mine, q[here, lanes], jnp.zeros((block, LANES), bf16)) * scale
                query = query.astype(bf16)
                cot = jnp.where(mine, att[here, lanes], jnp.zeros((block, LANES), bf16))
                level = jnp.sum(
                    jnp.where(which == pair * (LANES // HEAD) + head, lse[here, :], 0.0), axis=1, keepdims=True
                )
                scores = dot_t(query, k[:stop, lanes]) - level
                probs = jnp.where(allowed, jnp.exp(scores), 0.0)
                prob_grad = dot_t(cot, v[:stop, lanes])
                mean = jnp.sum(probs * prob_grad, axis=1, keepdims=True)
                score_grad = (probs * (prob_grad - mean)).astype(bf16)
                q_step = dot_n(score_grad, k[:stop, lanes])
                q_sum = jnp.where(mine, q_step * scale, q_sum)
                k_sum[:stop, :] += dot_s(score_grad, query)
                v_sum[:stop, :] += dot_s(probs.astype(bf16), cot)
            q[here, lanes] = turn(
                q_sum, own[here, :], sines[here, :], -1.0
            ).astype(bf16)
        k[:, lanes] = turn(k_sum[...], own[...], sines[...], -1.0).astype(bf16)
        v[:, lanes] = v_sum[...].astype(bf16)
        return carry

    def dh_tile(t):
        at = pl.ds(pl.multiple_of(t * width, width), width)
        total = dot_t(slope[...], wm[at, :])
        for r, grad in enumerate((q, k, v)):
            total = total + dot_t(grad[...], wa[at, r * local : (r + 1) * local])
        cs[t] = total.astype(bf16)

    def normalize_own():
        for j in range(strip_count):
            row_load(j).wait()
            at = slice(j * strip_rows, (j + 1) * strip_rows)
            value = wide[j % 2]
            mean = jnp.mean(value, axis=1, keepdims=True)
            centered = value - mean
            scale = lax.rsqrt(jnp.mean(centered * centered, axis=1, keepdims=True) + norm_eps)
            normed = (centered * scale).astype(bf16)
            to = pl.ds(pl.multiple_of(place * rows + j * strip_rows, strip_rows), strip_rows)
            for o in range(n):
                xs[o, to, :] = normed[:, o * width : (o + 1) * width]
            first = lax.broadcasted_iota(jnp.int32, (strip_rows, LANES), 1) == 0
            stats[at, :] = jnp.where(first, mean, scale)
            if j + 2 < 2 * strip_count:
                row_load(j + 2).start()

    def mask_cot():
        for j in range(strip_count, 2 * strip_count):
            row_load(j).wait()
            first = place * rows + (j - strip_count) * strip_rows
            places = first + lax.broadcasted_iota(jnp.int32, (strip_rows, 1), 0)
            masked = jnp.where(places < ends_of(lengths)[-1], wide[j % 2], 0.0).astype(bf16)
            to = pl.ds(pl.multiple_of(first, strip_rows), strip_rows)
            for o in range(n):
                cs[o, to, :] = masked[:, o * width : (o + 1) * width]
            if j + 2 < 2 * strip_count:
                row_load(j + 2).start()

    def make_tables():
        for load in table_loads:
            load.wait()
        block_rows = min(QUERY_ROWS, plan.group)
        ends = ends_of(lengths)
        at_ends = [pl.ds(jnp.minimum(end, plan.group - 1), 1) for end in ends]
        end_cosines, end_sines = [own[row, :] for row in at_ends], [sines[row, :] for row in at_ends]
        for start in range(0, plan.group, block_rows):
            at = pl.ds(start, block_rows)
            places = start + lax.broadcasted_iota(jnp.int32, (block_rows, LANES), 0)
            begin_cos, begin_sin = end_cosines[0], end_sines[0]
            for end, end_cos, end_sin in zip(ends[1:], end_cosines[1:], end_sines[1:]):
                begin_cos = jnp.where(places >= end, end_cos, begin_cos)
                begin_sin = jnp.where(places >= end, end_sin, begin_sin)
            place_c, place_s = own[at, :], sines[at, :]
            cosine = place_c * begin_cos + place_s * begin_sin
            sine = place_s * begin_cos - place_c * begin_sin
            lane = lax.rem(lax.broadcasted_iota(jnp.int32, (block_rows, LANES), 1), HEAD)
            own[at, :] = jnp.where(lane < ROT, cosine, 1.0)
            sines[at, :] = jnp.where(lane < ROT // 2, -sine, jnp.where(lane < ROT, sine, 0.0))

    def mixed_copy(t):
        cols = pl.ds(pl.multiple_of(owner_of(t) * width, width), width)
        return pltpu.make_async_copy(mixed.at[lax.rem(t, 2)], mixed_out.at[:, cols], mixed_sem.at[lax.rem(t, 2)])

    def finish_tile(t):
        @pl.when(t >= 2)
        def _():
            mixed_copy(t - 2).wait()
        out_sum.last(t, mixed.at[lax.rem(t, 2)])
        mixed_copy(t).start()

    small_load.wait()
    w_start(3)
    round_in(0, 3, wa)
    w_start(0)
    normalize_own()
    z_start(0, 1)
    round_in(3, 3 + plan.n_mlp, wm)
    mask_cot()
    round_down()
    make_tables()
    sums[...] = jnp.zeros_like(sums)
    lse[...] = jnp.zeros_like(lse)
    write(4)
    w_arrive(0, plan.single)
    w_start(1)
    w_arrive(3, plan.single)
    z_arrive(0, 1)
    cot_start(1)
    w_arrive(3, plan.several)
    w_arrive(0, plan.several)
    w_arrive(3, plan.odd)
    w_arrive(0, plan.odd)
    write(0, 2)
    at_distance(0, cot_rows)
    at_distance(0, attn_rows)
    if line > 2:
        at_distance(1, attn_rows)
    w_arrive(1, plan.single)
    w_start(2)
    for step in range(2, line - 1):
        z_arrive(0, step)
        cot_start(step)
        at_distance(step, attn_rows)
    w_arrive(1, plan.several)
    w_arrive(1, plan.odd)
    write(1)
    near = max(line - 2, 0)
    lax.fori_loop(
        jnp.maximum(place - near, 0), jnp.minimum(place + near, line - 1) + 1,
        lambda c, carry: (mlp_rows(c), carry)[1], 0,
    )
    w_arrive(2, plan.single)
    if line > 2:
        z_arrive(0, line - 1)
        cot_start(line - 1)
    at_distance(line - 1, lambda c: (attn_rows(c), mlp_rows(c))[0])
    write(*hidden_at)
    pairs = local // LANES
    lax.fori_loop(0, pairs // 2, attend, 0)
    w_arrive(2, plan.several)
    z_arrive(1, 1)
    lax.fori_loop(pairs // 2, pairs, attend, 0)
    write(6)
    if line > 2:
        at_distance(1, cot_rows)
    for step in range(1, line):
        for up in (True, False):
            left = place != step - 1 if up else place != line - step
            @pl.when(left & sends(step, up))
            def _():
                z_copy(0, step, up).wait_send()

    def some_tiles(first, stop):
        def step(t, carry):
            out_tile(t)
            return carry

        lax.fori_loop(first, stop, step, 0)

    split = min(6, n)
    w_arrive(2, [m for m in plan.odd if m < 2])
    some_tiles(0, min(2, n))
    out_sum.advance(2)
    w_arrive(2, [m for m in plan.odd if 2 <= m < split])
    some_tiles(min(2, n), split)
    w_arrive(2, [m for m in plan.odd if m >= split])
    some_tiles(split, n)
    out_copy(6).wait()
    def settle(near):
        for up in (True, False):
            now = (place < line // 2) if up == near else (place >= line // 2)

            @pl.when(now)
            def _():
                for step in range(1, line):
                    z_sent(1, step, up)

    settle(True)
    out_sum.advance(1)
    at_distance(0, back_rows)
    if line > 2:
        at_distance(1, back_rows)
    out_sum.advance(1)
    for step in range(2, line - 1):
        z_arrive(1, step)
        at_distance(step, lambda c: (cot_rows(c), back_rows(c))[0])
    out_sum.advance(1)
    if line > 2:
        z_arrive(1, line - 1)
    at_distance(line - 1, lambda c: (cot_rows(c), back_rows(c))[0])
    write(3, *da_at)
    settle(False)
    out_sum.advance(1)
    first = out_sum.take(pairs)

    def back_pair(pair, carry):
        attend_back(pair, carry)
        out_sum.step(first + pair)
        return carry

    lax.fori_loop(0, pairs, back_pair, 0)
    write(*qkv_at)
    count = plan.d_tiles
    then = out_sum.take(2)

    def dh_step(t, carry):
        dh_tile(t)

        @pl.when(lax.rem(t, count // 2) == count // 2 - 1)
        def _():
            out_sum.step(then + t // (count // 2))
        return carry

    lax.fori_loop(0, count, dh_step, 0)
    write(5)
    out_sum.finish_steps()
    all_tiles(finish_tile)
    for t in range(max(count - 2, 0), count):
        mixed_copy(t).wait()

    all_tiles(out_sum.sent)
    for flow in range(4):
        for mask in range(1, n):
            for half in halves(flow):
                w_copy(flow, mask, half).wait_send()
    for j in range(len(outs)):
        if j != 6:
            out_copy(j).wait()


def forward(plan, x, out_grad, w, wd, small, lengths):
    any_space = pl.BlockSpec(memory_space=pl.ANY)
    n, line, group, model, local, rows = (
        plan.n_dp, plan.n_line, plan.group, plan.model, plan.local, plan.rows
    )
    low = lambda *shape: jax.ShapeDtypeStruct(shape, bf16)
    full = lambda *shape: jax.ShapeDtypeStruct(shape, f32)
    tiles = 4 + 2 * plan.n_mlp
    out_shape = [
        low(model, plan.attn), low(model, plan.mlp), low(n, 16, LANES + plan.out_cols),
        full(8, model), full(rows, LANES), low(n, group, plan.width), low(tiles, group, local),
        low(n, plan.width, group), low(n, plan.width, group), full(rows, model),
    ]
    act = pltpu.VMEM((n, group, plan.width), bf16)
    head = pltpu.VMEM((group, local), bf16)
    hide = pltpu.VMEM((group, plan.mlp), bf16)
    lane = pltpu.VMEM((group, LANES), f32)
    scratch = lambda s: pltpu.VMEM(s.shape, s.dtype)
    dma = pltpu.SemaphoreType.DMA
    return pl.pallas_call(
        partial(forward_kernel, plan),
        in_specs=[any_space] * 5 + [pl.BlockSpec(memory_space=pltpu.SMEM)] + [any_space] * 2,
        out_specs=[any_space] * 10,
        out_shape=out_shape,
        scratch_shapes=[scratch(s) for s in out_shape[:2]]
        + [pltpu.VMEM((n, plan.down, plan.out_cols), bf16), scratch(out_shape[2]), act]
        + [pltpu.VMEM((max(rows, plan.width), model), bf16), scratch(out_shape[3]), act, head, head, head, head, lane]
        + [hide, hide] + [lane] * 4 + [scratch(out_shape[4])]
        + [pltpu.VMEM((plan.d_tiles, line + 1, rows, plan.width), bf16)]
        + [
            pltpu.VMEM((2, min(32, rows), model), f32), pltpu.VMEM((2, rows, plan.width), f32),
        ]
        + [dma((2,)), dma((2,)), dma((5,)), dma((2, 4)), dma((6 + tiles,)), dma((8 * n,)), dma((8 * n,))]
        + [dma((2 * line,))] * 4
        + [dma((plan.d_tiles, line + 1))] * 4,
        compiler_params=pltpu.CompilerParams(
            collective_id=0, has_side_effects=True, vmem_limit_bytes=63 << 20
        ),
        cost_estimate=pl.CostEstimate(flops=60 * 10**9, bytes_accessed=80 << 20, transcendentals=0),
    )(x, out_grad, w, wd, small, lengths, *angle_tables(group))


def backward_kernel(
    plan,
    xhat_in, cot_in, tiles_in, dh_in, wa_in, wm_in, sums_in,
    down_out, in_out, small_out, rows_out, dh_out,
    turned, operand, dh, sent, core_in, held, cube_in, land,
    w_own, fin, fin_turned, dh_fin, small, small_in, shares,
    load_sem, turn_sem, operand_sem, fin_sem, dh_sem, core_send, core_recv, cube_send, cube_recv,
    up_send, up_recv, down_send, down_recv,
    small_send, small_recv, share_send, share_recv, credit,
):
    n, line = plan.n_dp, plan.n_line
    me, place = lax.axis_index("dp"), lax.axis_index("tensor")
    rows, local, group, model, in_rows = plan.rows, plan.local, plan.group, plan.model, plan.in_rows
    MESH = pl.DeviceIdType.MESH
    half_rows, pairs_n, n_bits = in_rows // 2, n // 2, len(plan.bits)
    orders = (plan.bits, plan.bits[::-1])
    n_down, n_mlp = 1 + plan.n_mlp, plan.n_mlp
    def owner(mask):
        index = me
        for b in [1] + plan.bits:
            if mask & b:
                index = index + b - 2 * b * lax.rem(index // b, 2)
        return index

    def peer(bit):
        return {"dp": owner(bit)}

    def position(mask, order):
        return sum((1 if mask & b else 0) << (n_bits - 1 - p) for p, b in enumerate(order))

    width, d_tiles = plan.width, plan.d_tiles
    own_rows = pl.ds(pl.multiple_of(me * in_rows, in_rows), in_rows)

    whole = [
        (dh_in, dh),
        (wa_in.at[own_rows, :], w_own.at[:, pl.ds(0, plan.attn)]),
        (wm_in.at[own_rows, :], w_own.at[:, pl.ds(plan.attn, plan.mlp)]),
    ]
    for j, (a, b) in enumerate(whole):
        pltpu.make_async_copy(a, b, load_sem.at[j]).start()

    def loaded(*which):
        for j in which:
            pltpu.make_async_copy(whole[j][0], whole[j][1], load_sem.at[j]).wait()

    barrier = pltpu.get_barrier_semaphore()
    for b in [1] + plan.bits:
        pl.semaphore_signal(barrier, inc=1, device_id=peer(b), device_id_type=MESH)
    for d in range(1, line):
        pl.semaphore_signal(
            barrier, inc=1, device_id={"tensor": lax.rem(place + d, line)}, device_id_type=MESH
        )

    def share_copy(d, arriving):
        source = lax.rem(place + line - d, line) if arriving else place
        return pltpu.make_async_remote_copy(
            src_ref=shares, dst_ref=rows_out.at[source],
            send_sem=share_send.at[d], recv_sem=share_recv.at[d],
            device_id={"tensor": lax.rem(place + d, line)}, device_id_type=MESH,
        )

    share_own = pltpu.make_async_copy(shares, rows_out.at[place], share_send.at[0])

    masks = [2 * j + 1 for j in range(pairs_n)] + [2 * j for j in range(pairs_n)]

    def turned_copy(source, j):
        return pltpu.make_async_copy(
            source.at[owner(masks[j])], turned.at[pl.ds(j * in_rows, in_rows), :], turn_sem.at[j]
        )

    def turned_start(source):
        for j in range(n):
            turned_copy(source, j).start()

    def turned_wait(source):
        for j in range(n):
            turned_copy(source, j).wait()

    tiles_n = n_down + n_mlp + 3

    def operand_copy(t):
        slot = lax.rem(t, 3)
        return pltpu.make_async_copy(tiles_in.at[t], operand.at[slot], operand_sem.at[slot])

    def core_copy(t, base):
        return pltpu.make_async_remote_copy(
            src_ref=sent.at[lax.rem(t, 2)], dst_ref=core_in.at[t - base],
            send_sem=core_send.at[lax.rem(t, 2)], recv_sem=core_recv.at[t - base],
            device_id=peer(1), device_id_type=MESH,
        )

    def cube_copy(slot, half, phase):
        count = pairs_n >> (phase + 1)
        first = pairs_n - 2 * count
        at = half * n_bits + phase
        return pltpu.make_async_remote_copy(
            src_ref=held.at[slot, half, pl.ds(count, count)],
            dst_ref=cube_in.at[slot, half, pl.ds(first, count)],
            send_sem=cube_send.at[slot, at], recv_sem=cube_recv.at[slot, at],
            device_id=peer(orders[half][phase]), device_id_type=MESH,
        )

    piece = min(2, pairs_n) * in_rows

    def send_core(t, base):
        @pl.when(t >= base + 2)
        def _():
            core_copy(t - 2, base).wait_send()
        slot = lax.rem(t, 3)
        for at in range(0, pairs_n * in_rows, piece):
            sent[lax.rem(t, 2), at : at + piece, :] = dot_n(turned[at : at + piece, :], operand[slot]).astype(bf16)
        core_copy(t, base).start()
        if base:
            row = lax.rem(t - base + 3, n_mlp + 3)
            small[0, pl.ds(row, 1), :] = jnp.sum(operand[slot].astype(f32), axis=0, keepdims=True)

    def keep_core(t, base):
        core_copy(t, base).wait_recv()
        for first in range(0, pairs_n * in_rows, piece):
            kept = pairs_n * in_rows + first
            total = dot_n(turned[kept : kept + piece, :], operand[lax.rem(t, 3)])
            total = total + core_in[t - base, first : first + piece, :].astype(f32)
            for at in range(0, piece, half_rows):
                j, half = divmod((first + at) // half_rows, 2)
                held[t, half, position(2 * j, orders[half])] = total[at : at + half_rows].astype(bf16)
        for half in range(2):
            if n_bits:
                cube_copy(t, half, 0).start()

    def scatter(base, stop):
        def step(t, carry):
            operand_copy(t).wait()

            @pl.when(t + 1 < tiles_n)
            def _():
                operand_copy(t + 1).start()
            send_core(t, base)

            @pl.when(t >= base + 1)
            def _():
                keep_core(t - 1, base)
            return carry

        lax.fori_loop(base, stop, step, 0)
        keep_core(stop - 1, base)
        for t in range(max(stop - 2, base), stop):
            core_copy(t, base).wait_send()

    def cube_step(base, stop, phase):
        count = pairs_n >> (phase + 1)
        first = pairs_n - 2 * count
        down = base == 0
        depth = 1 if down else 2

        def result(t):
            return t if down else lax.rem(t - n_down + 3, n_mlp + 3)

        def fin_copy(t):
            source = fin_turned if down else fin.at[lax.rem(t, 2)]
            target = down_out if down else in_out
            return pltpu.make_async_copy(source, target.at[result(t)], fin_sem.at[lax.rem(t, 2)])

        def step(t, carry):
            slot = t
            if phase == n_bits - 1:
                @pl.when(t >= base + depth)
                def _():
                    fin_copy(t - depth).wait()
            for half in range(2):
                cube_copy(slot, half, phase).wait_recv()
                total = (
                    held[slot, half, 0:count].astype(f32)
                    + cube_in[slot, half, first : first + count].astype(f32)
                )
                if phase < n_bits - 1:
                    held[slot, half, 0:count] = total.astype(bf16)
                    cube_copy(slot, half, phase + 1).start()
                else:
                    fin[lax.rem(t, 2), half * half_rows : (half + 1) * half_rows, :] = total[0]
            if phase == n_bits - 1:
                if down:
                    fin_turned[...] = fin[lax.rem(t, 2)].T
                fin_copy(t).start()
                if not down:
                    weight = w_own[:, pl.ds(pl.multiple_of(result(t) * local, local), local)].astype(f32)
                    product = weight * fin[lax.rem(t, 2)]
                    extra = weight * small[n_bits + 1, pl.ds(result(t), 1), :]
                    for g in range(0, local, LANES):
                        shares[0] += product[:, g : g + LANES]
                        shares[1] += extra[:, g : g + LANES]
            return carry

        lax.fori_loop(base, stop, step, 0)
        if phase == n_bits - 1:
            for t in range(max(stop - depth, base), stop):
                fin_copy(t).wait()

    def cube_sent(t):
        for half in range(2):
            for phase in range(n_bits):
                cube_copy(t, half, phase).wait_send()

    def tile_of(buffer):
        def source(t, index):
            return buffer.at[t, pl.ds(pl.multiple_of(index * rows, rows), rows), :]
        return source

    dh_sum = LineSum(
        place, line, d_tiles, tile_of(dh), lambda t, slot: land.at[t, slot],
        (up_send, up_recv, down_send, down_recv),
    )
    def sum_copy(target, t):
        cols = pl.ds(pl.multiple_of(t * width, width), width)
        return pltpu.make_async_copy(dh_fin.at[lax.rem(t, 2)], target.at[:, cols], dh_sem.at[lax.rem(t, 2)])

    def finish(flow, target, count):
        def step(t):
            @pl.when(t >= 2)
            def _():
                sum_copy(target, t - 2).wait()
            flow.last(t, dh_fin.at[lax.rem(t, 2)])
            sum_copy(target, t).start()

        tiles(0, count, step)
        for t in range(max(count - 2, 0), count):
            sum_copy(target, t).wait()

    def tiles(first, stop, fn):
        lax.fori_loop(first, stop, lambda t, carry: (fn(t), carry)[1], 0)

    def small_copy(j):
        return pltpu.make_async_remote_copy(
            src_ref=small.at[j], dst_ref=small_in.at[j],
            send_sem=small_send.at[j], recv_sem=small_recv.at[j],
            device_id=peer(([1] + plan.bits)[j]), device_id_type=MESH,
        )

    def small_step(j):
        small_copy(j).wait_recv()
        small[j + 1] = small[j] + small_in[j]
        if j < n_bits:
            small_copy(j + 1).start()

    turned_start(cot_in)
    operand_copy(0).start()
    shares[...] = jnp.zeros_like(shares)
    small[0] = jnp.zeros_like(small[0])
    for r in range(model // local):
        small[0, 8 + r : 9 + r, :] = sums_in[0:1, r * local : (r + 1) * local]
    pl.semaphore_wait(barrier, 1 + n_bits + line - 1)
    loaded(0)
    dh_sum.advance(2)
    turned_wait(cot_in)
    scatter(0, n_down)
    pl.semaphore_signal(credit, inc=1, device_id=peer(1), device_id_type=MESH)
    turned_start(xhat_in)
    dh_sum.advance(2)
    turned_wait(xhat_in)
    pl.semaphore_wait(credit, 1)
    scatter(n_down, tiles_n)
    small_copy(0).start()
    dh_sum.advance(2)
    for phase in range(n_bits - 1):
        cube_step(0, n_down, phase)
    small_step(0)
    dh_sum.advance(1)
    for j in range(1, n_bits + 1):
        small_step(j)
    loaded(1, 2)
    for phase in range(n_bits - 1):
        cube_step(n_down, n_down + n_mlp, phase)
    dh_sum.advance(2)
    cube_step(0, n_down, n_bits - 1)
    dh_sum.advance(2)
    for phase in range(n_bits - 1):
        cube_step(n_down + n_mlp, tiles_n, phase)
    dh_sum.advance(1)
    cube_step(n_down, n_down + n_mlp, n_bits - 1)
    dh_sum.finish_steps()
    finish(dh_sum, dh_out, d_tiles)
    cube_step(n_down + n_mlp, tiles_n, n_bits - 1)
    share_own.start()
    for d in range(1, line):
        share_copy(d, False).start()
    small_done = pltpu.make_async_copy(small.at[n_bits + 1], small_out, load_sem.at[0])
    small_done.start()
    tiles(0, tiles_n, cube_sent)
    tiles(0, d_tiles, dh_sum.sent)
    for j in range(n_bits + 1):
        small_copy(j).wait_send()
    share_own.wait()
    for d in range(1, line):
        share_copy(d, False).wait_send()
        share_copy(d, True).wait_recv()
    small_done.wait()


def backward(plan, xhat, cot, tiles, dh, wa, wm, sums):
    any_space = pl.BlockSpec(memory_space=pl.ANY)
    vmem = pl.BlockSpec(memory_space=pltpu.VMEM)
    n, line, group, model, local = plan.n_dp, plan.n_line, plan.group, plan.model, plan.local
    rows, in_rows, n_bits, pairs_n = plan.rows, plan.in_rows, len(plan.bits), n // 2
    n_down = 1 + plan.n_mlp
    small_rows = 8 + -(-(model // local) // 8) * 8
    width, d_tiles = plan.width, plan.d_tiles
    low = lambda *shape: pltpu.VMEM(shape, bf16)
    full = lambda *shape: pltpu.VMEM(shape, f32)
    dma = pltpu.SemaphoreType.DMA
    out = lambda dtype, *shape: jax.ShapeDtypeStruct(shape, dtype)
    slots = n_down + plan.n_mlp + 3
    return pl.pallas_call(
        partial(backward_kernel, plan),
        in_specs=[any_space] * 6 + [vmem],
        out_specs=[any_space] * 5,
        out_shape=[
            out(f32, n_down, local, in_rows), out(f32, 3 + plan.n_mlp, in_rows, local),
            out(f32, small_rows, local),
            out(f32, line, 2, in_rows, LANES), out(f32, rows, model),
        ],
        scratch_shapes=[
            low(n * in_rows, group), low(3, group, local), low(d_tiles, group, width),
            low(2, pairs_n * in_rows, local), low(3 + plan.n_mlp, pairs_n * in_rows, local),
            low(slots, 2, pairs_n, in_rows // 2, local), low(slots, 2, max(pairs_n - 1, 1), in_rows // 2, local),
            low(d_tiles, line + 1, rows, width),
            low(in_rows, plan.attn + plan.mlp), full(2, in_rows, local), full(local, in_rows), full(2, rows, width),
            full(n_bits + 2, small_rows, local), full(n_bits + 1, small_rows, local), full(2, in_rows, LANES),
            dma((3,)), dma((n,)), dma((3,)), dma((2,)), dma((2,)), dma((2,)), dma((3 + plan.n_mlp,)),
            dma((slots, max(2 * n_bits, 1))), dma((slots, max(2 * n_bits, 1))),
            dma((d_tiles, line + 1)), dma((d_tiles, line + 1)), dma((d_tiles, line + 1)), dma((d_tiles, line + 1)),
            dma((n_bits + 1,)), dma((n_bits + 1,)), dma((line,)), dma((line,)),
            pltpu.SemaphoreType.REGULAR,
        ],
        compiler_params=pltpu.CompilerParams(
            collective_id=1, has_side_effects=True, vmem_limit_bytes=63 << 20
        ),
        cost_estimate=pl.CostEstimate(flops=80 * 10**9, bytes_accessed=80 << 20, transcendentals=0),
    )(xhat, cot, tiles, dh, wa, wm, sums)


def adam_update(weight, moment_one, moment_two, gradient, step_rate, decay_factor):
    first_new = beta_first * moment_one + (1.0 - beta_first) * gradient
    second_new = beta_second * moment_two + (1.0 - beta_second) * gradient * gradient
    corrected = first_new / (1.0 - beta_first**STEP)
    spread = jnp.sqrt(second_new / (1.0 - beta_second**STEP))
    return (
        weight - step_rate * (corrected / (spread + adam_eps) + decay_factor * weight),
        first_new,
        second_new,
    )


def per_device(
    block_input,
    out_grad,
    seq_lengths,
    in_weight,
    down_weight,
    column_bias,
    vector_params,
    in_first,
    in_second,
    down_first,
    down_second,
    bias_first,
    bias_second,
    vector_first,
    vector_second,
):
    n_dp = lax.axis_size("dp")
    n_tensor = lax.axis_size("tensor")
    own_rows, model = block_input.shape
    group = own_rows * n_tensor
    in_rows, widths, local = in_weight.shape
    out_cols = down_weight.shape[2]
    n_mlp = widths - 3
    attn_width, mlp_width = 3 * local, n_mlp * local

    me = lax.axis_index("dp")
    plan = Plan(n_dp, n_tensor, own_rows, model, in_rows, local, n_mlp, out_cols)
    share = LANES // plan.bias_cols
    lane = lax.broadcasted_iota(jnp.int32, (widths, LANES), 1) // plan.bias_cols
    bias_tile = jnp.where(lane == lax.rem(me, share), jnp.tile(column_bias, (1, share)), 0.0)
    small = jnp.concatenate(
        [jnp.pad(bias_tile, ((0, 16 - widths), (0, 0))), jnp.pad(vector_params, ((0, 13), (0, 0)))], axis=1
    ).astype(bf16)
    (
        w_attn, w_mlp, vectors, cot_sums, stats, dh_part, tiles, xhat_turned, cot_turned, mixed,
    ) = forward(plan, block_input, out_grad, in_weight.transpose(1, 0, 2), down_weight, small, seq_lengths)
    down_grad, in_grad, small_grad, shares, dh = backward(
        plan, xhat_turned, cot_turned, tiles, dh_part, w_attn, w_mlp, cot_sums
    )
    vector_vals = vectors[:, :3, LANES:].transpose(1, 0, 2).reshape(3, model).astype(f32)
    gain, out_bias = vector_vals[0], vector_vals[2]
    block_out = block_input + (mixed + out_bias)
    mean, inv_scale = stats[:, :1], stats[:, 1:2]
    xhat = (block_input - mean) * inv_scale
    places = lax.axis_index("tensor") * own_rows + lax.broadcasted_iota(jnp.int32, (own_rows, 1), 0)
    cot_live = jnp.where(places < jnp.sum(seq_lengths), out_grad, 0.0)

    dxhat = dh * gain
    input_grad = cot_live + inv_scale * (
        dxhat
        - jnp.mean(dxhat, axis=-1, keepdims=True)
        - xhat * jnp.mean(dxhat * xhat, axis=-1, keepdims=True)
    )

    bias_full = small_grad[:widths]
    own_vectors = vector_params.astype(bf16).astype(f32)
    in_reduced = (
        in_grad * own_vectors[0][None, :, None] + own_vectors[1][None, :, None] * bias_full[:, None, :]
    ).transpose(1, 0, 2)
    down_reduced = down_grad
    bias_reduced = lax.dynamic_slice_in_dim(bias_full, me * plan.bias_cols, plan.bias_cols, 1)
    out_sums = small_grad[8 : 8 + model // local].reshape(-1)
    vector_reduced = jnp.stack(
        [
            jnp.sum(shares[:, 0], axis=(0, 2)),
            jnp.sum(shares[:, 1], axis=(0, 2)),
            lax.dynamic_slice_in_dim(out_sums, me * out_cols, out_cols, 0),
        ]
    )

    in_new, in_one, in_two = adam_update(
        in_weight, in_first, in_second, in_reduced, rate_in, weight_decay
    )
    down_new, down_one, down_two = adam_update(
        down_weight, down_first, down_second, down_reduced, rate_down, weight_decay
    )
    bias_new, bias_one, bias_two = adam_update(
        column_bias, bias_first, bias_second, bias_reduced, rate_vector, 0.0
    )
    vector_new, vector_one, vector_two = adam_update(
        vector_params, vector_first, vector_second, vector_reduced, rate_vector, 0.0
    )
    return (
        block_out,
        input_grad,
        in_new,
        in_one,
        in_two,
        down_new,
        down_one,
        down_two,
        bias_new,
        bias_one,
        bias_two,
        vector_new,
        vector_one,
        vector_two,
    )


def widths_down(down_weight):
    return down_weight.shape[0] * down_weight.shape[1]


def solution(mesh):
    return jax.shard_map(
        per_device,
        mesh=mesh,
        in_specs=(
            P(("dp", "tensor"), None),
            P(("dp", "tensor"), None),
            P("dp", None),
            P("dp", None, "tensor"),
            P(None, "tensor", "dp"),
            P(None, ("tensor", "dp")),
            P(None, "dp"),
            P("dp", None, "tensor"),
            P("dp", None, "tensor"),
            P(None, "tensor", "dp"),
            P(None, "tensor", "dp"),
            P(None, ("tensor", "dp")),
            P(None, ("tensor", "dp")),
            P(None, "dp"),
            P(None, "dp"),
        ),
        out_specs=(
            P(("dp", "tensor"), None),
            P(("dp", "tensor"), None),
            P("dp", None, "tensor"),
            P("dp", None, "tensor"),
            P("dp", None, "tensor"),
            P(None, "tensor", "dp"),
            P(None, "tensor", "dp"),
            P(None, "tensor", "dp"),
            P(None, ("tensor", "dp")),
            P(None, ("tensor", "dp")),
            P(None, ("tensor", "dp")),
            P(None, "dp"),
            P(None, "dp"),
            P(None, "dp"),
        ),
        check_vma=False,
    )
```
